32 devices in a mesh: rows: 8 (over z, y), seq: 4 (over x, core).
Axes of the slice: x: 2, y: 2, z: 4, core: 2. Of those that a mesh axis runs over, the one named last changes fastest.
Arguments:
- layer_input: bfloat16 [16, 1280, 1024], P('rows', 'seq'), may hold values from -6 to 6
- doc_ids: int32 [16, 1280], P('rows'), may hold values from 0 to 8, as said below
- norm1_gain: float32 [1024], replicated, may hold values from 0.1 to 1.9
- w_query: bfloat16 [1024, 480], replicated, may hold values from -0.25 to 0.25
- w_keyval: bfloat16 [1024, 320], replicated, may hold values from -0.25 to 0.25
- w_out: bfloat16 [1024, 1024], replicated, may hold values from -0.75 to 0.75
- norm2_gain: float32 [1024], replicated, may hold values from 0.1 to 1.9
- w_gate: bfloat16 [1024, 2816], replicated, may hold values from -0.1875 to 0.1875
- w_up: bfloat16 [1024, 2816], replicated, may hold values from -0.1875 to 0.1875
- w_down: bfloat16 [2816, 1024], replicated, may hold values from -0.109375 to 0.109375
- cotangent: bfloat16 [16, 1280, 1024], P('rows', 'seq'), may hold values from -6 to 6
Outputs:
- layer_output: bfloat16 [16, 1280, 1024], P('rows', 'seq')
- input_grad: bfloat16 [16, 1280, 1024], P('rows', 'seq')
- grad_norm1: float32 [1024], P(('rows', 'seq'))
- grad_query: float32 [1024, 480], P(('rows', 'seq'))
- grad_keyval: float32 [1024, 320], P(('rows', 'seq'))
- grad_out: float32 [1024, 1024], P(None, ('rows', 'seq'))
- grad_norm2: float32 [1024], P(('rows', 'seq'))
- grad_gate: float32 [1024, 2816], P(('rows', 'seq'))
- grad_up: float32 [1024, 2816], P(('rows', 'seq'))
- grad_down: float32 [2816, 1024], P(None, ('rows', 'seq'))
The draws below stay inside these ranges and needn't reach their ends.
Inputs may be any that keep to these rules, and one draw needn't show every extreme that they name: `doc_ids`: along each row the ids never fall with the position. In every row document 1 starts within the first 160 positions and ends within the 160 positions before position 640; later documents are ragged.
All inputs are finite; a program needn't handle non-finite values.
Results may differ from the reference program's by a relative error of at most 0.015.
The reference program's roundings to bfloat16 on the way count: a program that leaves them out, or rounds other values in their place, can miss the bound.
Values may be sent and summed in bfloat16 or wider, within the bound.
No kernel may reach another device: no remote copies, remote signals or barrier semaphores. Data moves between devices by JAX's collectives and lax.ppermute only.
A program may use at most 256 MiB of HBM per device.

```python
import jax
import jax.numpy as jnp
from jax import lax

D = 1024
HEADS = 16
HEAD_DIM = 64
RANK_Q = 6
RANK_KV = 2
FF = 2816
SPAN = 160
BATCH = 16
LEN = 1280


extra_cuts = 6


def draw_doc_ids(key, part):
    key = jax.random.fold_in(key, 11)
    first, second, third = jax.random.split(key, 3)
    half_len = LEN // 2
    start = jax.random.randint(first, (BATCH, 1), 1, SPAN)
    finish = jax.random.randint(second, (BATCH, 1), half_len - SPAN + 1, half_len + 1)
    cuts = jax.random.randint(third, (BATCH, extra_cuts), finish + 1, LEN)
    places = jnp.arange(LEN, dtype=jnp.int32)[None, :]
    counted = (places >= start).astype(jnp.int32) + (places >= finish).astype(jnp.int32)
    counted = counted + jnp.sum((places[:, :, None] >= cuts[:, None, :]).astype(jnp.int32), axis=-1)
    return counted.astype(jnp.int32)


def strengthened(array, stream_key, source, target, parts, factor):
    owner, partner = [(jnp.arange(array.shape[position]) // (array.shape[position] // parts)).reshape([-1 if axis == position else 1 for axis in range(array.ndim)]) for position in (source, target)]
    chosen = jax.random.permutation(stream_key, parts)[partner]
    strong = (owner == chosen) | (owner == (partner + parts // 2) % parts)
    return jnp.where(strong, factor * array, array)


def shard_levels(own_key, extent, shards, least, high):
    level, own = 1.0, jax.random.fold_in(own_key, 6)
    for axis_at, parts in shards:
        heights = jnp.exp(jax.random.uniform(jax.random.fold_in(own, axis_at), (parts,), jnp.float32, least / len(shards), high / len(shards)))
        level = level * jnp.repeat(heights, extent[axis_at] // parts).reshape([-1 if axis == axis_at else 1 for axis in range(len(extent))])
    return level


def scatter_about(own_key, dims, scale, bound, cuts=(), kind=jnp.bfloat16):
    drawn = scale * jax.random.normal(own_key, dims, jnp.float32)
    if cuts:
        drawn = drawn * shard_levels(own_key, dims, cuts, -0.22, 0.18)
    return jnp.clip(drawn, -bound, bound).astype(kind)


def gaussian_with(own_key, extent, scale, most, shards, heavy, kind=jnp.bfloat16):
    array = scale * jax.random.normal(own_key, extent, jnp.float32)
    if shards:
        array = array * shard_levels(own_key, extent, shards, -0.22, 0.18)
    return jnp.clip(strengthened(array, jax.random.fold_in(own_key, 3), *heavy), -most, most).astype(kind)


def setup_inputs(seed: int = 0) -> dict:
    keys = jax.random.split(jax.random.key(seed), 12)
    layer_input = scatter_about(keys[0], (BATCH, LEN, D), 1.0, 6.0, ((0, 8), (1, 4)))
    doc_ids = draw_doc_ids(jax.random.fold_in(keys[11], 71), 0)
    norm1_gain = jnp.clip(1.0 + 0.18 * jax.random.normal(keys[2], (D,), jnp.float32), 0.1, 1.9)
    w_query = scatter_about(keys[3], (D, RANK_Q * (HEADS + HEAD_DIM)), (D // 2) ** -0.5, 0.25)
    w_keyval = scatter_about(keys[4], (D, 2 * RANK_KV * (HEADS + HEAD_DIM)), (D // 2) ** -0.5, 0.25)
    w_out = scatter_about(keys[5], (HEADS * HEAD_DIM, D), (HEADS * HEAD_DIM // 16) ** -0.5, 0.75)
    norm2_gain = jnp.clip(1.0 + 0.18 * jax.random.normal(keys[6], (D,), jnp.float32), 0.1, 1.9)
    w_gate = scatter_about(keys[7], (D, FF), D ** -0.5, 0.1875)
    w_up = scatter_about(keys[8], (D, FF), D ** -0.5, 0.1875)
    w_down = scatter_about(keys[9], (FF, D), FF ** -0.5, 0.109375)
    cotangent = gaussian_with(keys[10], (BATCH, LEN, D), 1.0, 6.0, ((0, 8), (1, 4)), (0, 2, 8, 2.0))
    return dict(layer_input=layer_input, doc_ids=doc_ids, norm1_gain=norm1_gain, w_query=w_query, w_keyval=w_keyval, w_out=w_out, norm2_gain=norm2_gain, w_gate=w_gate, w_up=w_up, w_down=w_down, cotangent=cotangent)


@jax.custom_vjp
def low(v):
    return lax.optimization_barrier(v.astype(jnp.bfloat16)).astype(jnp.float32)

@jax.custom_vjp
def low_back(v):
    return v

def low_keep(v):
    return (low(v), None)

def low_pass(kept, grad):
    return (grad,)

def back_keep(v):
    return (v, None)

def back_low(kept, grad):
    return (low(grad),)
low.defvjp(low_keep, low_pass)
low_back.defvjp(back_keep, back_low)
epsilon = 1e-06
rope_base = 10000.0
masked_score = -1e+30
highest = lax.Precision.HIGHEST

def rms_norm(values, gain):
    return values * lax.rsqrt(lax.optimization_barrier(jnp.mean(values * values, axis=-1, keepdims=True)) + epsilon) * gain

def rotate(factor, cosine, sine_term):
    middle = factor.shape[-1] // 2
    first, second = (factor[..., :middle], factor[..., middle:])
    return jnp.concatenate([first * cosine - second * sine_term, second * cosine + first * sine_term], axis=-1)

def stored_positions():
    slot_ids = jnp.arange(LEN, dtype=jnp.int32)
    holder = slot_ids // (2 * SPAN)
    within = slot_ids % (2 * SPAN)
    span_ids = jnp.where(within < SPAN, holder, LEN // SPAN - 1 - holder)
    return (span_ids * SPAN + within % SPAN).astype(jnp.int32)

def attention(queries, keys_b, values_b, allowed):
    scores = low_back(jnp.einsum('qhd,khd->hqk', queries, keys_b, precision=highest) * HEAD_DIM ** (-0.5))
    scores = jnp.where(allowed[None], scores, masked_score)
    probs = low(jax.nn.softmax(scores, axis=-1))
    return jnp.einsum('hqk,khd->qhd', probs, values_b, precision=highest)
checked_attention = jax.checkpoint(attention)

def expand(factors, length):
    part_a = RANK_KV * HEADS
    part_b = RANK_KV * HEAD_DIM
    key_a = factors[:, :part_a].reshape(length, RANK_KV, HEADS)
    key_b = factors[:, part_a:part_a + part_b].reshape(length, RANK_KV, HEAD_DIM)
    value_a = factors[:, part_a + part_b:2 * part_a + part_b].reshape(length, RANK_KV, HEADS)
    value_b = factors[:, 2 * part_a + part_b:].reshape(length, RANK_KV, HEAD_DIM)
    keys_b = low(jnp.einsum('trh,trd->thd', key_a, key_b, precision=highest) / RANK_KV)
    values_b = low(jnp.einsum('trh,trd->thd', value_a, value_b, precision=highest) / RANK_KV)
    return (keys_b, values_b)

def row_forward(layer_in, norm1_gain, w_query, w_keyval, w_out, norm2_gain, w_gate, w_up, w_down, allowed, cosine, sine_term):
    length = layer_in.shape[0]
    normed = low(rms_norm(layer_in, norm1_gain))
    query_f = low_back(jnp.dot(normed, w_query, precision=highest))
    keyval_f = low_back(jnp.dot(normed, w_keyval, precision=highest))
    split_q = RANK_Q * HEADS
    query_a = query_f[:, :split_q].reshape(length, RANK_Q, HEADS)
    query_b = rotate(query_f[:, split_q:].reshape(length, RANK_Q, HEAD_DIM), cosine, sine_term)
    queries = low(jnp.einsum('trh,trd->thd', query_a, query_b, precision=highest) / RANK_Q)
    part_a = RANK_KV * HEADS
    part_b = RANK_KV * HEAD_DIM
    key_b = rotate(keyval_f[:, part_a:part_a + part_b].reshape(length, RANK_KV, HEAD_DIM), cosine, sine_term)
    factors = low(jnp.concatenate([keyval_f[:, :part_a], key_b.reshape(length, part_b), keyval_f[:, part_a + part_b:]], axis=-1))
    keys_b, values_b = expand(factors, length)
    attended = checked_attention(queries, keys_b, values_b, allowed).reshape(length, HEADS * HEAD_DIM)
    attended = low_back(low(attended))
    resid = layer_in + low_back(jnp.dot(attended, w_out, precision=highest))
    normed2 = low(rms_norm(resid, norm2_gain))
    gate = low_back(jnp.dot(normed2, w_gate, precision=highest))
    up_proj = low_back(jnp.dot(normed2, w_up, precision=highest))
    hidden = low(jax.nn.silu(gate) * up_proj)
    return resid + low_back(jnp.dot(hidden, w_down, precision=highest))

def reference(layer_input, doc_ids, norm1_gain, w_query, w_keyval, w_out, norm2_gain, w_gate, w_up, w_down, cotangent):
    positions = stored_positions()
    stored_ids = jnp.take(doc_ids, positions, axis=1)
    causal = positions[None, :] <= positions[:, None]
    inv_freq = rope_base ** (-(jnp.arange(HEAD_DIM // 2, dtype=jnp.float32) * (2.0 / HEAD_DIM)))
    angles = positions.astype(jnp.float32)[:, None] * inv_freq[None, :]
    cosine = jnp.cos(angles)[:, None, :]
    sine_term = jnp.sin(angles)[:, None, :]
    weights = tuple((weight.astype(jnp.float32) for weight in (norm1_gain, w_query, w_keyval, w_out, norm2_gain, w_gate, w_up, w_down)))

    def one_row(totals, row_data):
        row_in, row_ids, row_cot = row_data
        allowed = causal & (row_ids[:, None] == row_ids[None, :])

        def forward(row_input, *params):
            return row_forward(row_input, *params, allowed, cosine, sine_term)
        result, pull = jax.vjp(forward, row_in.astype(jnp.float32), *weights)
        grads = pull(row_cot.astype(jnp.float32))
        totals = tuple((total + grad for total, grad in zip(totals, grads[1:])))
        return (totals, (result.astype(jnp.bfloat16), grads[0].astype(jnp.bfloat16)))
    start = tuple((jnp.zeros(weight.shape, jnp.float32) for weight in weights))
    totals, outputs = lax.scan(one_row, start, (layer_input, stored_ids, cotangent))
    return (outputs[0], outputs[1], totals[0], totals[1], totals[2], totals[3], totals[4], totals[5], totals[6], totals[7])
```

```python
import functools

import jax
import jax.numpy as jnp
from jax import lax
from jax.experimental import pallas as pl
from jax.experimental.pallas import tpu as pltpu
from jax.sharding import PartitionSpec as P

HEADS = 16
HEAD_DIM = 64
RANK_Q = 6
RANK_KV = 2
Q_COLS = RANK_Q * (HEADS + HEAD_DIM)
KV_COLS = 2 * RANK_KV * (HEADS + HEAD_DIM)
EPS = 1e-06
ROPE_BASE = 10000.0
MASKED = -1e30
SCORE_SCALE = HEAD_DIM ** (-0.5)
VALUE_BASE = RANK_KV * (HEADS + HEAD_DIM)
TILE = 128
TILES = 9
F32 = jnp.float32
BF16 = jnp.bfloat16
NT = (((1,), (1,)), ((), ()))
TN = (((0,), (0,)), ((), ()))
VMEM_LIMIT = 60 * 2**20


def dot(left, right, dims=None):
    if dims is None:
        return jnp.dot(left, right, preferred_element_type=F32)
    return lax.dot_general(left, right, dims, preferred_element_type=F32)


def params():
    return pltpu.CompilerParams(vmem_limit_bytes=VMEM_LIMIT)


def cost(flops, nbytes, trans=0):
    return pl.CostEstimate(flops=flops, bytes_accessed=nbytes, transcendentals=trans)


def aligned(value, factor):
    return pl.multiple_of(value, factor)


def project_kernel(x_ref, gain_ref, wq_ref, wkv_ref, cos_ref, sin_ref, normed_ref, qf_ref, kv_ref):
    x = x_ref[...].astype(F32)
    scale = lax.rsqrt(jnp.mean(x * x, axis=-1, keepdims=True) + EPS)
    normed = (x * scale * gain_ref[...]).astype(BF16)
    normed_ref[...] = normed
    qf = dot(normed, wq_ref[...])
    kvf = dot(normed, wkv_ref[...])
    cos, sin = cos_ref[0], sin_ref[0]
    half = HEAD_DIM // 2
    qt = qf.T
    split = RANK_Q * HEADS
    qf_ref[0, :split, :] = qt[:split]
    for r in range(RANK_Q):
        at = split + r * HEAD_DIM
        first, second = qt[at : at + half], qt[at + half : at + HEAD_DIM]
        qf_ref[0, at : at + half, :] = first * cos - second * sin
        qf_ref[0, at + half : at + HEAD_DIM, :] = second * cos + first * sin
    kvt = kvf.T
    split = RANK_KV * HEADS
    pieces = [kvt[:split]]
    for r in range(RANK_KV):
        at = split + r * HEAD_DIM
        first, second = kvt[at : at + half], kvt[at + half : at + HEAD_DIM]
        pieces += [first * cos - second * sin, second * cos + first * sin]
    pieces.append(kvt[split + RANK_KV * HEAD_DIM :])
    kv_ref[...] = jnp.concatenate(pieces, axis=0).T.astype(BF16)


def project(x, gain, w_query, w_keyval, cos, sin):
    tokens, width = x.shape
    span = cos.shape[-1]
    groups = tokens // span
    full = lambda i: (0, 0)
    return pl.pallas_call(
        project_kernel,
        grid=(groups,),
        in_specs=[
            pl.BlockSpec((span, width), lambda i: (i, 0)),
            pl.BlockSpec((1, width), full),
            pl.BlockSpec((width, Q_COLS), full),
            pl.BlockSpec((width, KV_COLS), full),
            pl.BlockSpec((1, HEAD_DIM // 2, span), lambda i: (i % 2, 0, 0)),
            pl.BlockSpec((1, HEAD_DIM // 2, span), lambda i: (i % 2, 0, 0)),
        ],
        out_specs=[
            pl.BlockSpec((span, width), lambda i: (i, 0)),
            pl.BlockSpec((1, Q_COLS, span), lambda i: (i, 0, 0)),
            pl.BlockSpec((span, KV_COLS), lambda i: (i, 0)),
        ],
        out_shape=[
            jax.ShapeDtypeStruct((tokens, width), BF16),
            jax.ShapeDtypeStruct((groups, Q_COLS, span), F32),
            jax.ShapeDtypeStruct((tokens, KV_COLS), BF16),
        ],
        compiler_params=params(),
        cost_estimate=cost(2 * tokens * width * (Q_COLS + KV_COLS), 8 * 2**20),
        name="project",
    )(x, gain, w_query, w_keyval, cos, sin)


def tile_place(tile, seq_id):
    low = tile < seq_id + 2
    return low, jnp.where(low, tile, tile + 1 - seq_id)


def gather_keys(seq_id, sources, qf_ref, qa, kvpos, kvt, kva, bias, doc_k, doc_q, span):
    for which, source in enumerate(sources):
        holder = seq_id ^ which
        kvpos[pl.ds(aligned(holder * span, 32), span), :] = source[0, :span, :]
        kvpos[pl.ds(aligned((7 - holder) * span, 32), span), :] = source[0, span:, :]
    for tile in range(TILES):
        low, place = tile_place(tile, seq_id)
        start = aligned(place * TILE, TILE)
        kvt[:, tile * TILE : (tile + 1) * TILE] = kvpos[pl.ds(start, TILE), :].astype(F32).T
        own = jnp.where(low, seq_id, 7 - seq_id) * span
        pos_q = own + lax.broadcasted_iota(jnp.int32, (span, TILE), 0)
        pos_k = start + lax.broadcasted_iota(jnp.int32, (span, TILE), 1)
        same = doc_q[jnp.where(low, 0, 1)] == doc_k[0, :, pl.ds(start, TILE)]
        bias[:, tile * TILE : (tile + 1) * TILE] = jnp.where(
            same & (pos_k <= pos_q), 0.0, MASKED
        )
    split = RANK_KV * HEADS
    kva[:split, 0, :] = kvt[:split, :]
    kva[split:, 0, :] = kvt[VALUE_BASE : VALUE_BASE + split, :]
    for s in range(2):
        qa[s, :, 0, :] = qf_ref[s, : RANK_Q * HEADS, :]


def expand_queries(qf_ref, qa, s, head):
    split = RANK_Q * HEADS
    total = None
    for r in range(RANK_Q):
        weight = qa[s, r * HEADS + head]
        term = weight * qf_ref[s, split + r * HEAD_DIM : split + (r + 1) * HEAD_DIM, :]
        total = term if total is None else total + term
    return ((total / RANK_Q).astype(BF16).astype(F32) * SCORE_SCALE)


def expand_pair(kvt, kva, base, head):
    split = RANK_KV * HEADS
    total = None
    for r in range(RANK_KV):
        at = base + split + r * HEAD_DIM
        weight = kva[(base // VALUE_BASE) * split + r * HEADS + head]
        term = weight * kvt[at : at + HEAD_DIM, :]
        total = term if total is None else total + term
    return (total / RANK_KV).astype(BF16)


def attend_kernel(
    seq_ref, qf_ref, kv0, kv1, kv2, kv3, dk_ref, dq_ref, out_ref, lse_ref, kvpos, kvt, bias, qh, ot,
    kva, qa,
):
    seq_id = seq_ref[0]
    span = qf_ref.shape[-1]
    gather_keys(
        seq_id, (kv0, kv1, kv2, kv3), qf_ref, qa, kvpos, kvt, kva, bias, dk_ref, dq_ref, span
    )
    lane = lax.broadcasted_iota(jnp.int32, (span, TILE), 1)

    def head_step(head, carry):
        for s in range(2):
            qh[s] = expand_queries(qf_ref, qa, s, head).T.astype(BF16)
        keys = expand_pair(kvt, kva, 0, head)
        values = expand_pair(kvt, kva, VALUE_BASE, head)
        lows, scores = [], []
        top = [None, None]
        for tile in range(TILES):
            low, _ = tile_place(tile, seq_id)
            lows.append(low)
            cols = slice(tile * TILE, (tile + 1) * TILE)
            s = 0 if tile < 2 else (1 if tile > 4 else jnp.where(low, 0, 1))
            score = dot(qh[s], keys[:, cols]) + bias[:, cols]
            scores.append(score)
            for side in range(2):
                if (tile < 2 and side == 1) or (tile > 4 and side == 0):
                    continue
                part = score
                if 2 <= tile <= 4:
                    part = jnp.where(low if side == 0 else ~low, score, MASKED)
                top[side] = part if top[side] is None else jnp.maximum(top[side], part)
        top = [jnp.max(t, axis=-1, keepdims=True) for t in top]

        def pick(tile, pair):
            if tile < 2:
                return pair[0]
            if tile > 4:
                return pair[1]
            return jnp.where(lows[tile], pair[0], pair[1])

        total = [None, None]
        raised = []
        for tile in range(TILES):
            r = jnp.exp(scores[tile] - pick(tile, top))
            raised.append(r)
            for side in range(2):
                if (tile < 2 and side == 1) or (tile > 4 and side == 0):
                    continue
                part = r
                if 2 <= tile <= 4:
                    part = jnp.where(lows[tile] if side == 0 else ~lows[tile], r, 0.0)
                total[side] = part if total[side] is None else total[side] + part
        total = [jnp.sum(t, axis=-1, keepdims=True) for t in total]
        inverse = [1.0 / t for t in total]
        probs = [(raised[t] * pick(t, inverse)).astype(BF16) for t in range(TILES)]

        def weigh(first, last):
            return dot(
                values[:, first * TILE : last * TILE],
                jnp.concatenate(probs[first:last], axis=1),
                NT,
            )

        out = [weigh(0, 2), weigh(5, 7) + weigh(7, 9)]
        for tile in range(2, 5):
            part = weigh(tile, tile + 1)
            out[0] = out[0] + jnp.where(lows[tile], part, 0.0)
            out[1] = out[1] + jnp.where(lows[tile], 0.0, part)
        for s in range(2):
            ot[s, pl.ds(aligned(head * HEAD_DIM, HEAD_DIM), HEAD_DIM), :] = out[s]
            lse_ref[s] = jnp.where(lane == head, top[s] + jnp.log(total[s]), lse_ref[s])
        return carry

    lse_ref[...] = jnp.zeros_like(lse_ref)
    lax.fori_loop(0, HEADS, head_step, 0)
    for s in range(2):
        out_ref[0, s * span : (s + 1) * span, :] = ot[s].T.astype(BF16)


def attention_specs(span, length):
    kv_spec = pl.BlockSpec((1, 2 * span, KV_COLS), lambda i, s: (i, 0, 0))
    return [
        pl.BlockSpec((2, Q_COLS, span), lambda i, s: (i, 0, 0)),
        kv_spec,
        kv_spec,
        kv_spec,
        kv_spec,
        pl.BlockSpec((1, 1, length), lambda i, s: (i, 0, 0)),
        pl.BlockSpec((2, span, 1), lambda i, s: (i, 0, 0)),
    ]


def attend(seq_id, qf, sources, doc_k, doc_q):
    rows, _, length = doc_k.shape
    span = qf.shape[-1]
    width = HEADS * HEAD_DIM
    return pl.pallas_call(
        attend_kernel,
        grid_spec=pltpu.PrefetchScalarGridSpec(
            num_scalar_prefetch=1,
            grid=(rows,),
            in_specs=attention_specs(span, length),
            out_specs=[
                pl.BlockSpec((1, 2 * span, width), lambda i, s: (i, 0, 0)),
                pl.BlockSpec((2, span, TILE), lambda i, s: (i, 0, 0)),
            ],
            scratch_shapes=[
                pltpu.VMEM((length, KV_COLS), BF16),
                pltpu.VMEM((KV_COLS, TILES * TILE), F32),
                pltpu.VMEM((span, TILES * TILE), F32),
                pltpu.VMEM((2, span, HEAD_DIM), BF16),
                pltpu.VMEM((2, width, span), F32),
                pltpu.VMEM((2 * RANK_KV * HEADS, 1, TILES * TILE), F32),
                pltpu.VMEM((2, RANK_Q * HEADS, 1, span), F32),
            ],
        ),
        out_shape=[
            jax.ShapeDtypeStruct((rows, 2 * span, width), BF16),
            jax.ShapeDtypeStruct((2 * rows, span, TILE), F32),
        ],
        compiler_params=params(),
        cost_estimate=cost(12 * 10**9, 8 * 2**20),
        name="attend",
    )(seq_id, qf, *sources, doc_k, doc_q)


def attend_back_kernel(
    seq_ref,
    qf_ref,
    kv0,
    kv1,
    kv2,
    kv3,
    dk_ref,
    dq_ref,
    lse_ref,
    att_ref,
    grad_ref,
    cos_ref,
    sin_ref,
    gq_ref,
    near_ref,
    far_ref,
    kvpos,
    kvt,
    bias,
    qt,
    dot_t,
    stats,
    gkvt,
    gkvpos,
    gqt,
    gka,
    gqa,
    kva,
    qa,
):
    seq_id = seq_ref[0]
    span = qf_ref.shape[-1]
    gather_keys(
        seq_id, (kv0, kv1, kv2, kv3), qf_ref, qa, kvpos, kvt, kva, bias, dk_ref, dq_ref, span
    )
    width = HEADS * HEAD_DIM
    chooser = (
        lax.broadcasted_iota(jnp.int32, (width, TILE), 0) // HEAD_DIM
        == lax.broadcasted_iota(jnp.int32, (width, TILE), 1)
    ).astype(BF16)
    for s in range(2):
        grad = grad_ref[0, s * span : (s + 1) * span, :].astype(F32)
        dot_t[s] = grad.T
        product = grad * att_ref[0, s * span : (s + 1) * span, :].astype(F32)
        coarse = product.astype(BF16)
        fine = (product - coarse.astype(F32)).astype(BF16)
        centre = dot(coarse, chooser) + dot(fine, chooser)
        for head in range(HEADS):
            stats[0, s, head] = jnp.broadcast_to(lse_ref[s, :, head : head + 1], (span, TILE))
            stats[1, s, head] = jnp.broadcast_to(centre[:, head : head + 1], (span, TILE))
    gkvt[...] = jnp.zeros_like(gkvt)
    gqt[...] = jnp.zeros_like(gqt)

    def head_step(head, carry):
        q_rows, g_rows = [], []
        rows = pl.ds(aligned(head * HEAD_DIM, HEAD_DIM), HEAD_DIM)
        for s in range(2):
            expanded = expand_queries(qf_ref, qa, s, head)
            qt[s] = expanded.astype(BF16)
            q_rows.append(expanded.T.astype(BF16))
            g_rows.append(dot_t[s, rows, :].T.astype(BF16))
        keys = expand_pair(kvt, kva, 0, head)
        values = expand_pair(kvt, kva, VALUE_BASE, head)
        grad_q = [None, None]
        split = RANK_KV * HEADS
        for tile in range(TILES):
            low, _ = tile_place(tile, seq_id)
            fixed = 0 if tile < 2 else (1 if tile > 4 else None)
            cols = slice(tile * TILE, (tile + 1) * TILE)
            if fixed is None:
                s = jnp.where(low, 0, 1)
                q_tile = jnp.where(low, q_rows[0], q_rows[1])
                g_tile = jnp.where(low, g_rows[0], g_rows[1])
            else:
                s = fixed
                q_tile, g_tile = q_rows[s], g_rows[s]
            score = dot(q_tile, keys[:, cols]) + bias[:, cols]
            probs = jnp.exp(score - stats[0, s, head])
            grad_p = dot(g_tile, values[:, cols])
            grad_s = (probs * (grad_p - stats[1, s, head])).astype(BF16)
            grad_v = dot(dot_t[s, rows, :].astype(BF16), probs.astype(BF16))
            grad_k = dot(qt[s], grad_s)
            part = dot(keys[:, cols], grad_s, NT)
            for side in range(2):
                if fixed is not None and fixed != side:
                    continue
                term = part
                if fixed is None:
                    term = jnp.where(low if side == 0 else ~low, part, 0.0)
                grad_q[side] = term if grad_q[side] is None else grad_q[side] + term
            for base, grad in ((0, grad_k), (VALUE_BASE, grad_v)):
                grad = grad * (1.0 / RANK_KV)
                for r in range(RANK_KV):
                    at = base + split + r * HEAD_DIM
                    b_rows = slice(at, at + HEAD_DIM)
                    gka[(base // VALUE_BASE) * split + r * HEADS + head, :, cols] = jnp.sum(
                        grad * kvt[b_rows, cols], axis=0, keepdims=True
                    )
                    gkvt[b_rows, cols] += grad * kva[(base // VALUE_BASE) * split + r * HEADS + head, :, cols]
        split = RANK_Q * HEADS
        for s in range(2):
            grad = grad_q[s] * (SCORE_SCALE / RANK_Q)
            for r in range(RANK_Q):
                at = split + r * HEAD_DIM
                b_rows = slice(at, at + HEAD_DIM)
                gqa[s, r * HEADS + head] = jnp.sum(
                    grad * qf_ref[s, b_rows, :], axis=0, keepdims=True
                )
                gqt[s, b_rows, :] += grad * qa[s, r * HEADS + head]
        return carry

    lax.fori_loop(0, HEADS, head_step, 0)
    half = HEAD_DIM // 2
    split = RANK_Q * HEADS
    for s in range(2):
        cos, sin = cos_ref[s], sin_ref[s]
        pieces = [gqa[s, :, 0, :]]
        for r in range(RANK_Q):
            at = split + r * HEAD_DIM
            first, second = gqt[s, at : at + half, :], gqt[s, at + half : at + HEAD_DIM, :]
            pieces += [first * cos + second * sin, second * cos - first * sin]
        gq_ref[0, s * span : (s + 1) * span, :] = jnp.concatenate(pieces, axis=0).T.astype(BF16)
    split = RANK_KV * HEADS
    gkvt[:split, :] = gka[:split, 0, :]
    gkvt[VALUE_BASE : VALUE_BASE + split, :] = gka[split:, 0, :]
    gkvpos[...] = jnp.zeros_like(gkvpos)
    for tile in range(TILES):
        _, place = tile_place(tile, seq_id)
        rows = pl.ds(aligned(place * TILE, TILE), TILE)
        gkvpos[rows, :] += gkvt[:, tile * TILE : (tile + 1) * TILE].T
    for which in range(4):
        holder = seq_id ^ which
        target = near_ref if which in (0, 2) else far_ref
        for s, at in enumerate((holder, 7 - holder)):
            target[which // 2, 0, s * span : (s + 1) * span, :] = gkvpos[
                pl.ds(aligned(at * span, 32), span), :
            ].astype(BF16)


def attend_back(seq_id, qf, sources, doc_k, doc_q, lse, attended, grad_attended, cos, sin):
    rows, _, length = doc_k.shape
    span = qf.shape[-1]
    width = HEADS * HEAD_DIM
    wide = pl.BlockSpec((1, 2 * span, width), lambda i, s: (i, 0, 0))
    rope = pl.BlockSpec((2, HEAD_DIM // 2, span), lambda i, s: (0, 0, 0))
    parts = pl.BlockSpec((2, 1, 2 * span, KV_COLS), lambda i, s: (0, i, 0, 0))
    return pl.pallas_call(
        attend_back_kernel,
        grid_spec=pltpu.PrefetchScalarGridSpec(
            num_scalar_prefetch=1,
            grid=(rows,),
            in_specs=attention_specs(span, length)
            + [pl.BlockSpec((2, span, TILE), lambda i, s: (i, 0, 0)), wide, wide, rope, rope],
            out_specs=[
                pl.BlockSpec((1, 2 * span, Q_COLS), lambda i, s: (i, 0, 0)),
                parts,
                parts,
            ],
            scratch_shapes=[
                pltpu.VMEM((length, KV_COLS), BF16),
                pltpu.VMEM((KV_COLS, TILES * TILE), F32),
                pltpu.VMEM((span, TILES * TILE), F32),
                pltpu.VMEM((2, HEAD_DIM, span), BF16),
                pltpu.VMEM((2, width, span), F32),
                pltpu.VMEM((2, 2, HEADS, span, TILE), F32),
                pltpu.VMEM((KV_COLS, TILES * TILE), F32),
                pltpu.VMEM((length, KV_COLS), F32),
                pltpu.VMEM((2, Q_COLS, span), F32),
                pltpu.VMEM((2 * RANK_KV * HEADS, 1, TILES * TILE), F32),
                pltpu.VMEM((2, RANK_Q * HEADS, 1, span), F32),
                pltpu.VMEM((2 * RANK_KV * HEADS, 1, TILES * TILE), F32),
                pltpu.VMEM((2, RANK_Q * HEADS, 1, span), F32),
            ],
        ),
        out_shape=[
            jax.ShapeDtypeStruct((rows, 2 * span, Q_COLS), BF16),
            jax.ShapeDtypeStruct((2, rows, 2 * span, KV_COLS), BF16),
            jax.ShapeDtypeStruct((2, rows, 2 * span, KV_COLS), BF16),
        ],
        compiler_params=params(),
        cost_estimate=cost(25 * 10**9, 12 * 2**20),
        name="attend_back",
    )(seq_id, qf, *sources, doc_k, doc_q, lse, attended, grad_attended, cos, sin)


def out_kernel(x_ref, att_ref, w_ref, gain_ref, resid_ref, normed_ref):
    resid = x_ref[...].astype(F32) + dot(att_ref[...], w_ref[...])
    scale = lax.rsqrt(jnp.mean(resid * resid, axis=-1, keepdims=True) + EPS)
    resid_ref[...] = resid
    normed_ref[...] = (resid * scale * gain_ref[...]).astype(BF16)


def out_project(x, attended, w_out, gain):
    tokens, width = x.shape
    step = tokens // 2
    tile = pl.BlockSpec((step, width), lambda i: (i, 0))
    return pl.pallas_call(
        out_kernel,
        grid=(2,),
        in_specs=[
            tile,
            tile,
            pl.BlockSpec(w_out.shape, lambda i: (0, 0)),
            pl.BlockSpec((1, width), lambda i: (0, 0)),
        ],
        out_specs=[tile, tile],
        out_shape=[
            jax.ShapeDtypeStruct((tokens, width), F32),
            jax.ShapeDtypeStruct((tokens, width), BF16),
        ],
        compiler_params=params(),
        cost_estimate=cost(2 * tokens * width * width, 10 * 2**20),
        name="out_project",
    )(x, attended, w_out, gain)


def out_back_kernel(
    cot_ref, own_ref, other_ref, resid_ref, w_ref, gain_ref, gr_ref, gb_ref, ga_ref, gain_grad_ref
):
    grad = own_ref[...] + other_ref[...].astype(F32)
    values = resid_ref[...]
    scale = lax.rsqrt(jnp.mean(values * values, axis=-1, keepdims=True) + EPS)
    weighted = grad * gain_ref[...]
    back = scale * weighted - values * (scale * scale * scale) * jnp.mean(
        weighted * values, axis=-1, keepdims=True
    )
    grad_resid = cot_ref[...].astype(F32) + back
    branch = grad_resid.astype(BF16)
    gr_ref[...] = grad_resid
    gb_ref[...] = branch
    ga_ref[...] = dot(branch, w_ref[...], NT).astype(BF16)

    @pl.when(pl.program_id(0) == 0)
    def _():
        gain_grad_ref[...] = jnp.zeros_like(gain_grad_ref)

    gain_grad_ref[...] += jnp.sum(grad * values * scale, axis=0, keepdims=True)


def out_back(cot, own, other, resid, w_out, gain):
    tokens, width = cot.shape
    step = tokens // 2
    tile = pl.BlockSpec((step, width), lambda i: (i, 0))
    row = pl.BlockSpec((1, width), lambda i: (0, 0))
    return pl.pallas_call(
        out_back_kernel,
        grid=(2,),
        in_specs=[tile, tile, tile, tile, pl.BlockSpec(w_out.shape, lambda i: (0, 0)), row],
        out_specs=[tile, tile, tile, row],
        out_shape=[
            jax.ShapeDtypeStruct((tokens, width), F32),
            jax.ShapeDtypeStruct((tokens, width), BF16),
            jax.ShapeDtypeStruct((tokens, width), BF16),
            jax.ShapeDtypeStruct((1, width), F32),
        ],
        compiler_params=params(),
        cost_estimate=cost(2 * tokens * width * width, 16 * 2**20),
        name="out_back",
    )(cot, own, other, resid, w_out, gain)


def ff_kernel(core_ref, n2_ref, cot_ref, wg_ref, wu_ref, wd_ref, h_ref, gg_ref, gu_ref):
    gate = dot(n2_ref[...], wg_ref[...])
    up = dot(n2_ref[...], wu_ref[...])
    grad_hidden = dot(cot_ref[...], wd_ref[...], NT)
    sigmoid = 1.0 / (1.0 + jnp.exp(-gate))
    silu = gate * sigmoid
    h_ref[...] = (silu * up).astype(BF16)
    gu_ref[...] = (grad_hidden * silu).astype(BF16)
    gg_ref[...] = (grad_hidden * up * (sigmoid + silu * (1.0 - sigmoid))).astype(BF16)


def feed_forward(core, n2, cot, w_gate, w_up, w_down):
    tokens, width = n2.shape
    half = w_gate.shape[1] // 2
    step = tokens // 2
    tile = pl.BlockSpec((step, width), lambda i, c: (i, 0))
    out = pl.BlockSpec((step, half), lambda i, c: (i, 0))
    return pl.pallas_call(
        ff_kernel,
        grid_spec=pltpu.PrefetchScalarGridSpec(
            num_scalar_prefetch=1,
            grid=(2,),
            in_specs=[
                tile,
                tile,
                pl.BlockSpec((width, half), lambda i, c: (0, c[0])),
                pl.BlockSpec((width, half), lambda i, c: (0, c[0])),
                pl.BlockSpec((half, width), lambda i, c: (c[0], 0)),
            ],
            out_specs=[out, out, out],
        ),
        out_shape=[jax.ShapeDtypeStruct((tokens, half), BF16)] * 3,
        compiler_params=params(),
        cost_estimate=cost(6 * tokens * width * half, 18 * 2**20),
        name="feed_forward",
    )(core, n2, cot, w_gate, w_up, w_down)


def ff_back_kernel(core_ref, gg_ref, gu_ref, wg_ref, wu_ref, out_ref):
    out_ref[...] = (
        dot(gg_ref[...], wg_ref[...], NT) + dot(gu_ref[...], wu_ref[...], NT)
    ).astype(out_ref.dtype)


def ff_back(core, gg, gu, w_gate, w_up, dtype):
    tokens, half = gg.shape
    width = w_gate.shape[0]
    step = tokens // 2
    tile = pl.BlockSpec((step, half), lambda i, c: (i, 0))
    weight = pl.BlockSpec((width, half), lambda i, c: (0, c[0]))
    return pl.pallas_call(
        ff_back_kernel,
        grid_spec=pltpu.PrefetchScalarGridSpec(
            num_scalar_prefetch=1,
            grid=(2,),
            in_specs=[tile, tile, weight, weight],
            out_specs=pl.BlockSpec((step, width), lambda i, c: (i, 0)),
        ),
        out_shape=jax.ShapeDtypeStruct((tokens, width), dtype),
        compiler_params=params(),
        cost_estimate=cost(4 * tokens * width * half, 12 * 2**20),
        name="ff_back",
    )(core, gg, gu, w_gate, w_up)


def down_kernel(core_ref, own_ref, other_ref, w_ref, own_out, other_out):
    own_out[...] = dot(own_ref[...], w_ref[...])
    other_out[...] = dot(other_ref[...], w_ref[...]).astype(BF16)


def down_project(core, own, other, w_down):
    tokens, half = own.shape
    width = w_down.shape[1]
    step = tokens // 2
    tile = pl.BlockSpec((step, half), lambda i, c: (i, 0))
    out = pl.BlockSpec((step, width), lambda i, c: (i, 0))
    return pl.pallas_call(
        down_kernel,
        grid_spec=pltpu.PrefetchScalarGridSpec(
            num_scalar_prefetch=1,
            grid=(2,),
            in_specs=[tile, tile, pl.BlockSpec((half, width), lambda i, c: (c[0], 0))],
            out_specs=[out, out],
        ),
        out_shape=[
            jax.ShapeDtypeStruct((tokens, width), F32),
            jax.ShapeDtypeStruct((tokens, width), BF16),
        ],
        compiler_params=params(),
        cost_estimate=cost(4 * tokens * width * half, 10 * 2**20),
        name="down_project",
    )(core, own, other, w_down)


def weight_kernel(x_first, id_ref, l0_ref, l1_ref, r0_ref, r1_ref, send_ref, keep_ref):
    total = dot(l0_ref[...], r0_ref[...], TN) + dot(l1_ref[...], r1_ref[...], TN)
    high, _, block, cols = send_ref.shape
    total = total.astype(BF16).reshape(high, 2, 2, block, cols)
    bit = id_ref[0]

    def put(mine):
        if x_first:
            send_ref[...] = total[:, :, 1 - mine]
            keep_ref[...] = total[:, :, mine]
        else:
            send_ref[...] = total[:, 1 - mine]
            keep_ref[...] = total[:, mine]

    @pl.when(bit == 0)
    def _():
        put(0)

    @pl.when(bit == 1)
    def _():
        put(1)


def weight_grad(bit, x_first, left, right, blocks):
    tokens, width = left[0].shape
    cols = right[0].shape[1]
    block = width // blocks
    step = 256
    steps = width // step
    high = step // (4 * block)
    l_spec = pl.BlockSpec((tokens, step), lambda i, b: (0, i))
    r_spec = pl.BlockSpec((tokens, cols), lambda i, b: (0, 0))
    out = pl.BlockSpec((high, 2, block, cols), lambda i, b: (i, 0, 0, 0))
    shape = jax.ShapeDtypeStruct((blocks // 4, 2, block, cols), BF16)
    return pl.pallas_call(
        functools.partial(weight_kernel, x_first),
        grid_spec=pltpu.PrefetchScalarGridSpec(
            num_scalar_prefetch=1,
            grid=(steps,),
            in_specs=[l_spec, l_spec, r_spec, r_spec],
            out_specs=[out, out],
        ),
        out_shape=[shape, shape],
        compiler_params=params(),
        cost_estimate=cost(4 * tokens * width * cols, 10 * 2**20),
        name="weight_grad",
    )(bit, left[0], left[1], right[0], right[1])


def half_kernel(core_ref, l_ref, r_ref, mine_ref, other_ref):
    total = dot(l_ref[...], r_ref[...], TN).astype(BF16)
    half = mine_ref.shape[-1]

    @pl.when(core_ref[0] == 0)
    def _():
        mine_ref[...] = total[:, :half]
        other_ref[...] = total[:, half:]

    @pl.when(core_ref[0] == 1)
    def _():
        mine_ref[...] = total[:, half:]
        other_ref[...] = total[:, :half]


def weight_halves(core, left, right):
    tokens, width = left.shape
    cols = right.shape[1]
    step = 256
    out = pl.BlockSpec((step, cols // 2), lambda i, b: (i, 0))
    shape = jax.ShapeDtypeStruct((width, cols // 2), BF16)
    return pl.pallas_call(
        half_kernel,
        grid_spec=pltpu.PrefetchScalarGridSpec(
            num_scalar_prefetch=1,
            grid=(width // step,),
            in_specs=[
                pl.BlockSpec((tokens, step), lambda i, b: (0, i)),
                pl.BlockSpec((tokens, cols), lambda i, b: (0, 0)),
            ],
            out_specs=[out, out],
        ),
        out_shape=[shape, shape],
        compiler_params=params(),
        cost_estimate=cost(2 * tokens * width * cols, 4 * 2**20),
        name="weight_halves",
    )(core, left, right)


def finish_kernel(
    k0_ref, r0_ref, x0_ref, gq_ref, wq_ref, wkv_ref, x_ref, gain_ref, gr_ref, cos_ref, sin_ref,
    gkv_ref, out_ref, gain_grad_ref,
):
    total = k0_ref[...].astype(F32) + r0_ref[...].astype(F32) + x0_ref[...].astype(F32)
    cos, sin = cos_ref[0], sin_ref[0]
    half = HEAD_DIM // 2
    split = RANK_KV * HEADS
    turned = total.T
    pieces = [turned[:split]]
    for r in range(RANK_KV):
        at = split + r * HEAD_DIM
        first, second = turned[at : at + half], turned[at + half : at + HEAD_DIM]
        pieces += [first * cos + second * sin, second * cos - first * sin]
    pieces.append(turned[split + RANK_KV * HEAD_DIM :])
    gkv = jnp.concatenate(pieces, axis=0).T.astype(BF16)
    gkv_ref[...] = gkv
    grad = dot(gq_ref[...], wq_ref[...], NT) + dot(gkv, wkv_ref[...], NT)
    values = x_ref[...].astype(F32)
    scale = lax.rsqrt(jnp.mean(values * values, axis=-1, keepdims=True) + EPS)
    weighted = grad * gain_ref[...]
    back = scale * weighted - values * (scale * scale * scale) * jnp.mean(
        weighted * values, axis=-1, keepdims=True
    )
    out_ref[...] = (gr_ref[...] + back).astype(BF16)

    @pl.when(pl.program_id(0) == 0)
    def _():
        gain_grad_ref[...] = jnp.zeros_like(gain_grad_ref)

    gain_grad_ref[...] += jnp.sum(grad * values * scale, axis=0, keepdims=True)


def finish(kept, near, far, gq, w_query, w_keyval, x, gain, grad_resid, cos, sin):
    tokens, width = x.shape
    span = cos.shape[-1]
    full = lambda i: (0, 0)
    tile = pl.BlockSpec((span, width), lambda i: (i, 0))
    narrow = pl.BlockSpec((span, KV_COLS), lambda i: (i, 0))
    rope = pl.BlockSpec((1, HEAD_DIM // 2, span), lambda i: (i % 2, 0, 0))
    row = pl.BlockSpec((1, width), full)
    return pl.pallas_call(
        finish_kernel,
        grid=(tokens // span,),
        in_specs=[
            narrow,
            narrow,
            narrow,
            pl.BlockSpec((span, Q_COLS), lambda i: (i, 0)),
            pl.BlockSpec((width, Q_COLS), full),
            pl.BlockSpec((width, KV_COLS), full),
            tile,
            row,
            tile,
            rope,
            rope,
        ],
        out_specs=[narrow, tile, row],
        out_shape=[
            jax.ShapeDtypeStruct((tokens, KV_COLS), BF16),
            jax.ShapeDtypeStruct((tokens, width), BF16),
            jax.ShapeDtypeStruct((1, width), F32),
        ],
        compiler_params=params(),
        cost_estimate=cost(2 * tokens * width * (Q_COLS + KV_COLS), 9 * 2**20),
        name="finish",
    )(kept, near, far, gq, w_query, w_keyval, x, gain, grad_resid, cos, sin)


def body(
    layer_input,
    doc_ids,
    norm1_gain,
    w_query,
    w_keyval,
    w_out,
    norm2_gain,
    w_gate,
    w_up,
    w_down,
    cotangent,
):
    row_count, local_len, width = layer_input.shape
    seq_size = lax.axis_size("seq")
    rows_size = lax.axis_size("rows")
    seq_id = lax.axis_index("seq")
    rows_id = lax.axis_index("rows")
    span = local_len // 2
    tokens = row_count * local_len
    length = local_len * seq_size
    core = seq_id % 2
    x_bit = (seq_id // 2) % 2
    y_bit = rows_id % 2
    blocks = rows_size * 2

    def swap(value, axis, mask):
        size = seq_size if axis == "seq" else rows_size
        return lax.ppermute(value, axis, [(i, i ^ mask) for i in range(size)])

    def scalar(value):
        return value.astype(jnp.int32).reshape(1)

    x = layer_input.reshape(tokens, width)
    cot = cotangent.reshape(tokens, width)
    cot_other = swap(cot, "seq", 1)
    gain1 = norm1_gain.reshape(1, width)
    gain2 = norm2_gain.reshape(1, width)

    spans = jnp.stack([seq_id, 2 * seq_size - 1 - seq_id])
    positions = spans[:, None] * span + jnp.arange(span, dtype=jnp.int32)[None, :]
    inv_freq = ROPE_BASE ** (-(jnp.arange(HEAD_DIM // 2, dtype=F32) * (2.0 / HEAD_DIM)))
    angles = positions.astype(F32)[:, None, :] * inv_freq[None, :, None]
    cos, sin = jnp.cos(angles), jnp.sin(angles)
    doc_k = doc_ids.reshape(row_count, 1, length)
    pieces = doc_ids.reshape(row_count, 2 * seq_size, span)
    doc_q = jnp.stack(
        [
            lax.dynamic_index_in_dim(pieces, seq_id, 1, keepdims=False),
            lax.dynamic_index_in_dim(pieces, 2 * seq_size - 1 - seq_id, 1, keepdims=False),
        ],
        axis=1,
    ).reshape(2 * row_count, span, 1)

    normed, qf, kv = project(x, gain1, w_query, w_keyval, cos, sin)
    kv = kv.reshape(row_count, local_len, KV_COLS)
    kv_core = swap(kv, "seq", 1)
    kv_x = swap(kv, "seq", 2)
    kv_both = swap(kv_x, "seq", 1)
    sources = (kv, kv_core, kv_x, kv_both)
    seq_arg, core_arg = scalar(seq_id), scalar(core)
    attended, lse = attend(seq_arg, qf, sources, doc_k, doc_q)
    att_flat = attended.reshape(tokens, width)
    resid, normed2 = out_project(x, att_flat, w_out, gain2)
    normed2_other = swap(normed2, "seq", 1)
    h_own, gg_own, gu_own = feed_forward(core_arg, normed2, cot, w_gate, w_up, w_down)
    h_oth, gg_oth, gu_oth = feed_forward(core_arg, normed2_other, cot_other, w_gate, w_up, w_down)

    def scatter(send, keep, x_first):
        held = [keep]
        steps = [("seq", 2, x_bit), ("rows", 1, y_bit)]
        if not x_first:
            steps.reverse()
        held.append(swap(send, *steps[0][:2]))

        def halve(axis, mask, bit, dim):
            def at(which):
                return [
                    lax.dynamic_index_in_dim(h, which, dim, keepdims=False).astype(F32)
                    for h in held
                ]

            out = functools.reduce(jnp.add, at(1 - bit)).astype(BF16)
            mine = at(bit)
            held[:] = [*mine, swap(out, axis, mask)]

        halve(*steps[1], 1)
        high = rows_size // 2
        mask = 2
        while high > 1:
            held[:] = [h.reshape((high // 2, 2) + h.shape[1:]) for h in held]
            halve("rows", mask, (rows_id // mask) % 2, 1)
            high //= 2
            mask *= 2
        held[:] = [
            h.reshape((2, width // (blocks * 2), h.shape[-1])) for h in held
        ]
        halve("seq", 1, core, 0)
        last = held.pop().astype(F32)
        own = functools.reduce(jnp.add, [h.astype(F32) for h in held])
        return jnp.where(
            core == 0,
            jnp.concatenate([own, last], axis=-1),
            jnp.concatenate([last, own], axis=-1),
        )

    def scatter_halves(mine, other, x_first):
        came = swap(other, "seq", 1)
        cols = mine.shape[-1]
        shape = (blocks // 4, 2, 2, width // blocks, cols)
        axis = 2 if x_first else 1
        bit = x_bit if x_first else y_bit

        def at(which):
            return (
                lax.dynamic_index_in_dim(mine.reshape(shape), which, axis, keepdims=False).astype(F32)
                + lax.dynamic_index_in_dim(came.reshape(shape), which, axis, keepdims=False).astype(F32)
            ).astype(BF16)

        return scatter(at(1 - bit), at(bit), x_first)

    def ff_grad(left, right, x_first):
        bit = scalar(x_bit if x_first else y_bit)
        send, keep = weight_grad(bit, x_first, left, right, blocks)
        return scatter(send, keep, x_first)

    grad_down = ff_grad((cot, cot_other), (h_own, h_oth), True)
    grad_gate = ff_grad((normed2, normed2_other), (gg_own, gg_oth), False)
    grad_up = ff_grad((normed2, normed2_other), (gu_own, gu_oth), True)

    gn2_send = ff_back(core_arg, gg_oth, gu_oth, w_gate, w_up, BF16)
    gn2_came = swap(gn2_send, "seq", 1)
    gn2_own = ff_back(core_arg, gg_own, gu_own, w_gate, w_up, F32)
    down_own, down_send = down_project(core_arg, h_own, h_oth, w_down)
    down_came = swap(down_send, "seq", 1)
    layer_output = (resid + down_own + down_came.astype(F32)).astype(BF16)

    grad_resid, branch, grad_att, grad_norm2 = out_back(cot, gn2_own, gn2_came, resid, w_out, gain2)
    grad_out = scatter_halves(*weight_halves(core_arg, branch, att_flat), False)

    gq, near, far = attend_back(
        seq_arg,
        qf,
        sources,
        doc_k,
        doc_q,
        lse,
        attended,
        grad_att.reshape(row_count, local_len, width),
        cos,
        sin,
    )
    gq = gq.reshape(tokens, Q_COLS)
    far_came = swap(far, "seq", 1)
    x_send = (near[1].astype(F32) + far_came[1].astype(F32)).astype(BF16)
    x_came = swap(x_send, "seq", 2)
    flat = lambda value: value.reshape(tokens, KV_COLS)
    gkv, input_grad, grad_norm1 = finish(
        flat(near[0]),
        flat(far_came[0]),
        flat(x_came),
        gq,
        w_query,
        w_keyval,
        x,
        gain1,
        grad_resid,
        cos,
        sin,
    )

    def with_gain(mine, other, gain_grad, spare):
        column = gain_grad.reshape(width, 1)
        coarse = column.astype(BF16)
        fine = (column - coarse.astype(F32)).astype(BF16)
        pair = jnp.concatenate([coarse, fine], axis=1)
        at = mine.shape[-1] - spare
        add = jnp.pad(pair, ((0, 0), (at, spare - 2)))
        return (
            mine + jnp.where(core == 1, add, jnp.zeros_like(add)),
            other + jnp.where(core == 0, add, jnp.zeros_like(add)),
        )

    def small_grad(right, gain_grad, x_first):
        cols = right.shape[1]
        padded = jnp.pad(right, ((0, 0), (0, 512 - cols)))
        mine, other = weight_halves(core_arg, normed, padded)
        mine, other = with_gain(mine, other, gain_grad, 512 - cols)
        out = scatter_halves(mine, other, x_first)
        return out[:, :cols], out[:, cols] + out[:, cols + 1]

    grad_query, grad_norm2 = small_grad(gq, grad_norm2, True)
    grad_keyval, grad_norm1 = small_grad(gkv, grad_norm1, False)
    return (
        layer_output.reshape(row_count, local_len, width),
        input_grad.reshape(row_count, local_len, width),
        grad_norm1,
        grad_query,
        grad_keyval,
        grad_out.T,
        grad_norm2,
        grad_gate,
        grad_up,
        grad_down.T,
    )


def solution(mesh):
    return jax.shard_map(
        body,
        mesh=mesh,
        in_specs=(
            P("rows", "seq", None),
            P("rows", None),
            P(),
            P(),
            P(),
            P(),
            P(),
            P(),
            P(),
            P(),
            P("rows", "seq", None),
        ),
        out_specs=(
            P("rows", "seq", None),
            P("rows", "seq", None),
            P(("rows", "seq")),
            P(("rows", "seq"), None),
            P(("rows", "seq"), None),
            P(None, ("rows", "seq")),
            P(("rows", "seq")),
            P(("rows", "seq"), None),
            P(("rows", "seq"), None),
            P(None, ("rows", "seq")),
        ),
        check_vma=False,
    )
```

```python
import functools

import jax
import jax.numpy as jnp
from jax import lax
from jax.experimental import pallas as pl
from jax.experimental.pallas import tpu as pltpu
from jax.sharding import PartitionSpec as P

HEADS = 16
HEAD_DIM = 64
RANK_Q = 6
RANK_KV = 2
Q_COLS = RANK_Q * (HEADS + HEAD_DIM)
KV_COLS = 2 * RANK_KV * (HEADS + HEAD_DIM)
EPS = 1e-06
ROPE_BASE = 10000.0
MASKED = -1e30
SCORE_SCALE = HEAD_DIM ** (-0.5)
VALUE_BASE = RANK_KV * (HEADS + HEAD_DIM)
TILE = 128
TILES = 9
F32 = jnp.float32
BF16 = jnp.bfloat16
NT = (((1,), (1,)), ((), ()))
TN = (((0,), (0,)), ((), ()))


def dot(left, right, dims=None):
    if dims is None:
        return jnp.dot(left, right, preferred_element_type=F32)
    return lax.dot_general(left, right, dims, preferred_element_type=F32)


def params(mib):
    return pltpu.CompilerParams(vmem_limit_bytes=mib * 2**20)


def cost(flops, nbytes, trans=0):
    return pl.CostEstimate(flops=flops, bytes_accessed=nbytes, transcendentals=trans)


def once(shape, index):
    return pl.BlockSpec(shape, index, pipeline_mode=pl.Buffered(1))


def aligned(value, factor):
    return pl.multiple_of(value, factor)


def project_kernel(x_ref, gain_ref, wq_ref, wkv_ref, cos_ref, sin_ref, normed_ref, qf_ref, kv_ref):
    x = x_ref[...].astype(F32)
    scale = lax.rsqrt(jnp.mean(x * x, axis=-1, keepdims=True) + EPS)
    normed = (x * scale * gain_ref[...]).astype(BF16)
    normed_ref[...] = normed
    qf = dot(normed, wq_ref[...], NT)
    kvf = dot(normed, wkv_ref[...], NT)
    cos, sin = cos_ref[0], sin_ref[0]
    half = HEAD_DIM // 2
    qt = qf.T
    split = RANK_Q * HEADS
    qf_ref[0, :split, :] = qt[:split]
    for r in range(RANK_Q):
        at = split + r * HEAD_DIM
        first, second = qt[at : at + half], qt[at + half : at + HEAD_DIM]
        qf_ref[0, at : at + half, :] = first * cos - second * sin
        qf_ref[0, at + half : at + HEAD_DIM, :] = second * cos + first * sin
    kvt = kvf.T
    split = RANK_KV * HEADS
    pieces = [kvt[:split]]
    for r in range(RANK_KV):
        at = split + r * HEAD_DIM
        first, second = kvt[at : at + half], kvt[at + half : at + HEAD_DIM]
        pieces += [first * cos - second * sin, second * cos + first * sin]
    pieces.append(kvt[split + RANK_KV * HEAD_DIM :])
    kv_ref[...] = jnp.concatenate(pieces, axis=0).T.astype(BF16)


def project(x, gain, w_query, w_keyval, cos, sin):
    tokens, width = x.shape
    span = cos.shape[-1]
    groups = tokens // span
    full = lambda i: (0, 0)
    return pl.pallas_call(
        project_kernel,
        grid=(groups,),
        in_specs=[
            pl.BlockSpec((span, width), lambda i: (i, 0)),
            pl.BlockSpec((1, width), full),
            once((Q_COLS, width), full),
            once((KV_COLS, width), full),
            pl.BlockSpec((1, HEAD_DIM // 2, span), lambda i: (i % 2, 0, 0)),
            pl.BlockSpec((1, HEAD_DIM // 2, span), lambda i: (i % 2, 0, 0)),
        ],
        out_specs=[
            pl.BlockSpec((span, width), lambda i: (i, 0)),
            pl.BlockSpec((1, Q_COLS, span), lambda i: (i, 0, 0)),
            pl.BlockSpec((span, KV_COLS), lambda i: (i, 0)),
        ],
        out_shape=[
            jax.ShapeDtypeStruct((tokens, width), BF16),
            jax.ShapeDtypeStruct((groups, Q_COLS, span), F32),
            jax.ShapeDtypeStruct((tokens, KV_COLS), BF16),
        ],
        compiler_params=params(20),
        cost_estimate=cost(2 * tokens * width * (Q_COLS + KV_COLS), 8 * 2**20),
        name="project",
    )(x, gain, w_query, w_keyval, cos, sin)


def tile_spans(seq_id):
    return ((seq_id, 0, seq_id + 2), (7 - seq_id, 3, 7 - seq_id))


def gather_keys(seq_id, sources, qf_ref, qa, kvpos, kvt, kva, bias, doc_ref, span):
    for which, source in enumerate(sources):
        holder = seq_id ^ which
        kvpos[holder * span : (holder + 1) * span, :] = source[0, :span, :]
        kvpos[(7 - holder) * span : (8 - holder) * span, :] = source[0, span:, :]
    docs = jnp.where(pl.program_id(0) == 0, doc_ref[0:1, :], doc_ref[1:2, :])
    at = 0
    for s, (number, first, count) in enumerate(tile_spans(seq_id)):
        own = jnp.broadcast_to(docs[:, number * span : (number + 1) * span].astype(F32), (8, span))
        doc_q = own.T[:, 0:1].astype(jnp.int32)
        for tile in range(first, first + count):
            start = tile * TILE
            cols = slice(at, at + TILE)
            kvt[:, cols] = kvpos[start : start + TILE, :].astype(F32).T
            allowed = doc_q == docs[:, start : start + TILE]
            if start + TILE > number * span + 1:
                pos_q = number * span + lax.broadcasted_iota(jnp.int32, (span, TILE), 0)
                pos_k = start + lax.broadcasted_iota(jnp.int32, (span, TILE), 1)
                allowed = allowed & (pos_k <= pos_q)
            bias[:, cols] = jnp.where(allowed, 0.0, MASKED)
            at += TILE
    split = RANK_KV * HEADS
    kva[:split, 0, :] = kvt[:split, :]
    kva[split:, 0, :] = kvt[VALUE_BASE : VALUE_BASE + split, :]
    for s in range(2):
        qa[s, :, 0, :] = qf_ref[s, : RANK_Q * HEADS, :]


def expand_queries(qf_ref, qa, s, head):
    split = RANK_Q * HEADS
    total = None
    for r in range(RANK_Q):
        weight = qa[s, r * HEADS + head]
        term = weight * qf_ref[s, split + r * HEAD_DIM : split + (r + 1) * HEAD_DIM, :]
        total = term if total is None else total + term
    return (total * (1.0 / RANK_Q)).astype(BF16) * BF16(SCORE_SCALE)


def expand_pair(kvt, kva, base, head):
    split = RANK_KV * HEADS
    total = None
    for r in range(RANK_KV):
        at = base + split + r * HEAD_DIM
        weight = kva[(base // VALUE_BASE) * split + r * HEADS + head]
        term = weight * kvt[at : at + HEAD_DIM, :]
        total = term if total is None else total + term
    return (total * (1.0 / RANK_KV)).astype(BF16)


def per_device(kernel):
    def run(seq_ref, *refs):
        for seq_id in range(4):

            @pl.when(seq_ref[0] == seq_id)
            def _():
                kernel(seq_id, *refs)

    return run


def weave(*streams):
    streams = list(streams)
    while streams:
        for stream in list(streams):
            try:
                next(stream)
            except StopIteration:
                streams.remove(stream)


def chunks(seq_id):
    at, out = 0, []
    for _, _, count in tile_spans(seq_id):
        edges = [*range(at, at + count * TILE, 2 * TILE), at + count * TILE]
        out.append([slice(lo, hi) for lo, hi in zip(edges, edges[1:])])
        at += count * TILE
    return out


def attend_kernel(
    seq_id, qf_ref, kv0, kv1, kv2, kv3, doc_ref, out_ref, lse_ref,
    kvpos, kvt, bias, kva, qa, heads_out, heads_lse, score_a, score_b, top_a, top_b,
):
    span = qf_ref.shape[-1]
    gather_keys(
        seq_id, (kv0, kv1, kv2, kv3), qf_ref, qa, kvpos, kvt, kva, bias, doc_ref, span
    )
    pieces = chunks(seq_id)

    def scores_of(head, score, top):
        keys = expand_pair(kvt, kva, 0, head)
        yield
        for s in range(2):
            queries = expand_queries(qf_ref, qa, s, head).T
            best = None
            for cols in pieces[s]:
                part = dot(queries, keys[:, cols]) + bias[:, cols]
                score[:, cols] = part
                for at in range(0, part.shape[1], TILE):
                    tile = part[:, at : at + TILE]
                    best = tile if best is None else jnp.maximum(best, tile)
                yield
            top[s] = jnp.max(best, axis=-1, keepdims=True)

    def weigh(head, score, top):
        values = expand_pair(kvt, kva, VALUE_BASE, head)
        values = jnp.concatenate([values, jnp.ones((16, values.shape[1]), BF16)], axis=0)
        yield
        for s in range(2):
            peak = top[s]
            out = None
            for cols in pieces[s]:
                part = dot(jnp.exp(score[:, cols] - peak).astype(BF16), values[:, cols], NT)
                out = part if out is None else out + part
                yield
            total = out[:, HEAD_DIM : HEAD_DIM + 1]
            heads_out[s, head] = out[:, :HEAD_DIM] * (1.0 / total)
            heads_lse[s, head] = peak + jnp.log(total)

    def pair_step(pair, carry):
        head = 2 * pair
        weave(scores_of(head + 1, score_b, top_b), weigh(head, score_a, top_a))
        following = jnp.minimum(head + 2, HEADS - 1)
        weave(scores_of(following, score_a, top_a), weigh(head + 1, score_b, top_b))
        return carry

    weave(scores_of(0, score_a, top_a))
    lax.fori_loop(0, HEADS // 2, pair_step, 0)
    lane = lax.broadcasted_iota(jnp.int32, (span, TILE), 1)
    for s in range(2):
        out_ref[0, s * span : (s + 1) * span, :] = jnp.concatenate(
            [heads_out[s, head] for head in range(HEADS)], axis=1
        ).astype(BF16)
        lse = jnp.zeros((span, TILE), F32)
        for head in range(HEADS):
            lse = jnp.where(lane == head, heads_lse[s, head], lse)
        lse_ref[s] = lse


def attention_specs(span, length):
    kv_spec = pl.BlockSpec((1, 2 * span, KV_COLS), lambda i, s: (i, 0, 0))
    return [
        pl.BlockSpec((2, Q_COLS, span), lambda i, s: (i, 0, 0)),
        kv_spec,
        kv_spec,
        kv_spec,
        kv_spec,
        pl.BlockSpec((2, length), lambda i, s: (0, 0)),
    ]


def attend(seq_id, qf, sources, docs):
    rows, length = docs.shape
    span = qf.shape[-1]
    width = HEADS * HEAD_DIM
    return pl.pallas_call(
        per_device(attend_kernel),
        grid_spec=pltpu.PrefetchScalarGridSpec(
            num_scalar_prefetch=1,
            grid=(rows,),
            in_specs=attention_specs(span, length),
            out_specs=[
                pl.BlockSpec((1, 2 * span, width), lambda i, s: (i, 0, 0)),
                pl.BlockSpec((2, span, TILE), lambda i, s: (i, 0, 0)),
            ],
            scratch_shapes=[
                pltpu.VMEM((length, KV_COLS), BF16),
                pltpu.VMEM((KV_COLS, TILES * TILE), F32),
                pltpu.VMEM((span, TILES * TILE), F32),
                pltpu.VMEM((2 * RANK_KV * HEADS, 1, TILES * TILE), F32),
                pltpu.VMEM((2, RANK_Q * HEADS, 1, span), F32),
                pltpu.VMEM((2, HEADS, span, HEAD_DIM), F32),
                pltpu.VMEM((2, HEADS, span, 1), F32),
                pltpu.VMEM((span, TILES * TILE), F32),
                pltpu.VMEM((span, TILES * TILE), F32),
                pltpu.VMEM((2, span, 1), F32),
                pltpu.VMEM((2, span, 1), F32),
            ],
        ),
        out_shape=[
            jax.ShapeDtypeStruct((rows, 2 * span, width), BF16),
            jax.ShapeDtypeStruct((2 * rows, span, TILE), F32),
        ],
        compiler_params=params(24),
        cost_estimate=cost(12 * 10**9, 8 * 2**20),
        name="attend",
    )(seq_id, qf, *sources, docs)


def attend_back_kernel(
    seq_id, qf_ref, kv0, kv1, kv2, kv3, doc_ref, lse_ref, att_ref, grad_ref,
    cos_ref, sin_ref, gq_ref, near_ref, far_ref,
    kvpos, kvt, bias, dot_t, stats, gkvt, gkvpos, gqt, gka, gqa, kva, qa,
    probs_a, probs_b, grads_a, grads_b, q_a, q_b,
):
    span = qf_ref.shape[-1]
    gather_keys(
        seq_id, (kv0, kv1, kv2, kv3), qf_ref, qa, kvpos, kvt, kva, bias, doc_ref, span
    )
    width = HEADS * HEAD_DIM
    chooser = (
        lax.broadcasted_iota(jnp.int32, (width, TILE), 0) // HEAD_DIM
        == lax.broadcasted_iota(jnp.int32, (width, TILE), 1)
    ).astype(BF16)
    for s in range(2):
        grad = grad_ref[0, s * span : (s + 1) * span, :]
        dot_t[s] = grad.T
        product = grad.astype(F32) * att_ref[0, s * span : (s + 1) * span, :].astype(F32)
        coarse = product.astype(BF16)
        fine = (product - coarse.astype(F32)).astype(BF16)
        centre = dot(coarse, chooser) + dot(fine, chooser)
        for head in range(HEADS):
            stats[0, s, head] = jnp.broadcast_to(lse_ref[s, :, head : head + 1], (span, TILE))
            stats[1, s, head] = jnp.broadcast_to(centre[:, head : head + 1], (span, TILE))
    gkvt[...] = jnp.zeros_like(gkvt)
    gqt[...] = jnp.zeros_like(gqt)

    pieces = chunks(seq_id)
    split = RANK_KV * HEADS

    def wide(value, cols):
        return jnp.concatenate([value] * ((cols.stop - cols.start) // TILE), axis=1)

    def scores_of(head, hold):
        probs_of, grads_of, q_of = hold
        rows = pl.ds(aligned(head * HEAD_DIM, HEAD_DIM), HEAD_DIM)
        keys = expand_pair(kvt, kva, 0, head)
        values = expand_pair(kvt, kva, VALUE_BASE, head)
        yield
        for s in range(2):
            q_t = expand_queries(qf_ref, qa, s, head)
            q_of[s] = q_t
            queries, grads = q_t.T, dot_t[s, rows, :].T
            for cols in pieces[s]:
                score = dot(queries, keys[:, cols]) + bias[:, cols]
                probs = jnp.exp(score - wide(stats[0, s, head], cols))
                grad_p = dot(grads, values[:, cols])
                probs_of[:, cols] = probs.astype(BF16)
                grads_of[:, cols] = (probs * (grad_p - wide(stats[1, s, head], cols))).astype(BF16)
                yield

    def grads_of_head(head, hold):
        probs_of, grads_of, q_of = hold
        rows = pl.ds(aligned(head * HEAD_DIM, HEAD_DIM), HEAD_DIM)
        keys = expand_pair(kvt, kva, 0, head)
        yield
        for s in range(2):
            q_t, g_t = q_of[s], dot_t[s, rows, :]
            grad_q = None
            for cols in pieces[s]:
                grad_s = grads_of[:, cols]
                part = dot(keys[:, cols], grad_s, NT)
                grad_q = part if grad_q is None else grad_q + part
                for base, grad in (
                    (0, dot(q_t, grad_s)),
                    (VALUE_BASE, dot(g_t, probs_of[:, cols])),
                ):
                    for r in range(RANK_KV):
                        where = base + split + r * HEAD_DIM
                        b_rows = slice(where, where + HEAD_DIM)
                        a_row = (base // VALUE_BASE) * split + r * HEADS + head
                        gka[a_row, :, cols] = jnp.sum(
                            grad * kvt[b_rows, cols], axis=0, keepdims=True
                        )
                        gkvt[b_rows, cols] += grad * kva[a_row, :, cols]
                yield
            where = RANK_Q * HEADS
            for r in range(RANK_Q):
                b_rows = slice(where + r * HEAD_DIM, where + (r + 1) * HEAD_DIM)
                a_row = r * HEADS + head
                gqa[s, a_row] = jnp.sum(grad_q * qf_ref[s, b_rows, :], axis=0, keepdims=True)
                gqt[s, b_rows, :] += grad_q * qa[s, a_row]
            yield

    def pair_step(pair, carry):
        head = 2 * pair
        weave(scores_of(head + 1, hold_b), grads_of_head(head, hold_a))
        following = jnp.minimum(head + 2, HEADS - 1)
        weave(scores_of(following, hold_a), grads_of_head(head + 1, hold_b))
        return carry

    hold_a, hold_b = (probs_a, grads_a, q_a), (probs_b, grads_b, q_b)
    weave(scores_of(0, hold_a))
    lax.fori_loop(0, HEADS // 2, pair_step, 0)
    half = HEAD_DIM // 2
    split = RANK_Q * HEADS
    for s in range(2):
        cos, sin = cos_ref[s], sin_ref[s]
        pieces = [gqa[s, :, 0, :]]
        for r in range(RANK_Q):
            at = split + r * HEAD_DIM
            first, second = gqt[s, at : at + half, :], gqt[s, at + half : at + HEAD_DIM, :]
            pieces += [first * cos + second * sin, second * cos - first * sin]
        back = jnp.concatenate(pieces, axis=0) * (SCORE_SCALE / RANK_Q)
        gq_ref[0, s * span : (s + 1) * span, :] = back.T.astype(BF16)
    split = RANK_KV * HEADS
    gkvt[:split, :] = gka[:split, 0, :]
    gkvt[VALUE_BASE : VALUE_BASE + split, :] = gka[split:, 0, :]
    gkvpos[...] = jnp.zeros_like(gkvpos)
    at = 0
    for _, first, count in tile_spans(seq_id):
        for tile in range(first, first + count):
            rows = slice(tile * TILE, (tile + 1) * TILE)
            gkvpos[rows, :] += (gkvt[:, at : at + TILE] * (1.0 / RANK_KV)).T
            at += TILE
    for which in range(4):
        holder = seq_id ^ which
        target = near_ref if which in (0, 2) else far_ref
        for s, number in enumerate((holder, 7 - holder)):
            target[which // 2, 0, s * span : (s + 1) * span, :] = gkvpos[
                number * span : (number + 1) * span, :
            ].astype(BF16)


def attend_back(seq_id, qf, sources, docs, lse, attended, grad_attended, cos, sin):
    rows, length = docs.shape
    span = qf.shape[-1]
    width = HEADS * HEAD_DIM
    wide = pl.BlockSpec((1, 2 * span, width), lambda i, s: (i, 0, 0))
    rope = pl.BlockSpec((2, HEAD_DIM // 2, span), lambda i, s: (0, 0, 0))
    parts = pl.BlockSpec((2, 1, 2 * span, KV_COLS), lambda i, s: (0, i, 0, 0))
    return pl.pallas_call(
        per_device(attend_back_kernel),
        grid_spec=pltpu.PrefetchScalarGridSpec(
            num_scalar_prefetch=1,
            grid=(rows,),
            in_specs=attention_specs(span, length)
            + [pl.BlockSpec((2, span, TILE), lambda i, s: (i, 0, 0)), wide, wide, rope, rope],
            out_specs=[
                pl.BlockSpec((1, 2 * span, Q_COLS), lambda i, s: (i, 0, 0)),
                parts,
                parts,
            ],
            scratch_shapes=[
                pltpu.VMEM((length, KV_COLS), BF16),
                pltpu.VMEM((KV_COLS, TILES * TILE), F32),
                pltpu.VMEM((span, TILES * TILE), F32),
                pltpu.VMEM((2, width, span), BF16),
                pltpu.VMEM((2, 2, HEADS, span, TILE), F32),
                pltpu.VMEM((KV_COLS, TILES * TILE), F32),
                pltpu.VMEM((length, KV_COLS), F32),
                pltpu.VMEM((2, Q_COLS, span), F32),
                pltpu.VMEM((2 * RANK_KV * HEADS, 1, TILES * TILE), F32),
                pltpu.VMEM((2, RANK_Q * HEADS, 1, span), F32),
                pltpu.VMEM((2 * RANK_KV * HEADS, 1, TILES * TILE), F32),
                pltpu.VMEM((2, RANK_Q * HEADS, 1, span), F32),
                pltpu.VMEM((span, TILES * TILE), BF16),
                pltpu.VMEM((span, TILES * TILE), BF16),
                pltpu.VMEM((span, TILES * TILE), BF16),
                pltpu.VMEM((span, TILES * TILE), BF16),
                pltpu.VMEM((2, HEAD_DIM, span), BF16),
                pltpu.VMEM((2, HEAD_DIM, span), BF16),
            ],
        ),
        out_shape=[
            jax.ShapeDtypeStruct((rows, 2 * span, Q_COLS), BF16),
            jax.ShapeDtypeStruct((2, rows, 2 * span, KV_COLS), BF16),
            jax.ShapeDtypeStruct((2, rows, 2 * span, KV_COLS), BF16),
        ],
        compiler_params=params(32),
        cost_estimate=cost(25 * 10**9, 12 * 2**20),
        name="attend_back",
    )(seq_id, qf, *sources, docs, lse, attended, grad_attended, cos, sin)


def out_kernel(x_ref, att_ref, w_ref, gain_ref, resid_ref, normed_ref):
    resid = x_ref[...].astype(F32) + dot(att_ref[...], w_ref[...])
    scale = lax.rsqrt(jnp.mean(resid * resid, axis=-1, keepdims=True) + EPS)
    resid_ref[...] = resid
    normed_ref[...] = (resid * scale * gain_ref[...]).astype(BF16)


def out_project(x, attended, w_out, gain):
    tokens, width = x.shape
    step = tokens // 2
    tile = pl.BlockSpec((step, width), lambda i: (i, 0))
    return pl.pallas_call(
        out_kernel,
        grid=(2,),
        in_specs=[
            tile,
            tile,
            once(w_out.shape, lambda i: (0, 0)),
            pl.BlockSpec((1, width), lambda i: (0, 0)),
        ],
        out_specs=[tile, tile],
        out_shape=[
            jax.ShapeDtypeStruct((tokens, width), F32),
            jax.ShapeDtypeStruct((tokens, width), BF16),
        ],
        compiler_params=params(20),
        cost_estimate=cost(2 * tokens * width * width, 10 * 2**20),
        name="out_project",
    )(x, attended, w_out, gain)


def out_back_kernel(
    cot_ref, own_ref, other_ref, resid_ref, w_ref, gain_ref, gr_ref, gb_ref, ga_ref, gain_grad_ref
):
    grad = own_ref[...] + other_ref[...].astype(F32)
    values = resid_ref[...]
    scale = lax.rsqrt(jnp.mean(values * values, axis=-1, keepdims=True) + EPS)
    weighted = grad * gain_ref[...]
    back = scale * weighted - values * (scale * scale * scale) * jnp.mean(
        weighted * values, axis=-1, keepdims=True
    )
    grad_resid = cot_ref[...].astype(F32) + back
    branch = grad_resid.astype(BF16)
    gr_ref[...] = grad_resid
    gb_ref[...] = branch
    ga_ref[...] = dot(branch, w_ref[...], NT).astype(BF16)

    @pl.when(pl.program_id(0) == 0)
    def _():
        gain_grad_ref[...] = jnp.zeros_like(gain_grad_ref)

    gain_grad_ref[...] += jnp.sum(grad * values * scale, axis=0, keepdims=True)


def out_back(cot, own, other, resid, w_out, gain):
    tokens, width = cot.shape
    step = tokens // 2
    tile = pl.BlockSpec((step, width), lambda i: (i, 0))
    row = pl.BlockSpec((1, width), lambda i: (0, 0))
    return pl.pallas_call(
        out_back_kernel,
        grid=(2,),
        in_specs=[tile, tile, tile, tile, once(w_out.shape, lambda i: (0, 0)), row],
        out_specs=[tile, tile, tile, row],
        out_shape=[
            jax.ShapeDtypeStruct((tokens, width), F32),
            jax.ShapeDtypeStruct((tokens, width), BF16),
            jax.ShapeDtypeStruct((tokens, width), BF16),
            jax.ShapeDtypeStruct((1, width), F32),
        ],
        compiler_params=params(26),
        cost_estimate=cost(2 * tokens * width * width, 16 * 2**20),
        name="out_back",
    )(cot, own, other, resid, w_out, gain)


def ff_kernel(core_ref, n2_ref, cot_ref, wg_ref, wu_ref, wd_ref, h_ref, gg_ref, gu_ref):
    gate = dot(n2_ref[...], wg_ref[...])
    up = dot(n2_ref[...], wu_ref[...])
    grad_hidden = dot(cot_ref[...], wd_ref[...], NT)
    sigmoid = 1.0 / (1.0 + jnp.exp(-gate))
    silu = gate * sigmoid
    h_ref[...] = (silu * up).astype(BF16)
    gu_ref[...] = (grad_hidden * silu).astype(BF16)
    gg_ref[...] = (grad_hidden * up * (sigmoid + silu * (1.0 - sigmoid))).astype(BF16)


def feed_forward(core, n2, cot, w_gate, w_up, w_down):
    tokens, width = n2.shape
    half = w_gate.shape[1] // 2
    step = tokens // 2
    tile = pl.BlockSpec((step, width), lambda i, c: (i, 0))
    out = pl.BlockSpec((step, half), lambda i, c: (i, 0))
    return pl.pallas_call(
        ff_kernel,
        grid_spec=pltpu.PrefetchScalarGridSpec(
            num_scalar_prefetch=1,
            grid=(2,),
            in_specs=[
                tile,
                tile,
                once((width, half), lambda i, c: (0, c[0])),
                once((width, half), lambda i, c: (0, c[0])),
                once((half, width), lambda i, c: (c[0], 0)),
            ],
            out_specs=[out, out, out],
        ),
        out_shape=[jax.ShapeDtypeStruct((tokens, half), BF16)] * 3,
        compiler_params=params(32),
        cost_estimate=cost(6 * tokens * width * half, 18 * 2**20),
        name="feed_forward",
    )(core, n2, cot, w_gate, w_up, w_down)


def ff_back_kernel(core_ref, gg_ref, gu_ref, wg_ref, wu_ref, out_ref):
    out_ref[...] = (
        dot(gg_ref[...], wg_ref[...], NT) + dot(gu_ref[...], wu_ref[...], NT)
    ).astype(out_ref.dtype)


def ff_back(core, gg, gu, w_gate, w_up, dtype):
    tokens, half = gg.shape
    width = w_gate.shape[0]
    step = tokens // 2
    tile = pl.BlockSpec((step, half), lambda i, c: (i, 0))
    weight = once((width, half), lambda i, c: (0, c[0]))
    return pl.pallas_call(
        ff_back_kernel,
        grid_spec=pltpu.PrefetchScalarGridSpec(
            num_scalar_prefetch=1,
            grid=(2,),
            in_specs=[tile, tile, weight, weight],
            out_specs=pl.BlockSpec((step, width), lambda i, c: (i, 0)),
        ),
        out_shape=jax.ShapeDtypeStruct((tokens, width), dtype),
        compiler_params=params(24),
        cost_estimate=cost(4 * tokens * width * half, 12 * 2**20),
        name="ff_back",
    )(core, gg, gu, w_gate, w_up)


def down_kernel(core_ref, own_ref, other_ref, w_ref, own_out, other_out):
    own_out[...] = dot(own_ref[...], w_ref[...])
    other_out[...] = dot(other_ref[...], w_ref[...]).astype(BF16)


def down_project(core, own, other, w_down):
    tokens, half = own.shape
    width = w_down.shape[1]
    step = tokens // 2
    tile = pl.BlockSpec((step, half), lambda i, c: (i, 0))
    out = pl.BlockSpec((step, width), lambda i, c: (i, 0))
    return pl.pallas_call(
        down_kernel,
        grid_spec=pltpu.PrefetchScalarGridSpec(
            num_scalar_prefetch=1,
            grid=(2,),
            in_specs=[tile, tile, once((half, width), lambda i, c: (c[0], 0))],
            out_specs=[out, out],
        ),
        out_shape=[
            jax.ShapeDtypeStruct((tokens, width), F32),
            jax.ShapeDtypeStruct((tokens, width), BF16),
        ],
        compiler_params=params(20),
        cost_estimate=cost(4 * tokens * width * half, 10 * 2**20),
        name="down_project",
    )(core, own, other, w_down)


def weight_kernel(x_first, id_ref, l0_ref, l1_ref, r0_ref, r1_ref, send_ref, keep_ref):
    total = dot(l0_ref[...], r0_ref[...], TN) + dot(l1_ref[...], r1_ref[...], TN)
    high, _, block, cols = send_ref.shape
    total = total.astype(BF16).reshape(high, 2, 2, block, cols)
    bit = id_ref[0]

    def put(mine):
        if x_first:
            send_ref[...] = total[:, :, 1 - mine]
            keep_ref[...] = total[:, :, mine]
        else:
            send_ref[...] = total[:, 1 - mine]
            keep_ref[...] = total[:, mine]

    @pl.when(bit == 0)
    def _():
        put(0)

    @pl.when(bit == 1)
    def _():
        put(1)


def weight_grad(bit, x_first, left, right, blocks):
    tokens, width = left[0].shape
    cols = right[0].shape[1]
    block = width // blocks
    step = 256
    steps = width // step
    high = step // (4 * block)
    l_spec = pl.BlockSpec((tokens, step), lambda i, b: (0, i))
    r_spec = once((tokens, cols), lambda i, b: (0, 0))
    out = pl.BlockSpec((high, 2, block, cols), lambda i, b: (i, 0, 0, 0))
    shape = jax.ShapeDtypeStruct((blocks // 4, 2, block, cols), BF16)
    return pl.pallas_call(
        functools.partial(weight_kernel, x_first),
        grid_spec=pltpu.PrefetchScalarGridSpec(
            num_scalar_prefetch=1,
            grid=(steps,),
            in_specs=[l_spec, l_spec, r_spec, r_spec],
            out_specs=[out, out],
        ),
        out_shape=[shape, shape],
        compiler_params=params(26),
        cost_estimate=cost(4 * tokens * width * cols, 10 * 2**20),
        name="weight_grad",
    )(bit, left[0], left[1], right[0], right[1])


def half_kernel(core_ref, l_ref, r_ref, mine_ref, other_ref):
    total = dot(l_ref[...], r_ref[...], TN).astype(BF16)
    half = mine_ref.shape[-1]

    @pl.when(core_ref[0] == 0)
    def _():
        mine_ref[...] = total[:, :half]
        other_ref[...] = total[:, half:]

    @pl.when(core_ref[0] == 1)
    def _():
        mine_ref[...] = total[:, half:]
        other_ref[...] = total[:, :half]


def weight_halves(core, left, right):
    tokens, width = left.shape
    cols = right.shape[1]
    step = 256
    out = pl.BlockSpec((step, cols // 2), lambda i, b: (i, 0))
    shape = jax.ShapeDtypeStruct((width, cols // 2), BF16)
    return pl.pallas_call(
        half_kernel,
        grid_spec=pltpu.PrefetchScalarGridSpec(
            num_scalar_prefetch=1,
            grid=(width // step,),
            in_specs=[
                pl.BlockSpec((tokens, step), lambda i, b: (0, i)),
                once((tokens, cols), lambda i, b: (0, 0)),
            ],
            out_specs=[out, out],
        ),
        out_shape=[shape, shape],
        compiler_params=params(16),
        cost_estimate=cost(2 * tokens * width * cols, 4 * 2**20),
        name="weight_halves",
    )(core, left, right)


def finish_kernel(
    k0_ref, r0_ref, x0_ref, gq_ref, wq_ref, wkv_ref, x_ref, gain_ref, gr_ref, cos_ref, sin_ref,
    gkv_ref, out_ref, gain_grad_ref,
):
    total = k0_ref[...].astype(F32) + r0_ref[...].astype(F32) + x0_ref[...].astype(F32)
    cos, sin = cos_ref[0], sin_ref[0]
    half = HEAD_DIM // 2
    split = RANK_KV * HEADS
    turned = total.T
    pieces = [turned[:split]]
    for r in range(RANK_KV):
        at = split + r * HEAD_DIM
        first, second = turned[at : at + half], turned[at + half : at + HEAD_DIM]
        pieces += [first * cos + second * sin, second * cos - first * sin]
    pieces.append(turned[split + RANK_KV * HEAD_DIM :])
    gkv = jnp.concatenate(pieces, axis=0).T.astype(BF16)
    gkv_ref[...] = gkv
    grad = dot(gq_ref[...], wq_ref[...]) + dot(gkv, wkv_ref[...])
    values = x_ref[...].astype(F32)
    scale = lax.rsqrt(jnp.mean(values * values, axis=-1, keepdims=True) + EPS)
    weighted = grad * gain_ref[...]
    back = scale * weighted - values * (scale * scale * scale) * jnp.mean(
        weighted * values, axis=-1, keepdims=True
    )
    out_ref[...] = (gr_ref[...] + back).astype(BF16)

    @pl.when(pl.program_id(0) == 0)
    def _():
        gain_grad_ref[...] = jnp.zeros_like(gain_grad_ref)

    gain_grad_ref[...] += jnp.sum(grad * values * scale, axis=0, keepdims=True)


def finish(kept, near, far, gq, w_query, w_keyval, x, gain, grad_resid, cos, sin):
    tokens, width = x.shape
    span = cos.shape[-1]
    full = lambda i: (0, 0)
    tile = pl.BlockSpec((span, width), lambda i: (i, 0))
    narrow = pl.BlockSpec((span, KV_COLS), lambda i: (i, 0))
    rope = pl.BlockSpec((1, HEAD_DIM // 2, span), lambda i: (i % 2, 0, 0))
    row = pl.BlockSpec((1, width), full)
    return pl.pallas_call(
        finish_kernel,
        grid=(tokens // span,),
        in_specs=[
            narrow,
            narrow,
            narrow,
            pl.BlockSpec((span, Q_COLS), lambda i: (i, 0)),
            once((Q_COLS, width), full),
            once((KV_COLS, width), full),
            tile,
            row,
            tile,
            rope,
            rope,
        ],
        out_specs=[narrow, tile, row],
        out_shape=[
            jax.ShapeDtypeStruct((tokens, KV_COLS), BF16),
            jax.ShapeDtypeStruct((tokens, width), BF16),
            jax.ShapeDtypeStruct((1, width), F32),
        ],
        compiler_params=params(20),
        cost_estimate=cost(2 * tokens * width * (Q_COLS + KV_COLS), 9 * 2**20),
        name="finish",
    )(kept, near, far, gq, w_query, w_keyval, x, gain, grad_resid, cos, sin)


def body(
    layer_input,
    doc_ids,
    norm1_gain,
    w_query,
    w_keyval,
    w_out,
    norm2_gain,
    w_gate,
    w_up,
    w_down,
    cotangent,
):
    row_count, local_len, width = layer_input.shape
    seq_size = lax.axis_size("seq")
    rows_size = lax.axis_size("rows")
    seq_id = lax.axis_index("seq")
    rows_id = lax.axis_index("rows")
    span = local_len // 2
    tokens = row_count * local_len
    length = local_len * seq_size
    core = seq_id % 2
    x_bit = (seq_id // 2) % 2
    y_bit = rows_id % 2
    blocks = rows_size * 2

    def swap(value, axis, mask):
        size = seq_size if axis == "seq" else rows_size
        return lax.ppermute(value, axis, [(i, i ^ mask) for i in range(size)])

    def scalar(value):
        return value.astype(jnp.int32).reshape(1)

    x = layer_input.reshape(tokens, width)
    cot = cotangent.reshape(tokens, width)
    cot_other = swap(cot, "seq", 1)
    gain1 = norm1_gain.reshape(1, width)
    gain2 = norm2_gain.reshape(1, width)

    spans = jnp.stack([seq_id, 2 * seq_size - 1 - seq_id])
    positions = spans[:, None] * span + jnp.arange(span, dtype=jnp.int32)[None, :]
    inv_freq = ROPE_BASE ** (-(jnp.arange(HEAD_DIM // 2, dtype=F32) * (2.0 / HEAD_DIM)))
    angles = positions.astype(F32)[:, None, :] * inv_freq[None, :, None]
    cos, sin = jnp.cos(angles), jnp.sin(angles)
    docs = doc_ids

    normed, qf, kv = project(x, gain1, w_query.T, w_keyval.T, cos, sin)
    kv = kv.reshape(row_count, local_len, KV_COLS)
    kv_core = swap(kv, "seq", 1)
    kv_x = swap(kv, "seq", 2)
    kv_both = swap(kv_x, "seq", 1)
    sources = (kv, kv_core, kv_x, kv_both)
    seq_arg, core_arg = scalar(seq_id), scalar(core)
    attended, lse = attend(seq_arg, qf, sources, docs)
    att_flat = attended.reshape(tokens, width)
    resid, normed2 = out_project(x, att_flat, w_out, gain2)
    normed2_other = swap(normed2, "seq", 1)
    h_own, gg_own, gu_own = feed_forward(core_arg, normed2, cot, w_gate, w_up, w_down)
    h_oth, gg_oth, gu_oth = feed_forward(core_arg, normed2_other, cot_other, w_gate, w_up, w_down)

    def scatter(send, keep, x_first):
        held = [keep]
        steps = [("seq", 2, x_bit), ("rows", 1, y_bit)]
        if not x_first:
            steps.reverse()
        held.append(swap(send, *steps[0][:2]))

        def halve(axis, mask, bit, dim):
            def at(which):
                return [
                    lax.dynamic_index_in_dim(h, which, dim, keepdims=False).astype(F32)
                    for h in held
                ]

            out = functools.reduce(jnp.add, at(1 - bit)).astype(BF16)
            mine = at(bit)
            held[:] = [*mine, swap(out, axis, mask)]

        halve(*steps[1], 1)
        high = rows_size // 2
        mask = 2
        while high > 1:
            held[:] = [h.reshape((high // 2, 2) + h.shape[1:]) for h in held]
            halve("rows", mask, (rows_id // mask) % 2, 1)
            high //= 2
            mask *= 2
        held[:] = [
            h.reshape((2, width // (blocks * 2), h.shape[-1])) for h in held
        ]
        halve("seq", 1, core, 0)
        last = held.pop().astype(F32)
        own = functools.reduce(jnp.add, [h.astype(F32) for h in held])
        return jnp.where(
            core == 0,
            jnp.concatenate([own, last], axis=-1),
            jnp.concatenate([last, own], axis=-1),
        )

    def scatter_halves(mine, other, x_first):
        came = swap(other, "seq", 1)
        cols = mine.shape[-1]
        shape = (blocks // 4, 2, 2, width // blocks, cols)
        axis = 2 if x_first else 1
        bit = x_bit if x_first else y_bit

        def at(which):
            return (
                lax.dynamic_index_in_dim(mine.reshape(shape), which, axis, keepdims=False).astype(F32)
                + lax.dynamic_index_in_dim(came.reshape(shape), which, axis, keepdims=False).astype(F32)
            ).astype(BF16)

        return scatter(at(1 - bit), at(bit), x_first)

    def ff_grad(left, right, x_first):
        bit = scalar(x_bit if x_first else y_bit)
        send, keep = weight_grad(bit, x_first, left, right, blocks)
        return scatter(send, keep, x_first)

    grad_down = ff_grad((cot, cot_other), (h_own, h_oth), True)
    grad_gate = ff_grad((normed2, normed2_other), (gg_own, gg_oth), False)
    grad_up = ff_grad((normed2, normed2_other), (gu_own, gu_oth), True)

    gn2_send = ff_back(core_arg, gg_oth, gu_oth, w_gate, w_up, BF16)
    gn2_came = swap(gn2_send, "seq", 1)
    gn2_own = ff_back(core_arg, gg_own, gu_own, w_gate, w_up, F32)
    down_own, down_send = down_project(core_arg, h_own, h_oth, w_down)
    down_came = swap(down_send, "seq", 1)
    layer_output = (resid + down_own + down_came.astype(F32)).astype(BF16)

    grad_resid, branch, grad_att, grad_norm2 = out_back(cot, gn2_own, gn2_came, resid, w_out, gain2)
    grad_out = scatter_halves(*weight_halves(core_arg, branch, att_flat), False)

    gq, near, far = attend_back(
        seq_arg,
        qf,
        sources,
        docs,
        lse,
        attended,
        grad_att.reshape(row_count, local_len, width),
        cos,
        sin,
    )
    gq = gq.reshape(tokens, Q_COLS)
    far_came = swap(far, "seq", 1)
    x_send = (near[1].astype(F32) + far_came[1].astype(F32)).astype(BF16)
    x_came = swap(x_send, "seq", 2)
    flat = lambda value: value.reshape(tokens, KV_COLS)
    gkv, input_grad, grad_norm1 = finish(
        flat(near[0]),
        flat(far_came[0]),
        flat(x_came),
        gq,
        w_query.T,
        w_keyval.T,
        x,
        gain1,
        grad_resid,
        cos,
        sin,
    )

    def with_gain(mine, other, gain_grad, spare):
        column = gain_grad.reshape(width, 1)
        coarse = column.astype(BF16)
        fine = (column - coarse.astype(F32)).astype(BF16)
        pair = jnp.concatenate([coarse, fine], axis=1)
        at = mine.shape[-1] - spare
        add = jnp.pad(pair, ((0, 0), (at, spare - 2)))
        return (
            mine + jnp.where(core == 1, add, jnp.zeros_like(add)),
            other + jnp.where(core == 0, add, jnp.zeros_like(add)),
        )

    def small_grad(right, gain_grad, x_first):
        cols = right.shape[1]
        padded = jnp.pad(right, ((0, 0), (0, 512 - cols)))
        mine, other = weight_halves(core_arg, normed, padded)
        mine, other = with_gain(mine, other, gain_grad, 512 - cols)
        out = scatter_halves(mine, other, x_first)
        return out[:, :cols], out[:, cols] + out[:, cols + 1]

    grad_query, grad_norm2 = small_grad(gq, grad_norm2, True)
    grad_keyval, grad_norm1 = small_grad(gkv, grad_norm1, False)
    return (
        layer_output.reshape(row_count, local_len, width),
        input_grad.reshape(row_count, local_len, width),
        grad_norm1,
        grad_query,
        grad_keyval,
        grad_out.T,
        grad_norm2,
        grad_gate,
        grad_up,
        grad_down.T,
    )


def solution(mesh):
    return jax.shard_map(
        body,
        mesh=mesh,
        in_specs=(
            P("rows", "seq", None),
            P("rows", None),
            P(),
            P(),
            P(),
            P(),
            P(),
            P(),
            P(),
            P(),
            P("rows", "seq", None),
        ),
        out_specs=(
            P("rows", "seq", None),
            P("rows", "seq", None),
            P(("rows", "seq")),
            P(("rows", "seq"), None),
            P(("rows", "seq"), None),
            P(None, ("rows", "seq")),
            P(("rows", "seq")),
            P(("rows", "seq"), None),
            P(("rows", "seq"), None),
            P(None, ("rows", "seq")),
        ),
        check_vma=False,
    )
```

```python
import functools

import jax
import jax.numpy as jnp
from jax import lax
from jax.experimental import pallas as pl
from jax.experimental.pallas import tpu as pltpu
from jax.sharding import PartitionSpec as P

HEADS = 16
HEAD_DIM = 64
RANK_Q = 6
RANK_KV = 2
Q_COLS = RANK_Q * (HEADS + HEAD_DIM)
KV_COLS = 2 * RANK_KV * (HEADS + HEAD_DIM)
Q_PAD = 512
KV_PAD = 512
EPS = 1e-06
ROPE_BASE = 10000.0
MASKED = -1e30
SCORE_SCALE = HEAD_DIM ** (-0.5)
VALUE_BASE = RANK_KV * (HEADS + HEAD_DIM)
TILE = 128
TILES = 9
F32 = jnp.float32
BF16 = jnp.bfloat16
NT = (((1,), (1,)), ((), ()))
TN = (((0,), (0,)), ((), ()))


def dot(left, right, dims=None):
    if dims is None:
        return jnp.dot(left, right, preferred_element_type=F32)
    return lax.dot_general(left, right, dims, preferred_element_type=F32)


def params(mib):
    return pltpu.CompilerParams(vmem_limit_bytes=mib * 2**20)


def cost(flops, nbytes, trans=0):
    return pl.CostEstimate(flops=flops, bytes_accessed=nbytes, transcendentals=trans)


def once(shape, index):
    return pl.BlockSpec(shape, index, pipeline_mode=pl.Buffered(1))


class Order:
    def __init__(self):
        self.token = None

    def call(self, kernel, args, *, grid, in_specs, out_specs, out_shape, mib, name, scalars=(), scratch=(), after=(), work=0, aliases=None):
        extra = [a for a in (self.token, *after) if a is not None]
        n_scalar, n_in, n_out = len(scalars), len(in_specs), len(out_specs)

        def run(*refs):
            head = refs[: n_scalar + n_in]
            rest = refs[n_scalar + n_in + len(extra) :]
            rest[n_out][...] = jnp.zeros_like(rest[n_out])
            kernel(*head, *rest[:n_out], *rest[n_out + 1 :])

        def spec(block, index, **kw):
            return pl.BlockSpec(block, index, **kw)

        token_spec = pl.BlockSpec((8, TILE), lambda *_: (0, 0))
        out = pl.pallas_call(
            run,
            grid_spec=pltpu.PrefetchScalarGridSpec(
                num_scalar_prefetch=n_scalar,
                grid=grid,
                in_specs=[*in_specs, *[pl.BlockSpec(memory_space=pl.ANY)] * len(extra)],
                out_specs=[*out_specs, token_spec],
                scratch_shapes=list(scratch),
            ),
            out_shape=[*out_shape, jax.ShapeDtypeStruct((8, TILE), F32)],
            compiler_params=params(mib),
            input_output_aliases={n_scalar + k: v for k, v in (aliases or {}).items()},
            cost_estimate=cost(work, 2**16),
            name=name,
        )(*scalars, *args, *extra)
        self.token = out[-1]
        return out[:-1]


def aligned(value, factor):
    return pl.multiple_of(value, factor)


def project_kernel(x_ref, gain_ref, wq_ref, wkv_ref, cos_ref, sin_ref, normed_ref, qf_ref, kv_ref):
    x = x_ref[...].astype(F32)
    scale = lax.rsqrt(jnp.mean(x * x, axis=-1, keepdims=True) + EPS)
    normed = (x * scale * gain_ref[...]).astype(BF16)
    normed_ref[...] = normed
    qf = dot(normed, wq_ref[...], NT)
    kvf = dot(normed, wkv_ref[...], NT)
    cos, sin = cos_ref[0], sin_ref[0]
    half = HEAD_DIM // 2
    qt = qf.T
    split = RANK_Q * HEADS
    qf_ref[0, :split, :] = qt[:split]
    for r in range(RANK_Q):
        at = split + r * HEAD_DIM
        first, second = qt[at : at + half], qt[at + half : at + HEAD_DIM]
        qf_ref[0, at : at + half, :] = first * cos - second * sin
        qf_ref[0, at + half : at + HEAD_DIM, :] = second * cos + first * sin
    kvt = kvf.T
    split = RANK_KV * HEADS
    pieces = [kvt[:split]]
    for r in range(RANK_KV):
        at = split + r * HEAD_DIM
        first, second = kvt[at : at + half], kvt[at + half : at + HEAD_DIM]
        pieces += [first * cos - second * sin, second * cos + first * sin]
    pieces.append(kvt[split + RANK_KV * HEAD_DIM :])
    kv_ref[...] = jnp.concatenate(pieces, axis=0).T.astype(BF16)


def project(order, x, gain, w_query, w_keyval, cos, sin):
    tokens, width = x.shape
    span = cos.shape[-1]
    groups = tokens // span
    full = lambda i: (0, 0)
    rope = pl.BlockSpec((1, HEAD_DIM // 2, span), lambda i: (i % 2, 0, 0))
    return order.call(
        project_kernel,
        (x, gain, w_query, w_keyval, cos, sin),
        grid=(groups,),
        in_specs=[
            pl.BlockSpec((span, width), lambda i: (i, 0)),
            pl.BlockSpec((1, width), full),
            once((Q_COLS, width), full),
            once((KV_COLS, width), full),
            rope,
            rope,
        ],
        out_specs=[
            pl.BlockSpec((span, width), lambda i: (i, 0)),
            pl.BlockSpec((1, Q_COLS, span), lambda i: (i, 0, 0)),
            pl.BlockSpec((span, KV_COLS), lambda i: (i, 0)),
        ],
        out_shape=[
            jax.ShapeDtypeStruct((tokens, width), BF16),
            jax.ShapeDtypeStruct((groups, Q_COLS, span), F32),
            jax.ShapeDtypeStruct((tokens, KV_COLS), BF16),
        ],
        mib=56,
        name="project",
    )


PIECES = ((0, 2), (2, 3), (3, 4), (4, 5), (5, 7), (7, 9))


def tile_place(tile, seq_id):
    low = tile < seq_id + 2
    return low, jnp.where(low, tile, tile + 1 - seq_id)


def piece_side(piece, seq_id):
    first, last = piece
    low = first < seq_id + 2
    side = 0 if last <= 2 else (1 if first > 4 else jnp.where(low, 0, 1))
    return slice(first * TILE, last * TILE), side, low


def choose(side, low, pair):
    return pair[side] if isinstance(side, int) else jnp.where(low, pair[0], pair[1])


def gather(totals, side, low, part, combine, empty):
    for s in range(2):
        if isinstance(side, int):
            if side != s:
                continue
            term = part
        else:
            term = jnp.where(low if s == 0 else ~low, part, empty)
        totals[s] = term if totals[s] is None else combine(totals[s], term)


def gather_keys(seq_id, sources, qf_ref, qa, kvpos, kvt, kva, bias, docs_ref, row, span):
    for which, source in enumerate(sources):
        holder = seq_id ^ which
        kvpos[pl.ds(aligned(holder * span, 32), span), :] = source[0, :span, :]
        kvpos[pl.ds(aligned((7 - holder) * span, 32), span), :] = source[0, span:, :]
    columns = []
    for number in (seq_id, 7 - seq_id):
        ids = None
        for place in range(8):
            part = docs_ref[row : row + 1, place * span : (place + 1) * span]
            ids = part if ids is None else jnp.where(number == place, part, ids)
        columns.append(jnp.broadcast_to(ids.astype(F32), (8, span)).T[:, 0:1].astype(jnp.int32))
    for tile in range(TILES):
        low, place = tile_place(tile, seq_id)
        start = aligned(place * TILE, TILE)
        cols = slice(tile * TILE, (tile + 1) * TILE)
        kvt[:, cols] = kvpos[pl.ds(start, TILE), :].astype(F32).T
        side = 0 if tile < 2 else (1 if tile > 4 else None)
        doc_q = jnp.where(low, columns[0], columns[1]) if side is None else columns[side]
        number = jnp.where(low, seq_id, 7 - seq_id)
        pos_q = number * span + lax.broadcasted_iota(jnp.int32, (span, TILE), 0)
        pos_k = start + lax.broadcasted_iota(jnp.int32, (span, TILE), 1)
        allowed = (doc_q == docs_ref[row : row + 1, pl.ds(start, TILE)]) & (pos_k <= pos_q)
        bias[:, cols] = jnp.where(allowed, 0.0, MASKED)
    split = RANK_KV * HEADS
    kva[:split, 0, :] = kvt[:split, :]
    kva[split:, 0, :] = kvt[VALUE_BASE : VALUE_BASE + split, :]
    for s in range(2):
        qa[s, :, 0, :] = qf_ref[s, : RANK_Q * HEADS, :]


def expand_queries(qf_ref, qa, s, head):
    split = RANK_Q * HEADS
    total = None
    for r in range(RANK_Q):
        weight = qa[s, r * HEADS + head]
        term = weight * qf_ref[s, split + r * HEAD_DIM : split + (r + 1) * HEAD_DIM, :]
        total = term if total is None else total + term
    return (total * (1.0 / RANK_Q)).astype(BF16) * BF16(SCORE_SCALE)


def expand_pair(kvt, kva, base, head):
    split = RANK_KV * HEADS
    total = None
    for r in range(RANK_KV):
        at = base + split + r * HEAD_DIM
        weight = kva[(base // VALUE_BASE) * split + r * HEADS + head]
        term = weight * kvt[at : at + HEAD_DIM, :]
        total = term if total is None else total + term
    return (total * (1.0 / RANK_KV)).astype(BF16)


def weave(*streams):
    streams = list(streams)
    while streams:
        for stream in list(streams):
            try:
                next(stream)
            except StopIteration:
                streams.remove(stream)


SEEN = ((0, 5), (3, 10))


def place_keys(seq_id, sources, kvpos, span):
    for which, source in enumerate(sources):
        holder = seq_id ^ which
        kvpos[pl.ds(aligned(holder * span, 32), span), :] = source[0, :span, :]
        kvpos[pl.ds(aligned((7 - holder) * span, 32), span), :] = source[0, span:, :]


def query_docs(number, docs_ref, row, span):
    ids = None
    for place in range(8):
        part = docs_ref[row : row + 1, place * span : (place + 1) * span]
        ids = part if ids is None else jnp.where(number == place, part, ids)
    return jnp.broadcast_to(ids.astype(F32), (8, span)).T[:, 0:1].astype(jnp.int32)


def attend_kernel(
    row, seq_ref, qf_ref, kv0, kv1, kv2, kv3, doc_ref, out_ref, lse_ref,
    kvpos, kvt, bias_low, bias_high, kva, qa, heads_out, heads_lse,
    low_a, low_b, high_a, high_b, top_a, top_b,
):
    seq_id = seq_ref[0]
    span = qf_ref.shape[-1]
    biases = (bias_low, bias_high)
    place_keys(seq_id, (kv0, kv1, kv2, kv3), kvpos, span)
    length = kvpos.shape[0]
    for at in range(0, length, TILE):
        kvt[:, at : at + TILE] = kvpos[at : at + TILE, :].astype(F32).T
    for s, number in enumerate((seq_id, 7 - seq_id)):
        doc_q = query_docs(number, doc_ref, row, span)
        pos_q = number * span + lax.broadcasted_iota(jnp.int32, (span, TILE), 0)
        for tile in range(*SEEN[s]):
            start = tile * TILE
            pos_k = start + lax.broadcasted_iota(jnp.int32, (span, TILE), 1)
            allowed = (doc_q == doc_ref[row : row + 1, start : start + TILE]) & (pos_k <= pos_q)
            at = start - SEEN[s][0] * TILE
            biases[s][:, at : at + TILE] = jnp.where(allowed, 0.0, MASKED)
    split = RANK_KV * HEADS
    kva[:split, 0, :] = kvt[:split, :] * (1.0 / RANK_KV)
    kva[split:, 0, :] = kvt[VALUE_BASE : VALUE_BASE + split, :] * (1.0 / RANK_KV)
    for s in range(2):
        qa[s, :, 0, :] = qf_ref[s, : RANK_Q * HEADS, :]

    def expand(base, head):
        total = None
        for r in range(RANK_KV):
            at = base + split + r * HEAD_DIM
            weight = kva[(base // VALUE_BASE) * split + r * HEADS + head]
            term = weight * kvt[at : at + HEAD_DIM, :]
            total = term if total is None else total + term
        return total.astype(BF16)

    def pieces(s):
        count = SEEN[s][1] - SEEN[s][0]
        edges = [*range(0, count, 2), count]
        shift = SEEN[s][0] * TILE
        for lo, hi in zip(edges, edges[1:]):
            yield slice(lo * TILE, hi * TILE), slice(shift + lo * TILE, shift + hi * TILE)

    def scores_of(head, scores, top):
        keys = expand(0, head)
        yield
        for s in range(2):
            queries = expand_queries(qf_ref, qa, s, head).T
            best = None
            for cols, places in pieces(s):
                part = dot(queries, keys[:, places]) + biases[s][:, cols]
                scores[s][:, cols] = part
                for at in range(0, part.shape[1], TILE):
                    tile = part[:, at : at + TILE]
                    best = tile if best is None else jnp.maximum(best, tile)
                yield
            top[s] = jnp.max(best, axis=-1, keepdims=True)

    def weigh(head, scores, top):
        values = expand(VALUE_BASE, head)
        values = jnp.concatenate([values, jnp.ones((16, values.shape[1]), BF16)], axis=0)
        yield
        for s in range(2):
            peak = top[s]
            out = None
            for cols, places in pieces(s):
                raised = jnp.exp(scores[s][:, cols] - peak).astype(BF16)
                part = dot(raised, values[:, places], NT)
                out = part if out is None else out + part
                yield
            total = out[:, HEAD_DIM : HEAD_DIM + 1]
            heads_out[s, head] = out[:, :HEAD_DIM] * (1.0 / total)
            heads_lse[s, head] = peak + jnp.log(total)

    scores_a, scores_b = (low_a, high_a), (low_b, high_b)

    def pair_step(pair, carry):
        head = 2 * pair
        weave(scores_of(head + 1, scores_b, top_b), weigh(head, scores_a, top_a))
        following = jnp.minimum(head + 2, HEADS - 1)
        weave(scores_of(following, scores_a, top_a), weigh(head + 1, scores_b, top_b))
        return carry

    weave(scores_of(0, scores_a, top_a))
    lax.fori_loop(0, HEADS // 2, pair_step, 0)
    lane = lax.broadcasted_iota(jnp.int32, (span, TILE), 1)
    for s in range(2):
        out_ref[s * span : (s + 1) * span, :] = jnp.concatenate(
            [heads_out[s, head] for head in range(HEADS)], axis=1
        ).astype(BF16)
        lse = jnp.zeros((span, TILE), F32)
        for head in range(HEADS):
            lse = jnp.where(lane == head, heads_lse[s, head], lse)
        lse_ref[s] = lse


def attention_specs(span, docs, row=None):
    at = lambda i: i if row is None else row
    kv_spec = pl.BlockSpec((1, 2 * span, KV_COLS), lambda i, s: (at(i), 0, 0))
    return [
        pl.BlockSpec((2, Q_COLS, span), lambda i, s: (at(i), 0, 0)),
        kv_spec,
        kv_spec,
        kv_spec,
        kv_spec,
        pl.BlockSpec(docs.shape, lambda i, s: (0, 0)),
    ]


def attend(order, row, seq_id, qf, sources, docs):
    length = docs.shape[1]
    span = qf.shape[-1]
    width = HEADS * HEAD_DIM
    return order.call(
        functools.partial(attend_kernel, row),
        (qf, *sources, docs),
        scalars=(seq_id,),
        grid=(1,),
        in_specs=attention_specs(span, docs, row),
        out_specs=[
            pl.BlockSpec((2 * span, width), lambda i, s: (0, 0)),
            pl.BlockSpec((2, span, TILE), lambda i, s: (0, 0, 0)),
        ],
        scratch=[
            pltpu.VMEM((length, KV_COLS), BF16),
            pltpu.VMEM((KV_COLS, length), F32),
            pltpu.VMEM((span, 5 * TILE), F32),
            pltpu.VMEM((span, 7 * TILE), F32),
            pltpu.VMEM((2 * RANK_KV * HEADS, 1, length), F32),
            pltpu.VMEM((2, RANK_Q * HEADS, 1, span), F32),
            pltpu.VMEM((2, HEADS, span, HEAD_DIM), F32),
            pltpu.VMEM((2, HEADS, span, 1), F32),
            pltpu.VMEM((span, 5 * TILE), F32),
            pltpu.VMEM((span, 5 * TILE), F32),
            pltpu.VMEM((span, 7 * TILE), F32),
            pltpu.VMEM((span, 7 * TILE), F32),
            pltpu.VMEM((2, span, 1), F32),
            pltpu.VMEM((2, span, 1), F32),
        ],
        out_shape=[
            jax.ShapeDtypeStruct((2 * span, width), BF16),
            jax.ShapeDtypeStruct((2, span, TILE), F32),
        ],
        mib=24,
        name="attend",
    )


def attend_back_kernel(
    row, seq_ref, qf_ref, kv0, kv1, kv2, kv3, doc_ref, lse_ref, att_ref, grad_ref,
    cos_ref, sin_ref, gq_ref, near_ref, far_ref,
    kvpos, kvt, bias, dot_t, stats, gkvt, gkvpos, gqt, gka, gqa, kva, qa,
    probs_a, probs_b, grads_a, grads_b, q_a, q_b,
):
    seq_id = seq_ref[0]
    span = qf_ref.shape[-1]
    gather_keys(seq_id, (kv0, kv1, kv2, kv3), qf_ref, qa, kvpos, kvt, kva, bias, doc_ref, row, span)
    width = HEADS * HEAD_DIM
    chooser = (
        lax.broadcasted_iota(jnp.int32, (width, TILE), 0) // HEAD_DIM
        == lax.broadcasted_iota(jnp.int32, (width, TILE), 1)
    ).astype(BF16)
    for s in range(2):
        grad = grad_ref[0, s * span : (s + 1) * span, :]
        dot_t[s] = grad.T
        product = grad.astype(F32) * att_ref[s * span : (s + 1) * span, :].astype(F32)
        coarse = product.astype(BF16)
        fine = (product - coarse.astype(F32)).astype(BF16)
        centre = dot(coarse, chooser) + dot(fine, chooser)
        for head in range(HEADS):
            stats[0, s, head] = jnp.broadcast_to(lse_ref[s, :, head : head + 1], (span, TILE))
            stats[1, s, head] = jnp.broadcast_to(centre[:, head : head + 1], (span, TILE))
    gkvt[...] = jnp.zeros_like(gkvt)
    gqt[...] = jnp.zeros_like(gqt)

    pieces = [piece_side(piece, seq_id) for piece in PIECES]
    split = RANK_KV * HEADS

    def wide(value, cols):
        return jnp.concatenate([value] * ((cols.stop - cols.start) // TILE), axis=1)

    def scores_of(head, hold):
        probs_of, grads_of, q_of = hold
        rows = pl.ds(aligned(head * HEAD_DIM, HEAD_DIM), HEAD_DIM)
        keys = expand_pair(kvt, kva, 0, head)
        values = expand_pair(kvt, kva, VALUE_BASE, head)
        yield
        queries, grads = [], []
        for s in range(2):
            q_t = expand_queries(qf_ref, qa, s, head)
            q_of[s] = q_t
            queries.append(q_t.T)
            grads.append(dot_t[s, rows, :].T)
        yield
        for cols, side, low in pieces:
            score = dot(choose(side, low, queries), keys[:, cols]) + bias[:, cols]
            probs = jnp.exp(score - wide(stats[0, side, head], cols))
            grad_p = dot(choose(side, low, grads), values[:, cols])
            probs_of[:, cols] = probs.astype(BF16)
            grads_of[:, cols] = (probs * (grad_p - wide(stats[1, side, head], cols))).astype(BF16)
            yield

    def grads_of_head(head, hold):
        probs_of, grads_of, q_of = hold
        rows = pl.ds(aligned(head * HEAD_DIM, HEAD_DIM), HEAD_DIM)
        keys = expand_pair(kvt, kva, 0, head)
        yield
        grad_q = [None, None]
        for cols, side, low in pieces:
            grad_s = grads_of[:, cols]
            gather(grad_q, side, low, dot(keys[:, cols], grad_s, NT), jnp.add, 0.0)
            for base, grad in (
                (0, dot(q_of[side], grad_s)),
                (VALUE_BASE, dot(dot_t[side, rows, :], probs_of[:, cols])),
            ):
                for r in range(RANK_KV):
                    where = base + split + r * HEAD_DIM
                    b_rows = slice(where, where + HEAD_DIM)
                    a_row = (base // VALUE_BASE) * split + r * HEADS + head
                    gka[a_row, :, cols] = jnp.sum(grad * kvt[b_rows, cols], axis=0, keepdims=True)
                    gkvt[b_rows, cols] += grad * kva[a_row, :, cols]
            yield
        where = RANK_Q * HEADS
        for s in range(2):
            for r in range(RANK_Q):
                b_rows = slice(where + r * HEAD_DIM, where + (r + 1) * HEAD_DIM)
                a_row = r * HEADS + head
                gqa[s, a_row] = jnp.sum(grad_q[s] * qf_ref[s, b_rows, :], axis=0, keepdims=True)
                gqt[s, b_rows, :] += grad_q[s] * qa[s, a_row]
            yield

    def pair_step(pair, carry):
        head = 2 * pair
        weave(scores_of(head + 1, hold_b), grads_of_head(head, hold_a))
        following = jnp.minimum(head + 2, HEADS - 1)
        weave(scores_of(following, hold_a), grads_of_head(head + 1, hold_b))
        return carry

    hold_a, hold_b = (probs_a, grads_a, q_a), (probs_b, grads_b, q_b)
    weave(scores_of(0, hold_a))
    lax.fori_loop(0, HEADS // 2, pair_step, 0)
    half = HEAD_DIM // 2
    split = RANK_Q * HEADS
    for s in range(2):
        cos, sin = cos_ref[s], sin_ref[s]
        pieces = [gqa[s, :, 0, :]]
        for r in range(RANK_Q):
            at = split + r * HEAD_DIM
            first, second = gqt[s, at : at + half, :], gqt[s, at + half : at + HEAD_DIM, :]
            pieces += [first * cos + second * sin, second * cos - first * sin]
        back = jnp.concatenate(pieces, axis=0) * (SCORE_SCALE / RANK_Q)
        back = jnp.concatenate([back, jnp.zeros((Q_PAD - Q_COLS, span), F32)], axis=0)
        gq_ref[s * span : (s + 1) * span, :] = back.T.astype(BF16)
    split = RANK_KV * HEADS
    gkvt[:split, :] = gka[:split, 0, :]
    gkvt[VALUE_BASE : VALUE_BASE + split, :] = gka[split:, 0, :]
    gkvpos[...] = jnp.zeros_like(gkvpos)
    for tile in range(TILES):
        _, place = tile_place(tile, seq_id)
        rows = pl.ds(aligned(place * TILE, TILE), TILE)
        gkvpos[rows, :] += (gkvt[:, tile * TILE : (tile + 1) * TILE] * (1.0 / RANK_KV)).T
    for which in range(4):
        holder = seq_id ^ which
        target = near_ref if which in (0, 2) else far_ref
        for s, number in enumerate((holder, 7 - holder)):
            target[which // 2, s * span : (s + 1) * span, :] = gkvpos[
                pl.ds(aligned(number * span, 32), span), :
            ].astype(BF16)


def attend_back(order, row, seq_id, qf, sources, docs, lse, attended, grad_attended, cos, sin, after):
    length = docs.shape[1]
    span = qf.shape[-1]
    width = HEADS * HEAD_DIM
    wide = pl.BlockSpec((1, 2 * span, width), lambda i, s: (row, 0, 0))
    rope = pl.BlockSpec((2, HEAD_DIM // 2, span), lambda i, s: (0, 0, 0))
    parts = pl.BlockSpec((2, 2 * span, KV_COLS), lambda i, s: (0, 0, 0))
    return order.call(
        functools.partial(attend_back_kernel, row),
        (qf, *sources, docs, lse, attended, grad_attended, cos, sin),
        scalars=(seq_id,),
        grid=(1,),
        in_specs=attention_specs(span, docs, row)
        + [
            pl.BlockSpec((2, span, TILE), lambda i, s: (0, 0, 0)),
            pl.BlockSpec((2 * span, width), lambda i, s: (0, 0)),
            wide,
            rope,
            rope,
        ],
        out_specs=[pl.BlockSpec((2 * span, Q_PAD), lambda i, s: (0, 0)), parts, parts],
        scratch=[
            pltpu.VMEM((length, KV_COLS), BF16),
            pltpu.VMEM((KV_COLS, TILES * TILE), F32),
            pltpu.VMEM((span, TILES * TILE), F32),
            pltpu.VMEM((2, width, span), BF16),
            pltpu.VMEM((2, 2, HEADS, span, TILE), F32),
            pltpu.VMEM((KV_COLS, TILES * TILE), F32),
            pltpu.VMEM((length, KV_COLS), F32),
            pltpu.VMEM((2, Q_COLS, span), F32),
            pltpu.VMEM((2 * RANK_KV * HEADS, 1, TILES * TILE), F32),
            pltpu.VMEM((2, RANK_Q * HEADS, 1, span), F32),
            pltpu.VMEM((2 * RANK_KV * HEADS, 1, TILES * TILE), F32),
            pltpu.VMEM((2, RANK_Q * HEADS, 1, span), F32),
            pltpu.VMEM((span, TILES * TILE), BF16),
            pltpu.VMEM((span, TILES * TILE), BF16),
            pltpu.VMEM((span, TILES * TILE), BF16),
            pltpu.VMEM((span, TILES * TILE), BF16),
            pltpu.VMEM((2, HEAD_DIM, span), BF16),
            pltpu.VMEM((2, HEAD_DIM, span), BF16),
        ],
        out_shape=[
            jax.ShapeDtypeStruct((2 * span, Q_PAD), BF16),
            jax.ShapeDtypeStruct((2, 2 * span, KV_COLS), BF16),
            jax.ShapeDtypeStruct((2, 2 * span, KV_COLS), BF16),
        ],
        mib=32,
        name="attend_back",
        after=after,
    )


def out_kernel(x_ref, att0_ref, att1_ref, w_ref, gain_ref, resid_ref, normed_ref):
    attended = jnp.where(pl.program_id(0) == 0, att0_ref[...], att1_ref[...])
    resid = x_ref[...].astype(F32) + dot(attended, w_ref[...])
    scale = lax.rsqrt(jnp.mean(resid * resid, axis=-1, keepdims=True) + EPS)
    resid_ref[...] = resid
    normed_ref[...] = (resid * scale * gain_ref[...]).astype(BF16)


def out_project(order, x, attended, w_out, gain):
    tokens, width = x.shape
    step = tokens // 2
    tile = pl.BlockSpec((step, width), lambda i: (i, 0))
    full = pl.BlockSpec((step, width), lambda i: (0, 0))
    return order.call(
        out_kernel,
        (x, *attended, w_out, gain),
        grid=(2,),
        in_specs=[
            tile,
            full,
            full,
            once(w_out.shape, lambda i: (0, 0)),
            pl.BlockSpec((1, width), lambda i: (0, 0)),
        ],
        out_specs=[tile, tile],
        out_shape=[
            jax.ShapeDtypeStruct((tokens, width), F32),
            jax.ShapeDtypeStruct((tokens, width), BF16),
        ],
        mib=20,
        name="out_project",
    )


def out_back_kernel(
    cot_ref, own_ref, other_ref, resid_ref, w_ref, gain_ref, gr_ref, gb_ref, ga_ref, gain_grad_ref
):
    grad = own_ref[...] + other_ref[...].astype(F32)
    values = resid_ref[...]
    scale = lax.rsqrt(jnp.mean(values * values, axis=-1, keepdims=True) + EPS)
    weighted = grad * gain_ref[...]
    back = scale * weighted - values * (scale * scale * scale) * jnp.mean(
        weighted * values, axis=-1, keepdims=True
    )
    grad_resid = cot_ref[...].astype(F32) + back
    branch = grad_resid.astype(BF16)
    gr_ref[...] = grad_resid
    gb_ref[...] = branch
    ga_ref[...] = dot(branch, w_ref[...], NT).astype(BF16)

    @pl.when(pl.program_id(0) == 0)
    def _():
        gain_grad_ref[...] = jnp.zeros_like(gain_grad_ref)

    gain_grad_ref[...] += jnp.sum(grad * values * scale, axis=0, keepdims=True)


def out_back(order, cot, own, other, resid, w_out, gain):
    tokens, width = cot.shape
    step = tokens // 2
    tile = pl.BlockSpec((step, width), lambda i: (i, 0))
    row = pl.BlockSpec((1, width), lambda i: (0, 0))
    return order.call(
        out_back_kernel,
        (cot, own, other, resid, w_out, gain),
        grid=(2,),
        in_specs=[tile, tile, tile, tile, once(w_out.shape, lambda i: (0, 0)), row],
        out_specs=[tile, tile, tile, row],
        out_shape=[
            jax.ShapeDtypeStruct((tokens, width), F32),
            jax.ShapeDtypeStruct((tokens, width), BF16),
            jax.ShapeDtypeStruct((tokens, width), BF16),
            jax.ShapeDtypeStruct((1, width), F32),
        ],
        mib=26,
        name="out_back",
    )


def hidden_back_kernel(own_ref, other_ref, w_ref, own_out, other_out):
    own_out[...] = dot(own_ref[...], w_ref[...], NT).astype(BF16)
    other_out[...] = dot(other_ref[...], w_ref[...], NT).astype(BF16)


def hidden_back(order, cot, cot_other, w_down, after):
    tokens, width = cot.shape
    half = w_down.shape[0]
    step = tokens // 2
    tile = pl.BlockSpec((step, width), lambda i: (i, 0))
    out = pl.BlockSpec((step, half), lambda i: (i, 0))
    shape = jax.ShapeDtypeStruct((tokens, half), BF16)
    return order.call(
        hidden_back_kernel,
        (cot, cot_other, w_down),
        grid=(2,),
        in_specs=[tile, tile, once(w_down.shape, lambda i: (0, 0))],
        out_specs=[out, out],
        out_shape=[shape, shape],
        mib=24,
        name="hidden_back",
        after=after,
    )


def ff_kernel(n2_ref, gh_ref, wg_ref, wu_ref, h_ref, gg_ref, gu_ref, back_ref):
    gate = dot(n2_ref[...], wg_ref[...])
    up = dot(n2_ref[...], wu_ref[...])
    grad_hidden = gh_ref[...].astype(F32)
    sigmoid = 1.0 / (1.0 + jnp.exp(-gate))
    silu = gate * sigmoid
    h_ref[...] = (silu * up).astype(BF16)
    gu = (grad_hidden * silu).astype(BF16)
    gg = (grad_hidden * up * (sigmoid + silu * (1.0 - sigmoid))).astype(BF16)
    gu_ref[...] = gu
    gg_ref[...] = gg
    back = dot(gg, wg_ref[...], NT) + dot(gu, wu_ref[...], NT)
    back_ref[...] = back.astype(back_ref.dtype)


def feed_forward(order, n2, grad_hidden, w_gate, w_up, dtype):
    tokens, width = n2.shape
    half = w_gate.shape[1]
    step = tokens // 2
    weight = once((width, half), lambda i: (0, 0))
    wide = pl.BlockSpec((step, width), lambda i: (i, 0))
    out = pl.BlockSpec((step, half), lambda i: (i, 0))
    return order.call(
        ff_kernel,
        (n2, grad_hidden, w_gate, w_up),
        grid=(2,),
        in_specs=[wide, out, weight, weight],
        out_specs=[out, out, out, wide],
        out_shape=[pltpu.HBM((tokens, half), BF16)] * 3
        + [jax.ShapeDtypeStruct((tokens, width), dtype)],
        mib=30,
        name="feed_forward",
    )


def down_other_kernel(h_ref, w_ref, out_ref):
    out_ref[...] = dot(h_ref[...], w_ref[...]).astype(BF16)


def down_own_kernel(h_ref, w_ref, resid_ref, came_ref, out_ref):
    total = resid_ref[...] + came_ref[...].astype(F32) + dot(h_ref[...], w_ref[...])
    out_ref[...] = total.astype(BF16)


def down_project(order, hidden, w_down, resid=None, came=None):
    tokens, half = hidden.shape
    width = w_down.shape[1]
    step = tokens // 2
    wide = pl.BlockSpec((step, width), lambda i: (i, 0))
    extra = () if resid is None else (resid, came)
    return order.call(
        down_own_kernel if extra else down_other_kernel,
        (hidden, w_down, *extra),
        grid=(2,),
        in_specs=[
            pl.BlockSpec((step, half), lambda i: (i, 0)),
            once((half, width), lambda i: (0, 0)),
            *[wide] * len(extra),
        ],
        out_specs=[wide],
        out_shape=[jax.ShapeDtypeStruct((tokens, width), BF16)],
        mib=20,
        name="down_project",
    )[0]


class Grid:
    def __init__(self, rows_size, seq_size, rows_id, seq_id, width):
        self.high = [f"b{i}" for i in range(rows_size.bit_length() - 2, 0, -1)]
        self.axes = (*self.high, "y", "x", "c")
        self.block = width // (rows_size * seq_size)
        self.route = {"x": ("seq", 2, seq_size), "c": ("seq", 1, seq_size), "y": ("rows", 1, rows_size)}
        for i in range(1, rows_size.bit_length() - 1):
            self.route[f"b{i}"] = ("rows", 1 << i, rows_size)
        bits = []
        for axis in self.axes:
            name, mask, _ = self.route[axis]
            bits.append(((seq_id if name == "seq" else rows_id) // mask) % 2)
        self.bits = jnp.stack(bits).astype(jnp.int32)

    def place(self, axis):
        return self.axes.index(axis)

    def swap(self, value, axis):
        name, mask, size = self.route[axis]
        return lax.ppermute(value, name, [(i, i ^ mask) for i in range(size)])


class Chain:
    def __init__(self, axes, pieces):
        self.axes, self.pieces = axes, pieces


def fold_specs(grid, chain, axis):
    specs = []
    for value, axes, _, _ in chain.pieces:
        block, kinds = [], []
        for name in axes:
            if name == axis:
                block.append(None)
                kinds.append((grid.place(name), True))
            elif name in chain.axes:
                block.append(2)
                kinds.append(None)
            else:
                block.append(None)
                kinds.append((grid.place(name), False))

        def index(i, bits, kinds=tuple(kinds)):
            out = []
            for kind in kinds:
                if kind is None:
                    out.append(0)
                else:
                    out.append(1 - bits[kind[0]] if kind[1] else bits[kind[0]])
            return (*out, 0, 0)

        specs.append(pl.BlockSpec((*block, *value.shape[-2:]), index))
    return specs


def fold(order, grid, groups, after=()):
    args, specs, layout, shapes = [], [], [], []
    for chains, axis in groups:
        parts = []
        for chain in chains:
            parts.append([(lo, hi) for _, _, lo, hi in chain.pieces])
            args += [value for value, _, _, _ in chain.pieces]
            specs += fold_specs(grid, chain, axis)
        layout.append(parts)
        left = tuple(a for a in chains[0].axes if a != axis)
        cols = sum(c.pieces[0][3] - c.pieces[0][2] for c in chains)
        shapes.append((2,) * len(left) + (grid.block, cols))

    def kernel(bits_ref, *refs):
        inputs, outputs = iter(refs[: len(args)]), refs[len(args) :]
        for out, parts in zip(outputs, layout):
            sums = []
            for ranges in parts:
                total = None
                for lo, hi in ranges:
                    value = next(inputs)[..., lo:hi].astype(F32)
                    total = value if total is None else total + value
                sums.append(total.astype(BF16))
            out[...] = sums[0] if len(sums) == 1 else jnp.concatenate(sums, axis=-1)

    def whole(shape):
        return pl.BlockSpec(shape, lambda i, bits: (0,) * len(shape))

    sends = order.call(
        kernel,
        args,
        scalars=(grid.bits,),
        grid=(1,),
        in_specs=specs,
        out_specs=[whole(shape) for shape in shapes],
        out_shape=[jax.ShapeDtypeStruct(shape, BF16) for shape in shapes],
        mib=26,
        name="fold",
        after=after,
    )
    for (chains, axis), send in zip(groups, sends):
        came = grid.swap(send, axis)
        at = 0
        for chain in chains:
            left = tuple(a for a in chain.axes if a != axis)
            cols = chain.pieces[0][3] - chain.pieces[0][2]
            chain.pieces.append((came, left, at, at + cols))
            chain.axes = left
            at += cols
    return sends


def weight_grad(order, grid, axis, left, right, after=()):
    tokens, width = left[0].shape
    cols = right[0].shape[1]
    step = width // 2
    inner = grid.axes[1:]
    place = grid.place(axis)
    shape = (2,) * (len(grid.axes) - 1) + (grid.block, cols)

    def kernel(bits_ref, l0_ref, l1_ref, r0_ref, r1_ref, send_ref, keep_ref):
        total = dot(l0_ref[...], r0_ref[...], TN) + dot(l1_ref[...], r1_ref[...], TN)
        at = inner.index(axis)
        parts = total.astype(BF16).reshape(2**at, 2, step // 2 ** (at + 1), cols)
        upper = bits_ref[place] == 1
        send_ref[...] = jnp.where(upper, parts[:, 0], parts[:, 1]).reshape(step // 2, cols)
        keep_ref[...] = jnp.where(upper, parts[:, 1], parts[:, 0]).reshape(step // 2, cols)

    l_spec = pl.BlockSpec((tokens, step), lambda i, b: (0, i))
    r_spec = once((tokens, cols), lambda i, b: (0, 0))
    out = pl.BlockSpec((step // 2, cols), lambda i, b: (i, 0))
    send, keep = order.call(
        kernel,
        (left[0], left[1], right[0], right[1]),
        scalars=(grid.bits,),
        grid=(2,),
        in_specs=[l_spec, l_spec, r_spec, r_spec],
        out_specs=[out, out],
        out_shape=[jax.ShapeDtypeStruct((width // 2, cols), BF16)] * 2,
        mib=28,
        name="weight_grad",
        after=after,
    )
    axes = tuple(a for a in grid.axes if a != axis)
    came = grid.swap(send.reshape(shape), axis)
    return Chain(axes, [(keep.reshape(shape), axes, 0, cols), (came, axes, 0, cols)]), send


PART = 256


def weight_halves(order, grid, lefts, rights, gain_grad=None, spare=0):
    step = 256
    pairs = len(rights)
    size, cols = rights[0].shape
    width = lefts[0][0].shape[1]
    half = cols // 2
    parts = half // PART
    gains = [] if gain_grad is None else [gain_grad]
    place = grid.place("c")

    def kernel(bits_ref, *refs):
        mine_ref, other_refs = refs[-1 - parts], refs[-parts:]
        upper = bits_ref[place] == 1
        total = None
        for l_ref, r_ref in zip(refs[:pairs], refs[pairs : 2 * pairs]):
            part = dot(l_ref[...], r_ref[...], TN)
            total = part if total is None else total + part
        if gains:
            column = jnp.broadcast_to(refs[2 * pairs][...], (8, step)).T[:, 0:1]
            coarse = column.astype(BF16).astype(F32)
            lane = lax.broadcasted_iota(jnp.int32, (step, cols), 1)
            total = jnp.where(lane == spare, coarse, total)
            total = jnp.where(lane == spare + 1, column - coarse, total)
        total = total.astype(BF16)
        first, second = total[:, :half], total[:, half:]
        mine_ref[...] = jnp.where(upper, second, first)
        other = jnp.where(upper, first, second)
        for k, other_ref in enumerate(other_refs):
            other_ref[...] = other[:, k * PART : (k + 1) * PART]

    mine, *others = order.call(
        kernel,
        (*[value for value, _ in lefts], *rights, *gains),
        scalars=(grid.bits,),
        grid=(width // step,),
        in_specs=[
            *[pl.BlockSpec((size, step), lambda i, b, at=at: (at, i)) for _, at in lefts],
            *[once((size, cols), lambda i, b: (0, 0))] * pairs,
            *[pl.BlockSpec((1, step), lambda i, b: (0, i))] * len(gains),
        ],
        out_specs=[
            pl.BlockSpec((step, half), lambda i, b: (i, 0)),
            *[pl.BlockSpec((step, PART), lambda i, b: (i, 0))] * parts,
        ],
        out_shape=[
            jax.ShapeDtypeStruct((width, half), BF16),
            *[jax.ShapeDtypeStruct((width, PART), BF16)] * parts,
        ],
        mib=16,
        name="weight_halves",
    )
    lead = (2,) * len(grid.axes) + (grid.block,)
    mine = mine.reshape(lead + (half,))
    chains = []
    for k, other in enumerate(others):
        came = grid.swap(other, "c").reshape(lead + (PART,))
        held = [(mine, grid.axes, k * PART, (k + 1) * PART), (came, grid.axes, 0, PART)]
        chains.append(Chain(grid.axes, held))
    return chains


def conclude(order, grid, groups, widths, gains, mib, after=()):
    args, specs, ranges = [], [], []
    for group in groups:
        parts = []
        for chain in group:
            specs += fold_specs(grid, chain, None)
            args += [value for value, _, _, _ in chain.pieces]
            parts.append([(lo, hi) for _, _, lo, hi in chain.pieces])
        ranges.append(parts)
    place = grid.place("c")

    def kernel(bits_ref, *refs):
        inputs, outputs = iter(refs[: len(args)]), iter(refs[len(args) :])
        for parts, width, gained in zip(ranges, widths, gains):
            owns, lasts = [], []
            for pieces in parts:
                values = [next(inputs)[..., lo:hi].astype(F32) for lo, hi in pieces]
                owns.append(functools.reduce(jnp.add, values[:-1]))
                lasts.append(values[-1])
            own = owns[0] if len(owns) == 1 else jnp.concatenate(owns, axis=1)
            last = lasts[0] if len(lasts) == 1 else jnp.concatenate(lasts, axis=1)
            cols = own.shape[-1]
            out = next(outputs)
            gain = next(outputs) if gained else None

            def put(first, second):
                out[:, :cols] = first
                out[:, cols:] = second[:, : width - cols]
                if gain is not None:
                    at = width - cols
                    column = second[:, at : at + 1] + second[:, at + 1 : at + 2]
                    gain[...] = jnp.broadcast_to(column, (column.shape[0], TILE)).T[0:1, :]

            @pl.when(bits_ref[place] == 0)
            def _():
                put(own, last)

            @pl.when(bits_ref[place] == 1)
            def _():
                put(last, own)

    shapes = []
    for width, gained in zip(widths, gains):
        shapes.append((grid.block, width))
        if gained:
            shapes.append((1, grid.block))
    return order.call(
        kernel,
        args,
        scalars=(grid.bits,),
        grid=(1,),
        in_specs=specs,
        out_specs=[pl.BlockSpec(shape, lambda i, b: (0, 0)) for shape in shapes],
        out_shape=[jax.ShapeDtypeStruct(shape, F32) for shape in shapes],
        mib=mib,
        name="conclude",
        after=after,
    )


def finish_kernel(
    k0_ref, r0_ref, x0_ref, gq_ref, wq_ref, wkv_ref, x_ref, gain_ref, gr_ref, cos_ref, sin_ref,
    came_ref, gkv_ref, out_ref, gain_grad_ref,
):
    total = k0_ref[...].astype(F32) + r0_ref[...].astype(F32) + x0_ref[...].astype(F32)
    cos, sin = cos_ref[0], sin_ref[0]
    half = HEAD_DIM // 2
    split = RANK_KV * HEADS
    turned = total.T
    pieces = [turned[:split]]
    for r in range(RANK_KV):
        at = split + r * HEAD_DIM
        first, second = turned[at : at + half], turned[at + half : at + HEAD_DIM]
        pieces += [first * cos + second * sin, second * cos - first * sin]
    pieces.append(turned[split + RANK_KV * HEAD_DIM :])
    gkv = jnp.concatenate(pieces, axis=0).T.astype(BF16)
    gkv_ref[:, :KV_COLS] = gkv
    gkv_ref[:, KV_COLS:] = jnp.zeros((gkv.shape[0], KV_PAD - KV_COLS), BF16)
    grad = dot(gq_ref[:, :Q_COLS], wq_ref[...]) + dot(gkv, wkv_ref[...])
    values = x_ref[...].astype(F32)
    scale = lax.rsqrt(jnp.mean(values * values, axis=-1, keepdims=True) + EPS)
    weighted = grad * gain_ref[...]
    back = scale * weighted - values * (scale * scale * scale) * jnp.mean(
        weighted * values, axis=-1, keepdims=True
    )
    out_ref[...] = (gr_ref[...] + back).astype(BF16)

    @pl.when(pl.program_id(0) == 0)
    def _():
        gain_grad_ref[...] = came_ref[...]

    gain_grad_ref[...] += jnp.sum(grad * values * scale, axis=0, keepdims=True)


def finish(order, row, kept, near, far, gq, w_query, w_keyval, x, gain, grad_resid, cos, sin, came, held):
    tokens, width = x.shape
    span = cos.shape[-1]
    full = lambda i: (0, 0)
    tile = pl.BlockSpec((span, width), lambda i: (2 * row + i, 0))
    part = pl.BlockSpec((None, span, KV_COLS), lambda i: (0, i, 0))
    rope = pl.BlockSpec((1, HEAD_DIM // 2, span), lambda i: (i, 0, 0))
    vector = pl.BlockSpec((1, width), full)
    extra = () if held is None else (held,)

    def kernel(*refs):
        finish_kernel(*refs[:12], *refs[12 + len(extra) :])

    return order.call(
        kernel,
        (kept, near, far, gq, w_query, w_keyval, x, gain, grad_resid, cos, sin, came, *extra),
        grid=(2,),
        in_specs=[
            part,
            part,
            pl.BlockSpec((None, span, KV_COLS), lambda i: (row, i, 0)),
            pl.BlockSpec((span, Q_PAD), lambda i: (i, 0)),
            once((Q_COLS, width), full),
            once((KV_COLS, width), full),
            tile,
            vector,
            tile,
            rope,
            rope,
            vector,
            *[pl.BlockSpec(memory_space=pl.ANY)] * len(extra),
        ],
        out_specs=[pl.BlockSpec((span, KV_PAD), lambda i: (i, 0)), tile, vector],
        out_shape=[
            jax.ShapeDtypeStruct((2 * span, KV_PAD), BF16),
            jax.ShapeDtypeStruct((tokens, width), BF16),
            jax.ShapeDtypeStruct((1, width), F32),
        ],
        mib=20,
        name="finish",
        aliases={12: 1} if extra else None,
    )


def meet_kernel(near0_ref, far0_ref, near1_ref, far1_ref, out_ref):
    out_ref[0] = (near0_ref[...].astype(F32) + far0_ref[...].astype(F32)).astype(BF16)
    out_ref[1] = (near1_ref[...].astype(F32) + far1_ref[...].astype(F32)).astype(BF16)


def meet(order, *parts):
    shape = parts[0].shape
    part = pl.BlockSpec((None, *shape[1:]), lambda i: (1, 0, 0))
    return order.call(
        meet_kernel,
        parts,
        grid=(1,),
        in_specs=[part] * 4,
        out_specs=[pl.BlockSpec(shape, lambda i: (0, 0, 0))],
        out_shape=[jax.ShapeDtypeStruct(shape, BF16)],
        mib=8,
        name="meet",
    )[0]


def body(
    layer_input,
    doc_ids,
    norm1_gain,
    w_query,
    w_keyval,
    w_out,
    norm2_gain,
    w_gate,
    w_up,
    w_down,
    cotangent,
):
    row_count, local_len, width = layer_input.shape
    seq_size = lax.axis_size("seq")
    rows_size = lax.axis_size("rows")
    seq_id = lax.axis_index("seq")
    rows_id = lax.axis_index("rows")
    span = local_len // 2
    tokens = row_count * local_len
    length = local_len * seq_size
    core = seq_id % 2
    order = Order()
    grid = Grid(rows_size, seq_size, rows_id, seq_id, width)
    seq_arg = seq_id.astype(jnp.int32).reshape(1)

    x = layer_input.reshape(tokens, width)
    cot = cotangent.reshape(tokens, width)
    cot_other = grid.swap(cot, "c")
    gain1 = norm1_gain.reshape(1, width)
    gain2 = norm2_gain.reshape(1, width)
    wq_t, wkv_t = w_query.T, w_keyval.T

    spans = jnp.stack([seq_id, 2 * seq_size - 1 - seq_id])
    positions = spans[:, None] * span + jnp.arange(span, dtype=jnp.int32)[None, :]
    inv_freq = ROPE_BASE ** (-(jnp.arange(HEAD_DIM // 2, dtype=F32) * (2.0 / HEAD_DIM)))
    angles = positions.astype(F32)[:, None, :] * inv_freq[None, :, None]
    cos, sin = jnp.cos(angles), jnp.sin(angles)

    normed, qf, kv = project(order, x, gain1, wq_t, wkv_t, cos, sin)
    kv = kv.reshape(row_count, local_len, KV_COLS)
    kv_x = grid.swap(kv, "x")
    kv_core = grid.swap(kv, "c")
    half = w_gate.shape[1] // 2
    wg = lax.dynamic_slice_in_dim(w_gate, core * half, half, 1)
    wu = lax.dynamic_slice_in_dim(w_up, core * half, half, 1)
    wd = lax.dynamic_slice_in_dim(w_down, core * half, half, 0)
    gh_own, gh_oth = hidden_back(order, cot, cot_other, wd, (wg, wu))
    kv_x, _ = lax.optimization_barrier((kv_x, order.token))
    kv_both = grid.swap(kv_x, "c")
    sources = (kv, kv_core, kv_x, kv_both)
    att0, lse0 = attend(order, 0, seq_arg, qf, sources, doc_ids)
    att1, lse1 = attend(order, 1, seq_arg, qf, sources, doc_ids)
    resid, normed2 = out_project(order, x, (att0, att1), w_out, gain2)
    normed2_other = grid.swap(normed2, "c")
    h_own, gg_own, gu_own, gn2_own = feed_forward(order, normed2, gh_own, wg, wu, F32)
    h_oth, gg_oth, gu_oth, gn2_send = feed_forward(order, normed2_other, gh_oth, wg, wu, BF16)
    gn2_came = grid.swap(gn2_send, "c")

    first, second = grid.high[-1], grid.high[:-1]
    down, _ = weight_grad(order, grid, "x", (cot, cot_other), (h_own, h_oth))
    gate, _ = weight_grad(order, grid, "y", (normed2, normed2_other), (gg_own, gg_oth))
    up, _ = weight_grad(order, grid, first, (normed2, normed2_other), (gu_own, gu_oth))
    grad_resid, branch, grad_att, grad_norm2 = out_back(
        order, cot, gn2_own, gn2_came, resid, w_out, gain2
    )
    out = weight_halves(order, grid, [(branch, 0), (branch, 1)], [att0, att1])
    grad_att = grad_att.reshape(row_count, local_len, width)

    def back(row, after=()):
        gq, near, far = attend_back(
            order, row, seq_arg, qf, sources, doc_ids, (lse0, lse1)[row], (att0, att1)[row],
            grad_att, cos, sin, after
        )
        return gq, near, grid.swap(far, "c")

    gq0, near0, far0 = back(0)
    fold(order, grid, [([down], "y")])
    fold(order, grid, [([gate], "x")])
    fold(order, grid, [(out, first)])
    gq1, near1, far1 = back(1)
    upper = [up, *out]
    fold(order, grid, [(upper, "y")])
    fold(order, grid, [([down, gate], first)])
    came = grid.swap(meet(order, near0, far0, near1, far1), "x")
    query = weight_halves(
        order, grid, [(normed, 0), (normed, 1)], [gq0, gq1], grad_norm2, Q_COLS
    )
    down_send = down_project(order, h_oth, wd)
    down_came = grid.swap(down_send, "c")
    zero = jnp.zeros((1, width), F32)
    gkv0, ig0, gain0 = finish(
        order, 0, near0, far0, came, gq0, wq_t, wkv_t, x, gain1, grad_resid, cos, sin, zero, None
    )
    gkv1, input_grad, grad_norm1 = finish(
        order, 1, near1, far1, came, gq1, wq_t, wkv_t, x, gain1, grad_resid, cos, sin, gain0, ig0
    )
    fold(order, grid, [(upper, "x"), ([down, gate], second[0])])
    keyval = weight_halves(
        order, grid, [(normed, 0), (normed, 1)], [gkv0, gkv1], grad_norm1, KV_COLS
    )
    fold(order, grid, [(keyval, "x"), (query, "y")])
    for axis in second[1:]:
        fold(order, grid, [([down, gate], axis)])
    fold(order, grid, [(upper, second[0])])
    for axis in second[1:]:
        fold(order, grid, [(upper, axis)])
    fold(order, grid, [(keyval, "y"), (query, "x")])
    late = [*keyval, *query]
    fold(order, grid, [(late, first)])
    fold(order, grid, [([down, gate, *upper], "c")])
    g_down, g_gate, g_up, g_out = conclude(
        order,
        grid,
        [[down], [gate], [up], out],
        [*[w.shape[1] for w in (w_gate, w_gate, w_up)], width],
        [False] * 4,
        24,
    )
    for axis in second:
        fold(order, grid, [(late, axis)])
    layer_output = down_project(order, h_own, wd, resid, down_came)
    fold(order, grid, [(late, "c")])
    g_query, g_norm2, g_keyval, g_norm1 = conclude(
        order, grid, [query, keyval], [Q_COLS, KV_COLS], [True, True], 8
    )
    return (
        layer_output.reshape(row_count, local_len, width),
        input_grad.reshape(row_count, local_len, width),
        g_norm1.reshape(-1),
        g_query,
        g_keyval,
        g_out.T,
        g_norm2.reshape(-1),
        g_gate,
        g_up,
        g_down.T,
    )


def solution(mesh):
    return jax.shard_map(
        body,
        mesh=mesh,
        in_specs=(
            P("rows", "seq", None),
            P("rows", None),
            P(),
            P(),
            P(),
            P(),
            P(),
            P(),
            P(),
            P(),
            P("rows", "seq", None),
        ),
        out_specs=(
            P("rows", "seq", None),
            P("rows", "seq", None),
            P(("rows", "seq")),
            P(("rows", "seq"), None),
            P(("rows", "seq"), None),
            P(None, ("rows", "seq")),
            P(("rows", "seq")),
            P(("rows", "seq"), None),
            P(("rows", "seq"), None),
            P(None, ("rows", "seq")),
        ),
        check_vma=False,
    )
```

```python
import functools

import jax
import jax.numpy as jnp
from jax import lax
from jax.experimental import pallas as pl
from jax.experimental.pallas import tpu as pltpu
from jax.sharding import PartitionSpec as P

HEADS = 16
HEAD_DIM = 64
RANK_Q = 6
RANK_KV = 2
Q_COLS = RANK_Q * (HEADS + HEAD_DIM)
KV_COLS = 2 * RANK_KV * (HEADS + HEAD_DIM)
Q_PAD = 512
KV_PAD = 384
EPS = 1e-06
ROPE_BASE = 10000.0
MASKED = -1e30
SCORE_SCALE = HEAD_DIM ** (-0.5)
VALUE_BASE = RANK_KV * (HEADS + HEAD_DIM)
TILE = 128
TILES = 9
F32 = jnp.float32
BF16 = jnp.bfloat16
NT = (((1,), (1,)), ((), ()))
TN = (((0,), (0,)), ((), ()))


def dot(left, right, dims=None):
    if dims is None:
        return jnp.dot(left, right, preferred_element_type=F32)
    return lax.dot_general(left, right, dims, preferred_element_type=F32)


def params(mib):
    return pltpu.CompilerParams(vmem_limit_bytes=mib * 2**20)


def cost(flops, nbytes, trans=0):
    return pl.CostEstimate(flops=flops, bytes_accessed=nbytes, transcendentals=trans)


def once(shape, index):
    return pl.BlockSpec(shape, index, pipeline_mode=pl.Buffered(1))


class Order:
    def __init__(self):
        self.token = None

    def call(self, kernel, args, *, grid, in_specs, out_specs, out_shape, mib, name, scalars=(), scratch=(), after=(), work=0, aliases=None):
        extra = [a for a in (self.token, *after) if a is not None]
        n_scalar, n_in, n_out = len(scalars), len(in_specs), len(out_specs)

        def run(*refs):
            head = refs[: n_scalar + n_in]
            rest = refs[n_scalar + n_in + len(extra) :]
            rest[n_out][...] = jnp.zeros_like(rest[n_out])
            kernel(*head, *rest[:n_out], *rest[n_out + 1 :])

        def spec(block, index, **kw):
            return pl.BlockSpec(block, index, **kw)

        token_spec = pl.BlockSpec((8, TILE), lambda *_: (0, 0))
        out = pl.pallas_call(
            run,
            grid_spec=pltpu.PrefetchScalarGridSpec(
                num_scalar_prefetch=n_scalar,
                grid=grid,
                in_specs=[*in_specs, *[pl.BlockSpec(memory_space=pl.ANY)] * len(extra)],
                out_specs=[*out_specs, token_spec],
                scratch_shapes=list(scratch),
            ),
            out_shape=[*out_shape, jax.ShapeDtypeStruct((8, TILE), F32)],
            compiler_params=params(mib),
            input_output_aliases={n_scalar + k: v for k, v in (aliases or {}).items()},
            cost_estimate=cost(work, 2**16),
            name=name,
        )(*scalars, *args, *extra)
        self.token = out[-1]
        return out[:-1]


def stay(value):
    return pltpu.with_memory_space_constraint(value, pltpu.HBM)


def aligned(value, factor):
    return pl.multiple_of(value, factor)


def project_kernel(x_ref, gain_ref, wq_ref, wkv_ref, cos_ref, sin_ref, normed_ref, qf_ref, kv_ref):
    x = x_ref[...].astype(F32)
    scale = lax.rsqrt(jnp.mean(x * x, axis=-1, keepdims=True) + EPS)
    normed = (x * scale * gain_ref[...]).astype(BF16)
    normed_ref[...] = normed
    qf = dot(normed, wq_ref[...], NT)
    kvf = dot(normed, wkv_ref[...], NT)
    cos, sin = cos_ref[0], sin_ref[0]
    half = HEAD_DIM // 2
    qt = qf.T
    split = RANK_Q * HEADS
    qf_ref[0, :split, :] = qt[:split]
    for r in range(RANK_Q):
        at = split + r * HEAD_DIM
        first, second = qt[at : at + half], qt[at + half : at + HEAD_DIM]
        qf_ref[0, at : at + half, :] = first * cos - second * sin
        qf_ref[0, at + half : at + HEAD_DIM, :] = second * cos + first * sin
    kvt = kvf.T
    split = RANK_KV * HEADS
    pieces = [kvt[:split]]
    for r in range(RANK_KV):
        at = split + r * HEAD_DIM
        first, second = kvt[at : at + half], kvt[at + half : at + HEAD_DIM]
        pieces += [first * cos - second * sin, second * cos + first * sin]
    pieces.append(kvt[split + RANK_KV * HEAD_DIM :])
    kv_ref[...] = jnp.concatenate(pieces, axis=0).T.astype(BF16)


def project(order, x, gain, w_query, w_keyval, cos, sin):
    tokens, width = x.shape
    span = cos.shape[-1]
    groups = tokens // span
    full = lambda i: (0, 0)
    rope = pl.BlockSpec((1, HEAD_DIM // 2, span), lambda i: (i % 2, 0, 0))
    return order.call(
        project_kernel,
        (x, gain, w_query, w_keyval, cos, sin),
        grid=(groups,),
        in_specs=[
            pl.BlockSpec((span, width), lambda i: (i, 0)),
            pl.BlockSpec((1, width), full),
            once((Q_COLS, width), full),
            once((KV_COLS, width), full),
            rope,
            rope,
        ],
        out_specs=[
            pl.BlockSpec((span, width), lambda i: (i, 0)),
            pl.BlockSpec((1, Q_COLS, span), lambda i: (i, 0, 0)),
            pl.BlockSpec((span, KV_COLS), lambda i: (i, 0)),
        ],
        out_shape=[
            jax.ShapeDtypeStruct((tokens, width), BF16),
            jax.ShapeDtypeStruct((groups, Q_COLS, span), F32),
            jax.ShapeDtypeStruct((tokens, KV_COLS), BF16),
        ],
        mib=56,
        name="project",
    )


PIECES = ((0, 2), (2, 3), (3, 4), (4, 5), (5, 7), (7, 9))


def tile_place(tile, seq_id):
    low = tile < seq_id + 2
    return low, jnp.where(low, tile, tile + 1 - seq_id)


def piece_side(piece, seq_id):
    first, last = piece
    low = first < seq_id + 2
    side = 0 if last <= 2 else (1 if first > 4 else jnp.where(low, 0, 1))
    return slice(first * TILE, last * TILE), side, low


def choose(side, low, pair):
    return pair[side] if isinstance(side, int) else jnp.where(low, pair[0], pair[1])


def gather(totals, side, low, part, combine, empty):
    for s in range(2):
        if isinstance(side, int):
            if side != s:
                continue
            term = part
        else:
            term = jnp.where(low if s == 0 else ~low, part, empty)
        totals[s] = term if totals[s] is None else combine(totals[s], term)


def gather_keys(seq_id, sources, qf_ref, qa, kvpos, kvt, kva, bias, docs_ref, row, span):
    for which, source in enumerate(sources):
        holder = seq_id ^ which
        kvpos[pl.ds(aligned(holder * span, 32), span), :] = source[0, :span, :]
        kvpos[pl.ds(aligned((7 - holder) * span, 32), span), :] = source[0, span:, :]
    columns = []
    for number in (seq_id, 7 - seq_id):
        ids = None
        for place in range(8):
            part = docs_ref[row : row + 1, place * span : (place + 1) * span]
            ids = part if ids is None else jnp.where(number == place, part, ids)
        columns.append(jnp.broadcast_to(ids.astype(F32), (8, span)).T[:, 0:1].astype(jnp.int32))
    for tile in range(TILES):
        low, place = tile_place(tile, seq_id)
        start = aligned(place * TILE, TILE)
        cols = slice(tile * TILE, (tile + 1) * TILE)
        kvt[:, cols] = kvpos[pl.ds(start, TILE), :].astype(F32).T
        side = 0 if tile < 2 else (1 if tile > 4 else None)
        doc_q = jnp.where(low, columns[0], columns[1]) if side is None else columns[side]
        number = jnp.where(low, seq_id, 7 - seq_id)
        pos_q = number * span + lax.broadcasted_iota(jnp.int32, (span, TILE), 0)
        pos_k = start + lax.broadcasted_iota(jnp.int32, (span, TILE), 1)
        allowed = (doc_q == docs_ref[row : row + 1, pl.ds(start, TILE)]) & (pos_k <= pos_q)
        bias[:, cols] = jnp.where(allowed, 0.0, MASKED)
    split = RANK_KV * HEADS
    kva[:split, 0, :] = kvt[:split, :] * (1.0 / RANK_KV)
    kva[split:, 0, :] = kvt[VALUE_BASE : VALUE_BASE + split, :] * (1.0 / RANK_KV)
    for s in range(2):
        qa[s, :, 0, :] = qf_ref[s, : RANK_Q * HEADS, :] * (1.0 / RANK_Q)


def expand_queries(qf_ref, qa, s, head):
    split = RANK_Q * HEADS
    total = None
    for r in range(RANK_Q):
        weight = qa[s, r * HEADS + head]
        term = weight * qf_ref[s, split + r * HEAD_DIM : split + (r + 1) * HEAD_DIM, :]
        total = term if total is None else total + term
    return total.astype(BF16) * BF16(SCORE_SCALE)


def expand_pair(kvt, kva, base, head):
    split = RANK_KV * HEADS
    total = None
    for r in range(RANK_KV):
        at = base + split + r * HEAD_DIM
        weight = kva[(base // VALUE_BASE) * split + r * HEADS + head]
        term = weight * kvt[at : at + HEAD_DIM, :]
        total = term if total is None else total + term
    return total.astype(BF16)


def weave(*streams):
    streams = list(streams)
    while streams:
        for stream in list(streams):
            try:
                next(stream)
            except StopIteration:
                streams.remove(stream)


SEEN = ((0, 5), (3, 10))


def place_keys(seq_id, sources, kvpos, span):
    for which, source in enumerate(sources):
        holder = seq_id ^ which
        kvpos[pl.ds(aligned(holder * span, 32), span), :] = source[0, :span, :]
        kvpos[pl.ds(aligned((7 - holder) * span, 32), span), :] = source[0, span:, :]


def query_docs(number, docs_ref, row, span):
    ids = None
    for place in range(8):
        part = docs_ref[row : row + 1, place * span : (place + 1) * span]
        ids = part if ids is None else jnp.where(number == place, part, ids)
    return jnp.broadcast_to(ids.astype(F32), (8, span)).T[:, 0:1].astype(jnp.int32)


def attend_kernel(
    row, seq_ref, qf_ref, kv0, kv1, kv2, kv3, doc_ref, out_ref, lse_ref,
    kvpos, kvt, bias_low, bias_high, kva, qa, heads_out, heads_lse,
    low_a, low_b, high_a, high_b, top_a, top_b,
):
    seq_id = seq_ref[0]
    span = qf_ref.shape[-1]
    biases = (bias_low, bias_high)
    place_keys(seq_id, (kv0, kv1, kv2, kv3), kvpos, span)
    length = kvpos.shape[0]
    for at in range(0, length, TILE):
        kvt[:, at : at + TILE] = kvpos[at : at + TILE, :].astype(F32).T
    for s, number in enumerate((seq_id, 7 - seq_id)):
        doc_q = query_docs(number, doc_ref, row, span)
        pos_q = number * span + lax.broadcasted_iota(jnp.int32, (span, TILE), 0)
        for tile in range(*SEEN[s]):
            start = tile * TILE
            pos_k = start + lax.broadcasted_iota(jnp.int32, (span, TILE), 1)
            allowed = (doc_q == doc_ref[row : row + 1, start : start + TILE]) & (pos_k <= pos_q)
            at = start - SEEN[s][0] * TILE
            biases[s][:, at : at + TILE] = jnp.where(allowed, 0.0, MASKED)
    split = RANK_KV * HEADS
    kva[:split, 0, :] = kvt[:split, :] * (1.0 / RANK_KV)
    kva[split:, 0, :] = kvt[VALUE_BASE : VALUE_BASE + split, :] * (1.0 / RANK_KV)
    for s in range(2):
        qa[s, :, 0, :] = qf_ref[s, : RANK_Q * HEADS, :] * (1.0 / RANK_Q)

    def expand(base, head):
        total = None
        for r in range(RANK_KV):
            at = base + split + r * HEAD_DIM
            weight = kva[(base // VALUE_BASE) * split + r * HEADS + head]
            term = weight * kvt[at : at + HEAD_DIM, :]
            total = term if total is None else total + term
        return total.astype(BF16)

    def pieces(s):
        count = SEEN[s][1] - SEEN[s][0]
        edges = [*range(0, count, 2), count]
        shift = SEEN[s][0] * TILE
        for lo, hi in zip(edges, edges[1:]):
            yield slice(lo * TILE, hi * TILE), slice(shift + lo * TILE, shift + hi * TILE)

    def scores_of(head, scores, top):
        keys = expand(0, head)
        yield
        for s in range(2):
            queries = expand_queries(qf_ref, qa, s, head).T
            best = None
            for cols, places in pieces(s):
                part = dot(queries, keys[:, places]) + biases[s][:, cols]
                scores[s][:, cols] = part
                for at in range(0, part.shape[1], TILE):
                    tile = part[:, at : at + TILE]
                    best = tile if best is None else jnp.maximum(best, tile)
                yield
            top[s] = jnp.max(best, axis=-1, keepdims=True)

    def weigh(head, scores, top):
        values = expand(VALUE_BASE, head)
        values = jnp.concatenate([values, jnp.ones((16, values.shape[1]), BF16)], axis=0)
        yield
        for s in range(2):
            peak = top[s]
            out = None
            for cols, places in pieces(s):
                raised = jnp.exp(scores[s][:, cols] - peak).astype(BF16)
                part = dot(raised, values[:, places], NT)
                out = part if out is None else out + part
                yield
            total = out[:, HEAD_DIM : HEAD_DIM + 1]
            heads_out[s, head] = out[:, :HEAD_DIM] * (1.0 / total)
            heads_lse[s, head] = peak + jnp.log(total)

    scores_a, scores_b = (low_a, high_a), (low_b, high_b)

    def pair_step(pair, carry):
        head = 2 * pair
        weave(scores_of(head + 1, scores_b, top_b), weigh(head, scores_a, top_a))
        following = jnp.minimum(head + 2, HEADS - 1)
        weave(scores_of(following, scores_a, top_a), weigh(head + 1, scores_b, top_b))
        return carry

    weave(scores_of(0, scores_a, top_a))
    lax.fori_loop(0, HEADS // 2, pair_step, 0)
    lane = lax.broadcasted_iota(jnp.int32, (span, TILE), 1)
    for s in range(2):
        out_ref[s * span : (s + 1) * span, :] = jnp.concatenate(
            [heads_out[s, head] for head in range(HEADS)], axis=1
        ).astype(BF16)
        lse = jnp.zeros((span, TILE), F32)
        for head in range(HEADS):
            lse = jnp.where(lane == head, heads_lse[s, head], lse)
        lse_ref[s] = lse


def attention_specs(span, docs, row=None):
    at = lambda i: i if row is None else row
    kv_spec = pl.BlockSpec((1, 2 * span, KV_COLS), lambda i, s: (at(i), 0, 0))
    return [
        pl.BlockSpec((2, Q_COLS, span), lambda i, s: (at(i), 0, 0)),
        kv_spec,
        kv_spec,
        kv_spec,
        kv_spec,
        pl.BlockSpec(docs.shape, lambda i, s: (0, 0)),
    ]


def attend(order, row, seq_id, qf, sources, docs):
    length = docs.shape[1]
    span = qf.shape[-1]
    width = HEADS * HEAD_DIM
    return order.call(
        functools.partial(attend_kernel, row),
        (qf, *sources, docs),
        scalars=(seq_id,),
        grid=(1,),
        in_specs=attention_specs(span, docs, row),
        out_specs=[
            pl.BlockSpec((2 * span, width), lambda i, s: (0, 0)),
            pl.BlockSpec((2, span, TILE), lambda i, s: (0, 0, 0)),
        ],
        scratch=[
            pltpu.VMEM((length, KV_COLS), BF16),
            pltpu.VMEM((KV_COLS, length), F32),
            pltpu.VMEM((span, 5 * TILE), F32),
            pltpu.VMEM((span, 7 * TILE), F32),
            pltpu.VMEM((2 * RANK_KV * HEADS, 1, length), F32),
            pltpu.VMEM((2, RANK_Q * HEADS, 1, span), F32),
            pltpu.VMEM((2, HEADS, span, HEAD_DIM), F32),
            pltpu.VMEM((2, HEADS, span, 1), F32),
            pltpu.VMEM((span, 5 * TILE), F32),
            pltpu.VMEM((span, 5 * TILE), F32),
            pltpu.VMEM((span, 7 * TILE), F32),
            pltpu.VMEM((span, 7 * TILE), F32),
            pltpu.VMEM((2, span, 1), F32),
            pltpu.VMEM((2, span, 1), F32),
        ],
        out_shape=[
            jax.ShapeDtypeStruct((2 * span, width), BF16),
            jax.ShapeDtypeStruct((2, span, TILE), F32),
        ],
        mib=24,
        name="attend",
    )


def attend_back_kernel(
    row, seq_ref, qf_ref, kv0, kv1, kv2, kv3, doc_ref, lse_ref, att_ref, grad_ref,
    cos_ref, sin_ref, gq_ref, near_ref, far_ref,
    kvpos, kvt, bias, dot_t, stats, gkvt, gkvpos, gqt, gka, gqa, kva, qa,
    probs_a, probs_b, grads_a, grads_b, q_a, q_b, k_a, k_b,
):
    seq_id = seq_ref[0]
    span = qf_ref.shape[-1]
    gather_keys(seq_id, (kv0, kv1, kv2, kv3), qf_ref, qa, kvpos, kvt, kva, bias, doc_ref, row, span)
    width = HEADS * HEAD_DIM
    chooser = (
        lax.broadcasted_iota(jnp.int32, (width, TILE), 0) // HEAD_DIM
        == lax.broadcasted_iota(jnp.int32, (width, TILE), 1)
    ).astype(BF16)
    for s in range(2):
        grad = grad_ref[0, s * span : (s + 1) * span, :]
        dot_t[s] = grad.T
        product = grad.astype(F32) * att_ref[s * span : (s + 1) * span, :].astype(F32)
        coarse = product.astype(BF16)
        fine = (product - coarse.astype(F32)).astype(BF16)
        centre = dot(coarse, chooser) + dot(fine, chooser)
        stats[0, s, :, 0, :] = -lse_ref[s].T[:HEADS, :]
        stats[1, s, :, 0, :] = -centre.T[:HEADS, :]
    gkvt[...] = jnp.zeros_like(gkvt)
    gqt[...] = jnp.zeros_like(gqt)

    pieces = [piece_side(piece, seq_id) for piece in PIECES]
    split = RANK_KV * HEADS

    extra = lax.broadcasted_iota(jnp.int32, (16, span), 0)
    ones = jnp.ones((16, TILES * TILE), BF16)

    def with_row(value, row):
        coarse = row.astype(BF16).astype(F32)
        middle = (row - coarse).astype(BF16).astype(F32)
        fine = row - coarse - middle
        rest = jnp.where(extra == 0, coarse, jnp.where(extra == 1, middle, fine))
        return jnp.concatenate([value, jnp.where(extra < 3, rest, 0.0).astype(BF16)], axis=0)

    def scores_of(head, hold):
        probs_of, grads_of, q_of, k_of = hold
        rows = pl.ds(aligned(head * HEAD_DIM, HEAD_DIM), HEAD_DIM)
        keys = expand_pair(kvt, kva, 0, head)
        k_of[...] = keys
        keys = jnp.concatenate([keys, ones], axis=0)
        values = jnp.concatenate([expand_pair(kvt, kva, VALUE_BASE, head), ones], axis=0)
        yield
        queries, grads = [], []
        for s in range(2):
            q_t = expand_queries(qf_ref, qa, s, head)
            q_of[s] = q_t
            queries.append(with_row(q_t, stats[0, s, head]).T)
            grads.append(with_row(dot_t[s, rows, :], stats[1, s, head]).T)
        yield
        for cols, side, low in pieces:
            score = dot(choose(side, low, queries), keys[:, cols]) + bias[:, cols]
            probs = jnp.exp(score)
            grad_p = dot(choose(side, low, grads), values[:, cols])
            probs_of[:, cols] = probs.astype(BF16)
            grads_of[:, cols] = (probs * grad_p).astype(BF16)
            yield

    def grads_of_head(head, hold):
        probs_of, grads_of, q_of, k_of = hold
        rows = pl.ds(aligned(head * HEAD_DIM, HEAD_DIM), HEAD_DIM)
        grad_q = [None, None]
        for cols, side, low in pieces:
            grad_s = grads_of[:, cols]
            gather(grad_q, side, low, dot(k_of[:, cols], grad_s, NT), jnp.add, 0.0)
            for base, grad in (
                (0, dot(q_of[side], grad_s)),
                (VALUE_BASE, dot(dot_t[side, rows, :], probs_of[:, cols])),
            ):
                for r in range(RANK_KV):
                    where = base + split + r * HEAD_DIM
                    b_rows = slice(where, where + HEAD_DIM)
                    a_row = (base // VALUE_BASE) * split + r * HEADS + head
                    gka[a_row, :, cols] = jnp.sum(grad * kvt[b_rows, cols], axis=0, keepdims=True)
                    gkvt[b_rows, cols] += grad * kva[a_row, :, cols]
            yield
        where = RANK_Q * HEADS
        for s in range(2):
            for r in range(RANK_Q):
                b_rows = slice(where + r * HEAD_DIM, where + (r + 1) * HEAD_DIM)
                a_row = r * HEADS + head
                gqa[s, a_row] = jnp.sum(grad_q[s] * qf_ref[s, b_rows, :], axis=0, keepdims=True)
                gqt[s, b_rows, :] += grad_q[s] * qa[s, a_row]
            yield

    def pair_step(pair, carry):
        head = 2 * pair
        weave(scores_of(head + 1, hold_b), grads_of_head(head, hold_a))
        following = jnp.minimum(head + 2, HEADS - 1)
        weave(scores_of(following, hold_a), grads_of_head(head + 1, hold_b))
        return carry

    hold_a, hold_b = (probs_a, grads_a, q_a, k_a), (probs_b, grads_b, q_b, k_b)
    weave(scores_of(0, hold_a))
    lax.fori_loop(0, HEADS // 2, pair_step, 0)
    half = HEAD_DIM // 2
    split = RANK_Q * HEADS
    for s in range(2):
        cos, sin = cos_ref[s], sin_ref[s]
        pieces = [gqa[s, :, 0, :] * (1.0 / RANK_Q)]
        for r in range(RANK_Q):
            at = split + r * HEAD_DIM
            first, second = gqt[s, at : at + half, :], gqt[s, at + half : at + HEAD_DIM, :]
            pieces += [first * cos + second * sin, second * cos - first * sin]
        back = jnp.concatenate(pieces, axis=0) * SCORE_SCALE
        back = jnp.concatenate([back, jnp.zeros((Q_PAD - Q_COLS, span), F32)], axis=0)
        gq_ref[s * span : (s + 1) * span, :] = back.T.astype(BF16)
    split = RANK_KV * HEADS
    gkvt[:split, :] = gka[:split, 0, :] * (1.0 / RANK_KV)
    gkvt[VALUE_BASE : VALUE_BASE + split, :] = gka[split:, 0, :] * (1.0 / RANK_KV)
    gkvpos[...] = jnp.zeros_like(gkvpos)
    for tile in range(TILES):
        _, place = tile_place(tile, seq_id)
        rows = pl.ds(aligned(place * TILE, TILE), TILE)
        gkvpos[rows, :] += gkvt[:, tile * TILE : (tile + 1) * TILE].T
    for which in range(4):
        holder = seq_id ^ which
        target = near_ref if which in (0, 2) else far_ref
        for s, number in enumerate((holder, 7 - holder)):
            target[which // 2, s * span : (s + 1) * span, :] = gkvpos[
                pl.ds(aligned(number * span, 32), span), :
            ].astype(BF16)


def attend_back(order, row, seq_id, qf, sources, docs, lse, attended, grad_attended, cos, sin, after):
    length = docs.shape[1]
    span = qf.shape[-1]
    width = HEADS * HEAD_DIM
    wide = pl.BlockSpec((1, 2 * span, width), lambda i, s: (row, 0, 0))
    rope = pl.BlockSpec((2, HEAD_DIM // 2, span), lambda i, s: (0, 0, 0))
    parts = pl.BlockSpec((2, 2 * span, KV_COLS), lambda i, s: (0, 0, 0))
    return order.call(
        functools.partial(attend_back_kernel, row),
        (qf, *sources, docs, lse, attended, grad_attended, cos, sin),
        scalars=(seq_id,),
        grid=(1,),
        in_specs=attention_specs(span, docs, row)
        + [
            pl.BlockSpec((2, span, TILE), lambda i, s: (0, 0, 0)),
            pl.BlockSpec((2 * span, width), lambda i, s: (0, 0)),
            wide,
            rope,
            rope,
        ],
        out_specs=[pl.BlockSpec((2 * span, Q_PAD), lambda i, s: (0, 0)), parts, parts],
        scratch=[
            pltpu.VMEM((length, KV_COLS), BF16),
            pltpu.VMEM((KV_COLS, TILES * TILE), F32),
            pltpu.VMEM((span, TILES * TILE), F32),
            pltpu.VMEM((2, width, span), BF16),
            pltpu.VMEM((2, 2, HEADS, 1, span), F32),
            pltpu.VMEM((KV_COLS, TILES * TILE), F32),
            pltpu.VMEM((length, KV_COLS), F32),
            pltpu.VMEM((2, Q_COLS, span), F32),
            pltpu.VMEM((2 * RANK_KV * HEADS, 1, TILES * TILE), F32),
            pltpu.VMEM((2, RANK_Q * HEADS, 1, span), F32),
            pltpu.VMEM((2 * RANK_KV * HEADS, 1, TILES * TILE), F32),
            pltpu.VMEM((2, RANK_Q * HEADS, 1, span), F32),
            pltpu.VMEM((span, TILES * TILE), BF16),
            pltpu.VMEM((span, TILES * TILE), BF16),
            pltpu.VMEM((span, TILES * TILE), BF16),
            pltpu.VMEM((span, TILES * TILE), BF16),
            pltpu.VMEM((2, HEAD_DIM, span), BF16),
            pltpu.VMEM((2, HEAD_DIM, span), BF16),
            pltpu.VMEM((HEAD_DIM, TILES * TILE), BF16),
            pltpu.VMEM((HEAD_DIM, TILES * TILE), BF16),
        ],
        out_shape=[
            jax.ShapeDtypeStruct((2 * span, Q_PAD), BF16),
            jax.ShapeDtypeStruct((2, 2 * span, KV_COLS), BF16),
            jax.ShapeDtypeStruct((2, 2 * span, KV_COLS), BF16),
        ],
        mib=32,
        name="attend_back",
        after=after,
    )


def out_kernel(x_ref, att0_ref, att1_ref, w_ref, gain_ref, resid_ref, normed_ref):
    attended = jnp.where(pl.program_id(0) == 0, att0_ref[...], att1_ref[...])
    resid = x_ref[...].astype(F32) + dot(attended, w_ref[...])
    scale = lax.rsqrt(jnp.mean(resid * resid, axis=-1, keepdims=True) + EPS)
    resid_ref[...] = resid
    normed_ref[...] = (resid * scale * gain_ref[...]).astype(BF16)


def out_project(order, x, attended, w_out, gain):
    tokens, width = x.shape
    step = tokens // 2
    tile = pl.BlockSpec((step, width), lambda i: (i, 0))
    full = pl.BlockSpec((step, width), lambda i: (0, 0))
    return order.call(
        out_kernel,
        (x, *attended, w_out, gain),
        grid=(2,),
        in_specs=[
            tile,
            full,
            full,
            once(w_out.shape, lambda i: (0, 0)),
            pl.BlockSpec((1, width), lambda i: (0, 0)),
        ],
        out_specs=[tile, tile],
        out_shape=[pltpu.HBM((tokens, width), F32), jax.ShapeDtypeStruct((tokens, width), BF16)],
        mib=20,
        name="out_project",
    )


def out_back_kernel(
    cot_ref, own_ref, other_ref, resid_ref, w_ref, gain_ref, gr_ref, gb_ref, ga_ref, gain_grad_ref
):
    grad = own_ref[...] + other_ref[...].astype(F32)
    values = resid_ref[...]
    scale = lax.rsqrt(jnp.mean(values * values, axis=-1, keepdims=True) + EPS)
    weighted = grad * gain_ref[...]
    back = scale * weighted - values * (scale * scale * scale) * jnp.mean(
        weighted * values, axis=-1, keepdims=True
    )
    grad_resid = cot_ref[...].astype(F32) + back
    branch = grad_resid.astype(BF16)
    gr_ref[...] = grad_resid
    gb_ref[...] = branch
    ga_ref[...] = dot(branch, w_ref[...], NT).astype(BF16)

    @pl.when(pl.program_id(0) == 0)
    def _():
        gain_grad_ref[...] = jnp.zeros_like(gain_grad_ref)

    gain_grad_ref[...] += jnp.sum(grad * values * scale, axis=0, keepdims=True)


def out_back(order, cot, own, other, resid, w_out, gain):
    tokens, width = cot.shape
    step = tokens // 2
    tile = pl.BlockSpec((step, width), lambda i: (i, 0))
    row = pl.BlockSpec((1, width), lambda i: (0, 0))
    return order.call(
        out_back_kernel,
        (cot, own, other, resid, w_out, gain),
        grid=(2,),
        in_specs=[tile, tile, tile, tile, once(w_out.shape, lambda i: (0, 0)), row],
        out_specs=[tile, tile, tile, row],
        out_shape=[
            jax.ShapeDtypeStruct((tokens, width), F32),
            jax.ShapeDtypeStruct((tokens, width), BF16),
            jax.ShapeDtypeStruct((tokens, width), BF16),
            jax.ShapeDtypeStruct((1, width), F32),
        ],
        mib=26,
        name="out_back",
    )


def hidden_back_kernel(own_ref, other_ref, w_ref, own_out, other_out):
    own_out[...] = dot(own_ref[...], w_ref[...], NT).astype(BF16)
    other_out[...] = dot(other_ref[...], w_ref[...], NT).astype(BF16)


def hidden_back(order, cot, cot_other, w_down, after):
    tokens, width = cot.shape
    half = w_down.shape[0]
    step = tokens // 2
    tile = pl.BlockSpec((step, width), lambda i: (i, 0))
    out = pl.BlockSpec((step, half), lambda i: (i, 0))
    shape = jax.ShapeDtypeStruct((tokens, half), BF16)
    return order.call(
        hidden_back_kernel,
        (cot, cot_other, w_down),
        grid=(2,),
        in_specs=[tile, tile, once(w_down.shape, lambda i: (0, 0))],
        out_specs=[out, out],
        out_shape=[shape, shape],
        mib=24,
        name="hidden_back",
        after=after,
    )


def ff_kernel(n2_ref, gh_ref, wg_ref, wu_ref, h_ref, gg_ref, gu_ref, back_ref):
    gate = dot(n2_ref[...], wg_ref[...])
    up = dot(n2_ref[...], wu_ref[...])
    grad_hidden = gh_ref[...].astype(F32)
    sigmoid = 1.0 / (1.0 + jnp.exp(-gate))
    silu = gate * sigmoid
    h_ref[...] = (silu * up).astype(BF16)
    gu = (grad_hidden * silu).astype(BF16)
    gg = (grad_hidden * up * (sigmoid + silu * (1.0 - sigmoid))).astype(BF16)
    gu_ref[...] = gu
    gg_ref[...] = gg
    back = dot(gg, wg_ref[...], NT) + dot(gu, wu_ref[...], NT)
    back_ref[...] = back.astype(back_ref.dtype)


def feed_forward(order, n2, grad_hidden, w_gate, w_up, dtype):
    tokens, width = n2.shape
    half = w_gate.shape[1]
    step = tokens // 2
    weight = once((width, half), lambda i: (0, 0))
    wide = pl.BlockSpec((step, width), lambda i: (i, 0))
    out = pl.BlockSpec((step, half), lambda i: (i, 0))
    return order.call(
        ff_kernel,
        (n2, grad_hidden, w_gate, w_up),
        grid=(2,),
        in_specs=[wide, out, weight, weight],
        out_specs=[out, out, out, wide],
        out_shape=[pltpu.HBM((tokens, half), BF16)] * 3
        + [(pltpu.HBM if dtype == F32 else jax.ShapeDtypeStruct)((tokens, width), dtype)],
        mib=30,
        name="feed_forward",
    )


def down_other_kernel(h_ref, w_ref, out_ref):
    out_ref[...] = dot(h_ref[...], w_ref[...]).astype(BF16)


def down_own_kernel(h_ref, w_ref, resid_ref, came_ref, out_ref):
    total = resid_ref[...] + came_ref[...].astype(F32) + dot(h_ref[...], w_ref[...])
    out_ref[...] = total.astype(BF16)


def down_project(order, hidden, w_down, resid=None, came=None):
    tokens, half = hidden.shape
    width = w_down.shape[1]
    step = tokens // 2
    wide = pl.BlockSpec((step, width), lambda i: (i, 0))
    extra = () if resid is None else (resid, came)
    return order.call(
        down_own_kernel if extra else down_other_kernel,
        (hidden, w_down, *extra),
        grid=(2,),
        in_specs=[
            pl.BlockSpec((step, half), lambda i: (i, 0)),
            once((half, width), lambda i: (0, 0)),
            *[wide] * len(extra),
        ],
        out_specs=[wide],
        out_shape=[jax.ShapeDtypeStruct((tokens, width), BF16)],
        mib=20,
        name="down_project",
    )[0]


class Grid:
    def __init__(self, rows_size, seq_size, rows_id, seq_id, width):
        self.high = [f"b{i}" for i in range(rows_size.bit_length() - 2, 0, -1)]
        self.axes = (*self.high, "y", "x", "c")
        self.block = width // (rows_size * seq_size)
        self.route = {"x": ("seq", 2, seq_size), "c": ("seq", 1, seq_size), "y": ("rows", 1, rows_size)}
        for i in range(1, rows_size.bit_length() - 1):
            self.route[f"b{i}"] = ("rows", 1 << i, rows_size)
        bits = []
        for axis in self.axes:
            name, mask, _ = self.route[axis]
            bits.append(((seq_id if name == "seq" else rows_id) // mask) % 2)
        self.bits = jnp.stack(bits).astype(jnp.int32)

    def place(self, axis):
        return self.axes.index(axis)

    def swap(self, value, axis):
        name, mask, size = self.route[axis]
        return lax.ppermute(value, name, [(i, i ^ mask) for i in range(size)])


class Chain:
    def __init__(self, axes, pieces):
        self.axes, self.pieces = axes, pieces


def fold_specs(grid, chain, axis):
    specs = []
    for value, axes, _, _ in chain.pieces:
        block, kinds = [], []
        for name in axes:
            if name == axis:
                block.append(None)
                kinds.append((grid.place(name), True))
            elif name in chain.axes:
                block.append(2)
                kinds.append(None)
            else:
                block.append(None)
                kinds.append((grid.place(name), False))

        def index(i, bits, kinds=tuple(kinds)):
            out = []
            for kind in kinds:
                if kind is None:
                    out.append(0)
                else:
                    out.append(1 - bits[kind[0]] if kind[1] else bits[kind[0]])
            return (*out, 0, 0)

        specs.append(pl.BlockSpec((*block, *value.shape[-2:]), index))
    return specs


def fold(order, grid, groups, after=()):
    args, specs, layout, shapes = [], [], [], []
    for chains, axis in groups:
        parts = []
        for chain in chains:
            parts.append([(lo, hi) for _, _, lo, hi in chain.pieces])
            args += [value for value, _, _, _ in chain.pieces]
            specs += fold_specs(grid, chain, axis)
        layout.append(parts)
        left = tuple(a for a in chains[0].axes if a != axis)
        cols = sum(c.pieces[0][3] - c.pieces[0][2] for c in chains)
        shapes.append((2,) * len(left) + (grid.block, cols))

    def kernel(bits_ref, *refs):
        inputs, outputs = iter(refs[: len(args)]), refs[len(args) :]
        for out, parts in zip(outputs, layout):
            sums = []
            for ranges in parts:
                total = None
                for lo, hi in ranges:
                    value = next(inputs)[..., lo:hi].astype(F32)
                    total = value if total is None else total + value
                sums.append(total.astype(BF16))
            out[...] = sums[0] if len(sums) == 1 else jnp.concatenate(sums, axis=-1)

    def whole(shape):
        return pl.BlockSpec(shape, lambda i, bits: (0,) * len(shape))

    sends = order.call(
        kernel,
        args,
        scalars=(grid.bits,),
        grid=(1,),
        in_specs=specs,
        out_specs=[whole(shape) for shape in shapes],
        out_shape=[jax.ShapeDtypeStruct(shape, BF16) for shape in shapes],
        mib=26,
        name="fold",
        after=after,
    )
    for (chains, axis), send in zip(groups, sends):
        came = grid.swap(send, axis)
        at = 0
        for chain in chains:
            left = tuple(a for a in chain.axes if a != axis)
            cols = chain.pieces[0][3] - chain.pieces[0][2]
            chain.pieces.append((came, left, at, at + cols))
            chain.axes = left
            at += cols
    return sends


def weight_grad(order, grid, axis, left, right, after=()):
    tokens, width = left[0].shape
    cols = right[0].shape[1]
    step = width // 2
    inner = grid.axes[1:]
    place = grid.place(axis)
    shape = (2,) * (len(grid.axes) - 1) + (grid.block, cols)

    def kernel(bits_ref, l0_ref, l1_ref, r0_ref, r1_ref, send_ref, keep_ref):
        total = dot(l0_ref[...], r0_ref[...], TN) + dot(l1_ref[...], r1_ref[...], TN)
        at = inner.index(axis)
        parts = total.astype(BF16).reshape(2**at, 2, step // 2 ** (at + 1), cols)
        upper = bits_ref[place] == 1
        send_ref[...] = jnp.where(upper, parts[:, 0], parts[:, 1]).reshape(step // 2, cols)
        keep_ref[...] = jnp.where(upper, parts[:, 1], parts[:, 0]).reshape(step // 2, cols)

    l_spec = pl.BlockSpec((tokens, step), lambda i, b: (0, i))
    r_spec = once((tokens, cols), lambda i, b: (0, 0))
    out = pl.BlockSpec((step // 2, cols), lambda i, b: (i, 0))
    send, keep = order.call(
        kernel,
        (left[0], left[1], right[0], right[1]),
        scalars=(grid.bits,),
        grid=(2,),
        in_specs=[l_spec, l_spec, r_spec, r_spec],
        out_specs=[out, out],
        out_shape=[jax.ShapeDtypeStruct((width // 2, cols), BF16)] * 2,
        mib=28,
        name="weight_grad",
        after=after,
    )
    axes = tuple(a for a in grid.axes if a != axis)
    came = grid.swap(send.reshape(shape), axis)
    return Chain(axes, [(keep.reshape(shape), axes, 0, cols), (came, axes, 0, cols)]), send


PART = 256


def weight_halves(order, grid, lefts, rights, gain_grad=None, spare=0):
    step = 256
    pairs = len(rights)
    size, cols = rights[0].shape
    width = lefts[0][0].shape[1]
    half = cols // 2
    parts = half // PART
    gains = [] if gain_grad is None else [gain_grad]
    place = grid.place("c")

    def kernel(bits_ref, *refs):
        mine_ref, other_refs = refs[-1 - parts], refs[-parts:]
        upper = bits_ref[place] == 1
        total = None
        for l_ref, r_ref in zip(refs[:pairs], refs[pairs : 2 * pairs]):
            part = dot(l_ref[...], r_ref[...], TN)
            total = part if total is None else total + part
        if gains:
            column = jnp.broadcast_to(refs[2 * pairs][...], (8, step)).T[:, 0:1]
            coarse = column.astype(BF16).astype(F32)
            lane = lax.broadcasted_iota(jnp.int32, (step, cols), 1)
            total = jnp.where(lane == spare, coarse, total)
            total = jnp.where(lane == spare + 1, column - coarse, total)
        total = total.astype(BF16)
        first, second = total[:, :half], total[:, half:]
        mine_ref[...] = jnp.where(upper, second, first)
        other = jnp.where(upper, first, second)
        for k, other_ref in enumerate(other_refs):
            other_ref[...] = other[:, k * PART : (k + 1) * PART]

    mine, *others = order.call(
        kernel,
        (*[value for value, _ in lefts], *rights, *gains),
        scalars=(grid.bits,),
        grid=(width // step,),
        in_specs=[
            *[pl.BlockSpec((size, step), lambda i, b, at=at: (at, i)) for _, at in lefts],
            *[once((size, cols), lambda i, b: (0, 0))] * pairs,
            *[pl.BlockSpec((1, step), lambda i, b: (0, i))] * len(gains),
        ],
        out_specs=[
            pl.BlockSpec((step, half), lambda i, b: (i, 0)),
            *[pl.BlockSpec((step, PART), lambda i, b: (i, 0))] * parts,
        ],
        out_shape=[
            jax.ShapeDtypeStruct((width, half), BF16),
            *[jax.ShapeDtypeStruct((width, PART), BF16)] * parts,
        ],
        mib=16,
        name="weight_halves",
    )
    lead = (2,) * len(grid.axes) + (grid.block,)
    mine = mine.reshape(lead + (half,))
    chains = []
    for k, other in enumerate(others):
        came = grid.swap(other, "c").reshape(lead + (PART,))
        held = [(mine, grid.axes, k * PART, (k + 1) * PART), (came, grid.axes, 0, PART)]
        chains.append(Chain(grid.axes, held))
    return chains


def weight_rows(order, grid, lefts, rights, gain_grad, spare):
    step = 256
    pairs = len(rights)
    size, cols = rights[0].shape
    width = lefts[0][0].shape[1]
    place = grid.place("c")
    block = grid.block

    def kernel(bits_ref, *refs):
        mine_ref, other_ref = refs[-2:]
        upper = bits_ref[place] == 1
        total = None
        for l_ref, r_ref in zip(refs[:pairs], refs[pairs : 2 * pairs]):
            part = dot(l_ref[...], r_ref[...], TN)
            total = part if total is None else total + part
        column = jnp.broadcast_to(refs[2 * pairs][...], (8, step)).T[:, 0:1]
        coarse = column.astype(BF16).astype(F32)
        lane = lax.broadcasted_iota(jnp.int32, (step, cols), 1)
        total = jnp.where(lane == spare, coarse, total)
        total = jnp.where(lane == spare + 1, column - coarse, total)
        parts = total.reshape(step // (2 * block), 2, block, cols)
        first, second = parts[:, 0], parts[:, 1]
        flat = (step // 2, cols)
        mine_ref[...] = jnp.where(upper, second, first).reshape(flat).astype(BF16)
        other_ref[...] = jnp.where(upper, first, second).reshape(flat).astype(BF16)

    out = pl.BlockSpec((step // 2, cols), lambda i, b: (i, 0))
    mine, other = order.call(
        kernel,
        (*[value for value, _ in lefts], *rights, gain_grad),
        scalars=(grid.bits,),
        grid=(width // step,),
        in_specs=[
            *[pl.BlockSpec((size, step), lambda i, b, at=at: (at, i)) for _, at in lefts],
            *[once((size, cols), lambda i, b: (0, 0))] * pairs,
            pl.BlockSpec((1, step), lambda i, b: (0, i)),
        ],
        out_specs=[out, out],
        out_shape=[jax.ShapeDtypeStruct((width // 2, cols), BF16)] * 2,
        mib=16,
        name="weight_rows",
    )
    axes = grid.axes[:-1]
    shape = (2,) * len(axes) + (block, cols)
    came = grid.swap(other.reshape(shape), "c")
    return Chain(axes, [(mine.reshape(shape), axes, 0, cols), (came, axes, 0, cols)])


def settle(order, grid, chains, widths, mib):
    args, specs, ranges = [], [], []
    for chain in chains:
        specs += fold_specs(grid, chain, None)
        args += [value for value, _, _, _ in chain.pieces]
        ranges.append([(lo, hi) for _, _, lo, hi in chain.pieces])

    def kernel(bits_ref, *refs):
        inputs, outputs = iter(refs[: len(args)]), iter(refs[len(args) :])
        for pieces, width in zip(ranges, widths):
            total = functools.reduce(
                jnp.add, [next(inputs)[..., lo:hi].astype(F32) for lo, hi in pieces]
            )
            next(outputs)[...] = total[:, :width]
            column = total[:, width : width + 1] + total[:, width + 1 : width + 2]
            next(outputs)[...] = jnp.broadcast_to(column, (column.shape[0], TILE)).T[0:1, :]

    shapes = []
    for width in widths:
        shapes += [(grid.block, width), (1, grid.block)]
    return order.call(
        kernel,
        args,
        scalars=(grid.bits,),
        grid=(1,),
        in_specs=specs,
        out_specs=[pl.BlockSpec(shape, lambda i, b: (0, 0)) for shape in shapes],
        out_shape=[jax.ShapeDtypeStruct(shape, F32) for shape in shapes],
        mib=mib,
        name="settle",
    )


def conclude(order, grid, groups, widths, gains, mib, after=()):
    args, specs, ranges = [], [], []
    for group in groups:
        parts = []
        for chain in group:
            specs += fold_specs(grid, chain, None)
            args += [value for value, _, _, _ in chain.pieces]
            parts.append([(lo, hi) for _, _, lo, hi in chain.pieces])
        ranges.append(parts)
    place = grid.place("c")

    def kernel(bits_ref, *refs):
        inputs, outputs = iter(refs[: len(args)]), iter(refs[len(args) :])
        for parts, width, gained in zip(ranges, widths, gains):
            owns, lasts = [], []
            for pieces in parts:
                values = [next(inputs)[..., lo:hi].astype(F32) for lo, hi in pieces]
                owns.append(functools.reduce(jnp.add, values[:-1]))
                lasts.append(values[-1])
            own = owns[0] if len(owns) == 1 else jnp.concatenate(owns, axis=1)
            last = lasts[0] if len(lasts) == 1 else jnp.concatenate(lasts, axis=1)
            cols = own.shape[-1]
            out = next(outputs)
            gain = next(outputs) if gained else None

            def put(first, second):
                out[:, :cols] = first
                out[:, cols:] = second[:, : width - cols]
                if gain is not None:
                    at = width - cols
                    column = second[:, at : at + 1] + second[:, at + 1 : at + 2]
                    gain[...] = jnp.broadcast_to(column, (column.shape[0], TILE)).T[0:1, :]

            @pl.when(bits_ref[place] == 0)
            def _():
                put(own, last)

            @pl.when(bits_ref[place] == 1)
            def _():
                put(last, own)

    shapes = []
    for width, gained in zip(widths, gains):
        shapes.append((grid.block, width))
        if gained:
            shapes.append((1, grid.block))
    return order.call(
        kernel,
        args,
        scalars=(grid.bits,),
        grid=(1,),
        in_specs=specs,
        out_specs=[pl.BlockSpec(shape, lambda i, b: (0, 0)) for shape in shapes],
        out_shape=[jax.ShapeDtypeStruct(shape, F32) for shape in shapes],
        mib=mib,
        name="conclude",
        after=after,
    )


def finish_kernel(
    k0_ref, r0_ref, x0_ref, gq_ref, wq_ref, wkv_ref, x_ref, gain_ref, gr_ref, cos_ref, sin_ref,
    came_ref, gkv_ref, out_ref, gain_grad_ref,
):
    total = k0_ref[...].astype(F32) + r0_ref[...].astype(F32) + x0_ref[...].astype(F32)
    cos, sin = cos_ref[0], sin_ref[0]
    half = HEAD_DIM // 2
    split = RANK_KV * HEADS
    turned = total.T
    pieces = [turned[:split]]
    for r in range(RANK_KV):
        at = split + r * HEAD_DIM
        first, second = turned[at : at + half], turned[at + half : at + HEAD_DIM]
        pieces += [first * cos + second * sin, second * cos - first * sin]
    pieces.append(turned[split + RANK_KV * HEAD_DIM :])
    gkv = jnp.concatenate(pieces, axis=0).T.astype(BF16)
    gkv_ref[:, :KV_COLS] = gkv
    gkv_ref[:, KV_COLS:] = jnp.zeros((gkv.shape[0], KV_PAD - KV_COLS), BF16)
    grad = dot(gq_ref[:, :Q_COLS], wq_ref[...]) + dot(gkv, wkv_ref[...])
    values = x_ref[...].astype(F32)
    scale = lax.rsqrt(jnp.mean(values * values, axis=-1, keepdims=True) + EPS)
    weighted = grad * gain_ref[...]
    back = scale * weighted - values * (scale * scale * scale) * jnp.mean(
        weighted * values, axis=-1, keepdims=True
    )
    out_ref[...] = (gr_ref[...] + back).astype(BF16)

    @pl.when(pl.program_id(0) == 0)
    def _():
        gain_grad_ref[...] = came_ref[...]

    gain_grad_ref[...] += jnp.sum(grad * values * scale, axis=0, keepdims=True)


def finish(order, row, kept, near, far, gq, w_query, w_keyval, x, gain, grad_resid, cos, sin, came, held):
    tokens, width = x.shape
    span = cos.shape[-1]
    full = lambda i: (0, 0)
    tile = pl.BlockSpec((span, width), lambda i: (2 * row + i, 0))
    part = pl.BlockSpec((None, span, KV_COLS), lambda i: (0, i, 0))
    rope = pl.BlockSpec((1, HEAD_DIM // 2, span), lambda i: (i, 0, 0))
    vector = pl.BlockSpec((1, width), full)
    extra = () if held is None else (held,)

    def kernel(*refs):
        finish_kernel(*refs[:12], *refs[12 + len(extra) :])

    return order.call(
        kernel,
        (kept, near, far, gq, w_query, w_keyval, x, gain, grad_resid, cos, sin, came, *extra),
        grid=(2,),
        in_specs=[
            part,
            part,
            pl.BlockSpec((span, KV_COLS), lambda i: (i, 0)),
            pl.BlockSpec((span, Q_PAD), lambda i: (i, 0)),
            once((Q_COLS, width), full),
            once((KV_COLS, width), full),
            tile,
            vector,
            tile,
            rope,
            rope,
            vector,
            *[pl.BlockSpec(memory_space=pl.ANY)] * len(extra),
        ],
        out_specs=[pl.BlockSpec((span, KV_PAD), lambda i: (i, 0)), tile, vector],
        out_shape=[
            jax.ShapeDtypeStruct((2 * span, KV_PAD), BF16),
            jax.ShapeDtypeStruct((tokens, width), BF16),
            jax.ShapeDtypeStruct((1, width), F32),
        ],
        mib=20,
        name="finish",
        aliases={12: 1} if extra else None,
    )


def meet_kernel(near_ref, far_ref, out_ref):
    out_ref[...] = (near_ref[...].astype(F32) + far_ref[...].astype(F32)).astype(BF16)


def meet(order, near, far):
    shape = near.shape[1:]
    part = pl.BlockSpec((None, *shape), lambda i: (1, 0, 0))
    return order.call(
        meet_kernel,
        (near, far),
        grid=(1,),
        in_specs=[part, part],
        out_specs=[pl.BlockSpec(shape, lambda i: (0, 0))],
        out_shape=[jax.ShapeDtypeStruct(shape, BF16)],
        mib=8,
        name="meet",
    )[0]


def body(
    layer_input,
    doc_ids,
    norm1_gain,
    w_query,
    w_keyval,
    w_out,
    norm2_gain,
    w_gate,
    w_up,
    w_down,
    cotangent,
):
    row_count, local_len, width = layer_input.shape
    seq_size = lax.axis_size("seq")
    rows_size = lax.axis_size("rows")
    seq_id = lax.axis_index("seq")
    rows_id = lax.axis_index("rows")
    span = local_len // 2
    tokens = row_count * local_len
    length = local_len * seq_size
    core = seq_id % 2
    order = Order()
    grid = Grid(rows_size, seq_size, rows_id, seq_id, width)
    seq_arg = seq_id.astype(jnp.int32).reshape(1)

    x = layer_input.reshape(tokens, width)
    cot = cotangent.reshape(tokens, width)
    cot_other = grid.swap(cot, "c")
    gain1 = norm1_gain.reshape(1, width)
    gain2 = norm2_gain.reshape(1, width)
    wq_t, wkv_t = w_query.T, w_keyval.T

    spans = jnp.stack([seq_id, 2 * seq_size - 1 - seq_id])
    positions = spans[:, None] * span + jnp.arange(span, dtype=jnp.int32)[None, :]
    inv_freq = ROPE_BASE ** (-(jnp.arange(HEAD_DIM // 2, dtype=F32) * (2.0 / HEAD_DIM)))
    angles = positions.astype(F32)[:, None, :] * inv_freq[None, :, None]
    cos, sin = jnp.cos(angles), jnp.sin(angles)

    normed, qf, kv = project(order, x, gain1, wq_t, wkv_t, cos, sin)
    kv = kv.reshape(row_count, local_len, KV_COLS)
    kv_x = grid.swap(kv, "x")
    kv_core = grid.swap(kv, "c")
    half = w_gate.shape[1] // 2
    wg = lax.dynamic_slice_in_dim(w_gate, core * half, half, 1)
    wu = lax.dynamic_slice_in_dim(w_up, core * half, half, 1)
    wd = lax.dynamic_slice_in_dim(w_down, core * half, half, 0)
    gh_own, gh_oth = hidden_back(order, cot, cot_other, wd, (wg, wu))
    kv_x, _ = lax.optimization_barrier((kv_x, order.token))
    kv_both = grid.swap(kv_x, "c")
    sources = (kv, kv_core, kv_x, kv_both)
    att0, lse0 = attend(order, 0, seq_arg, qf, sources, doc_ids)
    att1, lse1 = attend(order, 1, seq_arg, qf, sources, doc_ids)
    resid, normed2 = out_project(order, x, (att0, att1), w_out, gain2)
    normed2_other = grid.swap(normed2, "c")
    h_own, gg_own, gu_own, gn2_own = feed_forward(order, normed2, gh_own, wg, wu, F32)
    h_oth, gg_oth, gu_oth, gn2_send = feed_forward(order, normed2_other, gh_oth, wg, wu, BF16)
    gn2_came = grid.swap(gn2_send, "c")

    first, second = grid.high[-1], grid.high[:-1]
    down, _ = weight_grad(
        order, grid, "x", (stay(cot), stay(cot_other)), (stay(h_own), stay(h_oth))
    )
    gate, _ = weight_grad(order, grid, "y", (normed2, normed2_other), (gg_own, gg_oth))
    up, _ = weight_grad(order, grid, first, (normed2, normed2_other), (gu_own, gu_oth))
    grad_resid, branch, grad_att, grad_norm2 = out_back(
        order, cot, gn2_own, gn2_came, resid, w_out, gain2
    )
    out = weight_halves(order, grid, [(branch, 0), (branch, 1)], [att0, att1])
    grad_att = grad_att.reshape(row_count, local_len, width)

    def back(row, after=()):
        gq, near, far = attend_back(
            order, row, seq_arg, qf, sources, doc_ids, (lse0, lse1)[row], (att0, att1)[row],
            grad_att, cos, sin, after
        )
        return gq, near, grid.swap(far, "c")

    def end(row, near, far, came, gq, gain, held):
        return finish(
            order, row, near, far, came, gq, wq_t, wkv_t, x, gain1, grad_resid, cos, sin, gain, held
        )

    gq0, near0, far0 = back(0)
    fold(order, grid, [([down], "y")])
    fold(order, grid, [([gate], "x")])
    fold(order, grid, [(out, first)])
    came0 = grid.swap(meet(order, near0, far0), "x")
    gq1, near1, far1 = back(1)
    upper = [up, *out]
    fold(order, grid, [(upper, "y")], after=(came0,))
    fold(order, grid, [([down, gate], first)])
    came1 = grid.swap(meet(order, near1, far1), "x")
    gkv0, ig0, gain0 = end(0, near0, far0, came0, gq0, jnp.zeros((1, width), F32), None)
    query = weight_rows(
        order, grid, [(normed, 0), (normed, 1)], [gq0, gq1], grad_norm2, Q_COLS
    )
    down_send = down_project(order, h_oth, wd)
    down_came = grid.swap(down_send, "c")
    gkv1, input_grad, grad_norm1 = end(1, near1, far1, came1, gq1, gain0, ig0)
    keyval = weight_rows(
        order, grid, [(normed, 0), (normed, 1)], [gkv0, gkv1], grad_norm1, KV_COLS
    )
    fold(order, grid, [([down, gate], second[0])])
    fold(order, grid, [([keyval], "x"), ([query], "y")])
    fold(order, grid, [(upper, "x")])
    for axis in second[1:]:
        fold(order, grid, [([down, gate], axis)])
    fold(order, grid, [([keyval], "y"), ([query], "x")])
    fold(order, grid, [(upper, second[0])])
    for axis in second[1:]:
        fold(order, grid, [(upper, axis)])
    late = [keyval, query]
    fold(order, grid, [(late, first)])
    for axis in second:
        fold(order, grid, [(late, axis)])
    fold(order, grid, [([down, gate, *upper], "c")])
    layer_output = down_project(order, h_own, wd, resid, down_came)
    g_query, g_norm2, g_keyval, g_norm1 = settle(
        order, grid, [query, keyval], [Q_COLS, KV_COLS], 8
    )
    g_down, g_gate, g_up, g_out = conclude(
        order,
        grid,
        [[down], [gate], [up], out],
        [*[w.shape[1] for w in (w_gate, w_gate, w_up)], width],
        [False] * 4,
        24,
    )
    return (
        layer_output.reshape(row_count, local_len, width),
        input_grad.reshape(row_count, local_len, width),
        g_norm1.reshape(-1),
        g_query,
        g_keyval,
        g_out.T,
        g_norm2.reshape(-1),
        g_gate,
        g_up,
        g_down.T,
    )


def solution(mesh):
    return jax.shard_map(
        body,
        mesh=mesh,
        in_specs=(
            P("rows", "seq", None),
            P("rows", None),
            P(),
            P(),
            P(),
            P(),
            P(),
            P(),
            P(),
            P(),
            P("rows", "seq", None),
        ),
        out_specs=(
            P("rows", "seq", None),
            P("rows", "seq", None),
            P(("rows", "seq")),
            P(("rows", "seq"), None),
            P(("rows", "seq"), None),
            P(None, ("rows", "seq")),
            P(("rows", "seq")),
            P(("rows", "seq"), None),
            P(("rows", "seq"), None),
            P(None, ("rows", "seq")),
        ),
        check_vma=False,
    )
```

```python
import functools

import jax
import jax.numpy as jnp
from jax import lax
from jax.experimental import pallas as pl
from jax.experimental.pallas import tpu as pltpu
from jax.sharding import PartitionSpec as P

HEADS = 16
HEAD_DIM = 64
RANK_Q = 6
RANK_KV = 2
Q_COLS = RANK_Q * (HEADS + HEAD_DIM)
KV_COLS = 2 * RANK_KV * (HEADS + HEAD_DIM)
Q_PAD = 512
KV_PAD = 384
EPS = 1e-06
ROPE_BASE = 10000.0
MASKED = -1e30
SCORE_SCALE = HEAD_DIM ** (-0.5)
VALUE_BASE = RANK_KV * (HEADS + HEAD_DIM)
TILE = 128
TILES = 9
F32 = jnp.float32
BF16 = jnp.bfloat16
NT = (((1,), (1,)), ((), ()))
TN = (((0,), (0,)), ((), ()))


def dot(left, right, dims=None):
    if dims is None:
        return jnp.dot(left, right, preferred_element_type=F32)
    return lax.dot_general(left, right, dims, preferred_element_type=F32)


def params(mib):
    return pltpu.CompilerParams(vmem_limit_bytes=mib * 2**20)


def cost(flops, nbytes, trans=0):
    return pl.CostEstimate(flops=flops, bytes_accessed=nbytes, transcendentals=trans)


def once(shape, index):
    return pl.BlockSpec(shape, index, pipeline_mode=pl.Buffered(1))


class Order:
    def __init__(self):
        self.token = None

    def call(self, kernel, args, *, grid, in_specs, out_specs, out_shape, mib, name, scalars=(), scratch=(), after=(), work=0, aliases=None):
        extra = [a for a in (self.token, *after) if a is not None]
        n_scalar, n_in, n_out = len(scalars), len(in_specs), len(out_specs)

        def run(*refs):
            head = refs[: n_scalar + n_in]
            rest = refs[n_scalar + n_in + len(extra) :]
            rest[n_out][...] = jnp.zeros_like(rest[n_out])
            kernel(*head, *rest[:n_out], *rest[n_out + 1 :])

        def spec(block, index, **kw):
            return pl.BlockSpec(block, index, **kw)

        token_spec = pl.BlockSpec((8, TILE), lambda *_: (0, 0))
        out = pl.pallas_call(
            run,
            grid_spec=pltpu.PrefetchScalarGridSpec(
                num_scalar_prefetch=n_scalar,
                grid=grid,
                in_specs=[*in_specs, *[pl.BlockSpec(memory_space=pl.ANY)] * len(extra)],
                out_specs=[*out_specs, token_spec],
                scratch_shapes=list(scratch),
            ),
            out_shape=[*out_shape, jax.ShapeDtypeStruct((8, TILE), F32)],
            compiler_params=params(mib),
            input_output_aliases={n_scalar + k: v for k, v in (aliases or {}).items()},
            cost_estimate=cost(work, 2**16),
            name=name,
        )(*scalars, *args, *extra)
        self.token = out[-1]
        return out[:-1]


def stay(value):
    return pltpu.with_memory_space_constraint(value, pltpu.HBM)


def aligned(value, factor):
    return pl.multiple_of(value, factor)


def project_kernel(x_ref, gain_ref, wq_ref, wkv_ref, cos_ref, sin_ref, normed_ref, qf_ref, kv_ref):
    x = x_ref[...].astype(F32)
    scale = lax.rsqrt(jnp.mean(x * x, axis=-1, keepdims=True) + EPS)
    normed = (x * scale * gain_ref[...]).astype(BF16)
    normed_ref[...] = normed
    qf = dot(normed, wq_ref[...], NT)
    kvf = dot(normed, wkv_ref[...], NT)
    cos, sin = cos_ref[0], sin_ref[0]
    half = HEAD_DIM // 2
    qt = qf.T
    split = RANK_Q * HEADS
    qf_ref[0, :split, :] = qt[:split]
    for r in range(RANK_Q):
        at = split + r * HEAD_DIM
        first, second = qt[at : at + half], qt[at + half : at + HEAD_DIM]
        qf_ref[0, at : at + half, :] = first * cos - second * sin
        qf_ref[0, at + half : at + HEAD_DIM, :] = second * cos + first * sin
    kvt = kvf.T
    split = RANK_KV * HEADS
    pieces = [kvt[:split]]
    for r in range(RANK_KV):
        at = split + r * HEAD_DIM
        first, second = kvt[at : at + half], kvt[at + half : at + HEAD_DIM]
        pieces += [first * cos - second * sin, second * cos + first * sin]
    pieces.append(kvt[split + RANK_KV * HEAD_DIM :])
    kv_ref[...] = jnp.concatenate(pieces, axis=0).T.astype(BF16)


def project(order, x, gain, w_query, w_keyval, cos, sin):
    tokens, width = x.shape
    span = cos.shape[-1]
    groups = tokens // span
    full = lambda i: (0, 0)
    rope = pl.BlockSpec((1, HEAD_DIM // 2, span), lambda i: (i % 2, 0, 0))
    return order.call(
        project_kernel,
        (x, gain, w_query, w_keyval, cos, sin),
        grid=(groups,),
        in_specs=[
            pl.BlockSpec((span, width), lambda i: (i, 0)),
            pl.BlockSpec((1, width), full),
            once((Q_COLS, width), full),
            once((KV_COLS, width), full),
            rope,
            rope,
        ],
        out_specs=[
            pl.BlockSpec((span, width), lambda i: (i, 0)),
            pl.BlockSpec((1, Q_COLS, span), lambda i: (i, 0, 0)),
            pl.BlockSpec((span, KV_COLS), lambda i: (i, 0)),
        ],
        out_shape=[
            jax.ShapeDtypeStruct((tokens, width), BF16),
            jax.ShapeDtypeStruct((groups, Q_COLS, span), F32),
            jax.ShapeDtypeStruct((tokens, KV_COLS), BF16),
        ],
        mib=56,
        name="project",
    )


PIECES = ((0, 2), (2, 3), (3, 4), (4, 5), (5, 7), (7, 9))


def tile_place(tile, seq_id):
    low = tile < seq_id + 2
    return low, jnp.where(low, tile, tile + 1 - seq_id)


def piece_side(piece, seq_id):
    first, last = piece
    low = first < seq_id + 2
    side = 0 if last <= 2 else (1 if first > 4 else jnp.where(low, 0, 1))
    return slice(first * TILE, last * TILE), side, low


def choose(side, low, pair):
    return pair[side] if isinstance(side, int) else jnp.where(low, pair[0], pair[1])


def gather(totals, side, low, part, combine, empty):
    for s in range(2):
        if isinstance(side, int):
            if side != s:
                continue
            term = part
        else:
            term = jnp.where(low if s == 0 else ~low, part, empty)
        totals[s] = term if totals[s] is None else combine(totals[s], term)


def gather_keys(seq_id, sources, qf_ref, qa, kvpos, kvt, kva, bias, docs_ref, row, span):
    for which, source in enumerate(sources):
        holder = seq_id ^ which
        kvpos[pl.ds(aligned(holder * span, 32), span), :] = source[0, :span, :]
        kvpos[pl.ds(aligned((7 - holder) * span, 32), span), :] = source[0, span:, :]
    columns = []
    for number in (seq_id, 7 - seq_id):
        ids = None
        for place in range(8):
            part = docs_ref[row : row + 1, place * span : (place + 1) * span]
            ids = part if ids is None else jnp.where(number == place, part, ids)
        columns.append(jnp.broadcast_to(ids.astype(F32), (8, span)).T[:, 0:1].astype(jnp.int32))
    for tile in range(TILES):
        low, place = tile_place(tile, seq_id)
        start = aligned(place * TILE, TILE)
        cols = slice(tile * TILE, (tile + 1) * TILE)
        kvt[:, cols] = kvpos[pl.ds(start, TILE), :].astype(F32).T
        side = 0 if tile < 2 else (1 if tile > 4 else None)
        doc_q = jnp.where(low, columns[0], columns[1]) if side is None else columns[side]
        number = jnp.where(low, seq_id, 7 - seq_id)
        pos_q = number * span + lax.broadcasted_iota(jnp.int32, (span, TILE), 0)
        pos_k = start + lax.broadcasted_iota(jnp.int32, (span, TILE), 1)
        allowed = (doc_q == docs_ref[row : row + 1, pl.ds(start, TILE)]) & (pos_k <= pos_q)
        bias[:, cols] = jnp.where(allowed, 0.0, MASKED)
    split = RANK_KV * HEADS
    kva[:split, 0, :] = kvt[:split, :] * (1.0 / RANK_KV)
    kva[split:, 0, :] = kvt[VALUE_BASE : VALUE_BASE + split, :] * (1.0 / RANK_KV)
    for s in range(2):
        qa[s, :, 0, :] = qf_ref[s, : RANK_Q * HEADS, :] * (1.0 / RANK_Q)


def expand_queries(qf_ref, qa, s, head):
    split = RANK_Q * HEADS
    total = None
    for r in range(RANK_Q):
        weight = qa[s, r * HEADS + head]
        term = weight * qf_ref[s, split + r * HEAD_DIM : split + (r + 1) * HEAD_DIM, :]
        total = term if total is None else total + term
    return total.astype(BF16) * BF16(SCORE_SCALE)


def expand_pair(kvt, kva, base, head):
    split = RANK_KV * HEADS
    total = None
    for r in range(RANK_KV):
        at = base + split + r * HEAD_DIM
        weight = kva[(base // VALUE_BASE) * split + r * HEADS + head]
        term = weight * kvt[at : at + HEAD_DIM, :]
        total = term if total is None else total + term
    return total.astype(BF16)


def weave(*streams):
    streams = list(streams)
    while streams:
        for stream in list(streams):
            try:
                next(stream)
            except StopIteration:
                streams.remove(stream)


SEEN = ((0, 5), (3, 10))


def place_keys(seq_id, sources, kvpos, span):
    for which, source in enumerate(sources):
        holder = seq_id ^ which
        kvpos[pl.ds(aligned(holder * span, 32), span), :] = source[0, :span, :]
        kvpos[pl.ds(aligned((7 - holder) * span, 32), span), :] = source[0, span:, :]


def query_docs(number, docs_ref, row, span):
    ids = None
    for place in range(8):
        part = docs_ref[row : row + 1, place * span : (place + 1) * span]
        ids = part if ids is None else jnp.where(number == place, part, ids)
    return jnp.broadcast_to(ids.astype(F32), (8, span)).T[:, 0:1].astype(jnp.int32)


def attend_kernel(
    row, seq_ref, qf_ref, kv0, kv1, kv2, kv3, doc_ref, out_ref, lse_ref,
    kvpos, kvt, bias_low, bias_high, kva, qa, heads_out, heads_lse,
    low_a, low_b, high_a, high_b, top_a, top_b,
):
    seq_id = seq_ref[0]
    span = qf_ref.shape[-1]
    biases = (bias_low, bias_high)
    place_keys(seq_id, (kv0, kv1, kv2, kv3), kvpos, span)
    length = kvpos.shape[0]
    for at in range(0, length, TILE):
        kvt[:, at : at + TILE] = kvpos[at : at + TILE, :].astype(F32).T
    for s, number in enumerate((seq_id, 7 - seq_id)):
        doc_q = query_docs(number, doc_ref, row, span)
        pos_q = number * span + lax.broadcasted_iota(jnp.int32, (span, TILE), 0)
        for tile in range(*SEEN[s]):
            start = tile * TILE
            pos_k = start + lax.broadcasted_iota(jnp.int32, (span, TILE), 1)
            allowed = (doc_q == doc_ref[row : row + 1, start : start + TILE]) & (pos_k <= pos_q)
            at = start - SEEN[s][0] * TILE
            biases[s][:, at : at + TILE] = jnp.where(allowed, 0.0, MASKED)
    split = RANK_KV * HEADS
    kva[:split, 0, :] = kvt[:split, :] * (1.0 / RANK_KV)
    kva[split:, 0, :] = kvt[VALUE_BASE : VALUE_BASE + split, :] * (1.0 / RANK_KV)
    for s in range(2):
        qa[s, :, 0, :] = qf_ref[s, : RANK_Q * HEADS, :] * (1.0 / RANK_Q)

    def expand(base, head):
        total = None
        for r in range(RANK_KV):
            at = base + split + r * HEAD_DIM
            weight = kva[(base // VALUE_BASE) * split + r * HEADS + head]
            term = weight * kvt[at : at + HEAD_DIM, :]
            total = term if total is None else total + term
        return total.astype(BF16)

    def pieces(s):
        count = SEEN[s][1] - SEEN[s][0]
        edges = [*range(0, count, 2), count]
        shift = SEEN[s][0] * TILE
        for lo, hi in zip(edges, edges[1:]):
            yield slice(lo * TILE, hi * TILE), slice(shift + lo * TILE, shift + hi * TILE)

    def scores_of(head, scores, top):
        keys = expand(0, head)
        yield
        for s in range(2):
            queries = expand_queries(qf_ref, qa, s, head).T
            best = None
            for cols, places in pieces(s):
                part = dot(queries, keys[:, places]) + biases[s][:, cols]
                scores[s][:, cols] = part
                for at in range(0, part.shape[1], TILE):
                    tile = part[:, at : at + TILE]
                    best = tile if best is None else jnp.maximum(best, tile)
                yield
            top[s] = jnp.max(best, axis=-1, keepdims=True)

    def weigh(head, scores, top):
        values = expand(VALUE_BASE, head)
        values = jnp.concatenate([values, jnp.ones((16, values.shape[1]), BF16)], axis=0)
        yield
        for s in range(2):
            peak = top[s]
            out = None
            for cols, places in pieces(s):
                raised = jnp.exp(scores[s][:, cols] - peak).astype(BF16)
                part = dot(raised, values[:, places], NT)
                out = part if out is None else out + part
                yield
            total = out[:, HEAD_DIM : HEAD_DIM + 1]
            heads_out[s, head] = out[:, :HEAD_DIM] * (1.0 / total)
            heads_lse[s, head] = peak + jnp.log(total)

    scores_a, scores_b = (low_a, high_a), (low_b, high_b)

    def pair_step(pair, carry):
        head = 2 * pair
        weave(scores_of(head + 1, scores_b, top_b), weigh(head, scores_a, top_a))
        following = jnp.minimum(head + 2, HEADS - 1)
        weave(scores_of(following, scores_a, top_a), weigh(head + 1, scores_b, top_b))
        return carry

    weave(scores_of(0, scores_a, top_a))
    lax.fori_loop(0, HEADS // 2, pair_step, 0)
    lane = lax.broadcasted_iota(jnp.int32, (span, TILE), 1)
    for s in range(2):
        out_ref[s * span : (s + 1) * span, :] = jnp.concatenate(
            [heads_out[s, head] for head in range(HEADS)], axis=1
        ).astype(BF16)
        lse = jnp.zeros((span, TILE), F32)
        for head in range(HEADS):
            lse = jnp.where(lane == head, heads_lse[s, head], lse)
        lse_ref[s] = lse


def attention_specs(span, docs, row=None):
    at = lambda i: i if row is None else row
    kv_spec = pl.BlockSpec((1, 2 * span, KV_COLS), lambda i, s: (at(i), 0, 0))
    return [
        pl.BlockSpec((2, Q_COLS, span), lambda i, s: (at(i), 0, 0)),
        kv_spec,
        kv_spec,
        kv_spec,
        kv_spec,
        pl.BlockSpec((None, 1, docs.shape[-1]), lambda i, s: (at(i), 0, 0)),
    ]


def attend(order, seq_id, qf, sources, docs):
    rows, _, length = docs.shape
    span = qf.shape[-1]
    width = HEADS * HEAD_DIM
    return order.call(
        functools.partial(attend_kernel, 0),
        (qf, *sources, docs),
        scalars=(seq_id,),
        grid=(rows,),
        in_specs=attention_specs(span, docs),
        out_specs=[
            pl.BlockSpec((2 * span, width), lambda i, s: (i, 0)),
            pl.BlockSpec((2, span, TILE), lambda i, s: (i, 0, 0)),
        ],
        scratch=[
            pltpu.VMEM((length, KV_COLS), BF16),
            pltpu.VMEM((KV_COLS, length), F32),
            pltpu.VMEM((span, 5 * TILE), F32),
            pltpu.VMEM((span, 7 * TILE), F32),
            pltpu.VMEM((2 * RANK_KV * HEADS, 1, length), F32),
            pltpu.VMEM((2, RANK_Q * HEADS, 1, span), F32),
            pltpu.VMEM((2, HEADS, span, HEAD_DIM), F32),
            pltpu.VMEM((2, HEADS, span, 1), F32),
            pltpu.VMEM((span, 5 * TILE), F32),
            pltpu.VMEM((span, 5 * TILE), F32),
            pltpu.VMEM((span, 7 * TILE), F32),
            pltpu.VMEM((span, 7 * TILE), F32),
            pltpu.VMEM((2, span, 1), F32),
            pltpu.VMEM((2, span, 1), F32),
        ],
        out_shape=[
            jax.ShapeDtypeStruct((rows * 2 * span, width), BF16),
            jax.ShapeDtypeStruct((rows * 2, span, TILE), F32),
        ],
        mib=24,
        name="attend",
    )


def attend_back_kernel(
    row, seq_ref, qf_ref, kv0, kv1, kv2, kv3, doc_ref, lse_ref, att_ref, grad_ref,
    cos_ref, sin_ref, gq_ref, near_ref, far_ref,
    kvpos, kvt, bias, dot_t, stats, gkvt, gkvpos, gqt, gka, gqa, kva, qa,
    probs_a, probs_b, grads_a, grads_b, q_a, q_b, k_a, k_b,
):
    seq_id = seq_ref[0]
    span = qf_ref.shape[-1]
    gather_keys(seq_id, (kv0, kv1, kv2, kv3), qf_ref, qa, kvpos, kvt, kva, bias, doc_ref, row, span)
    width = HEADS * HEAD_DIM
    chooser = (
        lax.broadcasted_iota(jnp.int32, (width, TILE), 0) // HEAD_DIM
        == lax.broadcasted_iota(jnp.int32, (width, TILE), 1)
    ).astype(BF16)
    for s in range(2):
        grad = grad_ref[0, s * span : (s + 1) * span, :]
        dot_t[s] = grad.T
        product = grad.astype(F32) * att_ref[s * span : (s + 1) * span, :].astype(F32)
        coarse = product.astype(BF16)
        fine = (product - coarse.astype(F32)).astype(BF16)
        centre = dot(coarse, chooser) + dot(fine, chooser)
        stats[0, s, :, 0, :] = -lse_ref[s].T[:HEADS, :]
        stats[1, s, :, 0, :] = -centre.T[:HEADS, :]
    gkvt[...] = jnp.zeros_like(gkvt)
    gqt[...] = jnp.zeros_like(gqt)

    pieces = [piece_side(piece, seq_id) for piece in PIECES]
    split = RANK_KV * HEADS

    extra = lax.broadcasted_iota(jnp.int32, (16, span), 0)
    ones = jnp.ones((16, TILES * TILE), BF16)

    def with_row(value, row):
        coarse = row.astype(BF16).astype(F32)
        middle = (row - coarse).astype(BF16).astype(F32)
        fine = row - coarse - middle
        rest = jnp.where(extra == 0, coarse, jnp.where(extra == 1, middle, fine))
        return jnp.concatenate([value, jnp.where(extra < 3, rest, 0.0).astype(BF16)], axis=0)

    def scores_of(head, hold):
        probs_of, grads_of, q_of, k_of = hold
        rows = pl.ds(aligned(head * HEAD_DIM, HEAD_DIM), HEAD_DIM)
        keys = expand_pair(kvt, kva, 0, head)
        k_of[...] = keys
        keys = jnp.concatenate([keys, ones], axis=0)
        values = jnp.concatenate([expand_pair(kvt, kva, VALUE_BASE, head), ones], axis=0)
        yield
        queries, grads = [], []
        for s in range(2):
            q_t = expand_queries(qf_ref, qa, s, head)
            q_of[s] = q_t
            queries.append(with_row(q_t, stats[0, s, head]).T)
            grads.append(with_row(dot_t[s, rows, :], stats[1, s, head]).T)
        yield
        for cols, side, low in pieces:
            score = dot(choose(side, low, queries), keys[:, cols]) + bias[:, cols]
            probs = jnp.exp(score)
            grad_p = dot(choose(side, low, grads), values[:, cols])
            probs_of[:, cols] = probs.astype(BF16)
            grads_of[:, cols] = (probs * grad_p).astype(BF16)
            yield

    def grads_of_head(head, hold):
        probs_of, grads_of, q_of, k_of = hold
        rows = pl.ds(aligned(head * HEAD_DIM, HEAD_DIM), HEAD_DIM)
        grad_q = [None, None]
        for cols, side, low in pieces:
            grad_s = grads_of[:, cols]
            gather(grad_q, side, low, dot(k_of[:, cols], grad_s, NT), jnp.add, 0.0)
            for base, grad in (
                (0, dot(q_of[side], grad_s)),
                (VALUE_BASE, dot(dot_t[side, rows, :], probs_of[:, cols])),
            ):
                for r in range(RANK_KV):
                    where = base + split + r * HEAD_DIM
                    b_rows = slice(where, where + HEAD_DIM)
                    a_row = (base // VALUE_BASE) * split + r * HEADS + head
                    gka[a_row, :, cols] = jnp.sum(grad * kvt[b_rows, cols], axis=0, keepdims=True)
                    gkvt[b_rows, cols] += grad * kva[a_row, :, cols]
            yield
        where = RANK_Q * HEADS
        for s in range(2):
            for r in range(RANK_Q):
                b_rows = slice(where + r * HEAD_DIM, where + (r + 1) * HEAD_DIM)
                a_row = r * HEADS + head
                gqa[s, a_row] = jnp.sum(grad_q[s] * qf_ref[s, b_rows, :], axis=0, keepdims=True)
                gqt[s, b_rows, :] += grad_q[s] * qa[s, a_row]
            yield

    def pair_step(pair, carry):
        head = 2 * pair
        weave(scores_of(head + 1, hold_b), grads_of_head(head, hold_a))
        following = jnp.minimum(head + 2, HEADS - 1)
        weave(scores_of(following, hold_a), grads_of_head(head + 1, hold_b))
        return carry

    hold_a, hold_b = (probs_a, grads_a, q_a, k_a), (probs_b, grads_b, q_b, k_b)
    weave(scores_of(0, hold_a))
    lax.fori_loop(0, HEADS // 2, pair_step, 0)
    half = HEAD_DIM // 2
    split = RANK_Q * HEADS
    for s in range(2):
        cos, sin = cos_ref[s], sin_ref[s]
        pieces = [gqa[s, :, 0, :] * (1.0 / RANK_Q)]
        for r in range(RANK_Q):
            at = split + r * HEAD_DIM
            first, second = gqt[s, at : at + half, :], gqt[s, at + half : at + HEAD_DIM, :]
            pieces += [first * cos + second * sin, second * cos - first * sin]
        back = jnp.concatenate(pieces, axis=0) * SCORE_SCALE
        back = jnp.concatenate([back, jnp.zeros((Q_PAD - Q_COLS, span), F32)], axis=0)
        gq_ref[s * span : (s + 1) * span, :] = back.T.astype(BF16)
    split = RANK_KV * HEADS
    gkvt[:split, :] = gka[:split, 0, :] * (1.0 / RANK_KV)
    gkvt[VALUE_BASE : VALUE_BASE + split, :] = gka[split:, 0, :] * (1.0 / RANK_KV)
    gkvpos[...] = jnp.zeros_like(gkvpos)
    for tile in range(TILES):
        _, place = tile_place(tile, seq_id)
        rows = pl.ds(aligned(place * TILE, TILE), TILE)
        gkvpos[rows, :] += gkvt[:, tile * TILE : (tile + 1) * TILE].T
    for which in range(4):
        holder = seq_id ^ which
        target = near_ref if which in (0, 2) else far_ref
        for s, number in enumerate((holder, 7 - holder)):
            target[which // 2, s * span : (s + 1) * span, :] = gkvpos[
                pl.ds(aligned(number * span, 32), span), :
            ].astype(BF16)


def attend_back(order, row, seq_id, qf, sources, docs, lse, attended, grad_attended, cos, sin, after):
    length = docs.shape[-1]
    span = qf.shape[-1]
    width = HEADS * HEAD_DIM
    wide = pl.BlockSpec((1, 2 * span, width), lambda i, s: (row, 0, 0))
    rope = pl.BlockSpec((2, HEAD_DIM // 2, span), lambda i, s: (0, 0, 0))
    parts = pl.BlockSpec((2, 2 * span, KV_COLS), lambda i, s: (0, 0, 0))
    return order.call(
        functools.partial(attend_back_kernel, 0),
        (qf, *sources, docs, lse, attended, grad_attended, cos, sin),
        scalars=(seq_id,),
        grid=(1,),
        in_specs=attention_specs(span, docs, row)
        + [
            pl.BlockSpec((2, span, TILE), lambda i, s: (row, 0, 0)),
            pl.BlockSpec((2 * span, width), lambda i, s: (row, 0)),
            wide,
            rope,
            rope,
        ],
        out_specs=[pl.BlockSpec((2 * span, Q_PAD), lambda i, s: (0, 0)), parts, parts],
        scratch=[
            pltpu.VMEM((length, KV_COLS), BF16),
            pltpu.VMEM((KV_COLS, TILES * TILE), F32),
            pltpu.VMEM((span, TILES * TILE), F32),
            pltpu.VMEM((2, width, span), BF16),
            pltpu.VMEM((2, 2, HEADS, 1, span), F32),
            pltpu.VMEM((KV_COLS, TILES * TILE), F32),
            pltpu.VMEM((length, KV_COLS), F32),
            pltpu.VMEM((2, Q_COLS, span), F32),
            pltpu.VMEM((2 * RANK_KV * HEADS, 1, TILES * TILE), F32),
            pltpu.VMEM((2, RANK_Q * HEADS, 1, span), F32),
            pltpu.VMEM((2 * RANK_KV * HEADS, 1, TILES * TILE), F32),
            pltpu.VMEM((2, RANK_Q * HEADS, 1, span), F32),
            pltpu.VMEM((span, TILES * TILE), BF16),
            pltpu.VMEM((span, TILES * TILE), BF16),
            pltpu.VMEM((span, TILES * TILE), BF16),
            pltpu.VMEM((span, TILES * TILE), BF16),
            pltpu.VMEM((2, HEAD_DIM, span), BF16),
            pltpu.VMEM((2, HEAD_DIM, span), BF16),
            pltpu.VMEM((HEAD_DIM, TILES * TILE), BF16),
            pltpu.VMEM((HEAD_DIM, TILES * TILE), BF16),
        ],
        out_shape=[
            jax.ShapeDtypeStruct((2 * span, Q_PAD), BF16),
            jax.ShapeDtypeStruct((2, 2 * span, KV_COLS), BF16),
            jax.ShapeDtypeStruct((2, 2 * span, KV_COLS), BF16),
        ],
        mib=32,
        name="attend_back",
        after=after,
    )


def out_kernel(x_ref, att_ref, w_ref, gain_ref, resid_ref, normed_ref):
    resid = x_ref[...].astype(F32) + dot(att_ref[...], w_ref[...])
    scale = lax.rsqrt(jnp.mean(resid * resid, axis=-1, keepdims=True) + EPS)
    resid_ref[...] = resid
    normed_ref[...] = (resid * scale * gain_ref[...]).astype(BF16)


def out_project(order, x, attended, w_out, gain):
    tokens, width = x.shape
    step = tokens // 2
    tile = pl.BlockSpec((step, width), lambda i: (i, 0))
    return order.call(
        out_kernel,
        (x, attended, w_out, gain),
        grid=(2,),
        in_specs=[
            tile,
            tile,
            once(w_out.shape, lambda i: (0, 0)),
            pl.BlockSpec((1, width), lambda i: (0, 0)),
        ],
        out_specs=[tile, tile],
        out_shape=[pltpu.HBM((tokens, width), F32), jax.ShapeDtypeStruct((tokens, width), BF16)],
        mib=20,
        name="out_project",
    )


def out_back_kernel(
    cot_ref, own_ref, other_ref, resid_ref, w_ref, gain_ref, gr_ref, gb_ref, ga_ref, gain_grad_ref
):
    grad = own_ref[...].astype(F32) + other_ref[...].astype(F32)
    values = resid_ref[...]
    scale = lax.rsqrt(jnp.mean(values * values, axis=-1, keepdims=True) + EPS)
    weighted = grad * gain_ref[...]
    back = scale * weighted - values * (scale * scale * scale) * jnp.mean(
        weighted * values, axis=-1, keepdims=True
    )
    grad_resid = cot_ref[...].astype(F32) + back
    branch = grad_resid.astype(BF16)
    gr_ref[...] = grad_resid
    gb_ref[...] = branch
    ga_ref[...] = dot(branch, w_ref[...], NT).astype(BF16)

    @pl.when(pl.program_id(0) == 0)
    def _():
        gain_grad_ref[...] = jnp.zeros_like(gain_grad_ref)

    gain_grad_ref[...] += jnp.sum(grad * values * scale, axis=0, keepdims=True)


def out_back(order, cot, own, other, resid, w_out, gain):
    tokens, width = cot.shape
    step = tokens // 2
    tile = pl.BlockSpec((step, width), lambda i: (i, 0))
    row = pl.BlockSpec((1, width), lambda i: (0, 0))
    return order.call(
        out_back_kernel,
        (cot, own, other, resid, w_out, gain),
        grid=(2,),
        in_specs=[tile, tile, tile, tile, once(w_out.shape, lambda i: (0, 0)), row],
        out_specs=[tile, tile, tile, row],
        out_shape=[
            jax.ShapeDtypeStruct((tokens, width), F32),
            jax.ShapeDtypeStruct((tokens, width), BF16),
            jax.ShapeDtypeStruct((tokens, width), BF16),
            jax.ShapeDtypeStruct((1, width), F32),
        ],
        mib=26,
        name="out_back",
    )


def hidden_back_kernel(own_ref, other_ref, w_ref, own_out, other_out):
    own_out[...] = dot(own_ref[...], w_ref[...], NT).astype(BF16)
    other_out[...] = dot(other_ref[...], w_ref[...], NT).astype(BF16)


def hidden_back(order, cot, cot_other, w_down, after):
    tokens, width = cot.shape
    half = w_down.shape[0]
    step = tokens // 2
    tile = pl.BlockSpec((step, width), lambda i: (i, 0))
    out = pl.BlockSpec((step, half), lambda i: (i, 0))
    shape = jax.ShapeDtypeStruct((tokens, half), BF16)
    return order.call(
        hidden_back_kernel,
        (cot, cot_other, w_down),
        grid=(2,),
        in_specs=[tile, tile, once(w_down.shape, lambda i: (0, 0))],
        out_specs=[out, out],
        out_shape=[shape, shape],
        mib=24,
        name="hidden_back",
        after=after,
    )


def ff_kernel(n2_ref, gh_ref, wg_ref, wu_ref, h_ref, gg_ref, gu_ref, back_ref):
    gate = dot(n2_ref[...], wg_ref[...])
    up = dot(n2_ref[...], wu_ref[...])
    grad_hidden = gh_ref[...].astype(F32)
    sigmoid = 1.0 / (1.0 + jnp.exp(-gate))
    silu = gate * sigmoid
    h_ref[...] = (silu * up).astype(BF16)
    gu = (grad_hidden * silu).astype(BF16)
    gg = (grad_hidden * up * (sigmoid + silu * (1.0 - sigmoid))).astype(BF16)
    gu_ref[...] = gu
    gg_ref[...] = gg
    back = dot(gg, wg_ref[...], NT) + dot(gu, wu_ref[...], NT)
    back_ref[...] = back.astype(back_ref.dtype)


def feed_forward(order, n2, grad_hidden, w_gate, w_up, dtype):
    tokens, width = n2.shape
    half = w_gate.shape[1]
    step = tokens // 2
    weight = once((width, half), lambda i: (0, 0))
    wide = pl.BlockSpec((step, width), lambda i: (i, 0))
    out = pl.BlockSpec((step, half), lambda i: (i, 0))
    return order.call(
        ff_kernel,
        (n2, grad_hidden, w_gate, w_up),
        grid=(2,),
        in_specs=[wide, out, weight, weight],
        out_specs=[out, out, out, wide],
        out_shape=[pltpu.HBM((tokens, half), BF16)] * 3
        + [(pltpu.HBM if dtype == F32 else jax.ShapeDtypeStruct)((tokens, width), dtype)],
        mib=30,
        name="feed_forward",
    )


def down_other_kernel(h_ref, w_ref, out_ref):
    out_ref[...] = dot(h_ref[...], w_ref[...]).astype(BF16)


def down_own_kernel(h_ref, w_ref, resid_ref, came_ref, out_ref):
    total = resid_ref[...] + came_ref[...].astype(F32) + dot(h_ref[...], w_ref[...])
    out_ref[...] = total.astype(BF16)


def down_project(order, hidden, w_down, resid=None, came=None):
    tokens, half = hidden.shape
    width = w_down.shape[1]
    step = tokens // 2
    wide = pl.BlockSpec((step, width), lambda i: (i, 0))
    extra = () if resid is None else (resid, came)
    return order.call(
        down_own_kernel if extra else down_other_kernel,
        (hidden, w_down, *extra),
        grid=(2,),
        in_specs=[
            pl.BlockSpec((step, half), lambda i: (i, 0)),
            once((half, width), lambda i: (0, 0)),
            *[wide] * len(extra),
        ],
        out_specs=[wide],
        out_shape=[jax.ShapeDtypeStruct((tokens, width), BF16)],
        mib=20,
        name="down_project",
    )[0]


class Grid:
    def __init__(self, rows_size, seq_size, rows_id, seq_id, width):
        self.high = [f"b{i}" for i in range(rows_size.bit_length() - 2, 0, -1)]
        self.axes = (*self.high, "y", "x", "c")
        self.block = width // (rows_size * seq_size)
        self.route = {"x": ("seq", 2, seq_size), "c": ("seq", 1, seq_size), "y": ("rows", 1, rows_size)}
        for i in range(1, rows_size.bit_length() - 1):
            self.route[f"b{i}"] = ("rows", 1 << i, rows_size)
        bits = []
        for axis in self.axes:
            name, mask, _ = self.route[axis]
            bits.append(((seq_id if name == "seq" else rows_id) // mask) % 2)
        self.bits = jnp.stack(bits).astype(jnp.int32)

    def place(self, axis):
        return self.axes.index(axis)

    def swap(self, value, axis):
        name, mask, size = self.route[axis]
        return lax.ppermute(value, name, [(i, i ^ mask) for i in range(size)])


class Chain:
    def __init__(self, axes, pieces):
        self.axes, self.pieces = axes, pieces


def fold_specs(grid, chain, axis):
    specs = []
    for value, axes, _, _ in chain.pieces:
        block, kinds = [], []
        for name in axes:
            if name == axis:
                block.append(None)
                kinds.append((grid.place(name), True))
            elif name in chain.axes:
                block.append(2)
                kinds.append(None)
            else:
                block.append(None)
                kinds.append((grid.place(name), False))

        def index(i, bits, kinds=tuple(kinds)):
            out = []
            for kind in kinds:
                if kind is None:
                    out.append(0)
                else:
                    out.append(1 - bits[kind[0]] if kind[1] else bits[kind[0]])
            return (*out, 0, 0)

        specs.append(pl.BlockSpec((*block, *value.shape[-2:]), index))
    return specs


def fold(order, grid, groups, after=()):
    args, specs, layout, shapes = [], [], [], []
    for chains, axis in groups:
        parts = []
        for chain in chains:
            parts.append([(lo, hi) for _, _, lo, hi in chain.pieces])
            args += [value for value, _, _, _ in chain.pieces]
            specs += fold_specs(grid, chain, axis)
        layout.append(parts)
        left = tuple(a for a in chains[0].axes if a != axis)
        cols = sum(c.pieces[0][3] - c.pieces[0][2] for c in chains)
        shapes.append((2,) * len(left) + (grid.block, cols))

    def kernel(bits_ref, *refs):
        inputs, outputs = iter(refs[: len(args)]), refs[len(args) :]
        for out, parts in zip(outputs, layout):
            sums = []
            for ranges in parts:
                total = None
                for lo, hi in ranges:
                    value = next(inputs)[..., lo:hi].astype(F32)
                    total = value if total is None else total + value
                sums.append(total.astype(BF16))
            out[...] = sums[0] if len(sums) == 1 else jnp.concatenate(sums, axis=-1)

    def whole(shape):
        return pl.BlockSpec(shape, lambda i, bits: (0,) * len(shape))

    sends = order.call(
        kernel,
        args,
        scalars=(grid.bits,),
        grid=(1,),
        in_specs=specs,
        out_specs=[whole(shape) for shape in shapes],
        out_shape=[jax.ShapeDtypeStruct(shape, BF16) for shape in shapes],
        mib=26,
        name="fold",
        after=after,
    )
    for (chains, axis), send in zip(groups, sends):
        came = grid.swap(send, axis)
        at = 0
        for chain in chains:
            left = tuple(a for a in chain.axes if a != axis)
            cols = chain.pieces[0][3] - chain.pieces[0][2]
            chain.pieces.append((came, left, at, at + cols))
            chain.axes = left
            at += cols
    return sends


def weight_grad(order, grid, axis, left, right, after=()):
    tokens, width = left[0].shape
    cols = right[0].shape[1]
    step = width // 2
    inner = grid.axes[1:]
    place = grid.place(axis)
    shape = (2,) * (len(grid.axes) - 1) + (grid.block, cols)

    def kernel(bits_ref, l0_ref, l1_ref, r0_ref, r1_ref, send_ref, keep_ref):
        total = dot(l0_ref[...], r0_ref[...], TN) + dot(l1_ref[...], r1_ref[...], TN)
        at = inner.index(axis)
        parts = total.astype(BF16).reshape(2**at, 2, step // 2 ** (at + 1), cols)
        upper = bits_ref[place] == 1
        send_ref[...] = jnp.where(upper, parts[:, 0], parts[:, 1]).reshape(step // 2, cols)
        keep_ref[...] = jnp.where(upper, parts[:, 1], parts[:, 0]).reshape(step // 2, cols)

    l_spec = pl.BlockSpec((tokens, step), lambda i, b: (0, i))
    r_spec = once((tokens, cols), lambda i, b: (0, 0))
    out = pl.BlockSpec((step // 2, cols), lambda i, b: (i, 0))
    send, keep = order.call(
        kernel,
        (left[0], left[1], right[0], right[1]),
        scalars=(grid.bits,),
        grid=(2,),
        in_specs=[l_spec, l_spec, r_spec, r_spec],
        out_specs=[out, out],
        out_shape=[jax.ShapeDtypeStruct((width // 2, cols), BF16)] * 2,
        mib=28,
        name="weight_grad",
        after=after,
    )
    axes = tuple(a for a in grid.axes if a != axis)
    came = grid.swap(send.reshape(shape), axis)
    return Chain(axes, [(keep.reshape(shape), axes, 0, cols), (came, axes, 0, cols)]), send


PART = 256


def weight_halves(order, grid, lefts, rights, gain_grad=None, spare=0):
    step = 256
    pairs = len(rights)
    size, cols = rights[0].shape
    width = lefts[0][0].shape[1]
    half = cols // 2
    parts = half // PART
    gains = [] if gain_grad is None else [gain_grad]
    place = grid.place("c")

    def kernel(bits_ref, *refs):
        mine_ref, other_refs = refs[-1 - parts], refs[-parts:]
        upper = bits_ref[place] == 1
        total = None
        for l_ref, r_ref in zip(refs[:pairs], refs[pairs : 2 * pairs]):
            part = dot(l_ref[...], r_ref[...], TN)
            total = part if total is None else total + part
        if gains:
            column = jnp.broadcast_to(refs[2 * pairs][...], (8, step)).T[:, 0:1]
            coarse = column.astype(BF16).astype(F32)
            lane = lax.broadcasted_iota(jnp.int32, (step, cols), 1)
            total = jnp.where(lane == spare, coarse, total)
            total = jnp.where(lane == spare + 1, column - coarse, total)
        total = total.astype(BF16)
        first, second = total[:, :half], total[:, half:]
        mine_ref[...] = jnp.where(upper, second, first)
        other = jnp.where(upper, first, second)
        for k, other_ref in enumerate(other_refs):
            other_ref[...] = other[:, k * PART : (k + 1) * PART]

    mine, *others = order.call(
        kernel,
        (*[value for value, _ in lefts], *rights, *gains),
        scalars=(grid.bits,),
        grid=(width // step,),
        in_specs=[
            *[pl.BlockSpec((size, step), lambda i, b, at=at: (at, i)) for _, at in lefts],
            *[once((size, cols), lambda i, b: (0, 0))] * pairs,
            *[pl.BlockSpec((1, step), lambda i, b: (0, i))] * len(gains),
        ],
        out_specs=[
            pl.BlockSpec((step, half), lambda i, b: (i, 0)),
            *[pl.BlockSpec((step, PART), lambda i, b: (i, 0))] * parts,
        ],
        out_shape=[
            jax.ShapeDtypeStruct((width, half), BF16),
            *[jax.ShapeDtypeStruct((width, PART), BF16)] * parts,
        ],
        mib=16,
        name="weight_halves",
    )
    lead = (2,) * len(grid.axes) + (grid.block,)
    mine = mine.reshape(lead + (half,))
    chains = []
    for k, other in enumerate(others):
        came = grid.swap(other, "c").reshape(lead + (PART,))
        held = [(mine, grid.axes, k * PART, (k + 1) * PART), (came, grid.axes, 0, PART)]
        chains.append(Chain(grid.axes, held))
    return chains


def weight_rows(order, grid, lefts, rights, gain_grad, spare):
    step = 256
    pairs = len(rights)
    size, cols = rights[0].shape
    width = lefts[0][0].shape[1]
    place = grid.place("c")
    block = grid.block

    def kernel(bits_ref, *refs):
        mine_ref, other_ref = refs[-2:]
        upper = bits_ref[place] == 1
        total = None
        for l_ref, r_ref in zip(refs[:pairs], refs[pairs : 2 * pairs]):
            part = dot(l_ref[...], r_ref[...], TN)
            total = part if total is None else total + part
        column = jnp.broadcast_to(refs[2 * pairs][...], (8, step)).T[:, 0:1]
        coarse = column.astype(BF16).astype(F32)
        lane = lax.broadcasted_iota(jnp.int32, (step, cols), 1)
        total = jnp.where(lane == spare, coarse, total)
        total = jnp.where(lane == spare + 1, column - coarse, total)
        parts = total.reshape(step // (2 * block), 2, block, cols)
        first, second = parts[:, 0], parts[:, 1]
        flat = (step // 2, cols)
        mine_ref[...] = jnp.where(upper, second, first).reshape(flat).astype(BF16)
        other_ref[...] = jnp.where(upper, first, second).reshape(flat).astype(BF16)

    out = pl.BlockSpec((step // 2, cols), lambda i, b: (i, 0))
    mine, other = order.call(
        kernel,
        (*[value for value, _ in lefts], *rights, gain_grad),
        scalars=(grid.bits,),
        grid=(width // step,),
        in_specs=[
            *[pl.BlockSpec((size, step), lambda i, b, at=at: (at, i)) for _, at in lefts],
            *[once((size, cols), lambda i, b: (0, 0))] * pairs,
            pl.BlockSpec((1, step), lambda i, b: (0, i)),
        ],
        out_specs=[out, out],
        out_shape=[jax.ShapeDtypeStruct((width // 2, cols), BF16)] * 2,
        mib=16,
        name="weight_rows",
    )
    axes = grid.axes[:-1]
    shape = (2,) * len(axes) + (block, cols)
    came = grid.swap(other.reshape(shape), "c")
    return Chain(axes, [(mine.reshape(shape), axes, 0, cols), (came, axes, 0, cols)])


def settle(order, grid, chains, widths, mib):
    args, specs, ranges = [], [], []
    for chain in chains:
        specs += fold_specs(grid, chain, None)
        args += [value for value, _, _, _ in chain.pieces]
        ranges.append([(lo, hi) for _, _, lo, hi in chain.pieces])

    def kernel(bits_ref, *refs):
        inputs, outputs = iter(refs[: len(args)]), iter(refs[len(args) :])
        for pieces, width in zip(ranges, widths):
            total = functools.reduce(
                jnp.add, [next(inputs)[..., lo:hi].astype(F32) for lo, hi in pieces]
            )
            next(outputs)[...] = total[:, :width]
            column = total[:, width : width + 1] + total[:, width + 1 : width + 2]
            next(outputs)[...] = jnp.broadcast_to(column, (column.shape[0], TILE)).T[0:1, :]

    shapes = []
    for width in widths:
        shapes += [(grid.block, width), (1, grid.block)]
    return order.call(
        kernel,
        args,
        scalars=(grid.bits,),
        grid=(1,),
        in_specs=specs,
        out_specs=[pl.BlockSpec(shape, lambda i, b: (0, 0)) for shape in shapes],
        out_shape=[jax.ShapeDtypeStruct(shape, F32) for shape in shapes],
        mib=mib,
        name="settle",
    )


def conclude(order, grid, groups, widths, gains, mib, after=()):
    args, specs, ranges = [], [], []
    for group in groups:
        parts = []
        for chain in group:
            specs += fold_specs(grid, chain, None)
            args += [value for value, _, _, _ in chain.pieces]
            parts.append([(lo, hi) for _, _, lo, hi in chain.pieces])
        ranges.append(parts)
    place = grid.place("c")

    def kernel(bits_ref, *refs):
        inputs, outputs = iter(refs[: len(args)]), iter(refs[len(args) :])
        for parts, width, gained in zip(ranges, widths, gains):
            owns, lasts = [], []
            for pieces in parts:
                values = [next(inputs)[..., lo:hi].astype(F32) for lo, hi in pieces]
                owns.append(functools.reduce(jnp.add, values[:-1]))
                lasts.append(values[-1])
            own = owns[0] if len(owns) == 1 else jnp.concatenate(owns, axis=1)
            last = lasts[0] if len(lasts) == 1 else jnp.concatenate(lasts, axis=1)
            cols = own.shape[-1]
            out = next(outputs)
            gain = next(outputs) if gained else None

            def put(first, second):
                out[:, :cols] = first
                out[:, cols:] = second[:, : width - cols]
                if gain is not None:
                    at = width - cols
                    column = second[:, at : at + 1] + second[:, at + 1 : at + 2]
                    gain[...] = jnp.broadcast_to(column, (column.shape[0], TILE)).T[0:1, :]

            @pl.when(bits_ref[place] == 0)
            def _():
                put(own, last)

            @pl.when(bits_ref[place] == 1)
            def _():
                put(last, own)

    shapes = []
    for width, gained in zip(widths, gains):
        shapes.append((grid.block, width))
        if gained:
            shapes.append((1, grid.block))
    return order.call(
        kernel,
        args,
        scalars=(grid.bits,),
        grid=(1,),
        in_specs=specs,
        out_specs=[pl.BlockSpec(shape, lambda i, b: (0, 0)) for shape in shapes],
        out_shape=[jax.ShapeDtypeStruct(shape, F32) for shape in shapes],
        mib=mib,
        name="conclude",
        after=after,
    )


def finish_kernel(
    k0_ref, r0_ref, x0_ref, gq_ref, wq_ref, wkv_ref, x_ref, gain_ref, gr_ref, cos_ref, sin_ref,
    came_ref, gkv_ref, out_ref, gain_grad_ref,
):
    total = k0_ref[...].astype(F32) + r0_ref[...].astype(F32) + x0_ref[...].astype(F32)
    cos, sin = cos_ref[0], sin_ref[0]
    half = HEAD_DIM // 2
    split = RANK_KV * HEADS
    turned = total.T
    pieces = [turned[:split]]
    for r in range(RANK_KV):
        at = split + r * HEAD_DIM
        first, second = turned[at : at + half], turned[at + half : at + HEAD_DIM]
        pieces += [first * cos + second * sin, second * cos - first * sin]
    pieces.append(turned[split + RANK_KV * HEAD_DIM :])
    gkv = jnp.concatenate(pieces, axis=0).T.astype(BF16)
    gkv_ref[:, :KV_COLS] = gkv
    gkv_ref[:, KV_COLS:] = jnp.zeros((gkv.shape[0], KV_PAD - KV_COLS), BF16)
    grad = dot(gq_ref[:, :Q_COLS], wq_ref[...]) + dot(gkv, wkv_ref[...])
    values = x_ref[...].astype(F32)
    scale = lax.rsqrt(jnp.mean(values * values, axis=-1, keepdims=True) + EPS)
    weighted = grad * gain_ref[...]
    back = scale * weighted - values * (scale * scale * scale) * jnp.mean(
        weighted * values, axis=-1, keepdims=True
    )
    out_ref[...] = (gr_ref[...] + back).astype(BF16)

    @pl.when(pl.program_id(0) == 0)
    def _():
        gain_grad_ref[...] = came_ref[...]

    gain_grad_ref[...] += jnp.sum(grad * values * scale, axis=0, keepdims=True)


def finish(order, row, kept, near, far, gq, w_query, w_keyval, x, gain, grad_resid, cos, sin, came, held):
    tokens, width = x.shape
    span = cos.shape[-1]
    full = lambda i: (0, 0)
    tile = pl.BlockSpec((span, width), lambda i: (2 * row + i, 0))
    part = pl.BlockSpec((None, span, KV_COLS), lambda i: (0, i, 0))
    rope = pl.BlockSpec((1, HEAD_DIM // 2, span), lambda i: (i, 0, 0))
    vector = pl.BlockSpec((1, width), full)
    extra = () if held is None else (held,)

    def kernel(*refs):
        finish_kernel(*refs[:12], *refs[12 + len(extra) :])

    return order.call(
        kernel,
        (kept, near, far, gq, w_query, w_keyval, x, gain, grad_resid, cos, sin, came, *extra),
        grid=(2,),
        in_specs=[
            part,
            part,
            pl.BlockSpec((span, KV_COLS), lambda i: (i, 0)),
            pl.BlockSpec((span, Q_PAD), lambda i: (i, 0)),
            once((Q_COLS, width), full),
            once((KV_COLS, width), full),
            tile,
            vector,
            tile,
            rope,
            rope,
            vector,
            *[pl.BlockSpec(memory_space=pl.ANY)] * len(extra),
        ],
        out_specs=[pl.BlockSpec((span, KV_PAD), lambda i: (i, 0)), tile, vector],
        out_shape=[
            jax.ShapeDtypeStruct((2 * span, KV_PAD), BF16),
            jax.ShapeDtypeStruct((tokens, width), BF16),
            jax.ShapeDtypeStruct((1, width), F32),
        ],
        mib=20,
        name="finish",
        aliases={12: 1} if extra else None,
    )


def meet_kernel(near_ref, far_ref, out_ref):
    out_ref[...] = (near_ref[...].astype(F32) + far_ref[...].astype(F32)).astype(BF16)


def meet(order, near, far):
    shape = near.shape[1:]
    part = pl.BlockSpec((None, *shape), lambda i: (1, 0, 0))
    return order.call(
        meet_kernel,
        (near, far),
        grid=(1,),
        in_specs=[part, part],
        out_specs=[pl.BlockSpec(shape, lambda i: (0, 0))],
        out_shape=[jax.ShapeDtypeStruct(shape, BF16)],
        mib=8,
        name="meet",
    )[0]


def body(
    layer_input,
    doc_ids,
    norm1_gain,
    w_query,
    w_keyval,
    w_out,
    norm2_gain,
    w_gate,
    w_up,
    w_down,
    cotangent,
):
    row_count, local_len, width = layer_input.shape
    seq_size = lax.axis_size("seq")
    rows_size = lax.axis_size("rows")
    seq_id = lax.axis_index("seq")
    rows_id = lax.axis_index("rows")
    span = local_len // 2
    tokens = row_count * local_len
    length = local_len * seq_size
    core = seq_id % 2
    order = Order()
    grid = Grid(rows_size, seq_size, rows_id, seq_id, width)
    seq_arg = seq_id.astype(jnp.int32).reshape(1)

    x = layer_input.reshape(tokens, width)
    cot = cotangent.reshape(tokens, width)
    cot_other = grid.swap(cot, "c")
    gain1 = norm1_gain.reshape(1, width)
    gain2 = norm2_gain.reshape(1, width)
    wq_t, wkv_t = w_query.T, w_keyval.T
    docs = doc_ids.reshape(row_count, 1, length)

    spans = jnp.stack([seq_id, 2 * seq_size - 1 - seq_id])
    positions = spans[:, None] * span + jnp.arange(span, dtype=jnp.int32)[None, :]
    inv_freq = ROPE_BASE ** (-(jnp.arange(HEAD_DIM // 2, dtype=F32) * (2.0 / HEAD_DIM)))
    angles = positions.astype(F32)[:, None, :] * inv_freq[None, :, None]
    cos, sin = jnp.cos(angles), jnp.sin(angles)

    normed, qf, kv = project(order, x, gain1, wq_t, wkv_t, cos, sin)
    kv = kv.reshape(row_count, local_len, KV_COLS)
    kv_x = grid.swap(kv, "x")
    kv_core = grid.swap(kv, "c")
    half = w_gate.shape[1] // 2
    wg = lax.dynamic_slice_in_dim(w_gate, core * half, half, 1)
    wu = lax.dynamic_slice_in_dim(w_up, core * half, half, 1)
    wd = lax.dynamic_slice_in_dim(w_down, core * half, half, 0)
    gh_own, gh_oth = hidden_back(order, cot, cot_other, wd, (wg, wu))
    kv_x, _ = lax.optimization_barrier((kv_x, order.token))
    kv_both = grid.swap(kv_x, "c")
    sources = (kv, kv_core, kv_x, kv_both)
    attended, lse = attend(order, seq_arg, qf, sources, docs)
    resid, normed2 = out_project(order, x, attended, w_out, gain2)
    normed2_other = grid.swap(normed2, "c")
    h_own, gg_own, gu_own, gn2_own = feed_forward(order, normed2, gh_own, wg, wu, BF16)
    h_oth, gg_oth, gu_oth, gn2_send = feed_forward(order, normed2_other, gh_oth, wg, wu, BF16)
    gn2_came = grid.swap(gn2_send, "c")

    first, second = grid.high[-1], grid.high[:-1]
    down, _ = weight_grad(
        order, grid, "x", (stay(cot), stay(cot_other)), (stay(h_own), stay(h_oth))
    )
    gate, _ = weight_grad(order, grid, "y", (normed2, normed2_other), (gg_own, gg_oth))
    up, _ = weight_grad(order, grid, first, (normed2, normed2_other), (gu_own, gu_oth))
    grad_resid, branch, grad_att, grad_norm2 = out_back(
        order, cot, gn2_own, gn2_came, resid, w_out, gain2
    )
    out = weight_halves(order, grid, [(branch, 0)], [attended])
    grad_att = grad_att.reshape(row_count, local_len, width)

    def back(row, after=()):
        gq, near, far = attend_back(
            order, row, seq_arg, qf, sources, docs, lse, attended, grad_att, cos, sin, after
        )
        return gq, near, grid.swap(far, "c")

    def end(row, near, far, came, gq, gain, held):
        return finish(
            order, row, near, far, came, gq, wq_t, wkv_t, x, gain1, grad_resid, cos, sin, gain, held
        )

    gq0, near0, far0 = back(0)
    fold(order, grid, [([down], "y")])
    fold(order, grid, [([gate], "x")])
    fold(order, grid, [(out, first)])
    came0 = grid.swap(meet(order, near0, far0), "x")
    gq1, near1, far1 = back(1)
    upper = [up, *out]
    fold(order, grid, [(upper, "y")], after=(came0,))
    fold(order, grid, [([down, gate], first)])
    came1 = grid.swap(meet(order, near1, far1), "x")
    gkv0, ig0, gain0 = end(0, near0, far0, came0, gq0, jnp.zeros((1, width), F32), None)
    query = weight_rows(
        order, grid, [(normed, 0), (normed, 1)], [gq0, gq1], grad_norm2, Q_COLS
    )
    down_send = down_project(order, h_oth, wd)
    down_came = grid.swap(down_send, "c")
    gkv1, input_grad, grad_norm1 = end(1, near1, far1, came1, gq1, gain0, ig0)
    keyval = weight_rows(
        order, grid, [(normed, 0), (normed, 1)], [gkv0, gkv1], grad_norm1, KV_COLS
    )
    fold(order, grid, [([down, gate], second[0])])
    fold(order, grid, [([keyval], "x"), ([query], "y")])
    fold(order, grid, [(upper, "x")])
    for axis in second[1:]:
        fold(order, grid, [([down, gate], axis)])
    fold(order, grid, [([keyval], "y"), ([query], "x")])
    fold(order, grid, [(upper, second[0])])
    for axis in second[1:]:
        fold(order, grid, [(upper, axis)])
    late = [keyval, query]
    fold(order, grid, [(late, first)])
    for axis in second:
        fold(order, grid, [(late, axis)])
    fold(order, grid, [([down, gate, *upper], "c")])
    layer_output = down_project(order, h_own, wd, resid, down_came)
    g_query, g_norm2, g_keyval, g_norm1 = settle(
        order, grid, [query, keyval], [Q_COLS, KV_COLS], 8
    )
    g_down, g_gate, g_up, g_out = conclude(
        order,
        grid,
        [[down], [gate], [up], out],
        [*[w.shape[1] for w in (w_gate, w_gate, w_up)], width],
        [False] * 4,
        24,
    )
    return (
        layer_output.reshape(row_count, local_len, width),
        input_grad.reshape(row_count, local_len, width),
        g_norm1.reshape(-1),
        g_query,
        g_keyval,
        g_out.T,
        g_norm2.reshape(-1),
        g_gate,
        g_up,
        g_down.T,
    )


def solution(mesh):
    return jax.shard_map(
        body,
        mesh=mesh,
        in_specs=(
            P("rows", "seq", None),
            P("rows", None),
            P(),
            P(),
            P(),
            P(),
            P(),
            P(),
            P(),
            P(),
            P("rows", "seq", None),
        ),
        out_specs=(
            P("rows", "seq", None),
            P("rows", "seq", None),
            P(("rows", "seq")),
            P(("rows", "seq"), None),
            P(("rows", "seq"), None),
            P(None, ("rows", "seq")),
            P(("rows", "seq")),
            P(("rows", "seq"), None),
            P(("rows", "seq"), None),
            P(None, ("rows", "seq")),
        ),
        check_vma=False,
    )
```

```python
import functools

import jax
import jax.numpy as jnp
from jax import lax
from jax.experimental import pallas as pl
from jax.experimental.pallas import tpu as pltpu
from jax.sharding import PartitionSpec as P

HEADS = 16
HEAD_DIM = 64
RANK_Q = 6
RANK_KV = 2
Q_COLS = RANK_Q * (HEADS + HEAD_DIM)
KV_COLS = 2 * RANK_KV * (HEADS + HEAD_DIM)
Q_PAD = 512
KV_PAD = 384
EPS = 1e-06
ROPE_BASE = 10000.0
MASKED = -1e30
SCORE_SCALE = HEAD_DIM ** (-0.5)
VALUE_BASE = RANK_KV * (HEADS + HEAD_DIM)
TILE = 128
TILES = 9
F32 = jnp.float32
BF16 = jnp.bfloat16
NT = (((1,), (1,)), ((), ()))
TN = (((0,), (0,)), ((), ()))


def dot(left, right, dims=None):
    if dims is None:
        return jnp.dot(left, right, preferred_element_type=F32)
    return lax.dot_general(left, right, dims, preferred_element_type=F32)


def params(mib):
    return pltpu.CompilerParams(vmem_limit_bytes=mib * 2**20)


def cost(flops, nbytes, trans=0):
    return pl.CostEstimate(flops=flops, bytes_accessed=nbytes, transcendentals=trans)


def once(shape, index):
    return pl.BlockSpec(shape, index, pipeline_mode=pl.Buffered(1))


class Order:
    def __init__(self):
        self.token = None

    def call(self, kernel, args, *, grid, in_specs, out_specs, out_shape, mib, name, scalars=(), scratch=(), after=(), work=0, aliases=None):
        extra = [a for a in (self.token, *after) if a is not None]
        n_scalar, n_in, n_out = len(scalars), len(in_specs), len(out_specs)

        def run(*refs):
            head = refs[: n_scalar + n_in]
            rest = refs[n_scalar + n_in + len(extra) :]
            rest[n_out][...] = jnp.zeros_like(rest[n_out])
            kernel(*head, *rest[:n_out], *rest[n_out + 1 :])

        def spec(block, index, **kw):
            return pl.BlockSpec(block, index, **kw)

        token_spec = pl.BlockSpec((8, TILE), lambda *_: (0, 0))
        out = pl.pallas_call(
            run,
            grid_spec=pltpu.PrefetchScalarGridSpec(
                num_scalar_prefetch=n_scalar,
                grid=grid,
                in_specs=[*in_specs, *[pl.BlockSpec(memory_space=pl.ANY)] * len(extra)],
                out_specs=[*out_specs, token_spec],
                scratch_shapes=list(scratch),
            ),
            out_shape=[*out_shape, jax.ShapeDtypeStruct((8, TILE), F32)],
            compiler_params=params(mib),
            input_output_aliases={n_scalar + k: v for k, v in (aliases or {}).items()},
            cost_estimate=cost(work, 2**16),
            name=name,
        )(*scalars, *args, *extra)
        self.token = out[-1]
        return out[:-1]


def stay(value):
    return pltpu.with_memory_space_constraint(value, pltpu.HBM)


def aligned(value, factor):
    return pl.multiple_of(value, factor)


def project_kernel(x_ref, gain_ref, wq_ref, wkv_ref, cos_ref, sin_ref, normed_ref, qf_ref, kv_ref):
    x = x_ref[...].astype(F32)
    scale = lax.rsqrt(jnp.mean(x * x, axis=-1, keepdims=True) + EPS)
    normed = (x * scale * gain_ref[...]).astype(BF16)
    normed_ref[...] = normed
    kvf = dot(normed, wkv_ref[...], NT)
    qf = dot(normed, wq_ref[...], NT)
    half = HEAD_DIM // 2
    span = cos_ref.shape[-1]
    for s in range(2):
        cos, sin = cos_ref[s], sin_ref[s]
        rows = slice(s * span, (s + 1) * span)
        kvt = kvf[rows].T
        split = RANK_KV * HEADS
        pieces = [kvt[:split]]
        for r in range(RANK_KV):
            at = split + r * HEAD_DIM
            first, second = kvt[at : at + half], kvt[at + half : at + HEAD_DIM]
            pieces += [first * cos - second * sin, second * cos + first * sin]
        pieces.append(kvt[split + RANK_KV * HEAD_DIM :])
        kv_ref[rows, :] = jnp.concatenate(pieces, axis=0).T.astype(BF16)
        qt = qf[rows].T
        split = RANK_Q * HEADS
        qf_ref[s, :split, :] = qt[:split]
        for r in range(RANK_Q):
            at = split + r * HEAD_DIM
            first, second = qt[at : at + half], qt[at + half : at + HEAD_DIM]
            qf_ref[s, at : at + half, :] = first * cos - second * sin
            qf_ref[s, at + half : at + HEAD_DIM, :] = second * cos + first * sin


def project(order, x, gain, w_query, w_keyval, cos, sin):
    tokens, width = x.shape
    span = cos.shape[-1]
    groups = tokens // span
    full = lambda i: (0, 0)
    rope = pl.BlockSpec((2, HEAD_DIM // 2, span), lambda i: (0, 0, 0))
    return order.call(
        project_kernel,
        (x, gain, w_query, w_keyval, cos, sin),
        grid=(groups // 2,),
        in_specs=[
            pl.BlockSpec((2 * span, width), lambda i: (i, 0)),
            pl.BlockSpec((1, width), full),
            once((Q_COLS, width), full),
            once((KV_COLS, width), full),
            rope,
            rope,
        ],
        out_specs=[
            pl.BlockSpec((2 * span, width), lambda i: (i, 0)),
            pl.BlockSpec((2, Q_COLS, span), lambda i: (i, 0, 0)),
            pl.BlockSpec((2 * span, KV_COLS), lambda i: (i, 0)),
        ],
        out_shape=[
            jax.ShapeDtypeStruct((tokens, width), BF16),
            jax.ShapeDtypeStruct((groups, Q_COLS, span), F32),
            jax.ShapeDtypeStruct((tokens, KV_COLS), BF16),
        ],
        mib=56,
        name="project",
    )


PIECES = ((0, 2), (2, 3), (3, 4), (4, 5), (5, 7), (7, 9))


def tile_place(tile, seq_id):
    low = tile < seq_id + 2
    return low, jnp.where(low, tile, tile + 1 - seq_id)


def piece_side(piece, seq_id):
    first, last = piece
    low = first < seq_id + 2
    side = 0 if last <= 2 else (1 if first > 4 else jnp.where(low, 0, 1))
    return slice(first * TILE, last * TILE), side, low


def choose(side, low, pair):
    return pair[side] if isinstance(side, int) else jnp.where(low, pair[0], pair[1])


def gather(totals, side, low, part, combine, empty):
    for s in range(2):
        if isinstance(side, int):
            if side != s:
                continue
            term = part
        else:
            term = jnp.where(low if s == 0 else ~low, part, empty)
        totals[s] = term if totals[s] is None else combine(totals[s], term)


def gather_keys(seq_id, sources, qf_ref, qa, qb, kvpos, kvt, kva, bias, docs_ref, row, span):
    for which, source in enumerate(sources):
        holder = seq_id ^ which
        kvpos[pl.ds(aligned(holder * span, 32), span), :] = source[0, :span, :]
        kvpos[pl.ds(aligned((7 - holder) * span, 32), span), :] = source[0, span:, :]
    columns = []
    for number in (seq_id, 7 - seq_id):
        ids = None
        for place in range(8):
            part = docs_ref[row : row + 1, place * span : (place + 1) * span]
            ids = part if ids is None else jnp.where(number == place, part, ids)
        columns.append(jnp.broadcast_to(ids.astype(F32), (8, span)).T[:, 0:1].astype(jnp.int32))
    for tile in range(TILES):
        low, place = tile_place(tile, seq_id)
        start = aligned(place * TILE, TILE)
        cols = slice(tile * TILE, (tile + 1) * TILE)
        kvt[:, cols] = kvpos[pl.ds(start, TILE), :].astype(F32).T
        side = 0 if tile < 2 else (1 if tile > 4 else None)
        doc_q = jnp.where(low, columns[0], columns[1]) if side is None else columns[side]
        number = jnp.where(low, seq_id, 7 - seq_id)
        pos_q = number * span + lax.broadcasted_iota(jnp.int32, (span, TILE), 0)
        pos_k = start + lax.broadcasted_iota(jnp.int32, (span, TILE), 1)
        allowed = (doc_q == docs_ref[row : row + 1, pl.ds(start, TILE)]) & (pos_k <= pos_q)
        bias[:, cols] = jnp.where(allowed, 0.0, MASKED)
    split = RANK_KV * HEADS
    kva[:split, 0, :] = kvt[:split, :] * (1.0 / RANK_KV)
    kva[split:, 0, :] = kvt[VALUE_BASE : VALUE_BASE + split, :] * (1.0 / RANK_KV)
    both = jnp.concatenate([qf_ref[0], qf_ref[1]], axis=1)
    split = RANK_Q * HEADS
    qa[:, 0, :] = both[:split] * (1.0 / RANK_Q)
    qb[...] = both[split:]


def expand_queries(qf_ref, qa, s, head):
    split = RANK_Q * HEADS
    total = None
    for r in range(RANK_Q):
        weight = qa[s, r * HEADS + head]
        term = weight * qf_ref[s, split + r * HEAD_DIM : split + (r + 1) * HEAD_DIM, :]
        total = term if total is None else total + term
    return total.astype(BF16) * BF16(SCORE_SCALE)


def expand_pair(kvt, kva, base, head):
    split = RANK_KV * HEADS
    total = None
    for r in range(RANK_KV):
        at = base + split + r * HEAD_DIM
        weight = kva[(base // VALUE_BASE) * split + r * HEADS + head]
        term = weight * kvt[at : at + HEAD_DIM, :]
        total = term if total is None else total + term
    return total.astype(BF16)


def weave(*streams):
    streams = list(streams)
    while streams:
        for stream in list(streams):
            try:
                next(stream)
            except StopIteration:
                streams.remove(stream)


SEEN = ((0, 5), (3, 10))


def place_keys(seq_id, sources, kvpos, span):
    for which, source in enumerate(sources):
        holder = seq_id ^ which
        kvpos[pl.ds(aligned(holder * span, 32), span), :] = source[0, :span, :]
        kvpos[pl.ds(aligned((7 - holder) * span, 32), span), :] = source[0, span:, :]


def query_docs(number, docs_ref, row, span):
    ids = None
    for place in range(8):
        part = docs_ref[row : row + 1, place * span : (place + 1) * span]
        ids = part if ids is None else jnp.where(number == place, part, ids)
    return jnp.broadcast_to(ids.astype(F32), (8, span)).T[:, 0:1].astype(jnp.int32)


def attend_kernel(
    row, seq_ref, qf_ref, kv0, kv1, kv2, kv3, doc_ref, out_ref, lse_ref,
    kvpos, kvt, bias_low, bias_high, kva, qa, heads_out, heads_lse,
    low_a, low_b, high_a, high_b, top_a, top_b,
):
    seq_id = seq_ref[0]
    span = qf_ref.shape[-1]
    biases = (bias_low, bias_high)
    place_keys(seq_id, (kv0, kv1, kv2, kv3), kvpos, span)
    length = kvpos.shape[0]
    for at in range(0, length, TILE):
        kvt[:, at : at + TILE] = kvpos[at : at + TILE, :].astype(F32).T
    for s, number in enumerate((seq_id, 7 - seq_id)):
        doc_q = query_docs(number, doc_ref, row, span)
        pos_q = number * span + lax.broadcasted_iota(jnp.int32, (span, TILE), 0)
        for tile in range(*SEEN[s]):
            start = tile * TILE
            pos_k = start + lax.broadcasted_iota(jnp.int32, (span, TILE), 1)
            allowed = (doc_q == doc_ref[row : row + 1, start : start + TILE]) & (pos_k <= pos_q)
            at = start - SEEN[s][0] * TILE
            biases[s][:, at : at + TILE] = jnp.where(allowed, 0.0, MASKED)
    split = RANK_KV * HEADS
    kva[:split, 0, :] = kvt[:split, :] * (1.0 / RANK_KV)
    kva[split:, 0, :] = kvt[VALUE_BASE : VALUE_BASE + split, :] * (1.0 / RANK_KV)
    for s in range(2):
        qa[s, :, 0, :] = qf_ref[s, : RANK_Q * HEADS, :] * (1.0 / RANK_Q)

    def expand(base, head):
        total = None
        for r in range(RANK_KV):
            at = base + split + r * HEAD_DIM
            weight = kva[(base // VALUE_BASE) * split + r * HEADS + head]
            term = weight * kvt[at : at + HEAD_DIM, :]
            total = term if total is None else total + term
        return total.astype(BF16)

    def pieces(s):
        count = SEEN[s][1] - SEEN[s][0]
        edges = [*range(0, count, 2), count]
        shift = SEEN[s][0] * TILE
        for lo, hi in zip(edges, edges[1:]):
            yield slice(lo * TILE, hi * TILE), slice(shift + lo * TILE, shift + hi * TILE)

    def scores_of(head, scores, top):
        keys = expand(0, head)
        yield
        for s in range(2):
            queries = expand_queries(qf_ref, qa, s, head).T
            best = None
            for cols, places in pieces(s):
                part = dot(queries, keys[:, places]) + biases[s][:, cols]
                scores[s][:, cols] = part
                for at in range(0, part.shape[1], TILE):
                    tile = part[:, at : at + TILE]
                    best = tile if best is None else jnp.maximum(best, tile)
                yield
            top[s] = jnp.max(best, axis=-1, keepdims=True)

    def weigh(head, scores, top):
        values = expand(VALUE_BASE, head)
        values = jnp.concatenate([values, jnp.ones((16, values.shape[1]), BF16)], axis=0)
        yield
        for s in range(2):
            peak = top[s]
            out = None
            for cols, places in pieces(s):
                raised = jnp.exp(scores[s][:, cols] - peak).astype(BF16)
                part = dot(raised, values[:, places], NT)
                out = part if out is None else out + part
                yield
            total = out[:, HEAD_DIM : HEAD_DIM + 1]
            heads_out[s, head] = (out[:, :HEAD_DIM] * (1.0 / total)).astype(BF16)
            heads_lse[s, head] = peak + jnp.log(total)

    scores_a, scores_b = (low_a, high_a), (low_b, high_b)

    def pair_step(pair, carry):
        head = 2 * pair
        weave(scores_of(head + 1, scores_b, top_b), weigh(head, scores_a, top_a))
        following = jnp.minimum(head + 2, HEADS - 1)
        weave(scores_of(following, scores_a, top_a), weigh(head + 1, scores_b, top_b))
        return carry

    weave(scores_of(0, scores_a, top_a))
    lax.fori_loop(0, HEADS // 2, pair_step, 0)
    lane = lax.broadcasted_iota(jnp.int32, (span, TILE), 1)
    for s in range(2):
        out_ref[s * span : (s + 1) * span, :] = jnp.concatenate(
            [heads_out[s, head] for head in range(HEADS)], axis=1
        )
        lse = jnp.zeros((span, TILE), F32)
        for head in range(HEADS):
            lse = jnp.where(lane == head, heads_lse[s, head], lse)
        lse_ref[s] = lse


def attention_specs(span, docs, row=None):
    at = lambda i: i if row is None else row
    kv_spec = pl.BlockSpec((1, 2 * span, KV_COLS), lambda i, s: (at(i), 0, 0))
    return [
        pl.BlockSpec((2, Q_COLS, span), lambda i, s: (at(i), 0, 0)),
        kv_spec,
        kv_spec,
        kv_spec,
        kv_spec,
        pl.BlockSpec((None, 1, docs.shape[-1]), lambda i, s: (at(i), 0, 0)),
    ]


def attend(order, seq_id, qf, sources, docs):
    rows, _, length = docs.shape
    span = qf.shape[-1]
    width = HEADS * HEAD_DIM
    return order.call(
        functools.partial(attend_kernel, 0),
        (qf, *sources, docs),
        scalars=(seq_id,),
        grid=(rows,),
        in_specs=attention_specs(span, docs),
        out_specs=[
            pl.BlockSpec((2 * span, width), lambda i, s: (i, 0)),
            pl.BlockSpec((2, span, TILE), lambda i, s: (i, 0, 0)),
        ],
        scratch=[
            pltpu.VMEM((length, KV_COLS), BF16),
            pltpu.VMEM((KV_COLS, length), F32),
            pltpu.VMEM((span, 5 * TILE), F32),
            pltpu.VMEM((span, 7 * TILE), F32),
            pltpu.VMEM((2 * RANK_KV * HEADS, 1, length), F32),
            pltpu.VMEM((2, RANK_Q * HEADS, 1, span), F32),
            pltpu.VMEM((2, HEADS, span, HEAD_DIM), BF16),
            pltpu.VMEM((2, HEADS, span, 1), F32),
            pltpu.VMEM((span, 5 * TILE), F32),
            pltpu.VMEM((span, 5 * TILE), F32),
            pltpu.VMEM((span, 7 * TILE), F32),
            pltpu.VMEM((span, 7 * TILE), F32),
            pltpu.VMEM((2, span, 1), F32),
            pltpu.VMEM((2, span, 1), F32),
        ],
        out_shape=[
            jax.ShapeDtypeStruct((rows * 2 * span, width), BF16),
            jax.ShapeDtypeStruct((rows * 2, span, TILE), F32),
        ],
        mib=24,
        name="attend",
    )


def attend_back_kernel(
    row, seq_ref, qf_ref, kv0, kv1, kv2, kv3, doc_ref, lse_ref, att_ref, grad_ref,
    cos_ref, sin_ref, gq_ref, near_ref, far_ref,
    kvpos, kvt, bias, dot_t, stats, gkvt, gkvpos, gqt, gka, gqa, kva, qa,
    probs_a, probs_b, grads_a, grads_b, q_a, q_b, k_a, k_b, qb,
):
    seq_id = seq_ref[0]
    span = qf_ref.shape[-1]
    gather_keys(seq_id, (kv0, kv1, kv2, kv3), qf_ref, qa, qb, kvpos, kvt, kva, bias, doc_ref, row, span)
    width = HEADS * HEAD_DIM
    chooser = (
        lax.broadcasted_iota(jnp.int32, (width, TILE), 0) // HEAD_DIM
        == lax.broadcasted_iota(jnp.int32, (width, TILE), 1)
    ).astype(BF16)
    grad = grad_ref[0]
    dot_t[...] = grad.T
    product = grad.astype(F32) * att_ref[...].astype(F32)
    coarse = product.astype(BF16)
    fine = (product - coarse.astype(F32)).astype(BF16)
    centre = dot(coarse, chooser) + dot(fine, chooser)
    totals = jnp.concatenate([lse_ref[0], lse_ref[1]], axis=0)
    stats[0, :, 0, :] = -totals.T[:HEADS, :]
    stats[1, :, 0, :] = -centre.T[:HEADS, :]
    gkvt[...] = jnp.zeros_like(gkvt)
    gqt[...] = jnp.zeros_like(gqt)

    pieces = [piece_side(piece, seq_id) for piece in PIECES]
    split = RANK_KV * HEADS

    extra = lax.broadcasted_iota(jnp.int32, (16, 2 * span), 0)
    ones = jnp.ones((16, TILES * TILE), BF16)

    def with_row(value, row):
        coarse = row.astype(BF16).astype(F32)
        middle = (row - coarse).astype(BF16).astype(F32)
        fine = row - coarse - middle
        rest = jnp.where(extra == 0, coarse, jnp.where(extra == 1, middle, fine))
        return jnp.concatenate([value, jnp.where(extra < 3, rest, 0.0).astype(BF16)], axis=0)

    def scores_of(head, hold):
        probs_of, grads_of, q_of, k_of = hold
        rows = pl.ds(aligned(head * HEAD_DIM, HEAD_DIM), HEAD_DIM)
        keys = expand_pair(kvt, kva, 0, head)
        k_of[...] = keys
        keys = jnp.concatenate([keys, ones], axis=0)
        values = jnp.concatenate([expand_pair(kvt, kva, VALUE_BASE, head), ones], axis=0)
        yield
        total = None
        for r in range(RANK_Q):
            term = qa[r * HEADS + head] * qb[r * HEAD_DIM : (r + 1) * HEAD_DIM, :]
            total = term if total is None else total + term
        q_t = total.astype(BF16) * BF16(SCORE_SCALE)
        q_of[...] = q_t
        turned = with_row(q_t, stats[0, head]).T
        queries = [turned[:span], turned[span:]]
        turned = with_row(dot_t[rows, :], stats[1, head]).T
        grads = [turned[:span], turned[span:]]
        yield
        for cols, side, low in pieces:
            score = dot(choose(side, low, queries), keys[:, cols]) + bias[:, cols]
            probs = jnp.exp(score)
            grad_p = dot(choose(side, low, grads), values[:, cols])
            probs_of[:, cols] = probs.astype(BF16)
            grads_of[:, cols] = (probs * grad_p).astype(BF16)
            yield

    def grads_of_head(head, hold):
        probs_of, grads_of, q_of, k_of = hold
        rows = pl.ds(aligned(head * HEAD_DIM, HEAD_DIM), HEAD_DIM)
        q_t, g_t = q_of[...], dot_t[rows, :]
        q_sides = [q_t[:, :span], q_t[:, span:]]
        g_sides = [g_t[:, :span], g_t[:, span:]]
        yield
        grad_q = [None, None]
        for cols, side, low in pieces:
            grad_s = grads_of[:, cols]
            gather(grad_q, side, low, dot(k_of[:, cols], grad_s, NT), jnp.add, 0.0)
            for base, grad in (
                (0, dot(choose(side, low, q_sides), grad_s)),
                (VALUE_BASE, dot(choose(side, low, g_sides), probs_of[:, cols])),
            ):
                for r in range(RANK_KV):
                    where = base + split + r * HEAD_DIM
                    b_rows = slice(where, where + HEAD_DIM)
                    a_row = (base // VALUE_BASE) * split + r * HEADS + head
                    gka[a_row, :, cols] = jnp.sum(grad * kvt[b_rows, cols], axis=0, keepdims=True)
                    gkvt[b_rows, cols] += grad * kva[a_row, :, cols]
            yield
        both = jnp.concatenate(grad_q, axis=1)
        where = RANK_Q * HEADS
        for r in range(RANK_Q):
            b_rows = slice(r * HEAD_DIM, (r + 1) * HEAD_DIM)
            a_row = r * HEADS + head
            gqa[a_row] = jnp.sum(both * qb[b_rows, :], axis=0, keepdims=True)
            gqt[b_rows, :] += both * qa[a_row]
            if r % 2:
                yield

    def pair_step(pair, carry):
        head = 2 * pair
        weave(scores_of(head + 1, hold_b), grads_of_head(head, hold_a))
        following = jnp.minimum(head + 2, HEADS - 1)
        weave(scores_of(following, hold_a), grads_of_head(head + 1, hold_b))
        return carry

    hold_a, hold_b = (probs_a, grads_a, q_a, k_a), (probs_b, grads_b, q_b, k_b)
    weave(scores_of(0, hold_a))
    lax.fori_loop(0, HEADS // 2, pair_step, 0)
    half = HEAD_DIM // 2
    cos = jnp.concatenate([cos_ref[0], cos_ref[1]], axis=1)
    sin = jnp.concatenate([sin_ref[0], sin_ref[1]], axis=1)
    pieces = [gqa[:, 0, :] * (1.0 / RANK_Q)]
    for r in range(RANK_Q):
        at = r * HEAD_DIM
        first, second = gqt[at : at + half, :], gqt[at + half : at + HEAD_DIM, :]
        pieces += [first * cos + second * sin, second * cos - first * sin]
    back = jnp.concatenate(pieces, axis=0) * SCORE_SCALE
    back = jnp.concatenate([back, jnp.zeros((Q_PAD - Q_COLS, 2 * span), F32)], axis=0)
    gq_ref[...] = back.T.astype(BF16)
    split = RANK_KV * HEADS
    gkvt[:split, :] = gka[:split, 0, :] * (1.0 / RANK_KV)
    gkvt[VALUE_BASE : VALUE_BASE + split, :] = gka[split:, 0, :] * (1.0 / RANK_KV)
    gkvpos[...] = jnp.zeros_like(gkvpos)
    for tile in range(TILES):
        _, place = tile_place(tile, seq_id)
        rows = pl.ds(aligned(place * TILE, TILE), TILE)
        gkvpos[rows, :] += gkvt[:, tile * TILE : (tile + 1) * TILE].T
    for which in range(4):
        holder = seq_id ^ which
        target = near_ref if which in (0, 2) else far_ref
        for s, number in enumerate((holder, 7 - holder)):
            target[which // 2, s * span : (s + 1) * span, :] = gkvpos[
                pl.ds(aligned(number * span, 32), span), :
            ].astype(BF16)


def attend_back(order, row, seq_id, qf, sources, docs, lse, attended, grad_attended, cos, sin, after):
    length = docs.shape[-1]
    span = qf.shape[-1]
    width = HEADS * HEAD_DIM
    wide = pl.BlockSpec((1, 2 * span, width), lambda i, s: (row, 0, 0))
    rope = pl.BlockSpec((2, HEAD_DIM // 2, span), lambda i, s: (0, 0, 0))
    parts = pl.BlockSpec((2, 2 * span, KV_COLS), lambda i, s: (0, 0, 0))
    return order.call(
        functools.partial(attend_back_kernel, 0),
        (qf, *sources, docs, lse, attended, grad_attended, cos, sin),
        scalars=(seq_id,),
        grid=(1,),
        in_specs=attention_specs(span, docs, row)
        + [
            pl.BlockSpec((2, span, TILE), lambda i, s: (row, 0, 0)),
            pl.BlockSpec((2 * span, width), lambda i, s: (row, 0)),
            wide,
            rope,
            rope,
        ],
        out_specs=[pl.BlockSpec((2 * span, Q_PAD), lambda i, s: (0, 0)), parts, parts],
        scratch=[
            pltpu.VMEM((length, KV_COLS), BF16),
            pltpu.VMEM((KV_COLS, TILES * TILE), F32),
            pltpu.VMEM((span, TILES * TILE), F32),
            pltpu.VMEM((width, 2 * span), BF16),
            pltpu.VMEM((2, HEADS, 1, 2 * span), F32),
            pltpu.VMEM((KV_COLS, TILES * TILE), F32),
            pltpu.VMEM((length, KV_COLS), F32),
            pltpu.VMEM((RANK_Q * HEAD_DIM, 2 * span), F32),
            pltpu.VMEM((2 * RANK_KV * HEADS, 1, TILES * TILE), F32),
            pltpu.VMEM((RANK_Q * HEADS, 1, 2 * span), F32),
            pltpu.VMEM((2 * RANK_KV * HEADS, 1, TILES * TILE), F32),
            pltpu.VMEM((RANK_Q * HEADS, 1, 2 * span), F32),
            pltpu.VMEM((span, TILES * TILE), BF16),
            pltpu.VMEM((span, TILES * TILE), BF16),
            pltpu.VMEM((span, TILES * TILE), BF16),
            pltpu.VMEM((span, TILES * TILE), BF16),
            pltpu.VMEM((HEAD_DIM, 2 * span), BF16),
            pltpu.VMEM((HEAD_DIM, 2 * span), BF16),
            pltpu.VMEM((HEAD_DIM, TILES * TILE), BF16),
            pltpu.VMEM((HEAD_DIM, TILES * TILE), BF16),
            pltpu.VMEM((RANK_Q * HEAD_DIM, 2 * span), F32),
        ],
        out_shape=[
            jax.ShapeDtypeStruct((2 * span, Q_PAD), BF16),
            jax.ShapeDtypeStruct((2, 2 * span, KV_COLS), BF16),
            jax.ShapeDtypeStruct((2, 2 * span, KV_COLS), BF16),
        ],
        mib=32,
        name="attend_back",
        after=after,
    )


def out_kernel(x_ref, att_ref, w_ref, gain_ref, resid_ref, normed_ref):
    resid = x_ref[...].astype(F32) + dot(att_ref[...], w_ref[...])
    scale = lax.rsqrt(jnp.mean(resid * resid, axis=-1, keepdims=True) + EPS)
    resid_ref[...] = resid
    normed_ref[...] = (resid * scale * gain_ref[...]).astype(BF16)


def out_project(order, x, attended, w_out, gain):
    tokens, width = x.shape
    step = tokens // 2
    tile = pl.BlockSpec((step, width), lambda i: (i, 0))
    return order.call(
        out_kernel,
        (x, attended, w_out, gain),
        grid=(2,),
        in_specs=[
            tile,
            tile,
            once(w_out.shape, lambda i: (0, 0)),
            pl.BlockSpec((1, width), lambda i: (0, 0)),
        ],
        out_specs=[tile, tile],
        out_shape=[pltpu.HBM((tokens, width), F32), jax.ShapeDtypeStruct((tokens, width), BF16)],
        mib=20,
        name="out_project",
    )


def out_back_kernel(
    cot_ref, own_ref, other_ref, resid_ref, w_ref, gain_ref, gr_ref, gb_ref, ga_ref, gain_grad_ref
):
    grad = own_ref[...].astype(F32) + other_ref[...].astype(F32)
    values = resid_ref[...]
    scale = lax.rsqrt(jnp.mean(values * values, axis=-1, keepdims=True) + EPS)
    weighted = grad * gain_ref[...]
    back = scale * weighted - values * (scale * scale * scale) * jnp.mean(
        weighted * values, axis=-1, keepdims=True
    )
    grad_resid = cot_ref[...].astype(F32) + back
    branch = grad_resid.astype(BF16)
    gr_ref[...] = grad_resid
    gb_ref[...] = branch
    ga_ref[...] = dot(branch, w_ref[...], NT).astype(BF16)

    @pl.when(pl.program_id(0) == 0)
    def _():
        gain_grad_ref[...] = jnp.zeros_like(gain_grad_ref)

    gain_grad_ref[...] += jnp.sum(grad * values * scale, axis=0, keepdims=True)


def out_back(order, cot, own, other, resid, w_out, gain):
    tokens, width = cot.shape
    step = tokens // 2
    tile = pl.BlockSpec((step, width), lambda i: (i, 0))
    row = pl.BlockSpec((1, width), lambda i: (0, 0))
    return order.call(
        out_back_kernel,
        (cot, own, other, resid, w_out, gain),
        grid=(2,),
        in_specs=[tile, tile, tile, tile, once(w_out.shape, lambda i: (0, 0)), row],
        out_specs=[tile, tile, tile, row],
        out_shape=[
            jax.ShapeDtypeStruct((tokens, width), F32),
            jax.ShapeDtypeStruct((tokens, width), BF16),
            jax.ShapeDtypeStruct((tokens, width), BF16),
            jax.ShapeDtypeStruct((1, width), F32),
        ],
        mib=26,
        name="out_back",
    )


def hidden_back_kernel(own_ref, other_ref, w_ref, own_out, other_out):
    own_out[...] = dot(own_ref[...], w_ref[...], NT).astype(BF16)
    other_out[...] = dot(other_ref[...], w_ref[...], NT).astype(BF16)


def hidden_back(order, cot, cot_other, w_down, after):
    tokens, width = cot.shape
    half = w_down.shape[0]
    step = tokens // 2
    tile = pl.BlockSpec((step, width), lambda i: (i, 0))
    out = pl.BlockSpec((step, half), lambda i: (i, 0))
    shape = jax.ShapeDtypeStruct((tokens, half), BF16)
    return order.call(
        hidden_back_kernel,
        (cot, cot_other, w_down),
        grid=(2,),
        in_specs=[tile, tile, once(w_down.shape, lambda i: (0, 0))],
        out_specs=[out, out],
        out_shape=[shape, shape],
        mib=24,
        name="hidden_back",
        after=after,
    )


def ff_kernel(n2_ref, gh_ref, wg_ref, wu_ref, h_ref, gg_ref, gu_ref, back_ref):
    gate = dot(n2_ref[...], wg_ref[...])
    up = dot(n2_ref[...], wu_ref[...])
    grad_hidden = gh_ref[...].astype(F32)
    sigmoid = 1.0 / (1.0 + jnp.exp(-gate))
    silu = gate * sigmoid
    h_ref[...] = (silu * up).astype(BF16)
    gu = (grad_hidden * silu).astype(BF16)
    gg = (grad_hidden * up * (sigmoid + silu * (1.0 - sigmoid))).astype(BF16)
    gu_ref[...] = gu
    gg_ref[...] = gg
    back = dot(gg, wg_ref[...], NT) + dot(gu, wu_ref[...], NT)
    back_ref[...] = back.astype(back_ref.dtype)


def feed_forward(order, n2, grad_hidden, w_gate, w_up, dtype):
    tokens, width = n2.shape
    half = w_gate.shape[1]
    step = tokens // 2
    weight = once((width, half), lambda i: (0, 0))
    wide = pl.BlockSpec((step, width), lambda i: (i, 0))
    out = pl.BlockSpec((step, half), lambda i: (i, 0))
    return order.call(
        ff_kernel,
        (n2, grad_hidden, w_gate, w_up),
        grid=(2,),
        in_specs=[wide, out, weight, weight],
        out_specs=[out, out, out, wide],
        out_shape=[pltpu.HBM((tokens, half), BF16)] * 3
        + [(pltpu.HBM if dtype == F32 else jax.ShapeDtypeStruct)((tokens, width), dtype)],
        mib=30,
        name="feed_forward",
    )


def down_other_kernel(h_ref, w_ref, out_ref):
    out_ref[...] = dot(h_ref[...], w_ref[...]).astype(BF16)


def down_own_kernel(h_ref, w_ref, resid_ref, came_ref, out_ref):
    total = resid_ref[...] + came_ref[...].astype(F32) + dot(h_ref[...], w_ref[...])
    out_ref[...] = total.astype(BF16)


def down_project(order, hidden, w_down, resid=None, came=None):
    tokens, half = hidden.shape
    width = w_down.shape[1]
    step = tokens // 2
    wide = pl.BlockSpec((step, width), lambda i: (i, 0))
    extra = () if resid is None else (resid, came)
    return order.call(
        down_own_kernel if extra else down_other_kernel,
        (hidden, w_down, *extra),
        grid=(2,),
        in_specs=[
            pl.BlockSpec((step, half), lambda i: (i, 0)),
            once((half, width), lambda i: (0, 0)),
            *[wide] * len(extra),
        ],
        out_specs=[wide],
        out_shape=[jax.ShapeDtypeStruct((tokens, width), BF16)],
        mib=20,
        name="down_project",
    )[0]


class Grid:
    def __init__(self, rows_size, seq_size, rows_id, seq_id, width):
        self.high = [f"b{i}" for i in range(rows_size.bit_length() - 2, 0, -1)]
        self.axes = (*self.high, "y", "x", "c")
        self.block = width // (rows_size * seq_size)
        self.route = {"x": ("seq", 2, seq_size), "c": ("seq", 1, seq_size), "y": ("rows", 1, rows_size)}
        for i in range(1, rows_size.bit_length() - 1):
            self.route[f"b{i}"] = ("rows", 1 << i, rows_size)
        bits = []
        for axis in self.axes:
            name, mask, _ = self.route[axis]
            bits.append(((seq_id if name == "seq" else rows_id) // mask) % 2)
        self.bits = jnp.stack(bits).astype(jnp.int32)

    def place(self, axis):
        return self.axes.index(axis)

    def swap(self, value, axis):
        name, mask, size = self.route[axis]
        return lax.ppermute(value, name, [(i, i ^ mask) for i in range(size)])


class Chain:
    def __init__(self, axes, pieces):
        self.axes, self.pieces = axes, pieces


def fold_specs(grid, chain, axis):
    specs = []
    for value, axes, _, _ in chain.pieces:
        block, kinds = [], []
        for name in axes:
            if name == axis:
                block.append(None)
                kinds.append((grid.place(name), True))
            elif name in chain.axes:
                block.append(2)
                kinds.append(None)
            else:
                block.append(None)
                kinds.append((grid.place(name), False))

        def index(i, bits, kinds=tuple(kinds)):
            out = []
            for kind in kinds:
                if kind is None:
                    out.append(0)
                else:
                    out.append(1 - bits[kind[0]] if kind[1] else bits[kind[0]])
            return (*out, 0, 0)

        specs.append(pl.BlockSpec((*block, *value.shape[-2:]), index))
    return specs


def fold(order, grid, groups, after=()):
    args, specs, layout, shapes = [], [], [], []
    for chains, axis in groups:
        parts = []
        for chain in chains:
            parts.append([(lo, hi) for _, _, lo, hi in chain.pieces])
            args += [value for value, _, _, _ in chain.pieces]
            specs += fold_specs(grid, chain, axis)
        layout.append(parts)
        left = tuple(a for a in chains[0].axes if a != axis)
        cols = sum(c.pieces[0][3] - c.pieces[0][2] for c in chains)
        shapes.append((2,) * len(left) + (grid.block, cols))

    def kernel(bits_ref, *refs):
        inputs, outputs = iter(refs[: len(args)]), refs[len(args) :]
        for out, parts in zip(outputs, layout):
            sums = []
            for ranges in parts:
                total = None
                for lo, hi in ranges:
                    value = next(inputs)[..., lo:hi].astype(F32)
                    total = value if total is None else total + value
                sums.append(total.astype(BF16))
            out[...] = sums[0] if len(sums) == 1 else jnp.concatenate(sums, axis=-1)

    def whole(shape):
        return pl.BlockSpec(shape, lambda i, bits: (0,) * len(shape))

    sends = order.call(
        kernel,
        args,
        scalars=(grid.bits,),
        grid=(1,),
        in_specs=specs,
        out_specs=[whole(shape) for shape in shapes],
        out_shape=[jax.ShapeDtypeStruct(shape, BF16) for shape in shapes],
        mib=26,
        name="fold",
        after=after,
    )
    for (chains, axis), send in zip(groups, sends):
        came = grid.swap(send, axis)
        at = 0
        for chain in chains:
            left = tuple(a for a in chain.axes if a != axis)
            cols = chain.pieces[0][3] - chain.pieces[0][2]
            chain.pieces.append((came, left, at, at + cols))
            chain.axes = left
            at += cols
    return sends


def weight_grad(order, grid, axis, left, right, after=()):
    tokens, width = left[0].shape
    cols = right[0].shape[1]
    step = width // 2
    inner = grid.axes[1:]
    place = grid.place(axis)
    shape = (2,) * (len(grid.axes) - 1) + (grid.block, cols)

    def kernel(bits_ref, l0_ref, l1_ref, r0_ref, r1_ref, send_ref, keep_ref):
        total = dot(l0_ref[...], r0_ref[...], TN) + dot(l1_ref[...], r1_ref[...], TN)
        at = inner.index(axis)
        parts = total.astype(BF16).reshape(2**at, 2, step // 2 ** (at + 1), cols)
        upper = bits_ref[place] == 1
        send_ref[...] = jnp.where(upper, parts[:, 0], parts[:, 1]).reshape(step // 2, cols)
        keep_ref[...] = jnp.where(upper, parts[:, 1], parts[:, 0]).reshape(step // 2, cols)

    l_spec = pl.BlockSpec((tokens, step), lambda i, b: (0, i))
    r_spec = once((tokens, cols), lambda i, b: (0, 0))
    out = pl.BlockSpec((step // 2, cols), lambda i, b: (i, 0))
    send, keep = order.call(
        kernel,
        (left[0], left[1], right[0], right[1]),
        scalars=(grid.bits,),
        grid=(2,),
        in_specs=[l_spec, l_spec, r_spec, r_spec],
        out_specs=[out, out],
        out_shape=[jax.ShapeDtypeStruct((width // 2, cols), BF16)] * 2,
        mib=28,
        name="weight_grad",
        after=after,
    )
    axes = tuple(a for a in grid.axes if a != axis)
    came = grid.swap(send.reshape(shape), axis)
    return Chain(axes, [(keep.reshape(shape), axes, 0, cols), (came, axes, 0, cols)]), send


PART = 256


def weight_halves(order, grid, lefts, rights, gain_grad=None, spare=0):
    step = 256
    pairs = len(rights)
    size, cols = rights[0].shape
    width = lefts[0][0].shape[1]
    half = cols // 2
    parts = half // PART
    gains = [] if gain_grad is None else [gain_grad]
    place = grid.place("c")

    def kernel(bits_ref, *refs):
        mine_ref, other_refs = refs[-1 - parts], refs[-parts:]
        upper = bits_ref[place] == 1
        total = None
        for l_ref, r_ref in zip(refs[:pairs], refs[pairs : 2 * pairs]):
            part = dot(l_ref[...], r_ref[...], TN)
            total = part if total is None else total + part
        if gains:
            column = jnp.broadcast_to(refs[2 * pairs][...], (8, step)).T[:, 0:1]
            coarse = column.astype(BF16).astype(F32)
            lane = lax.broadcasted_iota(jnp.int32, (step, cols), 1)
            total = jnp.where(lane == spare, coarse, total)
            total = jnp.where(lane == spare + 1, column - coarse, total)
        total = total.astype(BF16)
        first, second = total[:, :half], total[:, half:]
        mine_ref[...] = jnp.where(upper, second, first)
        other = jnp.where(upper, first, second)
        for k, other_ref in enumerate(other_refs):
            other_ref[...] = other[:, k * PART : (k + 1) * PART]

    mine, *others = order.call(
        kernel,
        (*[value for value, _ in lefts], *rights, *gains),
        scalars=(grid.bits,),
        grid=(width // step,),
        in_specs=[
            *[pl.BlockSpec((size, step), lambda i, b, at=at: (at, i)) for _, at in lefts],
            *[once((size, cols), lambda i, b: (0, 0))] * pairs,
            *[pl.BlockSpec((1, step), lambda i, b: (0, i))] * len(gains),
        ],
        out_specs=[
            pl.BlockSpec((step, half), lambda i, b: (i, 0)),
            *[pl.BlockSpec((step, PART), lambda i, b: (i, 0))] * parts,
        ],
        out_shape=[
            jax.ShapeDtypeStruct((width, half), BF16),
            *[jax.ShapeDtypeStruct((width, PART), BF16)] * parts,
        ],
        mib=16,
        name="weight_halves",
    )
    lead = (2,) * len(grid.axes) + (grid.block,)
    mine = mine.reshape(lead + (half,))
    chains = []
    for k, other in enumerate(others):
        came = grid.swap(other, "c").reshape(lead + (PART,))
        held = [(mine, grid.axes, k * PART, (k + 1) * PART), (came, grid.axes, 0, PART)]
        chains.append(Chain(grid.axes, held))
    return chains


def weight_rows(order, grid, lefts, rights, gain_grad, spare):
    step = 256
    pairs = len(rights)
    size, cols = rights[0].shape
    width = lefts[0][0].shape[1]
    place = grid.place("c")
    block = grid.block

    def kernel(bits_ref, *refs):
        mine_ref, other_ref = refs[-2:]
        upper = bits_ref[place] == 1
        total = None
        for l_ref, r_ref in zip(refs[:pairs], refs[pairs : 2 * pairs]):
            part = dot(l_ref[...], r_ref[...], TN)
            total = part if total is None else total + part
        column = jnp.broadcast_to(refs[2 * pairs][...], (8, step)).T[:, 0:1]
        coarse = column.astype(BF16).astype(F32)
        lane = lax.broadcasted_iota(jnp.int32, (step, cols), 1)
        total = jnp.where(lane == spare, coarse, total)
        total = jnp.where(lane == spare + 1, column - coarse, total)
        parts = total.reshape(step // (2 * block), 2, block, cols)
        first, second = parts[:, 0], parts[:, 1]
        flat = (step // 2, cols)
        mine_ref[...] = jnp.where(upper, second, first).reshape(flat).astype(BF16)
        other_ref[...] = jnp.where(upper, first, second).reshape(flat).astype(BF16)

    out = pl.BlockSpec((step // 2, cols), lambda i, b: (i, 0))
    mine, other = order.call(
        kernel,
        (*[value for value, _ in lefts], *rights, gain_grad),
        scalars=(grid.bits,),
        grid=(width // step,),
        in_specs=[
            *[pl.BlockSpec((size, step), lambda i, b, at=at: (at, i)) for _, at in lefts],
            *[once((size, cols), lambda i, b: (0, 0))] * pairs,
            pl.BlockSpec((1, step), lambda i, b: (0, i)),
        ],
        out_specs=[out, out],
        out_shape=[jax.ShapeDtypeStruct((width // 2, cols), BF16)] * 2,
        mib=16,
        name="weight_rows",
    )
    axes = grid.axes[:-1]
    shape = (2,) * len(axes) + (block, cols)
    came = grid.swap(other.reshape(shape), "c")
    return Chain(axes, [(mine.reshape(shape), axes, 0, cols), (came, axes, 0, cols)])


def settle(order, grid, chains, widths, mib):
    args, specs, ranges = [], [], []
    for chain in chains:
        specs += fold_specs(grid, chain, None)
        args += [value for value, _, _, _ in chain.pieces]
        ranges.append([(lo, hi) for _, _, lo, hi in chain.pieces])

    def kernel(bits_ref, *refs):
        inputs, outputs = iter(refs[: len(args)]), iter(refs[len(args) :])
        for pieces, width in zip(ranges, widths):
            total = functools.reduce(
                jnp.add, [next(inputs)[..., lo:hi].astype(F32) for lo, hi in pieces]
            )
            next(outputs)[...] = total[:, :width]
            column = total[:, width : width + 1] + total[:, width + 1 : width + 2]
            next(outputs)[...] = jnp.broadcast_to(column, (column.shape[0], TILE)).T[0:1, :]

    shapes = []
    for width in widths:
        shapes += [(grid.block, width), (1, grid.block)]
    return order.call(
        kernel,
        args,
        scalars=(grid.bits,),
        grid=(1,),
        in_specs=specs,
        out_specs=[pl.BlockSpec(shape, lambda i, b: (0, 0)) for shape in shapes],
        out_shape=[jax.ShapeDtypeStruct(shape, F32) for shape in shapes],
        mib=mib,
        name="settle",
    )


def conclude(order, grid, groups, widths, gains, mib, after=()):
    args, specs, ranges = [], [], []
    for group in groups:
        parts = []
        for chain in group:
            specs += fold_specs(grid, chain, None)
            args += [value for value, _, _, _ in chain.pieces]
            parts.append([(lo, hi) for _, _, lo, hi in chain.pieces])
        ranges.append(parts)
    place = grid.place("c")

    def kernel(bits_ref, *refs):
        inputs, outputs = iter(refs[: len(args)]), iter(refs[len(args) :])
        for parts, width, gained in zip(ranges, widths, gains):
            owns, lasts = [], []
            for pieces in parts:
                values = [next(inputs)[..., lo:hi].astype(F32) for lo, hi in pieces]
                owns.append(functools.reduce(jnp.add, values[:-1]))
                lasts.append(values[-1])
            own = owns[0] if len(owns) == 1 else jnp.concatenate(owns, axis=1)
            last = lasts[0] if len(lasts) == 1 else jnp.concatenate(lasts, axis=1)
            cols = own.shape[-1]
            out = next(outputs)
            gain = next(outputs) if gained else None

            def put(first, second):
                out[:, :cols] = first
                out[:, cols:] = second[:, : width - cols]
                if gain is not None:
                    at = width - cols
                    column = second[:, at : at + 1] + second[:, at + 1 : at + 2]
                    gain[...] = jnp.broadcast_to(column, (column.shape[0], TILE)).T[0:1, :]

            @pl.when(bits_ref[place] == 0)
            def _():
                put(own, last)

            @pl.when(bits_ref[place] == 1)
            def _():
                put(last, own)

    shapes = []
    for width, gained in zip(widths, gains):
        shapes.append((grid.block, width))
        if gained:
            shapes.append((1, grid.block))
    return order.call(
        kernel,
        args,
        scalars=(grid.bits,),
        grid=(1,),
        in_specs=specs,
        out_specs=[pl.BlockSpec(shape, lambda i, b: (0, 0)) for shape in shapes],
        out_shape=[jax.ShapeDtypeStruct(shape, F32) for shape in shapes],
        mib=mib,
        name="conclude",
        after=after,
    )


def finish_kernel(
    k0_ref, r0_ref, x0_ref, gq_ref, wq_ref, wkv_ref, x_ref, gain_ref, gr_ref, cos_ref, sin_ref,
    came_ref, gkv_ref, out_ref, gain_grad_ref,
):
    total = k0_ref[...].astype(F32) + r0_ref[...].astype(F32) + x0_ref[...].astype(F32)
    cos, sin = cos_ref[0], sin_ref[0]
    half = HEAD_DIM // 2
    split = RANK_KV * HEADS
    turned = total.T
    pieces = [turned[:split]]
    for r in range(RANK_KV):
        at = split + r * HEAD_DIM
        first, second = turned[at : at + half], turned[at + half : at + HEAD_DIM]
        pieces += [first * cos + second * sin, second * cos - first * sin]
    pieces.append(turned[split + RANK_KV * HEAD_DIM :])
    gkv = jnp.concatenate(pieces, axis=0).T.astype(BF16)
    gkv_ref[:, :KV_COLS] = gkv
    gkv_ref[:, KV_COLS:] = jnp.zeros((gkv.shape[0], KV_PAD - KV_COLS), BF16)
    grad = dot(gq_ref[:, :Q_COLS], wq_ref[...]) + dot(gkv, wkv_ref[...])
    values = x_ref[...].astype(F32)
    scale = lax.rsqrt(jnp.mean(values * values, axis=-1, keepdims=True) + EPS)
    weighted = grad * gain_ref[...]
    back = scale * weighted - values * (scale * scale * scale) * jnp.mean(
        weighted * values, axis=-1, keepdims=True
    )
    out_ref[...] = (gr_ref[...] + back).astype(BF16)

    @pl.when(pl.program_id(0) == 0)
    def _():
        gain_grad_ref[...] = came_ref[...]

    gain_grad_ref[...] += jnp.sum(grad * values * scale, axis=0, keepdims=True)


def finish(order, row, kept, near, far, gq, w_query, w_keyval, x, gain, grad_resid, cos, sin, came, held):
    tokens, width = x.shape
    span = cos.shape[-1]
    full = lambda i: (0, 0)
    tile = pl.BlockSpec((span, width), lambda i: (2 * row + i, 0))
    part = pl.BlockSpec((None, span, KV_COLS), lambda i: (0, i, 0))
    rope = pl.BlockSpec((1, HEAD_DIM // 2, span), lambda i: (i, 0, 0))
    vector = pl.BlockSpec((1, width), full)
    extra = () if held is None else (held,)

    def kernel(*refs):
        finish_kernel(*refs[:12], *refs[12 + len(extra) :])

    return order.call(
        kernel,
        (kept, near, far, gq, w_query, w_keyval, x, gain, grad_resid, cos, sin, came, *extra),
        grid=(2,),
        in_specs=[
            part,
            part,
            pl.BlockSpec((span, KV_COLS), lambda i: (i, 0)),
            pl.BlockSpec((span, Q_PAD), lambda i: (i, 0)),
            once((Q_COLS, width), full),
            once((KV_COLS, width), full),
            tile,
            vector,
            tile,
            rope,
            rope,
            vector,
            *[pl.BlockSpec(memory_space=pl.ANY)] * len(extra),
        ],
        out_specs=[pl.BlockSpec((span, KV_PAD), lambda i: (i, 0)), tile, vector],
        out_shape=[
            jax.ShapeDtypeStruct((2 * span, KV_PAD), BF16),
            jax.ShapeDtypeStruct((tokens, width), BF16),
            jax.ShapeDtypeStruct((1, width), F32),
        ],
        mib=20,
        name="finish",
        aliases={12: 1} if extra else None,
    )


def meet_kernel(near_ref, far_ref, out_ref):
    out_ref[...] = (near_ref[...].astype(F32) + far_ref[...].astype(F32)).astype(BF16)


def meet(order, near, far):
    shape = near.shape[1:]
    part = pl.BlockSpec((None, *shape), lambda i: (1, 0, 0))
    return order.call(
        meet_kernel,
        (near, far),
        grid=(1,),
        in_specs=[part, part],
        out_specs=[pl.BlockSpec(shape, lambda i: (0, 0))],
        out_shape=[jax.ShapeDtypeStruct(shape, BF16)],
        mib=8,
        name="meet",
    )[0]


def body(
    layer_input,
    doc_ids,
    norm1_gain,
    w_query,
    w_keyval,
    w_out,
    norm2_gain,
    w_gate,
    w_up,
    w_down,
    cotangent,
):
    row_count, local_len, width = layer_input.shape
    seq_size = lax.axis_size("seq")
    rows_size = lax.axis_size("rows")
    seq_id = lax.axis_index("seq")
    rows_id = lax.axis_index("rows")
    span = local_len // 2
    tokens = row_count * local_len
    length = local_len * seq_size
    core = seq_id % 2
    order = Order()
    grid = Grid(rows_size, seq_size, rows_id, seq_id, width)
    seq_arg = seq_id.astype(jnp.int32).reshape(1)

    x = layer_input.reshape(tokens, width)
    cot = cotangent.reshape(tokens, width)
    cot_other = grid.swap(cot, "c")
    gain1 = norm1_gain.reshape(1, width)
    gain2 = norm2_gain.reshape(1, width)
    wq_t, wkv_t = w_query.T, w_keyval.T
    docs = doc_ids.reshape(row_count, 1, length)

    spans = jnp.stack([seq_id, 2 * seq_size - 1 - seq_id])
    positions = spans[:, None] * span + jnp.arange(span, dtype=jnp.int32)[None, :]
    inv_freq = ROPE_BASE ** (-(jnp.arange(HEAD_DIM // 2, dtype=F32) * (2.0 / HEAD_DIM)))
    angles = positions.astype(F32)[:, None, :] * inv_freq[None, :, None]
    cos, sin = jnp.cos(angles), jnp.sin(angles)

    normed, qf, kv = project(order, x, gain1, wq_t, wkv_t, cos, sin)
    kv = kv.reshape(row_count, local_len, KV_COLS)
    kv_x = grid.swap(kv, "x")
    kv_core = grid.swap(kv, "c")
    half = w_gate.shape[1] // 2
    wg = lax.dynamic_slice_in_dim(w_gate, core * half, half, 1)
    wu = lax.dynamic_slice_in_dim(w_up, core * half, half, 1)
    wd = lax.dynamic_slice_in_dim(w_down, core * half, half, 0)
    gh_own, gh_oth = hidden_back(order, cot, cot_other, wd, (wg, wu))
    kv_x, _ = lax.optimization_barrier((kv_x, order.token))
    kv_both = grid.swap(kv_x, "c")
    sources = (kv, kv_core, kv_x, kv_both)
    attended, lse = attend(order, seq_arg, qf, sources, docs)
    resid, normed2 = out_project(order, x, attended, w_out, gain2)
    normed2_other = grid.swap(normed2, "c")
    h_own, gg_own, gu_own, gn2_own = feed_forward(order, normed2, gh_own, wg, wu, BF16)
    h_oth, gg_oth, gu_oth, gn2_send = feed_forward(order, normed2_other, gh_oth, wg, wu, BF16)
    gn2_came = grid.swap(gn2_send, "c")

    first, second = grid.high[-1], grid.high[:-1]
    down, _ = weight_grad(
        order, grid, "x", (stay(cot), stay(cot_other)), (stay(h_own), stay(h_oth))
    )
    gate, _ = weight_grad(order, grid, "y", (normed2, normed2_other), (gg_own, gg_oth))
    up, _ = weight_grad(order, grid, first, (normed2, normed2_other), (gu_own, gu_oth))
    grad_resid, branch, grad_att, grad_norm2 = out_back(
        order, cot, gn2_own, gn2_came, resid, w_out, gain2
    )
    out = weight_halves(order, grid, [(branch, 0)], [attended])
    grad_att = grad_att.reshape(row_count, local_len, width)

    def back(row, after=()):
        gq, near, far = attend_back(
            order, row, seq_arg, qf, sources, docs, lse, attended, grad_att, cos, sin, after
        )
        return gq, near, grid.swap(far, "c")

    def end(row, near, far, came, gq, gain, held):
        return finish(
            order, row, near, far, came, gq, wq_t, wkv_t, x, gain1, grad_resid, cos, sin, gain, held
        )

    gq0, near0, far0 = back(0)
    fold(order, grid, [([down], "y"), ([gate], "x"), (out, first)])
    came0 = grid.swap(meet(order, near0, far0), "x")
    gq1, near1, far1 = back(1)
    upper = [up, *out]
    fold(order, grid, [(upper, "y")], after=(came0,))
    fold(order, grid, [([down, gate], first)])
    came1 = grid.swap(meet(order, near1, far1), "x")
    gkv0, ig0, gain0 = end(0, near0, far0, came0, gq0, jnp.zeros((1, width), F32), None)
    query = weight_rows(
        order, grid, [(normed, 0), (normed, 1)], [gq0, gq1], grad_norm2, Q_COLS
    )
    down_send = down_project(order, h_oth, wd)
    down_came = grid.swap(down_send, "c")
    gkv1, input_grad, grad_norm1 = end(1, near1, far1, came1, gq1, gain0, ig0)
    keyval = weight_rows(
        order, grid, [(normed, 0), (normed, 1)], [gkv0, gkv1], grad_norm1, KV_COLS
    )
    fold(order, grid, [([down, gate], second[0])])
    fold(order, grid, [([keyval], "x"), ([query], "y")])
    fold(order, grid, [(upper, "x")])
    for axis in second[1:]:
        fold(order, grid, [([down, gate], axis)])
    fold(order, grid, [([keyval], "y"), ([query], "x")])
    fold(order, grid, [(upper, second[0])])
    for axis in second[1:]:
        fold(order, grid, [(upper, axis)])
    late = [keyval, query]
    fold(order, grid, [(late, first)])
    for axis in second:
        fold(order, grid, [(late, axis)])
    fold(order, grid, [([down, gate, *upper], "c")])
    layer_output = down_project(order, h_own, wd, resid, down_came)
    g_query, g_norm2, g_keyval, g_norm1 = settle(
        order, grid, [query, keyval], [Q_COLS, KV_COLS], 8
    )
    g_down, g_gate, g_up, g_out = conclude(
        order,
        grid,
        [[down], [gate], [up], out],
        [*[w.shape[1] for w in (w_gate, w_gate, w_up)], width],
        [False] * 4,
        24,
    )
    return (
        layer_output.reshape(row_count, local_len, width),
        input_grad.reshape(row_count, local_len, width),
        g_norm1.reshape(-1),
        g_query,
        g_keyval,
        g_out.T,
        g_norm2.reshape(-1),
        g_gate,
        g_up,
        g_down.T,
    )


def solution(mesh):
    return jax.shard_map(
        body,
        mesh=mesh,
        in_specs=(
            P("rows", "seq", None),
            P("rows", None),
            P(),
            P(),
            P(),
            P(),
            P(),
            P(),
            P(),
            P(),
            P("rows", "seq", None),
        ),
        out_specs=(
            P("rows", "seq", None),
            P("rows", "seq", None),
            P(("rows", "seq")),
            P(("rows", "seq"), None),
            P(("rows", "seq"), None),
            P(None, ("rows", "seq")),
            P(("rows", "seq")),
            P(("rows", "seq"), None),
            P(("rows", "seq"), None),
            P(None, ("rows", "seq")),
        ),
        check_vma=False,
    )
```

```python
import functools

import jax
import jax.numpy as jnp
from jax import lax
from jax.experimental import pallas as pl
from jax.experimental.pallas import tpu as pltpu
from jax.sharding import PartitionSpec as P

HEADS = 16
HEAD_DIM = 64
RANK_Q = 6
RANK_KV = 2
Q_COLS = RANK_Q * (HEADS + HEAD_DIM)
KV_COLS = 2 * RANK_KV * (HEADS + HEAD_DIM)
Q_PAD = 512
KV_PAD = 384
EPS = 1e-06
ROPE_BASE = 10000.0
MASKED = -1e30
SCORE_SCALE = HEAD_DIM ** (-0.5)
VALUE_BASE = RANK_KV * (HEADS + HEAD_DIM)
TILE = 128
TILES = 9
F32 = jnp.float32
BF16 = jnp.bfloat16
NT = (((1,), (1,)), ((), ()))
TN = (((0,), (0,)), ((), ()))


def dot(left, right, dims=None):
    if dims is None:
        return jnp.dot(left, right, preferred_element_type=F32)
    return lax.dot_general(left, right, dims, preferred_element_type=F32)


def params(mib):
    return pltpu.CompilerParams(vmem_limit_bytes=mib * 2**20)


def cost(flops, nbytes, trans=0):
    return pl.CostEstimate(flops=flops, bytes_accessed=nbytes, transcendentals=trans)


def once(shape, index):
    return pl.BlockSpec(shape, index, pipeline_mode=pl.Buffered(1))


class Order:
    def __init__(self):
        self.token = None

    def call(self, kernel, args, *, grid, in_specs, out_specs, out_shape, mib, name, scalars=(), scratch=(), after=(), work=0, aliases=None):
        extra = [a for a in (self.token, *after) if a is not None]
        n_scalar, n_in, n_out = len(scalars), len(in_specs), len(out_specs)

        def run(*refs):
            head = refs[: n_scalar + n_in]
            rest = refs[n_scalar + n_in + len(extra) :]
            rest[n_out][...] = jnp.zeros_like(rest[n_out])
            kernel(*head, *rest[:n_out], *rest[n_out + 1 :])

        def spec(block, index, **kw):
            return pl.BlockSpec(block, index, **kw)

        token_spec = pl.BlockSpec((8, TILE), lambda *_: (0, 0))
        out = pl.pallas_call(
            run,
            grid_spec=pltpu.PrefetchScalarGridSpec(
                num_scalar_prefetch=n_scalar,
                grid=grid,
                in_specs=[*in_specs, *[pl.BlockSpec(memory_space=pl.ANY)] * len(extra)],
                out_specs=[*out_specs, token_spec],
                scratch_shapes=list(scratch),
            ),
            out_shape=[*out_shape, jax.ShapeDtypeStruct((8, TILE), F32)],
            compiler_params=params(mib),
            input_output_aliases={n_scalar + k: v for k, v in (aliases or {}).items()},
            cost_estimate=cost(work, 2**16),
            name=name,
        )(*scalars, *args, *extra)
        self.token = out[-1]
        return out[:-1]


def stay(value):
    return pltpu.with_memory_space_constraint(value, pltpu.HBM)


def aligned(value, factor):
    return pl.multiple_of(value, factor)


def project_kernel(x_ref, gain_ref, wq_ref, wkv_ref, cos_ref, sin_ref, normed_ref, qf_ref, kv_ref):
    x = x_ref[...].astype(F32)
    scale = lax.rsqrt(jnp.mean(x * x, axis=-1, keepdims=True) + EPS)
    normed = (x * scale * gain_ref[...]).astype(BF16)
    normed_ref[...] = normed
    kvf = dot(normed, wkv_ref[...], NT)
    qf = dot(normed, wq_ref[...], NT)
    half = HEAD_DIM // 2
    span = cos_ref.shape[-1]
    for s in range(2):
        cos, sin = cos_ref[s], sin_ref[s]
        rows = slice(s * span, (s + 1) * span)
        kvt = kvf[rows].T
        split = RANK_KV * HEADS
        pieces = [kvt[:split]]
        for r in range(RANK_KV):
            at = split + r * HEAD_DIM
            first, second = kvt[at : at + half], kvt[at + half : at + HEAD_DIM]
            pieces += [first * cos - second * sin, second * cos + first * sin]
        pieces.append(kvt[split + RANK_KV * HEAD_DIM :])
        kv_ref[rows, :] = jnp.concatenate(pieces, axis=0).T.astype(BF16)
        qt = qf[rows].T
        split = RANK_Q * HEADS
        qf_ref[s, :split, :] = qt[:split]
        for r in range(RANK_Q):
            at = split + r * HEAD_DIM
            first, second = qt[at : at + half], qt[at + half : at + HEAD_DIM]
            qf_ref[s, at : at + half, :] = first * cos - second * sin
            qf_ref[s, at + half : at + HEAD_DIM, :] = second * cos + first * sin


def project(order, x, gain, w_query, w_keyval, cos, sin):
    tokens, width = x.shape
    span = cos.shape[-1]
    groups = tokens // span
    full = lambda i: (0, 0)
    rope = pl.BlockSpec((2, HEAD_DIM // 2, span), lambda i: (0, 0, 0))
    return order.call(
        project_kernel,
        (x, gain, w_query, w_keyval, cos, sin),
        grid=(groups // 2,),
        in_specs=[
            pl.BlockSpec((2 * span, width), lambda i: (i, 0)),
            pl.BlockSpec((1, width), full),
            once((Q_COLS, width), full),
            once((KV_COLS, width), full),
            rope,
            rope,
        ],
        out_specs=[
            pl.BlockSpec((2 * span, width), lambda i: (i, 0)),
            pl.BlockSpec((2, Q_COLS, span), lambda i: (i, 0, 0)),
            pl.BlockSpec((2 * span, KV_COLS), lambda i: (i, 0)),
        ],
        out_shape=[
            jax.ShapeDtypeStruct((tokens, width), BF16),
            jax.ShapeDtypeStruct((groups, Q_COLS, span), F32),
            jax.ShapeDtypeStruct((tokens, KV_COLS), BF16),
        ],
        mib=56,
        name="project",
    )


PIECES = ((0, 2), (2, 3), (3, 4), (4, 5), (5, 7), (7, 9))


def tile_place(tile, seq_id):
    low = tile < seq_id + 2
    return low, jnp.where(low, tile, tile + 1 - seq_id)


def piece_side(piece, seq_id):
    first, last = piece
    low = first < seq_id + 2
    side = 0 if last <= 2 else (1 if first > 4 else jnp.where(low, 0, 1))
    return slice(first * TILE, last * TILE), side, low


def choose(side, low, pair):
    return pair[side] if isinstance(side, int) else jnp.where(low, pair[0], pair[1])


def gather(totals, side, low, part, combine, empty):
    for s in range(2):
        if isinstance(side, int):
            if side != s:
                continue
            term = part
        else:
            term = jnp.where(low if s == 0 else ~low, part, empty)
        totals[s] = term if totals[s] is None else combine(totals[s], term)


def gather_keys(seq_id, sources, qf_ref, qa, qb, kvpos, kvt, kva, bias, docs_ref, row, span):
    for which, source in enumerate(sources):
        holder = seq_id ^ which
        kvpos[pl.ds(aligned(holder * span, 32), span), :] = source[0, :span, :]
        kvpos[pl.ds(aligned((7 - holder) * span, 32), span), :] = source[0, span:, :]
    columns = []
    for number in (seq_id, 7 - seq_id):
        ids = None
        for place in range(8):
            part = docs_ref[row : row + 1, place * span : (place + 1) * span]
            ids = part if ids is None else jnp.where(number == place, part, ids)
        columns.append(jnp.broadcast_to(ids.astype(F32), (8, span)).T[:, 0:1].astype(jnp.int32))
    for tile in range(TILES):
        low, place = tile_place(tile, seq_id)
        start = aligned(place * TILE, TILE)
        cols = slice(tile * TILE, (tile + 1) * TILE)
        kvt[:, cols] = kvpos[pl.ds(start, TILE), :].astype(F32).T
        side = 0 if tile < 2 else (1 if tile > 4 else None)
        doc_q = jnp.where(low, columns[0], columns[1]) if side is None else columns[side]
        number = jnp.where(low, seq_id, 7 - seq_id)
        pos_q = number * span + lax.broadcasted_iota(jnp.int32, (span, TILE), 0)
        pos_k = start + lax.broadcasted_iota(jnp.int32, (span, TILE), 1)
        allowed = (doc_q == docs_ref[row : row + 1, pl.ds(start, TILE)]) & (pos_k <= pos_q)
        bias[:, cols] = jnp.where(allowed, 0.0, MASKED)
    split = RANK_KV * HEADS
    kva[:split, 0, :] = kvt[:split, :] * (1.0 / RANK_KV)
    kva[split:, 0, :] = kvt[VALUE_BASE : VALUE_BASE + split, :] * (1.0 / RANK_KV)
    both = jnp.concatenate([qf_ref[0], qf_ref[1]], axis=1)
    split = RANK_Q * HEADS
    qa[:, 0, :] = both[:split] * (1.0 / RANK_Q)
    qb[...] = both[split:]


def expand_queries(qf_ref, qa, s, head):
    split = RANK_Q * HEADS
    total = None
    for r in range(RANK_Q):
        weight = qa[s, r * HEADS + head]
        term = weight * qf_ref[s, split + r * HEAD_DIM : split + (r + 1) * HEAD_DIM, :]
        total = term if total is None else total + term
    return total.astype(BF16) * BF16(SCORE_SCALE)


def expand_pair(kvt, kva, base, head):
    split = RANK_KV * HEADS
    total = None
    for r in range(RANK_KV):
        at = base + split + r * HEAD_DIM
        weight = kva[(base // VALUE_BASE) * split + r * HEADS + head]
        term = weight * kvt[at : at + HEAD_DIM, :]
        total = term if total is None else total + term
    return total.astype(BF16)


def weave(*streams):
    streams = list(streams)
    while streams:
        for stream in list(streams):
            try:
                next(stream)
            except StopIteration:
                streams.remove(stream)


SEEN = ((0, 5), (3, 10))


def place_keys(seq_id, sources, kvpos, span):
    for which, source in enumerate(sources):
        holder = seq_id ^ which
        kvpos[pl.ds(aligned(holder * span, 32), span), :] = source[0, :span, :]
        kvpos[pl.ds(aligned((7 - holder) * span, 32), span), :] = source[0, span:, :]


def query_docs(number, docs_ref, row, span):
    ids = None
    for place in range(8):
        part = docs_ref[row : row + 1, place * span : (place + 1) * span]
        ids = part if ids is None else jnp.where(number == place, part, ids)
    return jnp.broadcast_to(ids.astype(F32), (8, span)).T[:, 0:1].astype(jnp.int32)


def attend_kernel(
    row, seq_ref, qf_ref, kv0, kv1, kv2, kv3, doc_ref, out_ref, lse_ref,
    kvpos, kvt, bias_low, bias_high, kva, qa, heads_out, heads_lse,
    low_a, low_b, high_a, high_b, top_a, top_b,
):
    seq_id = seq_ref[0]
    span = qf_ref.shape[-1]
    biases = (bias_low, bias_high)
    place_keys(seq_id, (kv0, kv1, kv2, kv3), kvpos, span)
    length = kvpos.shape[0]
    for at in range(0, length, TILE):
        kvt[:, at : at + TILE] = kvpos[at : at + TILE, :].astype(F32).T
    for s, number in enumerate((seq_id, 7 - seq_id)):
        doc_q = query_docs(number, doc_ref, row, span)
        pos_q = number * span + lax.broadcasted_iota(jnp.int32, (span, TILE), 0)
        for tile in range(*SEEN[s]):
            start = tile * TILE
            pos_k = start + lax.broadcasted_iota(jnp.int32, (span, TILE), 1)
            allowed = (doc_q == doc_ref[row : row + 1, start : start + TILE]) & (pos_k <= pos_q)
            at = start - SEEN[s][0] * TILE
            biases[s][:, at : at + TILE] = jnp.where(allowed, 0.0, MASKED)
    split = RANK_KV * HEADS
    kva[:split, 0, :] = kvt[:split, :] * (1.0 / RANK_KV)
    kva[split:, 0, :] = kvt[VALUE_BASE : VALUE_BASE + split, :] * (1.0 / RANK_KV)
    for s in range(2):
        qa[s, :, 0, :] = qf_ref[s, : RANK_Q * HEADS, :] * (1.0 / RANK_Q)

    def expand(base, head):
        total = None
        for r in range(RANK_KV):
            at = base + split + r * HEAD_DIM
            weight = kva[(base // VALUE_BASE) * split + r * HEADS + head]
            term = weight * kvt[at : at + HEAD_DIM, :]
            total = term if total is None else total + term
        return total.astype(BF16)

    def pieces(s):
        count = SEEN[s][1] - SEEN[s][0]
        edges = [*range(0, count, 2), count]
        shift = SEEN[s][0] * TILE
        for lo, hi in zip(edges, edges[1:]):
            yield slice(lo * TILE, hi * TILE), slice(shift + lo * TILE, shift + hi * TILE)

    def scores_of(head, scores, top):
        keys = expand(0, head)
        yield
        for s in range(2):
            queries = expand_queries(qf_ref, qa, s, head).T
            best = None
            for cols, places in pieces(s):
                part = dot(queries, keys[:, places]) + biases[s][:, cols]
                scores[s][:, cols] = part
                for at in range(0, part.shape[1], TILE):
                    tile = part[:, at : at + TILE]
                    best = tile if best is None else jnp.maximum(best, tile)
                yield
            top[s] = jnp.max(best, axis=-1, keepdims=True)

    def weigh(head, scores, top):
        values = expand(VALUE_BASE, head)
        values = jnp.concatenate([values, jnp.ones((16, values.shape[1]), BF16)], axis=0)
        yield
        for s in range(2):
            peak = top[s]
            out = None
            for cols, places in pieces(s):
                raised = jnp.exp(scores[s][:, cols] - peak).astype(BF16)
                part = dot(raised, values[:, places], NT)
                out = part if out is None else out + part
                yield
            total = out[:, HEAD_DIM : HEAD_DIM + 1]
            heads_out[s, head] = (out[:, :HEAD_DIM] * (1.0 / total)).astype(BF16)
            heads_lse[s, head] = peak + jnp.log(total)

    scores_a, scores_b = (low_a, high_a), (low_b, high_b)

    def pair_step(pair, carry):
        head = 2 * pair
        weave(scores_of(head + 1, scores_b, top_b), weigh(head, scores_a, top_a))
        following = jnp.minimum(head + 2, HEADS - 1)
        weave(scores_of(following, scores_a, top_a), weigh(head + 1, scores_b, top_b))
        return carry

    weave(scores_of(0, scores_a, top_a))
    lax.fori_loop(0, HEADS // 2, pair_step, 0)
    lane = lax.broadcasted_iota(jnp.int32, (span, TILE), 1)
    for s in range(2):
        out_ref[s * span : (s + 1) * span, :] = jnp.concatenate(
            [heads_out[s, head] for head in range(HEADS)], axis=1
        )
        lse = jnp.zeros((span, TILE), F32)
        for head in range(HEADS):
            lse = jnp.where(lane == head, heads_lse[s, head], lse)
        lse_ref[s] = lse


def attention_specs(span, docs, row=None):
    at = lambda i: i if row is None else row
    kv_spec = pl.BlockSpec((1, 2 * span, KV_COLS), lambda i, s: (at(i), 0, 0))
    return [
        pl.BlockSpec((2, Q_COLS, span), lambda i, s: (at(i), 0, 0)),
        kv_spec,
        kv_spec,
        kv_spec,
        kv_spec,
        pl.BlockSpec((None, 1, docs.shape[-1]), lambda i, s: (at(i), 0, 0)),
    ]


def attend(order, seq_id, qf, sources, docs):
    rows, _, length = docs.shape
    span = qf.shape[-1]
    width = HEADS * HEAD_DIM
    return order.call(
        functools.partial(attend_kernel, 0),
        (qf, *sources, docs),
        scalars=(seq_id,),
        grid=(rows,),
        in_specs=attention_specs(span, docs),
        out_specs=[
            pl.BlockSpec((2 * span, width), lambda i, s: (i, 0)),
            pl.BlockSpec((2, span, TILE), lambda i, s: (i, 0, 0)),
        ],
        scratch=[
            pltpu.VMEM((length, KV_COLS), BF16),
            pltpu.VMEM((KV_COLS, length), F32),
            pltpu.VMEM((span, 5 * TILE), F32),
            pltpu.VMEM((span, 7 * TILE), F32),
            pltpu.VMEM((2 * RANK_KV * HEADS, 1, length), F32),
            pltpu.VMEM((2, RANK_Q * HEADS, 1, span), F32),
            pltpu.VMEM((2, HEADS, span, HEAD_DIM), BF16),
            pltpu.VMEM((2, HEADS, span, 1), F32),
            pltpu.VMEM((span, 5 * TILE), F32),
            pltpu.VMEM((span, 5 * TILE), F32),
            pltpu.VMEM((span, 7 * TILE), F32),
            pltpu.VMEM((span, 7 * TILE), F32),
            pltpu.VMEM((2, span, 1), F32),
            pltpu.VMEM((2, span, 1), F32),
        ],
        out_shape=[
            jax.ShapeDtypeStruct((rows * 2 * span, width), BF16),
            jax.ShapeDtypeStruct((rows * 2, span, TILE), F32),
        ],
        mib=24,
        name="attend",
    )


def attend_back_kernel(
    row, seq_ref, qf_ref, kv0, kv1, kv2, kv3, doc_ref, lse_ref, att_ref, grad_ref,
    cos_ref, sin_ref, gq_ref, near_ref, far_ref,
    kvpos, kvt, bias, dot_t, stats, gkvt, gkvpos, gqt, gka, gqa, kva, qa,
    probs_a, probs_b, grads_a, grads_b, q_a, q_b, k_a, k_b, qb,
):
    seq_id = seq_ref[0]
    span = qf_ref.shape[-1]
    gather_keys(seq_id, (kv0, kv1, kv2, kv3), qf_ref, qa, qb, kvpos, kvt, kva, bias, doc_ref, row, span)
    width = HEADS * HEAD_DIM
    chooser = (
        lax.broadcasted_iota(jnp.int32, (width, TILE), 0) // HEAD_DIM
        == lax.broadcasted_iota(jnp.int32, (width, TILE), 1)
    ).astype(BF16)
    grad = grad_ref[0]
    dot_t[...] = grad.T
    product = grad.astype(F32) * att_ref[...].astype(F32)
    coarse = product.astype(BF16)
    fine = (product - coarse.astype(F32)).astype(BF16)
    centre = dot(coarse, chooser) + dot(fine, chooser)
    totals = jnp.concatenate([lse_ref[0], lse_ref[1]], axis=0)
    stats[0, :, 0, :] = -totals.T[:HEADS, :]
    stats[1, :, 0, :] = -centre.T[:HEADS, :]
    gkvt[...] = jnp.zeros_like(gkvt)
    gqt[...] = jnp.zeros_like(gqt)

    pieces = [piece_side(piece, seq_id) for piece in PIECES]
    split = RANK_KV * HEADS

    extra = lax.broadcasted_iota(jnp.int32, (16, 2 * span), 0)
    ones = jnp.ones((16, TILES * TILE), BF16)

    def with_row(value, row):
        coarse = row.astype(BF16).astype(F32)
        middle = (row - coarse).astype(BF16).astype(F32)
        fine = row - coarse - middle
        rest = jnp.where(extra == 0, coarse, jnp.where(extra == 1, middle, fine))
        return jnp.concatenate([value, jnp.where(extra < 3, rest, 0.0).astype(BF16)], axis=0)

    def scores_of(head, hold):
        probs_of, grads_of, q_of, k_of = hold
        rows = pl.ds(aligned(head * HEAD_DIM, HEAD_DIM), HEAD_DIM)
        keys = expand_pair(kvt, kva, 0, head)
        k_of[...] = keys
        keys = jnp.concatenate([keys, ones], axis=0)
        values = jnp.concatenate([expand_pair(kvt, kva, VALUE_BASE, head), ones], axis=0)
        yield
        total = None
        for r in range(RANK_Q):
            term = qa[r * HEADS + head] * qb[r * HEAD_DIM : (r + 1) * HEAD_DIM, :]
            total = term if total is None else total + term
        q_t = total.astype(BF16) * BF16(SCORE_SCALE)
        q_of[...] = q_t
        turned = with_row(q_t, stats[0, head]).T
        queries = [turned[:span], turned[span:]]
        turned = with_row(dot_t[rows, :], stats[1, head]).T
        grads = [turned[:span], turned[span:]]
        yield
        for cols, side, low in pieces:
            score = dot(choose(side, low, queries), keys[:, cols]) + bias[:, cols]
            probs = jnp.exp(score)
            grad_p = dot(choose(side, low, grads), values[:, cols])
            probs_of[:, cols] = probs.astype(BF16)
            grads_of[:, cols] = (probs * grad_p).astype(BF16)
            yield

    def grads_of_head(head, hold):
        probs_of, grads_of, q_of, k_of = hold
        rows = pl.ds(aligned(head * HEAD_DIM, HEAD_DIM), HEAD_DIM)
        q_t, g_t = q_of[...], dot_t[rows, :]
        q_sides = [q_t[:, :span], q_t[:, span:]]
        g_sides = [g_t[:, :span], g_t[:, span:]]
        yield
        grad_q = [None, None]
        for cols, side, low in pieces:
            grad_s = grads_of[:, cols]
            gather(grad_q, side, low, dot(k_of[:, cols], grad_s, NT), jnp.add, 0.0)
            for base, grad in (
                (0, dot(choose(side, low, q_sides), grad_s)),
                (VALUE_BASE, dot(choose(side, low, g_sides), probs_of[:, cols])),
            ):
                for r in range(RANK_KV):
                    where = base + split + r * HEAD_DIM
                    b_rows = slice(where, where + HEAD_DIM)
                    a_row = (base // VALUE_BASE) * split + r * HEADS + head
                    gka[a_row, :, cols] = jnp.sum(grad * kvt[b_rows, cols], axis=0, keepdims=True)
                    gkvt[b_rows, cols] += grad * kva[a_row, :, cols]
            yield
        both = jnp.concatenate(grad_q, axis=1)
        where = RANK_Q * HEADS
        for r in range(RANK_Q):
            b_rows = slice(r * HEAD_DIM, (r + 1) * HEAD_DIM)
            a_row = r * HEADS + head
            gqa[a_row] = jnp.sum(both * qb[b_rows, :], axis=0, keepdims=True)
            gqt[b_rows, :] += both * qa[a_row]
            if r % 2:
                yield

    def pair_step(pair, carry):
        head = 2 * pair
        weave(scores_of(head + 1, hold_b), grads_of_head(head, hold_a))
        following = jnp.minimum(head + 2, HEADS - 1)
        weave(scores_of(following, hold_a), grads_of_head(head + 1, hold_b))
        return carry

    hold_a, hold_b = (probs_a, grads_a, q_a, k_a), (probs_b, grads_b, q_b, k_b)
    weave(scores_of(0, hold_a))
    lax.fori_loop(0, HEADS // 2, pair_step, 0)
    half = HEAD_DIM // 2
    cos = jnp.concatenate([cos_ref[0], cos_ref[1]], axis=1)
    sin = jnp.concatenate([sin_ref[0], sin_ref[1]], axis=1)
    pieces = [gqa[:, 0, :] * (1.0 / RANK_Q)]
    for r in range(RANK_Q):
        at = r * HEAD_DIM
        first, second = gqt[at : at + half, :], gqt[at + half : at + HEAD_DIM, :]
        pieces += [first * cos + second * sin, second * cos - first * sin]
    back = jnp.concatenate(pieces, axis=0) * SCORE_SCALE
    back = jnp.concatenate([back, jnp.zeros((Q_PAD - Q_COLS, 2 * span), F32)], axis=0)
    gq_ref[...] = back.T.astype(BF16)
    split = RANK_KV * HEADS
    gkvt[:split, :] = gka[:split, 0, :] * (1.0 / RANK_KV)
    gkvt[VALUE_BASE : VALUE_BASE + split, :] = gka[split:, 0, :] * (1.0 / RANK_KV)
    gkvpos[...] = jnp.zeros_like(gkvpos)
    for tile in range(TILES):
        _, place = tile_place(tile, seq_id)
        rows = pl.ds(aligned(place * TILE, TILE), TILE)
        gkvpos[rows, :] += gkvt[:, tile * TILE : (tile + 1) * TILE].T
    for which in range(4):
        holder = seq_id ^ which
        target = near_ref if which in (0, 2) else far_ref
        for s, number in enumerate((holder, 7 - holder)):
            target[which // 2, s * span : (s + 1) * span, :] = gkvpos[
                pl.ds(aligned(number * span, 32), span), :
            ].astype(BF16)


def attend_back(order, row, seq_id, qf, sources, docs, lse, attended, grad_attended, cos, sin, after):
    length = docs.shape[-1]
    span = qf.shape[-1]
    width = HEADS * HEAD_DIM
    wide = pl.BlockSpec((1, 2 * span, width), lambda i, s: (row, 0, 0))
    rope = pl.BlockSpec((2, HEAD_DIM // 2, span), lambda i, s: (0, 0, 0))
    parts = pl.BlockSpec((2, 2 * span, KV_COLS), lambda i, s: (0, 0, 0))
    return order.call(
        functools.partial(attend_back_kernel, 0),
        (qf, *sources, docs, lse, attended, grad_attended, cos, sin),
        scalars=(seq_id,),
        grid=(1,),
        in_specs=attention_specs(span, docs, row)
        + [
            pl.BlockSpec((2, span, TILE), lambda i, s: (row, 0, 0)),
            pl.BlockSpec((2 * span, width), lambda i, s: (row, 0)),
            wide,
            rope,
            rope,
        ],
        out_specs=[pl.BlockSpec((2 * span, Q_PAD), lambda i, s: (0, 0)), parts, parts],
        scratch=[
            pltpu.VMEM((length, KV_COLS), BF16),
            pltpu.VMEM((KV_COLS, TILES * TILE), F32),
            pltpu.VMEM((span, TILES * TILE), F32),
            pltpu.VMEM((width, 2 * span), BF16),
            pltpu.VMEM((2, HEADS, 1, 2 * span), F32),
            pltpu.VMEM((KV_COLS, TILES * TILE), F32),
            pltpu.VMEM((length, KV_COLS), F32),
            pltpu.VMEM((RANK_Q * HEAD_DIM, 2 * span), F32),
            pltpu.VMEM((2 * RANK_KV * HEADS, 1, TILES * TILE), F32),
            pltpu.VMEM((RANK_Q * HEADS, 1, 2 * span), F32),
            pltpu.VMEM((2 * RANK_KV * HEADS, 1, TILES * TILE), F32),
            pltpu.VMEM((RANK_Q * HEADS, 1, 2 * span), F32),
            pltpu.VMEM((span, TILES * TILE), BF16),
            pltpu.VMEM((span, TILES * TILE), BF16),
            pltpu.VMEM((span, TILES * TILE), BF16),
            pltpu.VMEM((span, TILES * TILE), BF16),
            pltpu.VMEM((HEAD_DIM, 2 * span), BF16),
            pltpu.VMEM((HEAD_DIM, 2 * span), BF16),
            pltpu.VMEM((HEAD_DIM, TILES * TILE), BF16),
            pltpu.VMEM((HEAD_DIM, TILES * TILE), BF16),
            pltpu.VMEM((RANK_Q * HEAD_DIM, 2 * span), F32),
        ],
        out_shape=[
            jax.ShapeDtypeStruct((2 * span, Q_PAD), BF16),
            jax.ShapeDtypeStruct((2, 2 * span, KV_COLS), BF16),
            jax.ShapeDtypeStruct((2, 2 * span, KV_COLS), BF16),
        ],
        mib=32,
        name="attend_back",
        after=after,
    )


def out_kernel(x_ref, att_ref, w_ref, gain_ref, resid_ref, normed_ref):
    resid = x_ref[...].astype(F32) + dot(att_ref[...], w_ref[...])
    scale = lax.rsqrt(jnp.mean(resid * resid, axis=-1, keepdims=True) + EPS)
    resid_ref[...] = resid
    normed_ref[...] = (resid * scale * gain_ref[...]).astype(BF16)


def out_project(order, x, attended, w_out, gain):
    tokens, width = x.shape
    step = tokens // 2
    tile = pl.BlockSpec((step, width), lambda i: (i, 0))
    return order.call(
        out_kernel,
        (x, attended, w_out, gain),
        grid=(2,),
        in_specs=[
            tile,
            tile,
            once(w_out.shape, lambda i: (0, 0)),
            pl.BlockSpec((1, width), lambda i: (0, 0)),
        ],
        out_specs=[tile, tile],
        out_shape=[pltpu.HBM((tokens, width), F32), jax.ShapeDtypeStruct((tokens, width), BF16)],
        mib=20,
        name="out_project",
    )


def out_back_kernel(
    cot_ref, own_ref, other_ref, resid_ref, w_ref, gain_ref, gr_ref, gb_ref, ga_ref, gain_grad_ref
):
    grad = own_ref[...].astype(F32) + other_ref[...].astype(F32)
    values = resid_ref[...]
    scale = lax.rsqrt(jnp.mean(values * values, axis=-1, keepdims=True) + EPS)
    weighted = grad * gain_ref[...]
    back = scale * weighted - values * (scale * scale * scale) * jnp.mean(
        weighted * values, axis=-1, keepdims=True
    )
    grad_resid = cot_ref[...].astype(F32) + back
    branch = grad_resid.astype(BF16)
    gr_ref[...] = grad_resid
    gb_ref[...] = branch
    ga_ref[...] = dot(branch, w_ref[...], NT).astype(BF16)

    @pl.when(pl.program_id(0) == 0)
    def _():
        gain_grad_ref[...] = jnp.zeros_like(gain_grad_ref)

    gain_grad_ref[...] += jnp.sum(grad * values * scale, axis=0, keepdims=True)


def out_back(order, cot, own, other, resid, w_out, gain):
    tokens, width = cot.shape
    step = tokens // 2
    tile = pl.BlockSpec((step, width), lambda i: (i, 0))
    row = pl.BlockSpec((1, width), lambda i: (0, 0))
    return order.call(
        out_back_kernel,
        (cot, own, other, resid, w_out, gain),
        grid=(2,),
        in_specs=[tile, tile, tile, tile, once(w_out.shape, lambda i: (0, 0)), row],
        out_specs=[tile, tile, tile, row],
        out_shape=[
            jax.ShapeDtypeStruct((tokens, width), F32),
            jax.ShapeDtypeStruct((tokens, width), BF16),
            jax.ShapeDtypeStruct((tokens, width), BF16),
            jax.ShapeDtypeStruct((1, width), F32),
        ],
        mib=26,
        name="out_back",
    )


def hidden_back_kernel(own_ref, other_ref, w_ref, own_out, other_out):
    own_out[...] = dot(own_ref[...], w_ref[...], NT).astype(BF16)
    other_out[...] = dot(other_ref[...], w_ref[...], NT).astype(BF16)


def hidden_back(order, cot, cot_other, w_down, after):
    tokens, width = cot.shape
    half = w_down.shape[0]
    step = tokens // 2
    tile = pl.BlockSpec((step, width), lambda i: (i, 0))
    out = pl.BlockSpec((step, half), lambda i: (i, 0))
    shape = jax.ShapeDtypeStruct((tokens, half), BF16)
    return order.call(
        hidden_back_kernel,
        (cot, cot_other, w_down),
        grid=(2,),
        in_specs=[tile, tile, once(w_down.shape, lambda i: (0, 0))],
        out_specs=[out, out],
        out_shape=[shape, shape],
        mib=24,
        name="hidden_back",
        after=after,
    )


def ff_kernel(n2_ref, gh_ref, wg_ref, wu_ref, h_ref, gg_ref, gu_ref, back_ref):
    gate = dot(n2_ref[...], wg_ref[...])
    up = dot(n2_ref[...], wu_ref[...])
    grad_hidden = gh_ref[...].astype(F32)
    sigmoid = 1.0 / (1.0 + jnp.exp(-gate))
    silu = gate * sigmoid
    h_ref[...] = (silu * up).astype(BF16)
    gu = (grad_hidden * silu).astype(BF16)
    gg = (grad_hidden * up * (sigmoid + silu * (1.0 - sigmoid))).astype(BF16)
    gu_ref[...] = gu
    gg_ref[...] = gg
    back = dot(gg, wg_ref[...], NT) + dot(gu, wu_ref[...], NT)
    back_ref[...] = back.astype(back_ref.dtype)


def feed_forward(order, n2, grad_hidden, w_gate, w_up, dtype):
    tokens, width = n2.shape
    half = w_gate.shape[1]
    step = tokens // 2
    weight = once((width, half), lambda i: (0, 0))
    wide = pl.BlockSpec((step, width), lambda i: (i, 0))
    out = pl.BlockSpec((step, half), lambda i: (i, 0))
    return order.call(
        ff_kernel,
        (n2, grad_hidden, w_gate, w_up),
        grid=(2,),
        in_specs=[wide, out, weight, weight],
        out_specs=[out, out, out, wide],
        out_shape=[pltpu.HBM((tokens, half), BF16)] * 3
        + [(pltpu.HBM if dtype == F32 else jax.ShapeDtypeStruct)((tokens, width), dtype)],
        mib=30,
        name="feed_forward",
    )


def down_other_kernel(h_ref, w_ref, out_ref):
    out_ref[...] = dot(h_ref[...], w_ref[...]).astype(BF16)


def down_own_kernel(h_ref, w_ref, resid_ref, came_ref, out_ref):
    total = resid_ref[...] + came_ref[...].astype(F32) + dot(h_ref[...], w_ref[...])
    out_ref[...] = total.astype(BF16)


def down_project(order, hidden, w_down, resid=None, came=None):
    tokens, half = hidden.shape
    width = w_down.shape[1]
    step = tokens // 2
    wide = pl.BlockSpec((step, width), lambda i: (i, 0))
    extra = () if resid is None else (resid, came)
    return order.call(
        down_own_kernel if extra else down_other_kernel,
        (hidden, w_down, *extra),
        grid=(2,),
        in_specs=[
            pl.BlockSpec((step, half), lambda i: (i, 0)),
            once((half, width), lambda i: (0, 0)),
            *[wide] * len(extra),
        ],
        out_specs=[wide],
        out_shape=[jax.ShapeDtypeStruct((tokens, width), BF16)],
        mib=20,
        name="down_project",
    )[0]


class Grid:
    def __init__(self, rows_size, seq_size, rows_id, seq_id, width):
        self.high = [f"b{i}" for i in range(rows_size.bit_length() - 2, 0, -1)]
        self.axes = (*self.high, "y", "x", "c")
        self.block = width // (rows_size * seq_size)
        self.route = {"x": ("seq", 2, seq_size), "c": ("seq", 1, seq_size), "y": ("rows", 1, rows_size)}
        for i in range(1, rows_size.bit_length() - 1):
            self.route[f"b{i}"] = ("rows", 1 << i, rows_size)
        bits = []
        for axis in self.axes:
            name, mask, _ = self.route[axis]
            bits.append(((seq_id if name == "seq" else rows_id) // mask) % 2)
        self.bits = jnp.stack(bits).astype(jnp.int32)

    def place(self, axis):
        return self.axes.index(axis)

    def swap(self, value, axis):
        name, mask, size = self.route[axis]
        return lax.ppermute(value, name, [(i, i ^ mask) for i in range(size)])


class Chain:
    def __init__(self, axes, pieces):
        self.axes, self.pieces = axes, pieces


def fold_specs(grid, chain, axis):
    specs = []
    for value, axes, _, _ in chain.pieces:
        block, kinds = [], []
        for name in axes:
            if name == axis:
                block.append(None)
                kinds.append((grid.place(name), True))
            elif name in chain.axes:
                block.append(2)
                kinds.append(None)
            else:
                block.append(None)
                kinds.append((grid.place(name), False))

        def index(i, bits, kinds=tuple(kinds)):
            out = []
            for kind in kinds:
                if kind is None:
                    out.append(0)
                else:
                    out.append(1 - bits[kind[0]] if kind[1] else bits[kind[0]])
            return (*out, 0, 0)

        specs.append(pl.BlockSpec((*block, *value.shape[-2:]), index))
    return specs


def fold(order, grid, groups, after=()):
    args, specs, layout, shapes = [], [], [], []
    for chains, axis in groups:
        parts = []
        for chain in chains:
            parts.append([(lo, hi) for _, _, lo, hi in chain.pieces])
            args += [value for value, _, _, _ in chain.pieces]
            specs += fold_specs(grid, chain, axis)
        layout.append(parts)
        left = tuple(a for a in chains[0].axes if a != axis)
        cols = sum(c.pieces[0][3] - c.pieces[0][2] for c in chains)
        shapes.append((2,) * len(left) + (grid.block, cols))

    def kernel(bits_ref, *refs):
        inputs, outputs = iter(refs[: len(args)]), refs[len(args) :]
        for out, parts in zip(outputs, layout):
            sums = []
            for ranges in parts:
                total = None
                for lo, hi in ranges:
                    value = next(inputs)[..., lo:hi].astype(F32)
                    total = value if total is None else total + value
                sums.append(total.astype(BF16))
            out[...] = sums[0] if len(sums) == 1 else jnp.concatenate(sums, axis=-1)

    def whole(shape):
        return pl.BlockSpec(shape, lambda i, bits: (0,) * len(shape))

    sends = order.call(
        kernel,
        args,
        scalars=(grid.bits,),
        grid=(1,),
        in_specs=specs,
        out_specs=[whole(shape) for shape in shapes],
        out_shape=[jax.ShapeDtypeStruct(shape, BF16) for shape in shapes],
        mib=26,
        name="fold",
        after=after,
    )
    for (chains, axis), send in zip(groups, sends):
        came = grid.swap(send, axis)
        at = 0
        for chain in chains:
            left = tuple(a for a in chain.axes if a != axis)
            cols = chain.pieces[0][3] - chain.pieces[0][2]
            chain.pieces.append((came, left, at, at + cols))
            chain.axes = left
            at += cols
    return sends


def weight_grad(order, grid, axis, left, right, after=()):
    tokens, width = left[0].shape
    cols = right[0].shape[1]
    step = width // 2
    inner = grid.axes[1:]
    place = grid.place(axis)
    shape = (2,) * (len(grid.axes) - 1) + (grid.block, cols)

    def kernel(bits_ref, l0_ref, l1_ref, r0_ref, r1_ref, send_ref, keep_ref):
        total = dot(l0_ref[...], r0_ref[...], TN) + dot(l1_ref[...], r1_ref[...], TN)
        at = inner.index(axis)
        parts = total.astype(BF16).reshape(2**at, 2, step // 2 ** (at + 1), cols)
        upper = bits_ref[place] == 1
        send_ref[...] = jnp.where(upper, parts[:, 0], parts[:, 1]).reshape(step // 2, cols)
        keep_ref[...] = jnp.where(upper, parts[:, 1], parts[:, 0]).reshape(step // 2, cols)

    l_spec = pl.BlockSpec((tokens, step), lambda i, b: (0, i))
    r_spec = once((tokens, cols), lambda i, b: (0, 0))
    out = pl.BlockSpec((step // 2, cols), lambda i, b: (i, 0))
    send, keep = order.call(
        kernel,
        (left[0], left[1], right[0], right[1]),
        scalars=(grid.bits,),
        grid=(2,),
        in_specs=[l_spec, l_spec, r_spec, r_spec],
        out_specs=[out, out],
        out_shape=[jax.ShapeDtypeStruct((width // 2, cols), BF16)] * 2,
        mib=28,
        name="weight_grad",
        after=after,
    )
    axes = tuple(a for a in grid.axes if a != axis)
    came = grid.swap(send.reshape(shape), axis)
    return Chain(axes, [(keep.reshape(shape), axes, 0, cols), (came, axes, 0, cols)]), send


PART = 256


def weight_halves(order, grid, lefts, rights, gain_grad=None, spare=0):
    step = 256
    pairs = len(rights)
    size, cols = rights[0].shape
    width = lefts[0][0].shape[1]
    half = cols // 2
    parts = half // PART
    gains = [] if gain_grad is None else [gain_grad]
    place = grid.place("c")

    def kernel(bits_ref, *refs):
        mine_ref, other_refs = refs[-1 - parts], refs[-parts:]
        upper = bits_ref[place] == 1
        total = None
        for l_ref, r_ref in zip(refs[:pairs], refs[pairs : 2 * pairs]):
            part = dot(l_ref[...], r_ref[...], TN)
            total = part if total is None else total + part
        if gains:
            column = jnp.broadcast_to(refs[2 * pairs][...], (8, step)).T[:, 0:1]
            coarse = column.astype(BF16).astype(F32)
            lane = lax.broadcasted_iota(jnp.int32, (step, cols), 1)
            total = jnp.where(lane == spare, coarse, total)
            total = jnp.where(lane == spare + 1, column - coarse, total)
        total = total.astype(BF16)
        first, second = total[:, :half], total[:, half:]
        mine_ref[...] = jnp.where(upper, second, first)
        other = jnp.where(upper, first, second)
        for k, other_ref in enumerate(other_refs):
            other_ref[...] = other[:, k * PART : (k + 1) * PART]

    mine, *others = order.call(
        kernel,
        (*[value for value, _ in lefts], *rights, *gains),
        scalars=(grid.bits,),
        grid=(width // step,),
        in_specs=[
            *[pl.BlockSpec((size, step), lambda i, b, at=at: (at, i)) for _, at in lefts],
            *[once((size, cols), lambda i, b: (0, 0))] * pairs,
            *[pl.BlockSpec((1, step), lambda i, b: (0, i))] * len(gains),
        ],
        out_specs=[
            pl.BlockSpec((step, half), lambda i, b: (i, 0)),
            *[pl.BlockSpec((step, PART), lambda i, b: (i, 0))] * parts,
        ],
        out_shape=[
            jax.ShapeDtypeStruct((width, half), BF16),
            *[jax.ShapeDtypeStruct((width, PART), BF16)] * parts,
        ],
        mib=16,
        name="weight_halves",
    )
    lead = (2,) * len(grid.axes) + (grid.block,)
    mine = mine.reshape(lead + (half,))
    chains = []
    for k, other in enumerate(others):
        came = grid.swap(other, "c").reshape(lead + (PART,))
        held = [(mine, grid.axes, k * PART, (k + 1) * PART), (came, grid.axes, 0, PART)]
        chains.append(Chain(grid.axes, held))
    return chains


def weight_rows(order, grid, lefts, rights, gain_grad, spare):
    step = 256
    pairs = len(rights)
    size, cols = rights[0].shape
    width = lefts[0][0].shape[1]
    place = grid.place("c")
    block = grid.block

    def kernel(bits_ref, *refs):
        mine_ref, other_ref = refs[-2:]
        upper = bits_ref[place] == 1
        total = None
        for l_ref, r_ref in zip(refs[:pairs], refs[pairs : 2 * pairs]):
            part = dot(l_ref[...], r_ref[...], TN)
            total = part if total is None else total + part
        column = jnp.broadcast_to(refs[2 * pairs][...], (8, step)).T[:, 0:1]
        coarse = column.astype(BF16).astype(F32)
        lane = lax.broadcasted_iota(jnp.int32, (step, cols), 1)
        total = jnp.where(lane == spare, coarse, total)
        total = jnp.where(lane == spare + 1, column - coarse, total)
        parts = total.reshape(step // (2 * block), 2, block, cols)
        first, second = parts[:, 0], parts[:, 1]
        flat = (step // 2, cols)
        mine_ref[...] = jnp.where(upper, second, first).reshape(flat).astype(BF16)
        other_ref[...] = jnp.where(upper, first, second).reshape(flat).astype(BF16)

    out = pl.BlockSpec((step // 2, cols), lambda i, b: (i, 0))
    mine, other = order.call(
        kernel,
        (*[value for value, _ in lefts], *rights, gain_grad),
        scalars=(grid.bits,),
        grid=(width // step,),
        in_specs=[
            *[pl.BlockSpec((size, step), lambda i, b, at=at: (at, i)) for _, at in lefts],
            *[once((size, cols), lambda i, b: (0, 0))] * pairs,
            pl.BlockSpec((1, step), lambda i, b: (0, i)),
        ],
        out_specs=[out, out],
        out_shape=[jax.ShapeDtypeStruct((width // 2, cols), BF16)] * 2,
        mib=16,
        name="weight_rows",
    )
    axes = grid.axes[:-1]
    shape = (2,) * len(axes) + (block, cols)
    came = grid.swap(other.reshape(shape), "c")
    return Chain(axes, [(mine.reshape(shape), axes, 0, cols), (came, axes, 0, cols)])


def settle(order, grid, chains, widths, mib):
    args, specs, ranges = [], [], []
    for chain in chains:
        specs += fold_specs(grid, chain, None)
        args += [value for value, _, _, _ in chain.pieces]
        ranges.append([(lo, hi) for _, _, lo, hi in chain.pieces])

    def kernel(bits_ref, *refs):
        inputs, outputs = iter(refs[: len(args)]), iter(refs[len(args) :])
        for pieces, width in zip(ranges, widths):
            total = functools.reduce(
                jnp.add, [next(inputs)[..., lo:hi].astype(F32) for lo, hi in pieces]
            )
            next(outputs)[...] = total[:, :width]
            column = total[:, width : width + 1] + total[:, width + 1 : width + 2]
            next(outputs)[...] = jnp.broadcast_to(column, (column.shape[0], TILE)).T[0:1, :]

    shapes = []
    for width in widths:
        shapes += [(grid.block, width), (1, grid.block)]
    return order.call(
        kernel,
        args,
        scalars=(grid.bits,),
        grid=(1,),
        in_specs=specs,
        out_specs=[pl.BlockSpec(shape, lambda i, b: (0, 0)) for shape in shapes],
        out_shape=[jax.ShapeDtypeStruct(shape, F32) for shape in shapes],
        mib=mib,
        name="settle",
    )


def conclude(order, grid, groups, widths, gains, mib, after=()):
    args, specs, ranges = [], [], []
    for group in groups:
        parts = []
        for chain in group:
            specs += fold_specs(grid, chain, None)
            args += [value for value, _, _, _ in chain.pieces]
            parts.append([(lo, hi) for _, _, lo, hi in chain.pieces])
        ranges.append(parts)
    place = grid.place("c")

    def kernel(bits_ref, *refs):
        inputs, outputs = iter(refs[: len(args)]), iter(refs[len(args) :])
        for parts, width, gained in zip(ranges, widths, gains):
            owns, lasts = [], []
            for pieces in parts:
                values = [next(inputs)[..., lo:hi].astype(F32) for lo, hi in pieces]
                owns.append(functools.reduce(jnp.add, values[:-1]))
                lasts.append(values[-1])
            own = owns[0] if len(owns) == 1 else jnp.concatenate(owns, axis=1)
            last = lasts[0] if len(lasts) == 1 else jnp.concatenate(lasts, axis=1)
            cols = own.shape[-1]
            out = next(outputs)
            gain = next(outputs) if gained else None

            def put(first, second):
                out[:, :cols] = first
                out[:, cols:] = second[:, : width - cols]
                if gain is not None:
                    at = width - cols
                    column = second[:, at : at + 1] + second[:, at + 1 : at + 2]
                    gain[...] = jnp.broadcast_to(column, (column.shape[0], TILE)).T[0:1, :]

            @pl.when(bits_ref[place] == 0)
            def _():
                put(own, last)

            @pl.when(bits_ref[place] == 1)
            def _():
                put(last, own)

    shapes = []
    for width, gained in zip(widths, gains):
        shapes.append((grid.block, width))
        if gained:
            shapes.append((1, grid.block))
    return order.call(
        kernel,
        args,
        scalars=(grid.bits,),
        grid=(1,),
        in_specs=specs,
        out_specs=[pl.BlockSpec(shape, lambda i, b: (0, 0)) for shape in shapes],
        out_shape=[jax.ShapeDtypeStruct(shape, F32) for shape in shapes],
        mib=mib,
        name="conclude",
        after=after,
    )


def finish_kernel(
    k0_ref, r0_ref, x0_ref, gq_ref, wq_ref, wkv_ref, x_ref, gain_ref, gr_ref, cos_ref, sin_ref,
    came_ref, gkv_ref, out_ref, gain_grad_ref,
):
    total = k0_ref[...].astype(F32) + r0_ref[...].astype(F32) + x0_ref[...].astype(F32)
    cos, sin = cos_ref[0], sin_ref[0]
    half = HEAD_DIM // 2
    split = RANK_KV * HEADS
    turned = total.T
    pieces = [turned[:split]]
    for r in range(RANK_KV):
        at = split + r * HEAD_DIM
        first, second = turned[at : at + half], turned[at + half : at + HEAD_DIM]
        pieces += [first * cos + second * sin, second * cos - first * sin]
    pieces.append(turned[split + RANK_KV * HEAD_DIM :])
    gkv = jnp.concatenate(pieces, axis=0).T.astype(BF16)
    gkv_ref[:, :KV_COLS] = gkv
    gkv_ref[:, KV_COLS:] = jnp.zeros((gkv.shape[0], KV_PAD - KV_COLS), BF16)
    grad = dot(gq_ref[:, :Q_COLS], wq_ref[...]) + dot(gkv, wkv_ref[...])
    values = x_ref[...].astype(F32)
    scale = lax.rsqrt(jnp.mean(values * values, axis=-1, keepdims=True) + EPS)
    weighted = grad * gain_ref[...]
    back = scale * weighted - values * (scale * scale * scale) * jnp.mean(
        weighted * values, axis=-1, keepdims=True
    )
    out_ref[...] = (gr_ref[...] + back).astype(BF16)

    @pl.when(pl.program_id(0) == 0)
    def _():
        gain_grad_ref[...] = came_ref[...]

    gain_grad_ref[...] += jnp.sum(grad * values * scale, axis=0, keepdims=True)


def finish(order, row, kept, near, far, gq, w_query, w_keyval, x, gain, grad_resid, cos, sin, came, held):
    tokens, width = x.shape
    span = cos.shape[-1]
    full = lambda i: (0, 0)
    tile = pl.BlockSpec((span, width), lambda i: (2 * row + i, 0))
    part = pl.BlockSpec((None, span, KV_COLS), lambda i: (0, i, 0))
    rope = pl.BlockSpec((1, HEAD_DIM // 2, span), lambda i: (i, 0, 0))
    vector = pl.BlockSpec((1, width), full)
    extra = () if held is None else (held,)

    def kernel(*refs):
        finish_kernel(*refs[:12], *refs[12 + len(extra) :])

    return order.call(
        kernel,
        (kept, near, far, gq, w_query, w_keyval, x, gain, grad_resid, cos, sin, came, *extra),
        grid=(2,),
        in_specs=[
            part,
            part,
            pl.BlockSpec((span, KV_COLS), lambda i: (i, 0)),
            pl.BlockSpec((span, Q_PAD), lambda i: (i, 0)),
            once((Q_COLS, width), full),
            once((KV_COLS, width), full),
            tile,
            vector,
            tile,
            rope,
            rope,
            vector,
            *[pl.BlockSpec(memory_space=pl.ANY)] * len(extra),
        ],
        out_specs=[pl.BlockSpec((span, KV_PAD), lambda i: (i, 0)), tile, vector],
        out_shape=[
            jax.ShapeDtypeStruct((2 * span, KV_PAD), BF16),
            jax.ShapeDtypeStruct((tokens, width), BF16),
            jax.ShapeDtypeStruct((1, width), F32),
        ],
        mib=20,
        name="finish",
        aliases={12: 1} if extra else None,
    )


def meet_kernel(near_ref, far_ref, out_ref):
    out_ref[...] = (near_ref[...].astype(F32) + far_ref[...].astype(F32)).astype(BF16)


def meet(order, near, far):
    shape = near.shape[1:]
    part = pl.BlockSpec((None, *shape), lambda i: (1, 0, 0))
    return order.call(
        meet_kernel,
        (near, far),
        grid=(1,),
        in_specs=[part, part],
        out_specs=[pl.BlockSpec(shape, lambda i: (0, 0))],
        out_shape=[jax.ShapeDtypeStruct(shape, BF16)],
        mib=8,
        name="meet",
    )[0]


def body(
    layer_input,
    doc_ids,
    norm1_gain,
    w_query,
    w_keyval,
    w_out,
    norm2_gain,
    w_gate,
    w_up,
    w_down,
    cotangent,
):
    row_count, local_len, width = layer_input.shape
    seq_size = lax.axis_size("seq")
    rows_size = lax.axis_size("rows")
    seq_id = lax.axis_index("seq")
    rows_id = lax.axis_index("rows")
    span = local_len // 2
    tokens = row_count * local_len
    length = local_len * seq_size
    core = seq_id % 2
    order = Order()
    grid = Grid(rows_size, seq_size, rows_id, seq_id, width)
    seq_arg = seq_id.astype(jnp.int32).reshape(1)

    x = layer_input.reshape(tokens, width)
    cot = cotangent.reshape(tokens, width)
    cot_other = grid.swap(cot, "c")
    gain1 = norm1_gain.reshape(1, width)
    gain2 = norm2_gain.reshape(1, width)
    wq_t, wkv_t = w_query.T, w_keyval.T
    docs = doc_ids.reshape(row_count, 1, length)

    spans = jnp.stack([seq_id, 2 * seq_size - 1 - seq_id])
    positions = spans[:, None] * span + jnp.arange(span, dtype=jnp.int32)[None, :]
    inv_freq = ROPE_BASE ** (-(jnp.arange(HEAD_DIM // 2, dtype=F32) * (2.0 / HEAD_DIM)))
    angles = positions.astype(F32)[:, None, :] * inv_freq[None, :, None]
    cos, sin = jnp.cos(angles), jnp.sin(angles)

    normed, qf, kv = project(order, x, gain1, wq_t, wkv_t, cos, sin)
    kv = kv.reshape(row_count, local_len, KV_COLS)
    kv_x = grid.swap(kv, "x")
    kv_core = grid.swap(kv, "c")
    half = w_gate.shape[1] // 2
    wg = lax.dynamic_slice_in_dim(w_gate, core * half, half, 1)
    wu = lax.dynamic_slice_in_dim(w_up, core * half, half, 1)
    wd = lax.dynamic_slice_in_dim(w_down, core * half, half, 0)
    gh_own, gh_oth = hidden_back(order, cot, cot_other, wd, (wg, wu))
    kv_x, _ = lax.optimization_barrier((kv_x, order.token))
    kv_both = grid.swap(kv_x, "c")
    sources = (kv, kv_core, kv_x, kv_both)
    attended, lse = attend(order, seq_arg, qf, sources, docs)
    resid, normed2 = out_project(order, x, attended, w_out, gain2)
    normed2_other = grid.swap(normed2, "c")
    h_own, gg_own, gu_own, gn2_own = feed_forward(order, normed2, gh_own, wg, wu, BF16)
    h_oth, gg_oth, gu_oth, gn2_send = feed_forward(order, normed2_other, gh_oth, wg, wu, BF16)
    gn2_came = grid.swap(gn2_send, "c")

    first, second = grid.high[-1], grid.high[:-1]
    down, _ = weight_grad(
        order, grid, "x", (stay(cot), stay(cot_other)), (stay(h_own), stay(h_oth))
    )
    gate, _ = weight_grad(order, grid, "y", (normed2, normed2_other), (gg_own, gg_oth))
    up, _ = weight_grad(order, grid, first, (normed2, normed2_other), (gu_own, gu_oth))
    grad_resid, branch, grad_att, grad_norm2 = out_back(
        order, cot, gn2_own, gn2_came, resid, w_out, gain2
    )
    out = weight_halves(order, grid, [(branch, 0)], [attended])
    grad_att = grad_att.reshape(row_count, local_len, width)

    def back(row, after=()):
        gq, near, far = attend_back(
            order, row, seq_arg, qf, sources, docs, lse, attended, grad_att, cos, sin, after
        )
        return gq, near, grid.swap(far, "c")

    def end(row, near, far, came, gq, gain, held):
        return finish(
            order, row, near, far, came, gq, wq_t, wkv_t, x, gain1, grad_resid, cos, sin, gain, held
        )

    gq0, near0, far0 = back(0)
    fold(order, grid, [([down], "y"), ([gate], "x"), (out, first)])
    came0 = grid.swap(meet(order, near0, far0), "x")
    gq1, near1, far1 = back(1)
    upper = [up, *out]
    fold(order, grid, [([down, gate], first)])
    fold(order, grid, [(upper, "y")], after=(came0,))
    came1 = grid.swap(meet(order, near1, far1), "x")
    gkv0, ig0, gain0 = end(0, near0, far0, came0, gq0, jnp.zeros((1, width), F32), None)
    query = weight_rows(
        order, grid, [(normed, 0), (normed, 1)], [gq0, gq1], grad_norm2, Q_COLS
    )
    down_send = down_project(order, h_oth, wd)
    down_came = grid.swap(down_send, "c")
    gkv1, input_grad, grad_norm1 = end(1, near1, far1, came1, gq1, gain0, ig0)
    keyval = weight_rows(
        order, grid, [(normed, 0), (normed, 1)], [gkv0, gkv1], grad_norm1, KV_COLS
    )
    fold(order, grid, [([down, gate], second[0])])
    fold(order, grid, [([keyval], "x"), ([query], "y")])
    fold(order, grid, [(upper, "x")])
    for axis in second[1:]:
        fold(order, grid, [([down, gate], axis)])
    fold(order, grid, [([keyval], "y"), ([query], "x")])
    fold(order, grid, [(upper, second[0])])
    for axis in second[1:]:
        fold(order, grid, [(upper, axis)])
    late = [keyval, query]
    fold(order, grid, [(late, first)])
    for axis in second:
        fold(order, grid, [(late, axis)])
    fold(order, grid, [([down, gate, *upper], "c")])
    layer_output = down_project(order, h_own, wd, resid, down_came)
    g_query, g_norm2, g_keyval, g_norm1 = settle(
        order, grid, [query, keyval], [Q_COLS, KV_COLS], 8
    )
    g_down, g_gate, g_up, g_out = conclude(
        order,
        grid,
        [[down], [gate], [up], out],
        [*[w.shape[1] for w in (w_gate, w_gate, w_up)], width],
        [False] * 4,
        24,
    )
    return (
        layer_output.reshape(row_count, local_len, width),
        input_grad.reshape(row_count, local_len, width),
        g_norm1.reshape(-1),
        g_query,
        g_keyval,
        g_out.T,
        g_norm2.reshape(-1),
        g_gate,
        g_up,
        g_down.T,
    )


def solution(mesh):
    return jax.shard_map(
        body,
        mesh=mesh,
        in_specs=(
            P("rows", "seq", None),
            P("rows", None),
            P(),
            P(),
            P(),
            P(),
            P(),
            P(),
            P(),
            P(),
            P("rows", "seq", None),
        ),
        out_specs=(
            P("rows", "seq", None),
            P("rows", "seq", None),
            P(("rows", "seq")),
            P(("rows", "seq"), None),
            P(("rows", "seq"), None),
            P(None, ("rows", "seq")),
            P(("rows", "seq")),
            P(("rows", "seq"), None),
            P(("rows", "seq"), None),
            P(None, ("rows", "seq")),
        ),
        check_vma=False,
    )
```

```python
import functools

import jax
import jax.numpy as jnp
from jax import lax
from jax.experimental import pallas as pl
from jax.experimental.pallas import tpu as pltpu
from jax.sharding import PartitionSpec as P

HEADS = 16
HEAD_DIM = 64
RANK_Q = 6
RANK_KV = 2
Q_COLS = RANK_Q * (HEADS + HEAD_DIM)
KV_COLS = 2 * RANK_KV * (HEADS + HEAD_DIM)
Q_PAD = 512
KV_PAD = 384
EPS = 1e-06
ROPE_BASE = 10000.0
MASKED = -1e30
SCORE_SCALE = HEAD_DIM ** (-0.5)
VALUE_BASE = RANK_KV * (HEADS + HEAD_DIM)
TILE = 128
TILES = 9
F32 = jnp.float32
BF16 = jnp.bfloat16
NT = (((1,), (1,)), ((), ()))
TN = (((0,), (0,)), ((), ()))


def dot(left, right, dims=None):
    if dims is None:
        return jnp.dot(left, right, preferred_element_type=F32)
    return lax.dot_general(left, right, dims, preferred_element_type=F32)


def params(mib):
    return pltpu.CompilerParams(vmem_limit_bytes=mib * 2**20)


def cost(flops, nbytes, trans=0):
    return pl.CostEstimate(flops=flops, bytes_accessed=nbytes, transcendentals=trans)


def once(shape, index):
    return pl.BlockSpec(shape, index, pipeline_mode=pl.Buffered(1))


class Order:
    def __init__(self):
        self.token = None

    def call(self, kernel, args, *, grid, in_specs, out_specs, out_shape, mib, name, scalars=(), scratch=(), after=(), work=0, aliases=None):
        extra = [a for a in (self.token, *after) if a is not None]
        n_scalar, n_in, n_out = len(scalars), len(in_specs), len(out_specs)

        def run(*refs):
            head = refs[: n_scalar + n_in]
            rest = refs[n_scalar + n_in + len(extra) :]
            rest[n_out][...] = jnp.zeros_like(rest[n_out])
            kernel(*head, *rest[:n_out], *rest[n_out + 1 :])

        def spec(block, index, **kw):
            return pl.BlockSpec(block, index, **kw)

        token_spec = pl.BlockSpec((8, TILE), lambda *_: (0, 0))
        out = pl.pallas_call(
            run,
            grid_spec=pltpu.PrefetchScalarGridSpec(
                num_scalar_prefetch=n_scalar,
                grid=grid,
                in_specs=[*in_specs, *[pl.BlockSpec(memory_space=pl.ANY)] * len(extra)],
                out_specs=[*out_specs, token_spec],
                scratch_shapes=list(scratch),
            ),
            out_shape=[*out_shape, jax.ShapeDtypeStruct((8, TILE), F32)],
            compiler_params=params(mib),
            input_output_aliases={n_scalar + k: v for k, v in (aliases or {}).items()},
            cost_estimate=cost(work, 2**16),
            name=name,
        )(*scalars, *args, *extra)
        self.token = out[-1]
        return out[:-1]


def stay(value):
    return pltpu.with_memory_space_constraint(value, pltpu.HBM)


def aligned(value, factor):
    return pl.multiple_of(value, factor)


def project_kernel(x_ref, gain_ref, wq_ref, wkv_ref, cos_ref, sin_ref, normed_ref, qf_ref, kv_ref):
    x = x_ref[...].astype(F32)
    scale = lax.rsqrt(jnp.mean(x * x, axis=-1, keepdims=True) + EPS)
    normed = (x * scale * gain_ref[...]).astype(BF16)
    normed_ref[...] = normed
    kvf = dot(normed, wkv_ref[...], NT)
    qf = dot(normed, wq_ref[...], NT)
    half = HEAD_DIM // 2
    span = cos_ref.shape[-1]
    for s in range(2):
        cos, sin = cos_ref[s], sin_ref[s]
        rows = slice(s * span, (s + 1) * span)
        kvt = kvf[rows].T
        split = RANK_KV * HEADS
        pieces = [kvt[:split]]
        for r in range(RANK_KV):
            at = split + r * HEAD_DIM
            first, second = kvt[at : at + half], kvt[at + half : at + HEAD_DIM]
            pieces += [first * cos - second * sin, second * cos + first * sin]
        pieces.append(kvt[split + RANK_KV * HEAD_DIM :])
        kv_ref[rows, :] = jnp.concatenate(pieces, axis=0).T.astype(BF16)
        qt = qf[rows].T
        split = RANK_Q * HEADS
        qf_ref[s, :split, :] = qt[:split]
        for r in range(RANK_Q):
            at = split + r * HEAD_DIM
            first, second = qt[at : at + half], qt[at + half : at + HEAD_DIM]
            qf_ref[s, at : at + half, :] = first * cos - second * sin
            qf_ref[s, at + half : at + HEAD_DIM, :] = second * cos + first * sin


def project(order, x, gain, w_query, w_keyval, cos, sin):
    tokens, width = x.shape
    span = cos.shape[-1]
    groups = tokens // span
    full = lambda i: (0, 0)
    rope = pl.BlockSpec((2, HEAD_DIM // 2, span), lambda i: (0, 0, 0))
    return order.call(
        project_kernel,
        (x, gain, w_query, w_keyval, cos, sin),
        grid=(groups // 2,),
        in_specs=[
            pl.BlockSpec((2 * span, width), lambda i: (i, 0)),
            pl.BlockSpec((1, width), full),
            once((Q_COLS, width), full),
            once((KV_COLS, width), full),
            rope,
            rope,
        ],
        out_specs=[
            pl.BlockSpec((2 * span, width), lambda i: (i, 0)),
            pl.BlockSpec((2, Q_COLS, span), lambda i: (i, 0, 0)),
            pl.BlockSpec((2 * span, KV_COLS), lambda i: (i, 0)),
        ],
        out_shape=[
            jax.ShapeDtypeStruct((tokens, width), BF16),
            jax.ShapeDtypeStruct((groups, Q_COLS, span), F32),
            jax.ShapeDtypeStruct((tokens, KV_COLS), BF16),
        ],
        mib=56,
        name="project",
    )


PIECES = ((0, 2), (2, 3), (3, 4), (4, 5), (5, 7), (7, 9))


def tile_place(tile, seq_id):
    low = tile < seq_id + 2
    return low, jnp.where(low, tile, tile + 1 - seq_id)


def piece_side(piece, seq_id):
    first, last = piece
    low = first < seq_id + 2
    side = 0 if last <= 2 else (1 if first > 4 else jnp.where(low, 0, 1))
    return slice(first * TILE, last * TILE), side, low


def choose(side, low, pair):
    return pair[side] if isinstance(side, int) else jnp.where(low, pair[0], pair[1])


def gather(totals, side, low, part, combine, empty):
    for s in range(2):
        if isinstance(side, int):
            if side != s:
                continue
            term = part
        else:
            term = jnp.where(low if s == 0 else ~low, part, empty)
        totals[s] = term if totals[s] is None else combine(totals[s], term)


def gather_keys(seq_id, sources, qf_ref, qa, qb, kvpos, kvt, kva, bias, docs_ref, row, span):
    for which, source in enumerate(sources):
        holder = seq_id ^ which
        kvpos[pl.ds(aligned(holder * span, 32), span), :] = source[0, :span, :]
        kvpos[pl.ds(aligned((7 - holder) * span, 32), span), :] = source[0, span:, :]
    columns = []
    for number in (seq_id, 7 - seq_id):
        ids = None
        for place in range(8):
            part = docs_ref[row : row + 1, place * span : (place + 1) * span]
            ids = part if ids is None else jnp.where(number == place, part, ids)
        columns.append(jnp.broadcast_to(ids.astype(F32), (8, span)).T[:, 0:1].astype(jnp.int32))
    for tile in range(TILES):
        low, place = tile_place(tile, seq_id)
        start = aligned(place * TILE, TILE)
        cols = slice(tile * TILE, (tile + 1) * TILE)
        kvt[:, cols] = kvpos[pl.ds(start, TILE), :].astype(F32).T
        side = 0 if tile < 2 else (1 if tile > 4 else None)
        doc_q = jnp.where(low, columns[0], columns[1]) if side is None else columns[side]
        number = jnp.where(low, seq_id, 7 - seq_id)
        pos_q = number * span + lax.broadcasted_iota(jnp.int32, (span, TILE), 0)
        pos_k = start + lax.broadcasted_iota(jnp.int32, (span, TILE), 1)
        allowed = (doc_q == docs_ref[row : row + 1, pl.ds(start, TILE)]) & (pos_k <= pos_q)
        bias[:, cols] = jnp.where(allowed, 0.0, MASKED)
    split = RANK_KV * HEADS
    kva[:split, 0, :] = kvt[:split, :] * (1.0 / RANK_KV)
    kva[split:, 0, :] = kvt[VALUE_BASE : VALUE_BASE + split, :] * (1.0 / RANK_KV)
    both = jnp.concatenate([qf_ref[0], qf_ref[1]], axis=1)
    split = RANK_Q * HEADS
    qa[:, 0, :] = both[:split] * (1.0 / RANK_Q)
    qb[...] = both[split:]


def expand_queries(qf_ref, qa, s, head):
    split = RANK_Q * HEADS
    total = None
    for r in range(RANK_Q):
        weight = qa[s, r * HEADS + head]
        term = weight * qf_ref[s, split + r * HEAD_DIM : split + (r + 1) * HEAD_DIM, :]
        total = term if total is None else total + term
    return total.astype(BF16) * BF16(SCORE_SCALE)


def expand_pair(kvt, kva, base, head):
    split = RANK_KV * HEADS
    total = None
    for r in range(RANK_KV):
        at = base + split + r * HEAD_DIM
        weight = kva[(base // VALUE_BASE) * split + r * HEADS + head]
        term = weight * kvt[at : at + HEAD_DIM, :]
        total = term if total is None else total + term
    return total.astype(BF16)


def weave(*streams):
    streams = list(streams)
    while streams:
        for stream in list(streams):
            try:
                next(stream)
            except StopIteration:
                streams.remove(stream)


SEEN = ((0, 5), (3, 10))


def place_keys(seq_id, sources, kvpos, span):
    for which, source in enumerate(sources):
        holder = seq_id ^ which
        kvpos[pl.ds(aligned(holder * span, 32), span), :] = source[0, :span, :]
        kvpos[pl.ds(aligned((7 - holder) * span, 32), span), :] = source[0, span:, :]


def query_docs(number, docs_ref, row, span):
    ids = None
    for place in range(8):
        part = docs_ref[row : row + 1, place * span : (place + 1) * span]
        ids = part if ids is None else jnp.where(number == place, part, ids)
    return jnp.broadcast_to(ids.astype(F32), (8, span)).T[:, 0:1].astype(jnp.int32)


def attend_kernel(
    row, seq_ref, qf_ref, kv0, kv1, kv2, kv3, doc_ref, out_ref, lse_ref,
    kvpos, kvt, bias_low, bias_high, kva, qa, heads_out, heads_lse,
    low_a, low_b, high_a, high_b, top_a, top_b,
):
    seq_id = seq_ref[0]
    span = qf_ref.shape[-1]
    biases = (bias_low, bias_high)
    place_keys(seq_id, (kv0, kv1, kv2, kv3), kvpos, span)
    length = kvpos.shape[0]
    for at in range(0, length, TILE):
        kvt[:, at : at + TILE] = kvpos[at : at + TILE, :].astype(F32).T
    for s, number in enumerate((seq_id, 7 - seq_id)):
        doc_q = query_docs(number, doc_ref, row, span)
        pos_q = number * span + lax.broadcasted_iota(jnp.int32, (span, TILE), 0)
        for tile in range(*SEEN[s]):
            start = tile * TILE
            pos_k = start + lax.broadcasted_iota(jnp.int32, (span, TILE), 1)
            allowed = (doc_q == doc_ref[row : row + 1, start : start + TILE]) & (pos_k <= pos_q)
            at = start - SEEN[s][0] * TILE
            biases[s][:, at : at + TILE] = jnp.where(allowed, 0.0, MASKED)
    split = RANK_KV * HEADS
    kva[:split, 0, :] = kvt[:split, :] * (1.0 / RANK_KV)
    kva[split:, 0, :] = kvt[VALUE_BASE : VALUE_BASE + split, :] * (1.0 / RANK_KV)
    for s in range(2):
        qa[s, :, 0, :] = qf_ref[s, : RANK_Q * HEADS, :] * (1.0 / RANK_Q)

    def expand(base, head):
        total = None
        for r in range(RANK_KV):
            at = base + split + r * HEAD_DIM
            weight = kva[(base // VALUE_BASE) * split + r * HEADS + head]
            term = weight * kvt[at : at + HEAD_DIM, :]
            total = term if total is None else total + term
        return total.astype(BF16)

    def pieces(s):
        count = SEEN[s][1] - SEEN[s][0]
        edges = [*range(0, count, 2), count]
        shift = SEEN[s][0] * TILE
        for lo, hi in zip(edges, edges[1:]):
            yield slice(lo * TILE, hi * TILE), slice(shift + lo * TILE, shift + hi * TILE)

    def scores_of(head, scores, top):
        keys = expand(0, head)
        yield
        for s in range(2):
            queries = expand_queries(qf_ref, qa, s, head).T
            best = None
            for cols, places in pieces(s):
                part = dot(queries, keys[:, places]) + biases[s][:, cols]
                scores[s][:, cols] = part
                for at in range(0, part.shape[1], TILE):
                    tile = part[:, at : at + TILE]
                    best = tile if best is None else jnp.maximum(best, tile)
                yield
            top[s] = jnp.max(best, axis=-1, keepdims=True)

    def weigh(head, scores, top):
        values = expand(VALUE_BASE, head)
        values = jnp.concatenate([values, jnp.ones((16, values.shape[1]), BF16)], axis=0)
        yield
        for s in range(2):
            peak = top[s]
            out = None
            for cols, places in pieces(s):
                raised = jnp.exp(scores[s][:, cols] - peak).astype(BF16)
                part = dot(raised, values[:, places], NT)
                out = part if out is None else out + part
                yield
            total = out[:, HEAD_DIM : HEAD_DIM + 1]
            heads_out[s, head] = (out[:, :HEAD_DIM] * (1.0 / total)).astype(BF16)
            heads_lse[s, head] = peak + jnp.log(total)

    scores_a, scores_b = (low_a, high_a), (low_b, high_b)

    def pair_step(pair, carry):
        head = 2 * pair
        weave(scores_of(head + 1, scores_b, top_b), weigh(head, scores_a, top_a))
        following = jnp.minimum(head + 2, HEADS - 1)
        weave(scores_of(following, scores_a, top_a), weigh(head + 1, scores_b, top_b))
        return carry

    weave(scores_of(0, scores_a, top_a))
    lax.fori_loop(0, HEADS // 2, pair_step, 0)
    lane = lax.broadcasted_iota(jnp.int32, (span, TILE), 1)
    for s in range(2):
        out_ref[s * span : (s + 1) * span, :] = jnp.concatenate(
            [heads_out[s, head] for head in range(HEADS)], axis=1
        )
        lse = jnp.zeros((span, TILE), F32)
        for head in range(HEADS):
            lse = jnp.where(lane == head, heads_lse[s, head], lse)
        lse_ref[s] = lse


def attention_specs(span, docs, row=None):
    at = lambda i: i if row is None else row
    kv_spec = pl.BlockSpec((1, 2 * span, KV_COLS), lambda i, s: (at(i), 0, 0))
    return [
        pl.BlockSpec((2, Q_COLS, span), lambda i, s: (at(i), 0, 0)),
        kv_spec,
        kv_spec,
        kv_spec,
        kv_spec,
        pl.BlockSpec((None, 1, docs.shape[-1]), lambda i, s: (at(i), 0, 0)),
    ]


def attend(order, seq_id, qf, sources, docs):
    rows, _, length = docs.shape
    span = qf.shape[-1]
    width = HEADS * HEAD_DIM
    return order.call(
        functools.partial(attend_kernel, 0),
        (qf, *sources, docs),
        scalars=(seq_id,),
        grid=(rows,),
        in_specs=attention_specs(span, docs),
        out_specs=[
            pl.BlockSpec((2 * span, width), lambda i, s: (i, 0)),
            pl.BlockSpec((2, span, TILE), lambda i, s: (i, 0, 0)),
        ],
        scratch=[
            pltpu.VMEM((length, KV_COLS), BF16),
            pltpu.VMEM((KV_COLS, length), F32),
            pltpu.VMEM((span, 5 * TILE), F32),
            pltpu.VMEM((span, 7 * TILE), F32),
            pltpu.VMEM((2 * RANK_KV * HEADS, 1, length), F32),
            pltpu.VMEM((2, RANK_Q * HEADS, 1, span), F32),
            pltpu.VMEM((2, HEADS, span, HEAD_DIM), BF16),
            pltpu.VMEM((2, HEADS, span, 1), F32),
            pltpu.VMEM((span, 5 * TILE), F32),
            pltpu.VMEM((span, 5 * TILE), F32),
            pltpu.VMEM((span, 7 * TILE), F32),
            pltpu.VMEM((span, 7 * TILE), F32),
            pltpu.VMEM((2, span, 1), F32),
            pltpu.VMEM((2, span, 1), F32),
        ],
        out_shape=[
            jax.ShapeDtypeStruct((rows * 2 * span, width), BF16),
            jax.ShapeDtypeStruct((rows * 2, span, TILE), F32),
        ],
        mib=24,
        name="attend",
    )


def attend_back_kernel(
    row, seq_ref, qf_ref, kv0, kv1, kv2, kv3, doc_ref, lse_ref, att_ref, grad_ref,
    cos_ref, sin_ref, gq_ref, near_ref, far_ref,
    kvpos, kvt, bias, dot_t, stats, gkvt, gkvpos, gqt, gka, gqa, kva, qa,
    probs_a, probs_b, grads_a, grads_b, q_a, q_b, k_a, k_b, qb,
):
    seq_id = seq_ref[0]
    span = qf_ref.shape[-1]
    gather_keys(seq_id, (kv0, kv1, kv2, kv3), qf_ref, qa, qb, kvpos, kvt, kva, bias, doc_ref, row, span)
    width = HEADS * HEAD_DIM
    chooser = (
        lax.broadcasted_iota(jnp.int32, (width, TILE), 0) // HEAD_DIM
        == lax.broadcasted_iota(jnp.int32, (width, TILE), 1)
    ).astype(BF16)
    grad = grad_ref[0]
    dot_t[...] = grad.T
    product = grad.astype(F32) * att_ref[...].astype(F32)
    coarse = product.astype(BF16)
    fine = (product - coarse.astype(F32)).astype(BF16)
    centre = dot(coarse, chooser) + dot(fine, chooser)
    totals = jnp.concatenate([lse_ref[0], lse_ref[1]], axis=0)
    stats[0, :, 0, :] = -totals.T[:HEADS, :]
    stats[1, :, 0, :] = -centre.T[:HEADS, :]
    gkvt[...] = jnp.zeros_like(gkvt)
    gqt[...] = jnp.zeros_like(gqt)

    pieces = [piece_side(piece, seq_id) for piece in PIECES]
    split = RANK_KV * HEADS

    extra = lax.broadcasted_iota(jnp.int32, (16, 2 * span), 0)
    ones = jnp.ones((16, TILES * TILE), BF16)

    def with_row(value, row):
        coarse = row.astype(BF16).astype(F32)
        middle = (row - coarse).astype(BF16).astype(F32)
        fine = row - coarse - middle
        rest = jnp.where(extra == 0, coarse, jnp.where(extra == 1, middle, fine))
        return jnp.concatenate([value, jnp.where(extra < 3, rest, 0.0).astype(BF16)], axis=0)

    def scores_of(head, hold):
        probs_of, grads_of, q_of, k_of = hold
        rows = pl.ds(aligned(head * HEAD_DIM, HEAD_DIM), HEAD_DIM)
        keys = expand_pair(kvt, kva, 0, head)
        k_of[...] = keys
        keys = jnp.concatenate([keys, ones], axis=0)
        values = jnp.concatenate([expand_pair(kvt, kva, VALUE_BASE, head), ones], axis=0)
        yield
        total = None
        for r in range(RANK_Q):
            term = qa[r * HEADS + head] * qb[r * HEAD_DIM : (r + 1) * HEAD_DIM, :]
            total = term if total is None else total + term
        q_t = total.astype(BF16) * BF16(SCORE_SCALE)
        q_of[...] = q_t
        turned = with_row(q_t, stats[0, head]).T
        queries = [turned[:span], turned[span:]]
        turned = with_row(dot_t[rows, :], stats[1, head]).T
        grads = [turned[:span], turned[span:]]
        yield
        for cols, side, low in pieces:
            score = dot(choose(side, low, queries), keys[:, cols]) + bias[:, cols]
            probs = jnp.exp(score)
            grad_p = dot(choose(side, low, grads), values[:, cols])
            probs_of[:, cols] = probs.astype(BF16)
            grads_of[:, cols] = (probs * grad_p).astype(BF16)
            yield

    def grads_of_head(head, hold):
        probs_of, grads_of, q_of, k_of = hold
        rows = pl.ds(aligned(head * HEAD_DIM, HEAD_DIM), HEAD_DIM)
        q_t, g_t = q_of[...], dot_t[rows, :]
        q_sides = [q_t[:, :span], q_t[:, span:]]
        g_sides = [g_t[:, :span], g_t[:, span:]]
        yield
        grad_q = [None, None]
        for cols, side, low in pieces:
            grad_s = grads_of[:, cols]
            gather(grad_q, side, low, dot(k_of[:, cols], grad_s, NT), jnp.add, 0.0)
            for base, grad in (
                (0, dot(choose(side, low, q_sides), grad_s)),
                (VALUE_BASE, dot(choose(side, low, g_sides), probs_of[:, cols])),
            ):
                for r in range(RANK_KV):
                    where = base + split + r * HEAD_DIM
                    b_rows = slice(where, where + HEAD_DIM)
                    a_row = (base // VALUE_BASE) * split + r * HEADS + head
                    gka[a_row, :, cols] = jnp.sum(grad * kvt[b_rows, cols], axis=0, keepdims=True)
                    gkvt[b_rows, cols] += grad * kva[a_row, :, cols]
            yield
        both = jnp.concatenate(grad_q, axis=1)
        where = RANK_Q * HEADS
        for r in range(RANK_Q):
            b_rows = slice(r * HEAD_DIM, (r + 1) * HEAD_DIM)
            a_row = r * HEADS + head
            gqa[a_row] = jnp.sum(both * qb[b_rows, :], axis=0, keepdims=True)
            gqt[b_rows, :] += both * qa[a_row]
            if r % 2:
                yield

    def pair_step(pair, carry):
        head = 2 * pair
        weave(scores_of(head + 1, hold_b), grads_of_head(head, hold_a))
        following = jnp.minimum(head + 2, HEADS - 1)
        weave(scores_of(following, hold_a), grads_of_head(head + 1, hold_b))
        return carry

    hold_a, hold_b = (probs_a, grads_a, q_a, k_a), (probs_b, grads_b, q_b, k_b)
    weave(scores_of(0, hold_a))
    lax.fori_loop(0, HEADS // 2, pair_step, 0)
    half = HEAD_DIM // 2
    cos = jnp.concatenate([cos_ref[0], cos_ref[1]], axis=1)
    sin = jnp.concatenate([sin_ref[0], sin_ref[1]], axis=1)
    pieces = [gqa[:, 0, :] * (1.0 / RANK_Q)]
    for r in range(RANK_Q):
        at = r * HEAD_DIM
        first, second = gqt[at : at + half, :], gqt[at + half : at + HEAD_DIM, :]
        pieces += [first * cos + second * sin, second * cos - first * sin]
    back = jnp.concatenate(pieces, axis=0) * SCORE_SCALE
    back = jnp.concatenate([back, jnp.zeros((Q_PAD - Q_COLS, 2 * span), F32)], axis=0)
    gq_ref[...] = back.T.astype(BF16)
    split = RANK_KV * HEADS
    gkvt[:split, :] = gka[:split, 0, :] * (1.0 / RANK_KV)
    gkvt[VALUE_BASE : VALUE_BASE + split, :] = gka[split:, 0, :] * (1.0 / RANK_KV)
    gkvpos[...] = jnp.zeros_like(gkvpos)
    for tile in range(TILES):
        _, place = tile_place(tile, seq_id)
        rows = pl.ds(aligned(place * TILE, TILE), TILE)
        gkvpos[rows, :] += gkvt[:, tile * TILE : (tile + 1) * TILE].T
    for which in range(4):
        holder = seq_id ^ which
        target = near_ref if which in (0, 2) else far_ref
        for s, number in enumerate((holder, 7 - holder)):
            target[which // 2, s * span : (s + 1) * span, :] = gkvpos[
                pl.ds(aligned(number * span, 32), span), :
            ].astype(BF16)


def attend_back(order, row, seq_id, qf, sources, docs, lse, attended, grad_attended, cos, sin, after):
    length = docs.shape[-1]
    span = qf.shape[-1]
    width = HEADS * HEAD_DIM
    wide = pl.BlockSpec((1, 2 * span, width), lambda i, s: (row, 0, 0))
    rope = pl.BlockSpec((2, HEAD_DIM // 2, span), lambda i, s: (0, 0, 0))
    parts = pl.BlockSpec((2, 2 * span, KV_COLS), lambda i, s: (0, 0, 0))
    return order.call(
        functools.partial(attend_back_kernel, 0),
        (qf, *sources, docs, lse, attended, grad_attended, cos, sin),
        scalars=(seq_id,),
        grid=(1,),
        in_specs=attention_specs(span, docs, row)
        + [
            pl.BlockSpec((2, span, TILE), lambda i, s: (row, 0, 0)),
            pl.BlockSpec((2 * span, width), lambda i, s: (row, 0)),
            wide,
            rope,
            rope,
        ],
        out_specs=[pl.BlockSpec((2 * span, Q_PAD), lambda i, s: (0, 0)), parts, parts],
        scratch=[
            pltpu.VMEM((length, KV_COLS), BF16),
            pltpu.VMEM((KV_COLS, TILES * TILE), F32),
            pltpu.VMEM((span, TILES * TILE), F32),
            pltpu.VMEM((width, 2 * span), BF16),
            pltpu.VMEM((2, HEADS, 1, 2 * span), F32),
            pltpu.VMEM((KV_COLS, TILES * TILE), F32),
            pltpu.VMEM((length, KV_COLS), F32),
            pltpu.VMEM((RANK_Q * HEAD_DIM, 2 * span), F32),
            pltpu.VMEM((2 * RANK_KV * HEADS, 1, TILES * TILE), F32),
            pltpu.VMEM((RANK_Q * HEADS, 1, 2 * span), F32),
            pltpu.VMEM((2 * RANK_KV * HEADS, 1, TILES * TILE), F32),
            pltpu.VMEM((RANK_Q * HEADS, 1, 2 * span), F32),
            pltpu.VMEM((span, TILES * TILE), BF16),
            pltpu.VMEM((span, TILES * TILE), BF16),
            pltpu.VMEM((span, TILES * TILE), BF16),
            pltpu.VMEM((span, TILES * TILE), BF16),
            pltpu.VMEM((HEAD_DIM, 2 * span), BF16),
            pltpu.VMEM((HEAD_DIM, 2 * span), BF16),
            pltpu.VMEM((HEAD_DIM, TILES * TILE), BF16),
            pltpu.VMEM((HEAD_DIM, TILES * TILE), BF16),
            pltpu.VMEM((RANK_Q * HEAD_DIM, 2 * span), F32),
        ],
        out_shape=[
            jax.ShapeDtypeStruct((2 * span, Q_PAD), BF16),
            jax.ShapeDtypeStruct((2, 2 * span, KV_COLS), BF16),
            jax.ShapeDtypeStruct((2, 2 * span, KV_COLS), BF16),
        ],
        mib=32,
        name="attend_back",
        after=after,
    )


def out_kernel(x_ref, att_ref, w_ref, gain_ref, resid_ref, normed_ref):
    resid = x_ref[...].astype(F32) + dot(att_ref[...], w_ref[...])
    scale = lax.rsqrt(jnp.mean(resid * resid, axis=-1, keepdims=True) + EPS)
    resid_ref[...] = resid
    normed_ref[...] = (resid * scale * gain_ref[...]).astype(BF16)


def out_project(order, x, attended, w_out, gain):
    tokens, width = x.shape
    step = tokens // 2
    tile = pl.BlockSpec((step, width), lambda i: (i, 0))
    return order.call(
        out_kernel,
        (x, attended, w_out, gain),
        grid=(2,),
        in_specs=[
            tile,
            tile,
            once(w_out.shape, lambda i: (0, 0)),
            pl.BlockSpec((1, width), lambda i: (0, 0)),
        ],
        out_specs=[tile, tile],
        out_shape=[pltpu.HBM((tokens, width), F32), jax.ShapeDtypeStruct((tokens, width), BF16)],
        mib=20,
        name="out_project",
    )


def out_back_kernel(
    cot_ref, own_ref, other_ref, resid_ref, w_ref, gain_ref, gr_ref, gb_ref, ga_ref, gain_grad_ref
):
    grad = own_ref[...].astype(F32) + other_ref[...].astype(F32)
    values = resid_ref[...]
    scale = lax.rsqrt(jnp.mean(values * values, axis=-1, keepdims=True) + EPS)
    weighted = grad * gain_ref[...]
    back = scale * weighted - values * (scale * scale * scale) * jnp.mean(
        weighted * values, axis=-1, keepdims=True
    )
    grad_resid = cot_ref[...].astype(F32) + back
    branch = grad_resid.astype(BF16)
    gr_ref[...] = grad_resid
    gb_ref[...] = branch
    ga_ref[...] = dot(branch, w_ref[...], NT).astype(BF16)

    @pl.when(pl.program_id(0) == 0)
    def _():
        gain_grad_ref[...] = jnp.zeros_like(gain_grad_ref)

    gain_grad_ref[...] += jnp.sum(grad * values * scale, axis=0, keepdims=True)


def out_back(order, cot, own, other, resid, w_out, gain):
    tokens, width = cot.shape
    step = tokens // 2
    tile = pl.BlockSpec((step, width), lambda i: (i, 0))
    row = pl.BlockSpec((1, width), lambda i: (0, 0))
    return order.call(
        out_back_kernel,
        (cot, own, other, resid, w_out, gain),
        grid=(2,),
        in_specs=[tile, tile, tile, tile, once(w_out.shape, lambda i: (0, 0)), row],
        out_specs=[tile, tile, tile, row],
        out_shape=[
            jax.ShapeDtypeStruct((tokens, width), F32),
            jax.ShapeDtypeStruct((tokens, width), BF16),
            jax.ShapeDtypeStruct((tokens, width), BF16),
            jax.ShapeDtypeStruct((1, width), F32),
        ],
        mib=26,
        name="out_back",
    )


def hidden_back_kernel(own_ref, other_ref, w_ref, own_out, other_out):
    own_out[...] = dot(own_ref[...], w_ref[...], NT).astype(BF16)
    other_out[...] = dot(other_ref[...], w_ref[...], NT).astype(BF16)


def hidden_back(order, cot, cot_other, w_down, after):
    tokens, width = cot.shape
    half = w_down.shape[0]
    step = tokens // 2
    tile = pl.BlockSpec((step, width), lambda i: (i, 0))
    out = pl.BlockSpec((step, half), lambda i: (i, 0))
    shape = jax.ShapeDtypeStruct((tokens, half), BF16)
    return order.call(
        hidden_back_kernel,
        (cot, cot_other, w_down),
        grid=(2,),
        in_specs=[tile, tile, once(w_down.shape, lambda i: (0, 0))],
        out_specs=[out, out],
        out_shape=[shape, shape],
        mib=24,
        name="hidden_back",
        after=after,
    )


def ff_kernel(n2_ref, gh_ref, wg_ref, wu_ref, h_ref, gg_ref, gu_ref, back_ref):
    gate = dot(n2_ref[...], wg_ref[...])
    up = dot(n2_ref[...], wu_ref[...])
    grad_hidden = gh_ref[...].astype(F32)
    sigmoid = 1.0 / (1.0 + jnp.exp(-gate))
    silu = gate * sigmoid
    h_ref[...] = (silu * up).astype(BF16)
    gu = (grad_hidden * silu).astype(BF16)
    gg = (grad_hidden * up * (sigmoid + silu * (1.0 - sigmoid))).astype(BF16)
    gu_ref[...] = gu
    gg_ref[...] = gg
    back = dot(gg, wg_ref[...], NT) + dot(gu, wu_ref[...], NT)
    back_ref[...] = back.astype(back_ref.dtype)


def feed_forward(order, n2, grad_hidden, w_gate, w_up, dtype):
    tokens, width = n2.shape
    half = w_gate.shape[1]
    step = tokens // 2
    weight = once((width, half), lambda i: (0, 0))
    wide = pl.BlockSpec((step, width), lambda i: (i, 0))
    out = pl.BlockSpec((step, half), lambda i: (i, 0))
    return order.call(
        ff_kernel,
        (n2, grad_hidden, w_gate, w_up),
        grid=(2,),
        in_specs=[wide, out, weight, weight],
        out_specs=[out, out, out, wide],
        out_shape=[pltpu.HBM((tokens, half), BF16)] * 3
        + [(pltpu.HBM if dtype == F32 else jax.ShapeDtypeStruct)((tokens, width), dtype)],
        mib=30,
        name="feed_forward",
    )


def down_other_kernel(h_ref, w_ref, out_ref):
    out_ref[...] = dot(h_ref[...], w_ref[...]).astype(BF16)


def down_own_kernel(h_ref, w_ref, resid_ref, came_ref, out_ref):
    total = resid_ref[...] + came_ref[...].astype(F32) + dot(h_ref[...], w_ref[...])
    out_ref[...] = total.astype(BF16)


def down_project(order, hidden, w_down, resid=None, came=None):
    tokens, half = hidden.shape
    width = w_down.shape[1]
    step = tokens // 2
    wide = pl.BlockSpec((step, width), lambda i: (i, 0))
    extra = () if resid is None else (resid, came)
    return order.call(
        down_own_kernel if extra else down_other_kernel,
        (hidden, w_down, *extra),
        grid=(2,),
        in_specs=[
            pl.BlockSpec((step, half), lambda i: (i, 0)),
            once((half, width), lambda i: (0, 0)),
            *[wide] * len(extra),
        ],
        out_specs=[wide],
        out_shape=[jax.ShapeDtypeStruct((tokens, width), BF16)],
        mib=20,
        name="down_project",
    )[0]


class Grid:
    def __init__(self, rows_size, seq_size, rows_id, seq_id, width):
        self.high = [f"b{i}" for i in range(rows_size.bit_length() - 2, 0, -1)]
        self.axes = (*self.high, "y", "x", "c")
        self.block = width // (rows_size * seq_size)
        self.route = {"x": ("seq", 2, seq_size), "c": ("seq", 1, seq_size), "y": ("rows", 1, rows_size)}
        for i in range(1, rows_size.bit_length() - 1):
            self.route[f"b{i}"] = ("rows", 1 << i, rows_size)
        bits = []
        for axis in self.axes:
            name, mask, _ = self.route[axis]
            bits.append(((seq_id if name == "seq" else rows_id) // mask) % 2)
        self.bits = jnp.stack(bits).astype(jnp.int32)

    def place(self, axis):
        return self.axes.index(axis)

    def swap(self, value, axis):
        name, mask, size = self.route[axis]
        return lax.ppermute(value, name, [(i, i ^ mask) for i in range(size)])


class Chain:
    def __init__(self, axes, pieces):
        self.axes, self.pieces = axes, pieces


def fold_specs(grid, chain, axis):
    specs = []
    for value, axes, _, _ in chain.pieces:
        block, kinds = [], []
        for name in axes:
            if name == axis:
                block.append(None)
                kinds.append((grid.place(name), True))
            elif name in chain.axes:
                block.append(2)
                kinds.append(None)
            else:
                block.append(None)
                kinds.append((grid.place(name), False))

        def index(i, bits, kinds=tuple(kinds)):
            out = []
            for kind in kinds:
                if kind is None:
                    out.append(0)
                else:
                    out.append(1 - bits[kind[0]] if kind[1] else bits[kind[0]])
            return (*out, 0, 0)

        specs.append(pl.BlockSpec((*block, *value.shape[-2:]), index))
    return specs


def fold(order, grid, groups, after=()):
    args, specs, layout, shapes = [], [], [], []
    for chains, axis in groups:
        parts = []
        for chain in chains:
            parts.append([(lo, hi) for _, _, lo, hi in chain.pieces])
            args += [value for value, _, _, _ in chain.pieces]
            specs += fold_specs(grid, chain, axis)
        layout.append(parts)
        left = tuple(a for a in chains[0].axes if a != axis)
        cols = sum(c.pieces[0][3] - c.pieces[0][2] for c in chains)
        shapes.append((2,) * len(left) + (grid.block, cols))

    def kernel(bits_ref, *refs):
        inputs, outputs = iter(refs[: len(args)]), refs[len(args) :]
        for out, parts in zip(outputs, layout):
            sums = []
            for ranges in parts:
                total = None
                for lo, hi in ranges:
                    value = next(inputs)[..., lo:hi].astype(F32)
                    total = value if total is None else total + value
                sums.append(total.astype(BF16))
            out[...] = sums[0] if len(sums) == 1 else jnp.concatenate(sums, axis=-1)

    def whole(shape):
        return pl.BlockSpec(shape, lambda i, bits: (0,) * len(shape))

    sends = order.call(
        kernel,
        args,
        scalars=(grid.bits,),
        grid=(1,),
        in_specs=specs,
        out_specs=[whole(shape) for shape in shapes],
        out_shape=[jax.ShapeDtypeStruct(shape, BF16) for shape in shapes],
        mib=26,
        name="fold",
        after=after,
    )
    for (chains, axis), send in zip(groups, sends):
        came = grid.swap(send, axis)
        at = 0
        for chain in chains:
            left = tuple(a for a in chain.axes if a != axis)
            cols = chain.pieces[0][3] - chain.pieces[0][2]
            chain.pieces.append((came, left, at, at + cols))
            chain.axes = left
            at += cols
    return sends


def weight_grad(order, grid, axis, left, right, after=()):
    tokens, width = left[0].shape
    cols = right[0].shape[1]
    step = width // 2
    inner = grid.axes[1:]
    place = grid.place(axis)
    shape = (2,) * (len(grid.axes) - 1) + (grid.block, cols)

    def kernel(bits_ref, l0_ref, l1_ref, r0_ref, r1_ref, send_ref, keep_ref):
        total = dot(l0_ref[...], r0_ref[...], TN) + dot(l1_ref[...], r1_ref[...], TN)
        at = inner.index(axis)
        parts = total.astype(BF16).reshape(2**at, 2, step // 2 ** (at + 1), cols)
        upper = bits_ref[place] == 1
        send_ref[...] = jnp.where(upper, parts[:, 0], parts[:, 1]).reshape(step // 2, cols)
        keep_ref[...] = jnp.where(upper, parts[:, 1], parts[:, 0]).reshape(step // 2, cols)

    l_spec = pl.BlockSpec((tokens, step), lambda i, b: (0, i))
    r_spec = once((tokens, cols), lambda i, b: (0, 0))
    out = pl.BlockSpec((step // 2, cols), lambda i, b: (i, 0))
    send, keep = order.call(
        kernel,
        (left[0], left[1], right[0], right[1]),
        scalars=(grid.bits,),
        grid=(2,),
        in_specs=[l_spec, l_spec, r_spec, r_spec],
        out_specs=[out, out],
        out_shape=[jax.ShapeDtypeStruct((width // 2, cols), BF16)] * 2,
        mib=28,
        name="weight_grad",
        after=after,
    )
    axes = tuple(a for a in grid.axes if a != axis)
    came = grid.swap(send.reshape(shape), axis)
    return Chain(axes, [(keep.reshape(shape), axes, 0, cols), (came, axes, 0, cols)]), send


PART = 256


def weight_halves(order, grid, lefts, rights, gain_grad=None, spare=0):
    step = 256
    pairs = len(rights)
    size, cols = rights[0].shape
    width = lefts[0][0].shape[1]
    half = cols // 2
    parts = half // PART
    gains = [] if gain_grad is None else [gain_grad]
    place = grid.place("c")

    def kernel(bits_ref, *refs):
        mine_ref, other_refs = refs[-1 - parts], refs[-parts:]
        upper = bits_ref[place] == 1
        total = None
        for l_ref, r_ref in zip(refs[:pairs], refs[pairs : 2 * pairs]):
            part = dot(l_ref[...], r_ref[...], TN)
            total = part if total is None else total + part
        if gains:
            column = jnp.broadcast_to(refs[2 * pairs][...], (8, step)).T[:, 0:1]
            coarse = column.astype(BF16).astype(F32)
            lane = lax.broadcasted_iota(jnp.int32, (step, cols), 1)
            total = jnp.where(lane == spare, coarse, total)
            total = jnp.where(lane == spare + 1, column - coarse, total)
        total = total.astype(BF16)
        first, second = total[:, :half], total[:, half:]
        mine_ref[...] = jnp.where(upper, second, first)
        other = jnp.where(upper, first, second)
        for k, other_ref in enumerate(other_refs):
            other_ref[...] = other[:, k * PART : (k + 1) * PART]

    mine, *others = order.call(
        kernel,
        (*[value for value, _ in lefts], *rights, *gains),
        scalars=(grid.bits,),
        grid=(width // step,),
        in_specs=[
            *[pl.BlockSpec((size, step), lambda i, b, at=at: (at, i)) for _, at in lefts],
            *[once((size, cols), lambda i, b: (0, 0))] * pairs,
            *[pl.BlockSpec((1, step), lambda i, b: (0, i))] * len(gains),
        ],
        out_specs=[
            pl.BlockSpec((step, half), lambda i, b: (i, 0)),
            *[pl.BlockSpec((step, PART), lambda i, b: (i, 0))] * parts,
        ],
        out_shape=[
            jax.ShapeDtypeStruct((width, half), BF16),
            *[jax.ShapeDtypeStruct((width, PART), BF16)] * parts,
        ],
        mib=16,
        name="weight_halves",
    )
    lead = (2,) * len(grid.axes) + (grid.block,)
    mine = mine.reshape(lead + (half,))
    chains = []
    for k, other in enumerate(others):
        came = grid.swap(other, "c").reshape(lead + (PART,))
        held = [(mine, grid.axes, k * PART, (k + 1) * PART), (came, grid.axes, 0, PART)]
        chains.append(Chain(grid.axes, held))
    return chains


def weight_rows(order, grid, lefts, rights, gain_grad, spare):
    step = 256
    pairs = len(rights)
    size, cols = rights[0].shape
    width = lefts[0][0].shape[1]
    place = grid.place("c")
    block = grid.block

    def kernel(bits_ref, *refs):
        mine_ref, other_ref = refs[-2:]
        upper = bits_ref[place] == 1
        total = None
        for l_ref, r_ref in zip(refs[:pairs], refs[pairs : 2 * pairs]):
            part = dot(l_ref[...], r_ref[...], TN)
            total = part if total is None else total + part
        column = jnp.broadcast_to(refs[2 * pairs][...], (8, step)).T[:, 0:1]
        coarse = column.astype(BF16).astype(F32)
        lane = lax.broadcasted_iota(jnp.int32, (step, cols), 1)
        total = jnp.where(lane == spare, coarse, total)
        total = jnp.where(lane == spare + 1, column - coarse, total)
        parts = total.reshape(step // (2 * block), 2, block, cols)
        first, second = parts[:, 0], parts[:, 1]
        flat = (step // 2, cols)
        mine_ref[...] = jnp.where(upper, second, first).reshape(flat).astype(BF16)
        other_ref[...] = jnp.where(upper, first, second).reshape(flat).astype(BF16)

    out = pl.BlockSpec((step // 2, cols), lambda i, b: (i, 0))
    mine, other = order.call(
        kernel,
        (*[value for value, _ in lefts], *rights, gain_grad),
        scalars=(grid.bits,),
        grid=(width // step,),
        in_specs=[
            *[pl.BlockSpec((size, step), lambda i, b, at=at: (at, i)) for _, at in lefts],
            *[once((size, cols), lambda i, b: (0, 0))] * pairs,
            pl.BlockSpec((1, step), lambda i, b: (0, i)),
        ],
        out_specs=[out, out],
        out_shape=[jax.ShapeDtypeStruct((width // 2, cols), BF16)] * 2,
        mib=16,
        name="weight_rows",
    )
    axes = grid.axes[:-1]
    shape = (2,) * len(axes) + (block, cols)
    came = grid.swap(other.reshape(shape), "c")
    return Chain(axes, [(mine.reshape(shape), axes, 0, cols), (came, axes, 0, cols)])


def settle(order, grid, chains, widths, mib):
    args, specs, ranges = [], [], []
    for chain in chains:
        specs += fold_specs(grid, chain, None)
        args += [value for value, _, _, _ in chain.pieces]
        ranges.append([(lo, hi) for _, _, lo, hi in chain.pieces])

    def kernel(bits_ref, *refs):
        inputs, outputs = iter(refs[: len(args)]), iter(refs[len(args) :])
        for pieces, width in zip(ranges, widths):
            total = functools.reduce(
                jnp.add, [next(inputs)[..., lo:hi].astype(F32) for lo, hi in pieces]
            )
            next(outputs)[...] = total[:, :width]
            column = total[:, width : width + 1] + total[:, width + 1 : width + 2]
            next(outputs)[...] = jnp.broadcast_to(column, (column.shape[0], TILE)).T[0:1, :]

    shapes = []
    for width in widths:
        shapes += [(grid.block, width), (1, grid.block)]
    return order.call(
        kernel,
        args,
        scalars=(grid.bits,),
        grid=(1,),
        in_specs=specs,
        out_specs=[pl.BlockSpec(shape, lambda i, b: (0, 0)) for shape in shapes],
        out_shape=[jax.ShapeDtypeStruct(shape, F32) for shape in shapes],
        mib=mib,
        name="settle",
    )


def conclude(order, grid, groups, widths, gains, mib, after=()):
    args, specs, ranges = [], [], []
    for group in groups:
        parts = []
        for chain in group:
            specs += fold_specs(grid, chain, None)
            args += [value for value, _, _, _ in chain.pieces]
            parts.append([(lo, hi) for _, _, lo, hi in chain.pieces])
        ranges.append(parts)
    place = grid.place("c")

    def kernel(bits_ref, *refs):
        inputs, outputs = iter(refs[: len(args)]), iter(refs[len(args) :])
        for parts, width, gained in zip(ranges, widths, gains):
            owns, lasts = [], []
            for pieces in parts:
                values = [next(inputs)[..., lo:hi].astype(F32) for lo, hi in pieces]
                owns.append(functools.reduce(jnp.add, values[:-1]))
                lasts.append(values[-1])
            own = owns[0] if len(owns) == 1 else jnp.concatenate(owns, axis=1)
            last = lasts[0] if len(lasts) == 1 else jnp.concatenate(lasts, axis=1)
            cols = own.shape[-1]
            out = next(outputs)
            gain = next(outputs) if gained else None

            def put(first, second):
                out[:, :cols] = first
                out[:, cols:] = second[:, : width - cols]
                if gain is not None:
                    at = width - cols
                    column = second[:, at : at + 1] + second[:, at + 1 : at + 2]
                    gain[...] = jnp.broadcast_to(column, (column.shape[0], TILE)).T[0:1, :]

            @pl.when(bits_ref[place] == 0)
            def _():
                put(own, last)

            @pl.when(bits_ref[place] == 1)
            def _():
                put(last, own)

    shapes = []
    for width, gained in zip(widths, gains):
        shapes.append((grid.block, width))
        if gained:
            shapes.append((1, grid.block))
    return order.call(
        kernel,
        args,
        scalars=(grid.bits,),
        grid=(1,),
        in_specs=specs,
        out_specs=[pl.BlockSpec(shape, lambda i, b: (0, 0)) for shape in shapes],
        out_shape=[jax.ShapeDtypeStruct(shape, F32) for shape in shapes],
        mib=mib,
        name="conclude",
        after=after,
    )


def finish_kernel(
    k0_ref, r0_ref, x0_ref, gq_ref, wq_ref, wkv_ref, x_ref, gain_ref, gr_ref, cos_ref, sin_ref,
    came_ref, gkv_ref, out_ref, gain_grad_ref,
):
    total = k0_ref[...].astype(F32) + r0_ref[...].astype(F32) + x0_ref[...].astype(F32)
    cos, sin = cos_ref[0], sin_ref[0]
    half = HEAD_DIM // 2
    split = RANK_KV * HEADS
    turned = total.T
    pieces = [turned[:split]]
    for r in range(RANK_KV):
        at = split + r * HEAD_DIM
        first, second = turned[at : at + half], turned[at + half : at + HEAD_DIM]
        pieces += [first * cos + second * sin, second * cos - first * sin]
    pieces.append(turned[split + RANK_KV * HEAD_DIM :])
    gkv = jnp.concatenate(pieces, axis=0).T.astype(BF16)
    gkv_ref[:, :KV_COLS] = gkv
    gkv_ref[:, KV_COLS:] = jnp.zeros((gkv.shape[0], KV_PAD - KV_COLS), BF16)
    grad = dot(gq_ref[:, :Q_COLS], wq_ref[...]) + dot(gkv, wkv_ref[...])
    values = x_ref[...].astype(F32)
    scale = lax.rsqrt(jnp.mean(values * values, axis=-1, keepdims=True) + EPS)
    weighted = grad * gain_ref[...]
    back = scale * weighted - values * (scale * scale * scale) * jnp.mean(
        weighted * values, axis=-1, keepdims=True
    )
    out_ref[...] = (gr_ref[...] + back).astype(BF16)

    @pl.when(pl.program_id(0) == 0)
    def _():
        gain_grad_ref[...] = came_ref[...]

    gain_grad_ref[...] += jnp.sum(grad * values * scale, axis=0, keepdims=True)


def finish(order, row, kept, near, far, gq, w_query, w_keyval, x, gain, grad_resid, cos, sin, came, held):
    tokens, width = x.shape
    span = cos.shape[-1]
    full = lambda i: (0, 0)
    tile = pl.BlockSpec((span, width), lambda i: (2 * row + i, 0))
    part = pl.BlockSpec((None, span, KV_COLS), lambda i: (0, i, 0))
    rope = pl.BlockSpec((1, HEAD_DIM // 2, span), lambda i: (i, 0, 0))
    vector = pl.BlockSpec((1, width), full)
    extra = () if held is None else (held,)

    def kernel(*refs):
        finish_kernel(*refs[:12], *refs[12 + len(extra) :])

    return order.call(
        kernel,
        (kept, near, far, gq, w_query, w_keyval, x, gain, grad_resid, cos, sin, came, *extra),
        grid=(2,),
        in_specs=[
            part,
            part,
            pl.BlockSpec((span, KV_COLS), lambda i: (i, 0)),
            pl.BlockSpec((span, Q_PAD), lambda i: (i, 0)),
            once((Q_COLS, width), full),
            once((KV_COLS, width), full),
            tile,
            vector,
            tile,
            rope,
            rope,
            vector,
            *[pl.BlockSpec(memory_space=pl.ANY)] * len(extra),
        ],
        out_specs=[pl.BlockSpec((span, KV_PAD), lambda i: (i, 0)), tile, vector],
        out_shape=[
            jax.ShapeDtypeStruct((2 * span, KV_PAD), BF16),
            jax.ShapeDtypeStruct((tokens, width), BF16),
            jax.ShapeDtypeStruct((1, width), F32),
        ],
        mib=20,
        name="finish",
        aliases={12: 1} if extra else None,
    )


def meet_kernel(near_ref, far_ref, out_ref):
    out_ref[...] = (near_ref[...].astype(F32) + far_ref[...].astype(F32)).astype(BF16)


def meet(order, near, far):
    shape = near.shape[1:]
    part = pl.BlockSpec((None, *shape), lambda i: (1, 0, 0))
    return order.call(
        meet_kernel,
        (near, far),
        grid=(1,),
        in_specs=[part, part],
        out_specs=[pl.BlockSpec(shape, lambda i: (0, 0))],
        out_shape=[jax.ShapeDtypeStruct(shape, BF16)],
        mib=8,
        name="meet",
    )[0]


def body(
    layer_input,
    doc_ids,
    norm1_gain,
    w_query,
    w_keyval,
    w_out,
    norm2_gain,
    w_gate,
    w_up,
    w_down,
    cotangent,
):
    row_count, local_len, width = layer_input.shape
    seq_size = lax.axis_size("seq")
    rows_size = lax.axis_size("rows")
    seq_id = lax.axis_index("seq")
    rows_id = lax.axis_index("rows")
    span = local_len // 2
    tokens = row_count * local_len
    length = local_len * seq_size
    core = seq_id % 2
    order = Order()
    grid = Grid(rows_size, seq_size, rows_id, seq_id, width)
    seq_arg = seq_id.astype(jnp.int32).reshape(1)

    x = layer_input.reshape(tokens, width)
    cot = cotangent.reshape(tokens, width)
    cot_other = grid.swap(cot, "c")
    gain1 = norm1_gain.reshape(1, width)
    gain2 = norm2_gain.reshape(1, width)
    wq_t, wkv_t = w_query.T, w_keyval.T
    docs = doc_ids.reshape(row_count, 1, length)

    spans = jnp.stack([seq_id, 2 * seq_size - 1 - seq_id])
    positions = spans[:, None] * span + jnp.arange(span, dtype=jnp.int32)[None, :]
    inv_freq = ROPE_BASE ** (-(jnp.arange(HEAD_DIM // 2, dtype=F32) * (2.0 / HEAD_DIM)))
    angles = positions.astype(F32)[:, None, :] * inv_freq[None, :, None]
    cos, sin = jnp.cos(angles), jnp.sin(angles)

    normed, qf, kv = project(order, x, gain1, wq_t, wkv_t, cos, sin)
    kv = kv.reshape(row_count, local_len, KV_COLS)
    kv_x = grid.swap(kv, "x")
    kv_core = grid.swap(kv, "c")
    half = w_gate.shape[1] // 2
    wg = lax.dynamic_slice_in_dim(w_gate, core * half, half, 1)
    wu = lax.dynamic_slice_in_dim(w_up, core * half, half, 1)
    wd = lax.dynamic_slice_in_dim(w_down, core * half, half, 0)
    gh_own, gh_oth = hidden_back(order, cot, cot_other, wd, (wg, wu))
    kv_x, _ = lax.optimization_barrier((kv_x, order.token))
    kv_both = grid.swap(kv_x, "c")
    sources = (kv, kv_core, kv_x, kv_both)
    attended, lse = attend(order, seq_arg, qf, sources, docs)
    resid, normed2 = out_project(order, x, attended, w_out, gain2)
    normed2_other = grid.swap(normed2, "c")
    h_own, gg_own, gu_own, gn2_own = feed_forward(order, normed2, gh_own, wg, wu, BF16)
    h_oth, gg_oth, gu_oth, gn2_send = feed_forward(order, normed2_other, gh_oth, wg, wu, BF16)
    gn2_came = grid.swap(gn2_send, "c")

    first, second = grid.high[-1], grid.high[:-1]
    down, _ = weight_grad(
        order, grid, "x", (stay(cot), stay(cot_other)), (stay(h_own), stay(h_oth))
    )
    gate, _ = weight_grad(order, grid, "y", (normed2, normed2_other), (gg_own, gg_oth))
    up, _ = weight_grad(order, grid, first, (normed2, normed2_other), (gu_own, gu_oth))
    grad_resid, branch, grad_att, grad_norm2 = out_back(
        order, cot, gn2_own, gn2_came, resid, w_out, gain2
    )
    out = weight_halves(order, grid, [(branch, 0)], [attended])
    grad_att = grad_att.reshape(row_count, local_len, width)

    def back(row, after=()):
        gq, near, far = attend_back(
            order, row, seq_arg, qf, sources, docs, lse, attended, grad_att, cos, sin, after
        )
        return gq, near, grid.swap(far, "c")

    def end(row, near, far, came, gq, gain, held):
        return finish(
            order, row, near, far, came, gq, wq_t, wkv_t, x, gain1, grad_resid, cos, sin, gain, held
        )

    gq0, near0, far0 = back(0)
    fold(order, grid, [([down], "y"), ([gate], "x"), (out, first)])
    came0 = grid.swap(meet(order, near0, far0), "x")
    gq1, near1, far1 = back(1)
    upper = [up, *out]
    fold(order, grid, [([down, gate], first)])
    fold(order, grid, [(upper, "y")], after=(came0,))
    came1 = grid.swap(meet(order, near1, far1), "x")
    gkv0, ig0, gain0 = end(0, near0, far0, came0, gq0, jnp.zeros((1, width), F32), None)
    query = weight_rows(
        order, grid, [(normed, 0), (normed, 1)], [gq0, gq1], grad_norm2, Q_COLS
    )
    down_send = down_project(order, h_oth, wd)
    down_came = grid.swap(down_send, "c")
    gkv1, input_grad, grad_norm1 = end(1, near1, far1, came1, gq1, gain0, ig0)
    keyval = weight_rows(
        order, grid, [(normed, 0), (normed, 1)], [gkv0, gkv1], grad_norm1, KV_COLS
    )
    fold(order, grid, [([down, gate], second[0])])
    fold(order, grid, [([keyval], "x"), ([query], "y")])
    fold(order, grid, [(upper, "x")])
    for axis in second[1:]:
        fold(order, grid, [([down, gate], axis)])
    fold(order, grid, [([keyval], "y"), ([query], "x")])
    fold(order, grid, [(upper, second[0])])
    for axis in second[1:]:
        fold(order, grid, [(upper, axis)])
    late = [keyval, query]
    fold(order, grid, [(late, first)])
    for axis in second:
        fold(order, grid, [(late, axis)])
    fold(order, grid, [([down, gate, *upper], "c")])
    layer_output = down_project(order, h_own, wd, resid, down_came)
    g_down, g_gate, g_up, g_out = conclude(
        order,
        grid,
        [[down], [gate], [up], out],
        [*[w.shape[1] for w in (w_gate, w_gate, w_up)], width],
        [False] * 4,
        24,
    )
    g_query, g_norm2, g_keyval, g_norm1 = settle(
        order, grid, [query, keyval], [Q_COLS, KV_COLS], 8
    )
    return (
        layer_output.reshape(row_count, local_len, width),
        input_grad.reshape(row_count, local_len, width),
        g_norm1.reshape(-1),
        g_query,
        g_keyval,
        g_out.T,
        g_norm2.reshape(-1),
        g_gate,
        g_up,
        g_down.T,
    )


def solution(mesh):
    return jax.shard_map(
        body,
        mesh=mesh,
        in_specs=(
            P("rows", "seq", None),
            P("rows", None),
            P(),
            P(),
            P(),
            P(),
            P(),
            P(),
            P(),
            P(),
            P("rows", "seq", None),
        ),
        out_specs=(
            P("rows", "seq", None),
            P("rows", "seq", None),
            P(("rows", "seq")),
            P(("rows", "seq"), None),
            P(("rows", "seq"), None),
            P(None, ("rows", "seq")),
            P(("rows", "seq")),
            P(("rows", "seq"), None),
            P(("rows", "seq"), None),
            P(None, ("rows", "seq")),
        ),
        check_vma=False,
    )
```
